32 devices in a mesh: expert: 4 (over y, x), dp: 4 (over z), segment: 2 (over core).
Axes of the slice: x: 2, y: 2, z: 4, core: 2. Of those that a mesh axis runs over, the one named last changes fastest.
Arguments:
- hidden_in: bfloat16 [256, 4, 4096], P(('expert', 'dp'), None, 'segment'), may hold values from -6 to 6
- cotangent: bfloat16 [256, 4, 4096], P(('expert', 'dp'), None, 'segment'), may hold values from -6 to 6
- cluster_ids: int32 [256], P(('expert', 'dp')), may hold values from 0 to 3, as said below
- w_down: bfloat16 [4, 2, 4096, 256], P('expert', 'segment'), may hold values from -0.09375 to 0.09375
- w_up: bfloat16 [4, 2, 256, 4096], P('expert', 'segment'), may hold values from -0.375 to 0.375
- gain: bfloat16 [4, 2, 4096], P('expert', 'segment'), may hold values from 0.25 to 1.75
Outputs:
- out_hidden: bfloat16 [256, 4, 4096], P(('expert', 'dp'), None, 'segment')
- grad_down: bfloat16 [4, 2, 4096, 256], P('expert', 'segment', 'dp')
- grad_up: bfloat16 [4, 2, 256, 4096], P('expert', 'segment', None, 'dp')
The draws below stay inside these ranges and needn't reach their ends.
Inputs may be any that keep to these rules, and one draw needn't show every extreme that they name: `cluster_ids`: within each aligned block of 16 sequences (the sequences of one loader) no cluster appears more than 8 times, and one cluster, the same in every block, appears exactly 8 times in each block.
All inputs are finite; a program needn't handle non-finite values.
Results may differ from the reference program's by a relative error of at most 0.034.
Values may be sent and summed in bfloat16 or wider, within the bound.
No kernel may reach another device: no remote copies, remote signals or barrier semaphores. Data moves between devices by JAX's collectives and lax.ppermute only.
A program may use at most 64 MiB of HBM per device.

```python
import jax
import jax.numpy as jnp
from jax import lax

D = 4096
R = 256
L = 4
S_DEV = 16
EXPERTS = 4
SEGMENTS = 2
REPLICAS = 4
CAP = 8
SEQS = 256


def draw_cluster_ids(key, part):
    key = jax.random.fold_in(key, 7)
    key_hot, key_blocks = jax.random.split(key)
    favored = jax.random.randint(key_hot, (), 0, EXPERTS, dtype=jnp.int32)
    pool = jnp.arange(EXPERTS * CAP, dtype=jnp.int32) // CAP

    def one_block(block_key):
        first_key, second_key = jax.random.split(block_key)
        shuffled = pool[jax.random.permutation(first_key, EXPERTS * CAP)]
        order = jnp.argsort((shuffled != favored).astype(jnp.int32), stable=True)
        picked = shuffled[order][:S_DEV]
        return picked[jax.random.permutation(second_key, S_DEV)]
    block_keys = jax.random.split(key_blocks, SEQS // S_DEV)
    return jax.vmap(one_block)(block_keys).reshape(-1).astype(jnp.int32)


def block_scale(rng, extent, shards, smallest, high):
    loudness, own = 1.0, jax.random.fold_in(rng, 6)
    for axis_at, blocks in shards:
        steps = jnp.exp(jax.random.uniform(jax.random.fold_in(own, axis_at), (blocks,), jnp.float32, smallest / len(shards), high / len(shards)))
        loudness = loudness * jnp.repeat(steps, extent[axis_at] // blocks).reshape([-1 if axis == axis_at else 1 for axis in range(len(extent))])
    return loudness


def scatter_about(stream_key, extent, spread, most, shards=(), held_as=jnp.bfloat16):
    values = jax.random.normal(stream_key, extent, jnp.float32) * spread
    if len(shards) > 0:
        values = block_scale(stream_key, extent, shards, -0.22, 0.18) * values
    return jnp.clip(values, min=-most, max=most).astype(held_as)


def setup_inputs(seed: int = 0) -> dict:
    key_list = jax.random.split(jax.random.key(seed), 7)
    hidden_in = scatter_about(key_list[0], (SEQS, L, D), 1.0, 6.0, ((0, 16), (2, 2)))
    cotangent = scatter_about(key_list[1], (SEQS, L, D), 1.0, 6.0, ((0, 16), (2, 2)))
    cluster_ids = draw_cluster_ids(jax.random.fold_in(key_list[6], 71), 0)
    w_down = scatter_about(key_list[3], (EXPERTS, SEGMENTS, D, R), D ** -0.5, 0.09375, ((0, 4), (1, 2)))
    w_up = scatter_about(key_list[4], (EXPERTS, SEGMENTS, R, D), R ** -0.5, 0.375, ((0, 4), (1, 2)))
    gain = jnp.clip(1.0 + 0.15 * jax.random.normal(key_list[5], (EXPERTS, SEGMENTS, D), jnp.float32), 0.25, 1.75).astype(jnp.bfloat16)
    return {"hidden_in": hidden_in, "cotangent": cotangent, "cluster_ids": cluster_ids, "w_down": w_down, "w_up": w_up, "gain": gain}


EPS = 1e-05
C_ZERO = 0.7978845608028654
C_ONE = 0.044715

def gelu_value(z):
    return 0.5 * z * (1.0 + jnp.tanh(C_ZERO * (z + C_ONE * z * z * z)))

def gelu_slope(z):
    tval = jnp.tanh(C_ZERO * (z + C_ONE * z * z * z))
    return 0.5 * (1.0 + tval) + 0.5 * z * (1.0 - tval * tval) * C_ZERO * (1.0 + 3.0 * C_ONE * z * z)

def normalize(hidden):
    wide = hidden.astype(jnp.float32)
    center = wide - lax.optimization_barrier(jnp.mean(wide, axis=-1, keepdims=True))
    inverse = lax.rsqrt(lax.optimization_barrier(jnp.mean(center * center, axis=-1, keepdims=True)) + EPS)
    return (wide, center * inverse, inverse)

def phase_forward(hidden, w_dn, w_upper, scale):
    wide, normed, inverse = normalize(hidden)
    lowered = (normed * scale).astype(jnp.bfloat16)
    pre = jnp.dot(lowered, w_dn, preferred_element_type=jnp.float32)
    act = gelu_value(pre).astype(jnp.bfloat16)
    return (wide + jnp.dot(act, w_upper, preferred_element_type=jnp.float32)).astype(jnp.bfloat16)

def phase_backward(hidden, grad_in, w_dn, w_upper, scale):
    wide, normed, inverse = normalize(hidden)
    lowered = (normed * scale).astype(jnp.bfloat16)
    pre = jnp.dot(lowered, w_dn, preferred_element_type=jnp.float32)
    act = gelu_value(pre).astype(jnp.bfloat16)
    d_act = jnp.dot(grad_in, w_upper.T, preferred_element_type=jnp.float32)
    d_pre = (d_act * gelu_slope(pre)).astype(jnp.bfloat16)
    d_low = jnp.dot(d_pre, w_dn.T, preferred_element_type=jnp.float32)
    d_norm = d_low * scale
    d_wide = inverse * (d_norm - lax.optimization_barrier(jnp.mean(d_norm, axis=-1, keepdims=True)) - normed * lax.optimization_barrier(jnp.mean(d_norm * normed, axis=-1, keepdims=True)))
    grad_out = (grad_in.astype(jnp.float32) + d_wide).astype(jnp.bfloat16)
    return (grad_out, lowered, act, d_pre)

def group_product(left, right):
    lf = left.astype(jnp.float32).reshape(REPLICAS, -1, left.shape[-1])
    rf = right.astype(jnp.float32).reshape(REPLICAS, -1, right.shape[-1])
    part = jnp.einsum('gtx,gty->gxy', lf, rf, precision=lax.Precision.HIGHEST)
    rounded = lax.optimization_barrier(part.astype(jnp.bfloat16))
    return lax.optimization_barrier(jnp.sum(rounded.astype(jnp.float32), axis=0)).astype(jnp.bfloat16)

def reference(hidden_in, cotangent, cluster_ids, w_down, w_up, gain):
    per = EXPERTS * CAP
    replica = jnp.arange(SEQS, dtype=jnp.int32) // S_DEV % REPLICAS

    def one_cluster(total, cluster):

        def pick(which):
            mask = (cluster_ids == cluster) & (replica == which)
            index = jnp.nonzero(mask, size=per, fill_value=0)[0].astype(jnp.int32)
            live = jnp.arange(per, dtype=jnp.int32) < jnp.sum(mask.astype(jnp.int32))
            return (index, live)
        index, live = jax.vmap(pick)(jnp.arange(REPLICAS, dtype=jnp.int32))
        index = index.reshape(-1)
        live = live.reshape(-1)[:, None, None]
        zero = jnp.zeros((), jnp.bfloat16)
        state = jnp.where(live, hidden_in[index], zero).reshape(-1, D)
        grad = jnp.where(live, cotangent[index], zero).reshape(-1, D)
        saved = []
        for phase in range(SEGMENTS):
            saved.append(state)
            state = phase_forward(state, w_down[cluster, phase], w_up[cluster, phase], gain[cluster, phase].astype(jnp.float32))
        result = jnp.where(live, state.reshape(-1, L, D), zero)
        total = total.at[index].add(result)
        downs, uppers = ([], [])
        for phase in reversed(range(SEGMENTS)):
            grad_next = grad
            grad, lowered, act, d_pre = phase_backward(saved[phase], grad_next, w_down[cluster, phase], w_up[cluster, phase], gain[cluster, phase].astype(jnp.float32))
            downs.append(group_product(lowered, d_pre))
            uppers.append(group_product(act, grad_next))
        return (total, (jnp.stack(downs[::-1]), jnp.stack(uppers[::-1])))
    total, (grad_down, grad_up) = lax.scan(one_cluster, jnp.zeros((SEQS, L, D), jnp.bfloat16), jnp.arange(EXPERTS, dtype=jnp.int32))
    return (total, grad_down, grad_up)
```

```python
import functools

import jax
import jax.numpy as jnp
from jax import lax
from jax.experimental import pallas as pl
from jax.experimental.pallas import tpu as pltpu
from jax.sharding import PartitionSpec as P

MICRO = 4


EPS = 1e-05
C_ZERO = 0.7978845608028654
C_ONE = 0.044715


def shifted(block, axis, distance):
    devices = range(lax.axis_size(axis))
    route = [(i - distance, i) for i in devices if i - distance in devices]
    return lax.ppermute(block, axis, route)


def from_root(block, axis, holder):
    block = jnp.where(lax.axis_index(axis) == holder, block, jnp.zeros_like(block))
    return lax.psum(block, axis)


def gelu_value(z):
    return 0.5 * z * (1.0 + jnp.tanh(C_ZERO * (z + C_ONE * z * z * z)))


def gelu_slope(z):
    tval = jnp.tanh(C_ZERO * (z + C_ONE * z * z * z))
    return 0.5 * (1.0 + tval) + 0.5 * z * (1.0 - tval * tval) * C_ZERO * (1.0 + 3.0 * C_ONE * z * z)


def normalize(hidden):
    wide = hidden.astype(jnp.float32)
    center = wide - jnp.mean(wide, axis=-1, keepdims=True)
    inverse = lax.rsqrt(jnp.mean(center * center, axis=-1, keepdims=True) + EPS)
    return (wide, center * inverse, inverse)


def phase_forward(hidden, w_dn, w_upper, scale):
    wide, normed, inverse = normalize(hidden)
    lowered = (normed * scale).astype(jnp.bfloat16)
    pre = jnp.dot(lowered, w_dn, preferred_element_type=jnp.float32)
    act = gelu_value(pre).astype(jnp.bfloat16)
    leaving = (wide + jnp.dot(act, w_upper, preferred_element_type=jnp.float32)).astype(
        jnp.bfloat16
    )
    return (leaving, pre)


def phase_backward(hidden, grad_in, pre, w_dn, w_upper, scale):
    wide, normed, inverse = normalize(hidden)
    lowered = (normed * scale).astype(jnp.bfloat16)
    act = gelu_value(pre).astype(jnp.bfloat16)
    d_act = jnp.dot(grad_in, w_upper.T, preferred_element_type=jnp.float32)
    d_pre = (d_act * gelu_slope(pre)).astype(jnp.bfloat16)
    d_low = jnp.dot(d_pre, w_dn.T, preferred_element_type=jnp.float32)
    d_norm = d_low * scale
    d_wide = inverse * (
        d_norm
        - jnp.mean(d_norm, axis=-1, keepdims=True)
        - normed * jnp.mean(d_norm * normed, axis=-1, keepdims=True)
    )
    grad_out = (grad_in.astype(jnp.float32) + d_wide).astype(jnp.bfloat16)
    return (grad_out, lowered, act, d_pre)


def put_slot(buffer, value, slot, valid):
    old_value = lax.dynamic_index_in_dim(buffer, slot, 0, keepdims=False)
    return lax.dynamic_update_index_in_dim(buffer, jnp.where(valid, value, old_value), slot, 0)


def on_device_pipelined(hidden_in, cotangent, cluster_ids, w_down, w_up, gain):
    experts = lax.axis_size("expert")
    phases = lax.axis_size("segment")
    phase = lax.axis_index("segment")
    s_local, length, quarter = hidden_in.shape
    capacity = 2 * s_local // experts
    slots = experts * capacity
    same = (cluster_ids[:, None] == cluster_ids[None, :]).astype(jnp.int32)
    earlier = jnp.sum(jnp.tril(same, -1), axis=1)
    target = cluster_ids * capacity + earlier
    place = (jnp.arange(slots, dtype=jnp.int32)[:, None] == target[None, :]).astype(jnp.bfloat16)

    def to_slots(local):
        flat = local.reshape(s_local, -1)
        moved = jnp.dot(place, flat, preferred_element_type=jnp.float32).astype(jnp.bfloat16)
        return moved.reshape((slots,) + local.shape[1:])

    full_in, full_cot = (
        lax.all_gather(hidden_in, "segment", axis=2, tiled=True),
        lax.all_gather(cotangent, "segment", axis=2, tiled=True),
    )
    slot_in, slot_cot = (
        lax.all_to_all(to_slots(full_in), "expert", split_axis=0, concat_axis=0, tiled=True),
        lax.all_to_all(to_slots(full_cot), "expert", split_axis=0, concat_axis=0, tiled=True),
    )
    width = slot_in.shape[2]
    micro_rows = slots * length // MICRO
    inputs = slot_in.reshape(MICRO, micro_rows, width)
    cots = slot_cot.reshape(MICRO, micro_rows, width)
    w_dn = w_down[0, 0]
    w_upper = w_up[0, 0]
    rank = w_dn.shape[1]
    scale = gain[0, 0].astype(jnp.float32)
    ticks = MICRO + phases - 1

    def forward_tick(tick, carry):
        received, saved, pres, results = carry
        which = tick - phase
        valid = (which >= 0) & (which < MICRO)
        slot = jnp.clip(which, 0, MICRO - 1)
        first = lax.dynamic_index_in_dim(inputs, jnp.minimum(tick, MICRO - 1), 0, keepdims=False)
        entering = jnp.where(phase == 0, first, received)
        leaving, pre = phase_forward(entering, w_dn, w_upper, scale)
        saved = put_slot(saved, entering, slot, valid)
        pres = put_slot(pres, pre, slot, valid)
        results = put_slot(results, leaving, slot, valid & (phase == phases - 1))
        received = shifted(leaving, "segment", 1)
        return (received, saved, pres, results)

    start = (
        jnp.zeros((micro_rows, width), jnp.bfloat16),
        jnp.zeros((MICRO, micro_rows, width), jnp.bfloat16),
        jnp.zeros((MICRO, micro_rows, rank), jnp.float32),
        jnp.zeros((MICRO, micro_rows, width), jnp.bfloat16),
    )
    received, saved, pres, results = lax.fori_loop(0, ticks, forward_tick, start)

    def backward_tick(tick, carry):
        received, lows, acts, dpres, grads = carry
        which = tick - (phases - 1 - phase)
        valid = (which >= 0) & (which < MICRO)
        slot = jnp.clip(which, 0, MICRO - 1)
        last = lax.dynamic_index_in_dim(cots, jnp.minimum(tick, MICRO - 1), 0, keepdims=False)
        grad_in = jnp.where(phase == phases - 1, last, received)
        hidden = lax.dynamic_index_in_dim(saved, slot, 0, keepdims=False)
        pre = lax.dynamic_index_in_dim(pres, slot, 0, keepdims=False)
        grad_out, lowered, act, d_pre = phase_backward(hidden, grad_in, pre, w_dn, w_upper, scale)
        lows = put_slot(lows, lowered, slot, valid)
        acts = put_slot(acts, act, slot, valid)
        dpres = put_slot(dpres, d_pre, slot, valid)
        grads = put_slot(grads, grad_in, slot, valid)
        received = shifted(grad_out, "segment", -1)
        return (received, lows, acts, dpres, grads)

    start_back = (
        jnp.zeros((micro_rows, width), jnp.bfloat16),
        jnp.zeros((MICRO, micro_rows, width), jnp.bfloat16),
        jnp.zeros((MICRO, micro_rows, rank), jnp.bfloat16),
        jnp.zeros((MICRO, micro_rows, rank), jnp.bfloat16),
        jnp.zeros((MICRO, micro_rows, width), jnp.bfloat16),
    )
    received, lows, acts, dpres, grads = lax.fori_loop(0, ticks, backward_tick, start_back)
    contract = (((0,), (0,)), ((), ()))
    grad_dn = lax.dot_general(
        lows.reshape(-1, width),
        dpres.reshape(-1, rank),
        contract,
        preferred_element_type=jnp.float32,
    )
    grad_upper = lax.dot_general(
        acts.reshape(-1, rank),
        grads.reshape(-1, width),
        contract,
        preferred_element_type=jnp.float32,
    )
    summed_dn, summed_upper = (
        lax.psum_scatter(
            grad_dn.astype(jnp.bfloat16), "dp", scatter_dimension=0, tiled=True
        ).astype(jnp.float32),
        lax.psum_scatter(
            grad_upper.astype(jnp.bfloat16), "dp", scatter_dimension=1, tiled=True
        ).astype(jnp.float32),
    )
    returned = from_root(results, "segment", phases - 1)
    returned = returned.reshape(slots, length, width)
    own = lax.dynamic_slice_in_dim(returned, phase * quarter, quarter, 2)
    back = lax.all_to_all(own, "expert", split_axis=0, concat_axis=0, tiled=True)
    out_hidden = jnp.dot(place.T, back.reshape(slots, -1), preferred_element_type=jnp.float32)
    out_hidden = out_hidden.astype(jnp.bfloat16).reshape(s_local, length, quarter)
    return (
        out_hidden,
        summed_dn.astype(jnp.bfloat16)[None, None],
        summed_upper.astype(jnp.bfloat16)[None, None],
    )


CHUNK = 512
VMEM_LIMIT = 56 * 1024 * 1024
TRANS_RHS = (((1,), (1,)), ((), ()))
TRANS_LHS = (((0,), (0,)), ((), ()))


def matmul(left, right):
    return jnp.dot(left, right, preferred_element_type=jnp.float32)


def placement(ids_row, ids_col, length, capacity, slots):
    rows = ids_row.shape[1]
    at_col = lax.broadcasted_iota(jnp.int32, (rows, rows), 0)
    at_row = lax.broadcasted_iota(jnp.int32, (rows, rows), 1)
    first_token = lax.rem(at_col, length) == 0
    before = at_col // length < at_row // length
    counted = (ids_col == ids_row) & first_token & before
    rank = jnp.sum(counted.astype(jnp.int32), axis=0, keepdims=True)
    token = lax.rem(at_row[:1], length)
    target = (ids_row * capacity + rank) * length + token
    packed = lax.broadcasted_iota(jnp.int32, (slots * length, rows), 0)
    return (packed == target).astype(jnp.float32).astype(jnp.bfloat16)


def pack_kernel(length, capacity, slots, ids_row, ids_col, hidden, cot, send):
    place = placement(ids_row[...], ids_col[...], length, capacity, slots)
    groups, _, rows, _ = send.shape
    for which, source in enumerate((hidden, cot)):
        moved = matmul(place, source[...]).astype(jnp.bfloat16)
        for group in range(groups):
            send[group, which] = moved[group * rows : (group + 1) * rows]


def unpack_kernel(length, capacity, slots, ids_row, ids_col, back, out):
    place = placement(ids_row[...], ids_col[...], length, capacity, slots)
    groups, rows, width = back.shape
    stacked = back[...].reshape(groups * rows, width)
    out[...] = lax.dot_general(
        place, stacked, TRANS_LHS, preferred_element_type=jnp.float32
    ).astype(jnp.bfloat16)


def split_three(value):
    top = value.astype(jnp.bfloat16)
    rest = value - top.astype(jnp.float32)
    mid = rest.astype(jnp.bfloat16)
    low = (rest - mid.astype(jnp.float32)).astype(jnp.bfloat16)
    return [top.astype(jnp.float32), mid.astype(jnp.float32), low.astype(jnp.float32)]


def chain_kernel(
    recv, own_dn, own_up, own_gain, other_dn, other_up, other_gain,
    out, small,
    dn_buf, up_buf, gain_buf, entering, middle, d_norms, sems,
):
    phase = lax.axis_index("segment")
    experts, phases, _, rows, part = recv.shape
    tokens = experts * rows
    width = phases * part
    rank = dn_buf.shape[2]

    def fetch(source, buffer, index):
        return pltpu.make_async_copy(source, buffer.at[index], sems.at[index])

    own = ((own_dn, dn_buf, 0), (own_up, up_buf, 2), (own_gain, gain_buf, 4))
    other = ((other_dn, dn_buf, 0), (other_up, up_buf, 2), (other_gain, gain_buf, 4))

    def copies(sources, at):
        return [
            pltpu.make_async_copy(source, buffer.at[at], sems.at[base + at])
            for source, buffer, base in sources
        ]

    for at in range(2):
        mine = phase == at

        @pl.when(mine)
        def _():
            for copy in copies(own, at):
                copy.start()

        @pl.when(jnp.logical_not(mine))
        def _():
            for copy in copies(other, at):
                copy.start()

    waits = [copies(own, at) for at in range(2)]

    def block(which, col):
        half, start = col // part, col % part
        return jnp.concatenate(
            [recv[e, half, which, :, start : start + CHUNK] for e in range(experts)], axis=0
        )

    def lanes(value):
        total = value[:, :128]
        for start in range(128, value.shape[1], 128):
            total = total + value[:, start : start + 128]
        return total

    def row_sum(parts):
        return jnp.sum(parts, axis=1, keepdims=True)

    cols = range(0, width, CHUNK)
    total = jnp.zeros((tokens, 128), jnp.float32)
    for col in cols:
        value = block(0, col)
        entering[:, col : col + CHUNK] = value
        total = total + lanes(value.astype(jnp.float32))
    mean_0 = row_sum(total) / width
    total = jnp.zeros((tokens, 128), jnp.float32)
    for col in cols:
        center = entering[:, col : col + CHUNK].astype(jnp.float32) - mean_0
        total = total + lanes(center * center)
    inverse_0 = lax.rsqrt(row_sum(total) / width + EPS)

    waits[0][0].wait()
    waits[0][2].wait()
    pre_0 = jnp.zeros((tokens, rank), jnp.float32)
    for col in cols:
        at = slice(col, col + CHUNK)
        normed = (entering[:, at].astype(jnp.float32) - mean_0) * inverse_0
        lowered = (normed * gain_buf[0, :, at].astype(jnp.float32)).astype(jnp.bfloat16)
        pre_0 = pre_0 + matmul(lowered, dn_buf[0, at, :])
    act_0 = gelu_value(pre_0).astype(jnp.bfloat16)
    slope_0 = gelu_slope(pre_0)

    waits[0][1].wait()
    total = jnp.zeros((tokens, 128), jnp.float32)
    for col in cols:
        at = slice(col, col + CHUNK)
        value = (
            entering[:, at].astype(jnp.float32) + matmul(act_0, up_buf[0, :, at])
        ).astype(jnp.bfloat16)
        middle[:, at] = value
        total = total + lanes(value.astype(jnp.float32))
    mean_1 = row_sum(total) / width
    total = jnp.zeros((tokens, 128), jnp.float32)
    for col in cols:
        center = middle[:, col : col + CHUNK].astype(jnp.float32) - mean_1
        total = total + lanes(center * center)
    inverse_1 = lax.rsqrt(row_sum(total) / width + EPS)

    waits[1][0].wait()
    waits[1][2].wait()
    pre_1 = jnp.zeros((tokens, rank), jnp.float32)
    for col in cols:
        at = slice(col, col + CHUNK)
        normed = (middle[:, at].astype(jnp.float32) - mean_1) * inverse_1
        lowered = (normed * gain_buf[1, :, at].astype(jnp.float32)).astype(jnp.bfloat16)
        pre_1 = pre_1 + matmul(lowered, dn_buf[1, at, :])
    act_1 = gelu_value(pre_1).astype(jnp.bfloat16)
    slope_1 = gelu_slope(pre_1)

    waits[1][1].wait()
    d_act = jnp.zeros((tokens, rank), jnp.float32)
    for col in cols:
        at = slice(col, col + CHUNK)
        leaving = (
            middle[:, at].astype(jnp.float32) + matmul(act_1, up_buf[1, :, at])
        ).astype(jnp.bfloat16)
        half, start = col // part, col % part
        for e in range(experts):
            out[e, half, :, start : start + CHUNK] = leaving[e * rows : (e + 1) * rows]
        d_act = d_act + lax.dot_general(
            block(1, col), up_buf[1, :, at], TRANS_RHS, preferred_element_type=jnp.float32
        )
    d_pre_1 = (d_act * slope_1).astype(jnp.bfloat16)

    total = jnp.zeros((tokens, 128), jnp.float32)
    cross = jnp.zeros((tokens, 128), jnp.float32)
    for col in cols:
        at = slice(col, col + CHUNK)
        d_low = lax.dot_general(
            d_pre_1, dn_buf[1, at, :], TRANS_RHS, preferred_element_type=jnp.float32
        )
        d_norm = d_low * gain_buf[1, :, at].astype(jnp.float32)
        normed = (middle[:, at].astype(jnp.float32) - mean_1) * inverse_1
        d_norms[:, at] = d_norm
        total = total + lanes(d_norm)
        cross = cross + lanes(d_norm * normed)
    shift = row_sum(total) / width
    along = row_sum(cross) / width
    d_act = jnp.zeros((tokens, rank), jnp.float32)
    for col in cols:
        at = slice(col, col + CHUNK)
        normed = (middle[:, at].astype(jnp.float32) - mean_1) * inverse_1
        grad = (
            block(1, col).astype(jnp.float32)
            + inverse_1 * (d_norms[:, at] - shift - normed * along)
        ).astype(jnp.bfloat16)
        d_act = d_act + lax.dot_general(
            grad, up_buf[0, :, at], TRANS_RHS, preferred_element_type=jnp.float32
        )
    d_pre_0 = (d_act * slope_0).astype(jnp.bfloat16)

    for at, value in enumerate((act_0, act_1, d_pre_0, d_pre_1)):
        small[:, at * rank : (at + 1) * rank] = value
    lane = lax.broadcasted_iota(jnp.int32, (tokens, 128), 1)
    stats = jnp.zeros((tokens, 128), jnp.float32)
    at = 0
    for column in (mean_0, inverse_0, mean_1, inverse_1, shift, along):
        for piece in split_three(column):
            stats = jnp.where(lane == at, piece, stats)
            at += 1
    small[:, 4 * rank :] = stats.astype(jnp.bfloat16)


def gradient_kernel(
    mine, theirs, small, own_dn, own_up, own_gain, other_dn, other_up, other_gain,
    grad_dn, grad_upper,
    dn_buf, up_buf, gain_buf, lows, grads, sems,
):
    phase = lax.axis_index("segment")
    place = lax.axis_index("dp")
    sources, _, rows, half = mine.shape
    tokens = sources * rows
    slab = 2 * half
    rank = dn_buf.shape[1]
    features = pl.ds(pl.multiple_of(place * slab, slab), slab)

    def copies(up, gain_first, dn, gain_second):
        return (
            pltpu.make_async_copy(up.at[:, features], up_buf, sems.at[0]),
            pltpu.make_async_copy(dn.at[features, :], dn_buf, sems.at[1]),
            pltpu.make_async_copy(gain_first.at[:, features], gain_buf.at[0], sems.at[2]),
            pltpu.make_async_copy(gain_second.at[:, features], gain_buf.at[1], sems.at[3]),
        )

    @pl.when(phase == 0)
    def _():
        for copy in copies(own_up, own_gain, other_dn, other_gain):
            copy.start()

    @pl.when(phase != 0)
    def _():
        for copy in copies(other_up, other_gain, own_dn, own_gain):
            copy.start()

    for copy in copies(own_up, own_gain, other_dn, other_gain):
        copy.wait()

    def column(at, index):
        stats = small[at, 4 * rank :].astype(jnp.float32)
        base = 3 * index
        return (
            stats[:, base : base + 1]
            + stats[:, base + 1 : base + 2]
            + stats[:, base + 2 : base + 3]
        )

    for source in range(sources):
        at = slice(source * rows, (source + 1) * rows)
        mean_0, inverse_0, mean_1, inverse_1, shift, along = [
            column(at, index) for index in range(6)
        ]
        act_0 = small[at, :rank]
        d_pre_1 = small[at, 3 * rank : 4 * rank]
        for near, data in ((True, mine), (False, theirs)):
            core = phase if near else 1 - phase
            cols = pl.ds(pl.multiple_of(core * half, half), half)
            wide = data[source, 0].astype(jnp.float32)
            grad_in = data[source, 1]
            middle = (wide + matmul(act_0, up_buf[:, cols])).astype(jnp.bfloat16)
            normed = (middle.astype(jnp.float32) - mean_1) * inverse_1

            @pl.when(phase == 0)
            def _():
                first = (wide - mean_0) * inverse_0 * gain_buf[0, :, cols].astype(jnp.float32)
                lows[at, cols] = first.astype(jnp.bfloat16)
                d_norm = lax.dot_general(
                    d_pre_1, dn_buf[cols, :], TRANS_RHS, preferred_element_type=jnp.float32
                ) * gain_buf[1, :, cols].astype(jnp.float32)
                grads[at, cols] = (
                    grad_in.astype(jnp.float32)
                    + inverse_1 * (d_norm - shift - normed * along)
                ).astype(jnp.bfloat16)

            @pl.when(phase != 0)
            def _():
                second = normed * gain_buf[1, :, cols].astype(jnp.float32)
                lows[at, cols] = second.astype(jnp.bfloat16)
                grads[at, cols] = grad_in

    def finish(act, d_pre):
        grad_dn[...] = lax.dot_general(
            lows[...], d_pre, TRANS_LHS, preferred_element_type=jnp.float32
        ).astype(jnp.bfloat16)
        grad_upper[...] = lax.dot_general(
            act, grads[...], TRANS_LHS, preferred_element_type=jnp.float32
        ).astype(jnp.bfloat16)

    @pl.when(phase == 0)
    def _():
        finish(small[:, :rank], small[:, 2 * rank : 3 * rank])

    @pl.when(phase != 0)
    def _():
        finish(small[:, rank : 2 * rank], small[:, 3 * rank : 4 * rank])


VMEM = pl.BlockSpec(memory_space=pltpu.VMEM)
HBM = pl.BlockSpec(memory_space=pl.ANY)
PARAMS = pltpu.CompilerParams(vmem_limit_bytes=VMEM_LIMIT)


def on_device_two_phases(hidden_in, cotangent, cluster_ids, w_down, w_up, gain):
    experts = lax.axis_size("expert")
    replicas = lax.axis_size("dp")
    phases = lax.axis_size("segment")
    s_local, length, part = hidden_in.shape
    width = part * phases
    capacity = 2 * s_local // experts
    slots = experts * capacity
    groups = experts * phases
    rows = slots * length // groups
    tokens = experts * rows
    locals_ = s_local * length
    own = (w_down[0, 0], w_up[0, 0], gain[0])
    rank = own[0].shape[1]
    bf16 = jnp.bfloat16
    swap = [(i, phases - 1 - i) for i in range(phases)]
    other = tuple(lax.ppermute(array, "segment", swap) for array in own)

    ids = jnp.repeat(cluster_ids, length)
    ids_row, ids_col = ids[None, :], ids[:, None]
    sizes = (length, capacity, slots)
    send = pl.pallas_call(
        functools.partial(pack_kernel, *sizes),
        out_shape=jax.ShapeDtypeStruct((groups, 2, rows, part), bf16),
        in_specs=[VMEM] * 4,
        out_specs=VMEM,
        compiler_params=PARAMS,
        name="pack",
    )(ids_row, ids_col, hidden_in.reshape(locals_, part), cotangent.reshape(locals_, part))
    recv = lax.all_to_all(send, ("expert", "segment"), split_axis=0, concat_axis=0, tiled=True)
    recv = recv.reshape(experts, phases, 2, rows, part)

    lanes = replicas * phases
    piece = width // lanes
    per_half = part // piece
    slabs = recv.reshape(experts, phases, 2, rows, per_half, piece)
    slabs = slabs.transpose(1, 4, 2, 0, 3, 5).reshape(lanes, 2, tokens, piece)
    mine = lax.all_to_all(slabs, ("dp", "segment"), split_axis=0, concat_axis=0, tiled=True)
    theirs = lax.ppermute(mine, "segment", swap)

    out, small = pl.pallas_call(
        chain_kernel,
        out_shape=(
            jax.ShapeDtypeStruct((experts, phases, rows, part), bf16),
            jax.ShapeDtypeStruct((tokens, 4 * rank + 128), bf16),
        ),
        in_specs=[VMEM] + [HBM] * 6,
        out_specs=(VMEM, VMEM),
        scratch_shapes=[
            pltpu.VMEM((2, width, rank), bf16),
            pltpu.VMEM((2, rank, width), bf16),
            pltpu.VMEM((2, 1, width), bf16),
            pltpu.VMEM((tokens, width), bf16),
            pltpu.VMEM((tokens, width), bf16),
            pltpu.VMEM((tokens, width), jnp.float32),
            pltpu.SemaphoreType.DMA((6,)),
        ],
        compiler_params=PARAMS,
        name="chain",
    )(recv, *own, *other)

    back = lax.all_to_all(
        out.reshape(groups, rows, part), ("expert", "segment"), split_axis=0, concat_axis=0, tiled=True
    )
    out_hidden = pl.pallas_call(
        functools.partial(unpack_kernel, *sizes),
        out_shape=jax.ShapeDtypeStruct((locals_, part), bf16),
        in_specs=[VMEM] * 3,
        out_specs=VMEM,
        compiler_params=PARAMS,
        name="unpack",
    )(ids_row, ids_col, back).reshape(s_local, length, part)

    gathered = lax.all_gather(small, ("dp", "segment"), axis=0, tiled=True)
    slab = width // replicas
    grad_dn, grad_upper = pl.pallas_call(
        gradient_kernel,
        out_shape=(
            jax.ShapeDtypeStruct((slab, rank), bf16),
            jax.ShapeDtypeStruct((rank, slab), bf16),
        ),
        in_specs=[VMEM] * 3 + [HBM] * 6,
        out_specs=(VMEM, VMEM),
        scratch_shapes=[
            pltpu.VMEM((slab, rank), bf16),
            pltpu.VMEM((rank, slab), bf16),
            pltpu.VMEM((2, 1, slab), bf16),
            pltpu.VMEM((lanes * tokens, slab), bf16),
            pltpu.VMEM((lanes * tokens, slab), bf16),
            pltpu.SemaphoreType.DMA((4,)),
        ],
        compiler_params=PARAMS,
        name="gradients",
    )(mine, theirs, gathered, *own, *other)
    return (out_hidden, grad_dn[None, None], grad_upper[None, None])


def solution(mesh):
    two = mesh.shape["segment"] == 2
    on_device = on_device_two_phases if two else on_device_pipelined
    return jax.shard_map(
        on_device,
        mesh=mesh,
        in_specs=(
            P(("expert", "dp"), None, "segment"),
            P(("expert", "dp"), None, "segment"),
            P(("expert", "dp")),
            P("expert", "segment", None, None),
            P("expert", "segment", None, None),
            P("expert", "segment", None),
        ),
        out_specs=(
            P(("expert", "dp"), None, "segment"),
            P("expert", "segment", "dp", None),
            P("expert", "segment", None, "dp"),
        ),
        check_vma=False,
    )
```

```python
import functools

import jax
import jax.numpy as jnp
from jax import lax
from jax.experimental import pallas as pl
from jax.experimental.pallas import tpu as pltpu
from jax.sharding import PartitionSpec as P

MICRO = 4


EPS = 1e-05
C_ZERO = 0.7978845608028654
C_ONE = 0.044715


def shifted(block, axis, distance):
    devices = range(lax.axis_size(axis))
    route = [(i - distance, i) for i in devices if i - distance in devices]
    return lax.ppermute(block, axis, route)


def from_root(block, axis, holder):
    block = jnp.where(lax.axis_index(axis) == holder, block, jnp.zeros_like(block))
    return lax.psum(block, axis)


def gelu_value(z):
    return 0.5 * z * (1.0 + jnp.tanh(C_ZERO * (z + C_ONE * z * z * z)))


def gelu_slope(z):
    tval = jnp.tanh(C_ZERO * (z + C_ONE * z * z * z))
    return 0.5 * (1.0 + tval) + 0.5 * z * (1.0 - tval * tval) * C_ZERO * (1.0 + 3.0 * C_ONE * z * z)


def normalize(hidden):
    wide = hidden.astype(jnp.float32)
    center = wide - jnp.mean(wide, axis=-1, keepdims=True)
    inverse = lax.rsqrt(jnp.mean(center * center, axis=-1, keepdims=True) + EPS)
    return (wide, center * inverse, inverse)


def phase_forward(hidden, w_dn, w_upper, scale):
    wide, normed, inverse = normalize(hidden)
    lowered = (normed * scale).astype(jnp.bfloat16)
    pre = jnp.dot(lowered, w_dn, preferred_element_type=jnp.float32)
    act = gelu_value(pre).astype(jnp.bfloat16)
    leaving = (wide + jnp.dot(act, w_upper, preferred_element_type=jnp.float32)).astype(
        jnp.bfloat16
    )
    return (leaving, pre)


def phase_backward(hidden, grad_in, pre, w_dn, w_upper, scale):
    wide, normed, inverse = normalize(hidden)
    lowered = (normed * scale).astype(jnp.bfloat16)
    act = gelu_value(pre).astype(jnp.bfloat16)
    d_act = jnp.dot(grad_in, w_upper.T, preferred_element_type=jnp.float32)
    d_pre = (d_act * gelu_slope(pre)).astype(jnp.bfloat16)
    d_low = jnp.dot(d_pre, w_dn.T, preferred_element_type=jnp.float32)
    d_norm = d_low * scale
    d_wide = inverse * (
        d_norm
        - jnp.mean(d_norm, axis=-1, keepdims=True)
        - normed * jnp.mean(d_norm * normed, axis=-1, keepdims=True)
    )
    grad_out = (grad_in.astype(jnp.float32) + d_wide).astype(jnp.bfloat16)
    return (grad_out, lowered, act, d_pre)


def put_slot(buffer, value, slot, valid):
    old_value = lax.dynamic_index_in_dim(buffer, slot, 0, keepdims=False)
    return lax.dynamic_update_index_in_dim(buffer, jnp.where(valid, value, old_value), slot, 0)


def on_device_pipelined(hidden_in, cotangent, cluster_ids, w_down, w_up, gain):
    experts = lax.axis_size("expert")
    phases = lax.axis_size("segment")
    phase = lax.axis_index("segment")
    s_local, length, quarter = hidden_in.shape
    capacity = 2 * s_local // experts
    slots = experts * capacity
    same = (cluster_ids[:, None] == cluster_ids[None, :]).astype(jnp.int32)
    earlier = jnp.sum(jnp.tril(same, -1), axis=1)
    target = cluster_ids * capacity + earlier
    place = (jnp.arange(slots, dtype=jnp.int32)[:, None] == target[None, :]).astype(jnp.bfloat16)

    def to_slots(local):
        flat = local.reshape(s_local, -1)
        moved = jnp.dot(place, flat, preferred_element_type=jnp.float32).astype(jnp.bfloat16)
        return moved.reshape((slots,) + local.shape[1:])

    full_in, full_cot = (
        lax.all_gather(hidden_in, "segment", axis=2, tiled=True),
        lax.all_gather(cotangent, "segment", axis=2, tiled=True),
    )
    slot_in, slot_cot = (
        lax.all_to_all(to_slots(full_in), "expert", split_axis=0, concat_axis=0, tiled=True),
        lax.all_to_all(to_slots(full_cot), "expert", split_axis=0, concat_axis=0, tiled=True),
    )
    width = slot_in.shape[2]
    micro_rows = slots * length // MICRO
    inputs = slot_in.reshape(MICRO, micro_rows, width)
    cots = slot_cot.reshape(MICRO, micro_rows, width)
    w_dn = w_down[0, 0]
    w_upper = w_up[0, 0]
    rank = w_dn.shape[1]
    scale = gain[0, 0].astype(jnp.float32)
    ticks = MICRO + phases - 1

    def forward_tick(tick, carry):
        received, saved, pres, results = carry
        which = tick - phase
        valid = (which >= 0) & (which < MICRO)
        slot = jnp.clip(which, 0, MICRO - 1)
        first = lax.dynamic_index_in_dim(inputs, jnp.minimum(tick, MICRO - 1), 0, keepdims=False)
        entering = jnp.where(phase == 0, first, received)
        leaving, pre = phase_forward(entering, w_dn, w_upper, scale)
        saved = put_slot(saved, entering, slot, valid)
        pres = put_slot(pres, pre, slot, valid)
        results = put_slot(results, leaving, slot, valid & (phase == phases - 1))
        received = shifted(leaving, "segment", 1)
        return (received, saved, pres, results)

    start = (
        jnp.zeros((micro_rows, width), jnp.bfloat16),
        jnp.zeros((MICRO, micro_rows, width), jnp.bfloat16),
        jnp.zeros((MICRO, micro_rows, rank), jnp.float32),
        jnp.zeros((MICRO, micro_rows, width), jnp.bfloat16),
    )
    received, saved, pres, results = lax.fori_loop(0, ticks, forward_tick, start)

    def backward_tick(tick, carry):
        received, lows, acts, dpres, grads = carry
        which = tick - (phases - 1 - phase)
        valid = (which >= 0) & (which < MICRO)
        slot = jnp.clip(which, 0, MICRO - 1)
        last = lax.dynamic_index_in_dim(cots, jnp.minimum(tick, MICRO - 1), 0, keepdims=False)
        grad_in = jnp.where(phase == phases - 1, last, received)
        hidden = lax.dynamic_index_in_dim(saved, slot, 0, keepdims=False)
        pre = lax.dynamic_index_in_dim(pres, slot, 0, keepdims=False)
        grad_out, lowered, act, d_pre = phase_backward(hidden, grad_in, pre, w_dn, w_upper, scale)
        lows = put_slot(lows, lowered, slot, valid)
        acts = put_slot(acts, act, slot, valid)
        dpres = put_slot(dpres, d_pre, slot, valid)
        grads = put_slot(grads, grad_in, slot, valid)
        received = shifted(grad_out, "segment", -1)
        return (received, lows, acts, dpres, grads)

    start_back = (
        jnp.zeros((micro_rows, width), jnp.bfloat16),
        jnp.zeros((MICRO, micro_rows, width), jnp.bfloat16),
        jnp.zeros((MICRO, micro_rows, rank), jnp.bfloat16),
        jnp.zeros((MICRO, micro_rows, rank), jnp.bfloat16),
        jnp.zeros((MICRO, micro_rows, width), jnp.bfloat16),
    )
    received, lows, acts, dpres, grads = lax.fori_loop(0, ticks, backward_tick, start_back)
    contract = (((0,), (0,)), ((), ()))
    grad_dn = lax.dot_general(
        lows.reshape(-1, width),
        dpres.reshape(-1, rank),
        contract,
        preferred_element_type=jnp.float32,
    )
    grad_upper = lax.dot_general(
        acts.reshape(-1, rank),
        grads.reshape(-1, width),
        contract,
        preferred_element_type=jnp.float32,
    )
    summed_dn, summed_upper = (
        lax.psum_scatter(
            grad_dn.astype(jnp.bfloat16), "dp", scatter_dimension=0, tiled=True
        ).astype(jnp.float32),
        lax.psum_scatter(
            grad_upper.astype(jnp.bfloat16), "dp", scatter_dimension=1, tiled=True
        ).astype(jnp.float32),
    )
    returned = from_root(results, "segment", phases - 1)
    returned = returned.reshape(slots, length, width)
    own = lax.dynamic_slice_in_dim(returned, phase * quarter, quarter, 2)
    back = lax.all_to_all(own, "expert", split_axis=0, concat_axis=0, tiled=True)
    out_hidden = jnp.dot(place.T, back.reshape(slots, -1), preferred_element_type=jnp.float32)
    out_hidden = out_hidden.astype(jnp.bfloat16).reshape(s_local, length, quarter)
    return (
        out_hidden,
        summed_dn.astype(jnp.bfloat16)[None, None],
        summed_upper.astype(jnp.bfloat16)[None, None],
    )


CHUNK = 512
VMEM_LIMIT = 56 * 1024 * 1024
TRANS_RHS = (((1,), (1,)), ((), ()))
TRANS_LHS = (((0,), (0,)), ((), ()))


def matmul(left, right, dims=(((1,), (0,)), ((), ()))):
    return lax.dot_general(left, right, dims, preferred_element_type=jnp.float32)


def spread_ids(ids, shape, length):
    lane = lax.broadcasted_iota(jnp.int32, shape, 1)
    spread = jnp.zeros(shape, jnp.int32)
    for n in range(ids.shape[0]):
        spread = jnp.where(lane // length == n, ids[n], spread)
    return spread


def placement(ids_row, length, capacity, slots):
    tokens = ids_row.shape[1]
    expert, core = lax.axis_index("expert"), lax.axis_index("segment")
    per_core = capacity // 2
    kinds = lax.broadcasted_iota(jnp.int32, (8, tokens), 0)
    member = (kinds == ids_row).astype(jnp.float32)
    at_col = lax.broadcasted_iota(jnp.int32, (tokens, tokens), 0)
    at_row = lax.broadcasted_iota(jnp.int32, (tokens, tokens), 1)
    before = (lax.rem(at_col, length) == 0) & (at_col // length < at_row // length)
    counts = matmul(member.astype(jnp.bfloat16), before.astype(jnp.float32).astype(jnp.bfloat16))
    rank = jnp.sum(member * counts, axis=0, keepdims=True).astype(jnp.int32)
    token = lax.rem(at_row[:1], length)
    group = (ids_row ^ expert) * 2 + ((rank // per_core) ^ core)
    target = (group * per_core + lax.rem(rank, per_core)) * length + token
    packed = lax.broadcasted_iota(jnp.int32, (slots * length, tokens), 0)
    return (packed == target).astype(jnp.float32).astype(jnp.bfloat16)


def pack_kernel(length, capacity, slots, ids, hidden, cot, *outs):
    groups = len(outs) - 4
    sends, slabs = outs[:groups], outs[groups:]
    s_local, _, part = hidden.shape
    tokens = s_local * length
    piece = part // 4
    replica = lax.axis_index("dp")
    ids_row = spread_ids(ids, (8, tokens), length)[:1]
    place = placement(ids_row, length, capacity, slots)
    rows = slots * length // groups
    wide_ids = spread_ids(ids, (16, piece), length).astype(jnp.float32).astype(jnp.bfloat16)
    for which, source in enumerate((hidden, cot)):
        for quarter_pair in range(2):
            for low in range(2):
                turn = (quarter_pair ^ (replica & 1)) * 2 + (low ^ (replica >> 1))
                cols = pl.ds(pl.multiple_of(turn * piece, piece), piece)
                slabs[2 * quarter_pair + low][which * tokens : (which + 1) * tokens] = source[
                    :, :, cols
                ].reshape(tokens, piece)
        moved = matmul(place, source[...].reshape(tokens, part)).astype(jnp.bfloat16)
        for group in range(groups):
            sends[group][which] = moved[group * rows : (group + 1) * rows]
    for slab in slabs:
        slab[2 * tokens :] = wide_ids


def repack_kernel(length, capacity, slots, *refs):
    slabs, outs = refs[:4], refs[4:]
    tokens = (slabs[0].shape[0] - 16) // 2
    rows = slots * length // len(outs)
    core, replica = lax.axis_index("segment"), lax.axis_index("dp")
    for turn, slab in enumerate(slabs):
        near = turn // 2 + 2 * ((turn % 2) ^ (replica >> 1) ^ core)
        ids_row = slab[2 * tokens :, :tokens].astype(jnp.float32)[:1].astype(jnp.int32)
        place = placement(ids_row, length, capacity, slots)
        for which in range(2):
            moved = matmul(place, slab[which * tokens : (which + 1) * tokens])
            moved = moved.astype(jnp.bfloat16)
            for step, out in enumerate(outs):
                out[which, near] = moved[step * rows : (step + 1) * rows]


def unpack_kernel(length, capacity, slots, ids, *refs):
    backs, out, stacked = refs[:-2], refs[-2], refs[-1]
    rows, width = backs[0].shape
    s_local = out.shape[0]
    for group, back in enumerate(backs):
        stacked[group * rows : (group + 1) * rows] = back[...]
    ids_row = spread_ids(ids, (8, s_local * length), length)[:1]
    place = placement(ids_row, length, capacity, slots)
    moved = matmul(place, stacked[...], TRANS_LHS).astype(jnp.bfloat16)
    out[...] = moved.reshape(s_local, length, width)


def split_three(value):
    top = value.astype(jnp.bfloat16).astype(jnp.float32)
    mid = (value - top).astype(jnp.bfloat16).astype(jnp.float32)
    low = (value - top - mid).astype(jnp.bfloat16).astype(jnp.float32)
    return [top, mid, low]


def side_by_side(columns, tokens):
    lane = lax.broadcasted_iota(jnp.int32, (tokens, 128), 1)
    block = jnp.zeros((tokens, 128), jnp.float32)
    at = 0
    for column in columns:
        for piece in split_three(column):
            block = jnp.where(lane == at, piece, block)
            at += 1
    return block.astype(jnp.bfloat16)


def column(block, index):
    at = 3 * index
    return block[:, at : at + 1] + block[:, at + 1 : at + 2] + block[:, at + 2 : at + 3]


def lanes(value):
    total = value[:, :128]
    for start in range(128, value.shape[1], 128):
        total = total + value[:, start : start + 128]
    return total


def row_sum(parts):
    return jnp.sum(parts, axis=1, keepdims=True)


def weight_copies(core, half, sources, buffers, sems):
    copies = []
    for at, (source, buffer, axis) in enumerate(zip(sources, buffers, (0, 1, 1))):
        for near in range(2):
            start = (near ^ core) * half
            part = pl.ds(start, half)
            here = pl.ds(near * half, half)
            from_, to = (part, here) if axis == 0 else ((slice(None), part), (slice(None), here))
            copies.append(pltpu.make_async_copy(source.at[from_], buffer.at[to], sems.at[at, near]))
    return copies


def forward_kernel(groups, *refs):
    recvs, refs = refs[:groups], refs[groups:]
    own, other, refs = refs[:3], refs[3:6], refs[6:]
    outs, refs = refs[:groups], refs[groups:]
    small, middle, slope_out, moments, dn_buf, up_buf, gain_buf, entering, sems = refs
    core = lax.axis_index("segment")
    _, rows, part = recvs[0].shape
    experts = groups // 2
    tokens = experts * rows
    width = 2 * part
    rank = dn_buf.shape[2]

    def copies(at, this):
        sources = own if at == this else other
        buffers = (dn_buf.at[at], up_buf.at[at], gain_buf.at[at])
        return weight_copies(this, part, sources, buffers, sems.at[at])

    for this in range(2):

        @pl.when(core == this)
        def _():
            for at in range(2):
                for copy in copies(at, this):
                    copy.start()

    waits = [copies(at, 0) for at in range(2)]

    def wait(at, which):
        for copy in waits[at][2 * which : 2 * which + 2]:
            copy.wait()

    cols = range(0, width, CHUNK)

    def block(which, col):
        near, start = col // part, col % part
        return jnp.concatenate(
            [recvs[2 * e + near][which, :, start : start + CHUNK] for e in range(experts)], axis=0
        )

    def inverse_of(ref, mean):
        total = jnp.zeros((tokens, 128), jnp.float32)
        for col in cols:
            center = ref[:, col : col + CHUNK].astype(jnp.float32) - mean
            total = total + lanes(center * center)
        return lax.rsqrt(row_sum(total) / width + EPS)

    def down(ref, mean, inverse, at):
        pre = jnp.zeros((tokens, rank), jnp.float32)
        for col in cols:
            here = slice(col, col + CHUNK)
            normed = (ref[:, here].astype(jnp.float32) - mean) * inverse
            lowered = (normed * gain_buf[at, :, here].astype(jnp.float32)).astype(jnp.bfloat16)
            pre = pre + matmul(lowered, dn_buf[at, here, :])
        return pre

    total = jnp.zeros((tokens, 128), jnp.float32)
    for col in cols:
        value = block(0, col)
        entering[:, col : col + CHUNK] = value
        total = total + lanes(value.astype(jnp.float32))
    mean_0 = row_sum(total) / width
    inverse_0 = inverse_of(entering, mean_0)
    wait(0, 0)
    wait(0, 2)
    pre_0 = down(entering, mean_0, inverse_0, 0)
    act_0 = gelu_value(pre_0).astype(jnp.bfloat16)
    slope_out[...] = gelu_slope(pre_0)

    wait(0, 1)
    total = jnp.zeros((tokens, 128), jnp.float32)
    for col in cols:
        here = slice(col, col + CHUNK)
        value = entering[:, here].astype(jnp.float32) + matmul(act_0, up_buf[0, :, here])
        value = value.astype(jnp.bfloat16)
        middle[:, here] = value
        total = total + lanes(value.astype(jnp.float32))
    mean_1 = row_sum(total) / width
    inverse_1 = inverse_of(middle, mean_1)
    wait(1, 0)
    wait(1, 2)
    pre_1 = down(middle, mean_1, inverse_1, 1)
    act_1 = gelu_value(pre_1).astype(jnp.bfloat16)

    wait(1, 1)
    d_act = jnp.zeros((tokens, rank), jnp.float32)
    for col in cols:
        here = slice(col, col + CHUNK)
        d_act = d_act + matmul(block(1, col), up_buf[1, :, here], TRANS_RHS)
        leaving = middle[:, here].astype(jnp.float32) + matmul(act_1, up_buf[1, :, here])
        leaving = leaving.astype(jnp.bfloat16)
        near, start = col // part, col % part
        for e in range(experts):
            outs[2 * e + near][:, start : start + CHUNK] = leaving[e * rows : (e + 1) * rows]
    d_pre_1 = (d_act * gelu_slope(pre_1)).astype(jnp.bfloat16)
    for at, value in enumerate((act_0, act_1, d_pre_1)):
        small[:, at * rank : (at + 1) * rank] = value
    small[:, 3 * rank :] = side_by_side((mean_0, inverse_0, mean_1, inverse_1), tokens)
    moments[...] = jnp.concatenate(
        [jnp.broadcast_to(mean_1, (tokens, 128)), jnp.broadcast_to(inverse_1, (tokens, 128))], axis=1
    )


def backward_kernel(groups, *refs):
    recvs, refs = refs[:groups], refs[groups:]
    own, other, refs = refs[:3], refs[3:6], refs[6:]
    small_in, middle, slope, moments, small, dn_buf, up_buf, gain_buf, d_norms, sems = refs
    core = lax.axis_index("segment")
    _, rows, part = recvs[0].shape
    experts = groups // 2
    tokens = experts * rows
    width = 2 * part
    rank = dn_buf.shape[1]
    buffers = (dn_buf, up_buf, gain_buf)

    def copies(this):
        first, second = (own, other) if this == 0 else (other, own)
        return weight_copies(this, part, (second[0], first[1], second[2]), buffers, sems)

    for this in range(2):

        @pl.when(core == this)
        def _():
            for copy in copies(this):
                copy.start()

    waits = copies(0)
    mean_1, inverse_1 = moments[:, :1], moments[:, 128:129]
    d_pre_1 = small_in[:, 2 * rank : 3 * rank]
    for copy in waits[:2] + waits[4:]:
        copy.wait()
    total = jnp.zeros((tokens, 128), jnp.float32)
    cross = jnp.zeros((tokens, 128), jnp.float32)
    cols = range(0, width, CHUNK)
    for col in cols:
        here = slice(col, col + CHUNK)
        d_norm = matmul(d_pre_1, dn_buf[here, :], TRANS_RHS) * gain_buf[:, here].astype(jnp.float32)
        normed = (middle[:, here].astype(jnp.float32) - mean_1) * inverse_1
        d_norms[:, here] = d_norm
        total = total + lanes(d_norm)
        cross = cross + lanes(d_norm * normed)
    shift = row_sum(total) / width
    along = row_sum(cross) / width
    for copy in waits[2:4]:
        copy.wait()
    d_act = jnp.zeros((tokens, rank), jnp.float32)
    for col in cols:
        here = slice(col, col + CHUNK)
        near, start = col // part, col % part
        grad_in = jnp.concatenate(
            [recvs[2 * e + near][1, :, start : start + CHUNK] for e in range(experts)], axis=0
        )
        normed = (middle[:, here].astype(jnp.float32) - mean_1) * inverse_1
        grad = grad_in.astype(jnp.float32) + inverse_1 * (d_norms[:, here] - shift - normed * along)
        d_act = d_act + matmul(grad.astype(jnp.bfloat16), up_buf[:, here], TRANS_RHS)
    small[:, :rank] = (d_act * slope[...]).astype(jnp.bfloat16)
    small[:, rank:] = side_by_side((shift, along), tokens)


def gradient_kernel(experts, replicas, *refs):
    mine, refs = refs[:experts], refs[experts:]
    theirs, refs = refs[:experts], refs[experts:]
    firsts, refs = refs[: 2 * replicas], refs[2 * replicas :]
    seconds, refs = refs[: 2 * replicas], refs[2 * replicas :]
    own, other, refs = refs[:3], refs[3:6], refs[6:]
    (grad_dn, grad_upper, dn_buf, up_buf, gain_buf, first, second, hiddens, grads, lows, ups, downs,
     sems) = refs
    core = lax.axis_index("segment")
    place = lax.axis_index("dp")
    half = mine[0].shape[3]
    rows = mine[0].shape[2] // 2
    slab = 2 * half
    rank = dn_buf.shape[1]
    tokens = hiddens.shape[0]

    def copies(up, gain_first, dn, gain_second):
        started = []
        for near in range(2):
            start = pl.multiple_of(place * slab + (near ^ core) * half, half)
            part, here = pl.ds(start, half), pl.ds(near * half, half)
            moves = (
                (up.at[:, part], up_buf.at[:, here]),
                (dn.at[part, :], dn_buf.at[here, :]),
                (gain_first.at[:, part], gain_buf.at[0, :, here]),
                (gain_second.at[:, part], gain_buf.at[1, :, here]),
            )
            for at, (source, target) in enumerate(moves):
                started.append(pltpu.make_async_copy(source, target, sems.at[near, at]))
        return started

    @pl.when(core == 0)
    def _():
        for copy in copies(own[1], own[2], other[0], other[2]):
            copy.start()

    @pl.when(core != 0)
    def _():
        for copy in copies(other[1], other[2], own[0], own[2]):
            copy.start()

    block_rows = experts * rows
    for source in range(2 * replicas):
        near_core, turn = source // replicas, source % replicas
        at = slice(source * block_rows, (source + 1) * block_rows)
        first[at] = firsts[source][...]
        second[at] = seconds[source][...]
        for near, (data, core_at) in enumerate(((mine, near_core), (theirs, 1 - near_core))):
            for step in range(experts):
                to = slice(at.start + step * rows, at.start + (step + 1) * rows)
                from_ = slice(core_at * rows, (core_at + 1) * rows)
                hiddens[to, near * half : (near + 1) * half] = data[step][0, turn, from_, :]
                grads[to, near * half : (near + 1) * half] = data[step][1, turn, from_, :]

    for copy in copies(own[1], own[2], other[0], other[2]):
        copy.wait()

    columns = 256
    strip = 128
    for col in range(0, slab, columns):
        here = slice(col, col + columns)
        ups[...] = matmul(first[:, :rank], up_buf[:, here])

        @pl.when(core == 0)
        def _():
            downs[...] = matmul(first[:, 2 * rank : 3 * rank], dn_buf[here, :], TRANS_RHS)

        for start in range(0, tokens, strip):
            at = slice(start, start + strip)
            stats = first[at, 3 * rank :].astype(jnp.float32)
            mean_1, inverse_1 = column(stats, 2), column(stats, 3)
            wide = hiddens[at, here].astype(jnp.float32)
            middle = (wide + ups[at]).astype(jnp.bfloat16).astype(jnp.float32)
            normed = (middle - mean_1) * inverse_1

            @pl.when(core == 0)
            def _():
                mean_0, inverse_0 = column(stats, 0), column(stats, 1)
                normed_0 = (wide - mean_0) * inverse_0
                lows[at, here] = (normed_0 * gain_buf[0, :, here].astype(jnp.float32)).astype(jnp.bfloat16)
                more = second[at, rank:].astype(jnp.float32)
                shift, along = column(more, 0), column(more, 1)
                d_norm = downs[at] * gain_buf[1, :, here].astype(jnp.float32)
                grads[at, here] = (
                    grads[at, here].astype(jnp.float32)
                    + inverse_1 * (d_norm - shift - normed * along)
                ).astype(jnp.bfloat16)

            @pl.when(core != 0)
            def _():
                lows[at, here] = (normed * gain_buf[1, :, here].astype(jnp.float32)).astype(jnp.bfloat16)

    def finish(act, d_pre):
        for near in range(2):
            here = slice(near * half, (near + 1) * half)
            there = pl.ds(pl.multiple_of((near ^ core) * half, half), half)
            grad_dn[there, :] = matmul(lows[:, here], d_pre, TRANS_LHS).astype(jnp.bfloat16)
            grad_upper[:, there] = matmul(act, grads[:, here], TRANS_LHS).astype(jnp.bfloat16)

    @pl.when(core == 0)
    def _():
        finish(first[:, :rank], second[:, :rank])

    @pl.when(core != 0)
    def _():
        finish(first[:, rank : 2 * rank], first[:, 2 * rank : 3 * rank])


VMEM = pl.BlockSpec(memory_space=pltpu.VMEM)
SMEM = pl.BlockSpec(memory_space=pltpu.SMEM)
HBM = pl.BlockSpec(memory_space=pl.ANY)


def call(kernel, name, in_specs, outs, scratch=()):
    return pl.pallas_call(
        kernel,
        out_shape=tuple(jax.ShapeDtypeStruct(*out) for out in outs),
        in_specs=in_specs,
        out_specs=tuple(VMEM for _ in outs),
        scratch_shapes=list(scratch),
        compiler_params=pltpu.CompilerParams(vmem_limit_bytes=VMEM_LIMIT),
        name=name,
    )


def across(block, axis, distance):
    size = lax.axis_size(axis)
    return lax.ppermute(block, axis, [(i, i ^ distance) for i in range(size)])


def exchanged(blocks):
    cores = lax.axis_size("segment")
    size = lax.axis_size("expert") * cores
    return [
        block
        if step == 0
        else lax.ppermute(block, ("expert", "segment"), [(i, i ^ step) for i in range(size)])
        for step, block in enumerate(blocks)
    ]


def slab_route(replicas, pair, low):
    route = []
    for replica in range(replicas):
        for core in range(2):
            chip = 2 * core + ((replica & 1) ^ pair)
            route.append((2 * replica + core, 2 * chip + ((replica >> 1) ^ low)))
    return route


def on_device_two_phases(hidden_in, cotangent, cluster_ids, w_down, w_up, gain):
    experts = lax.axis_size("expert")
    replicas = lax.axis_size("dp")
    s_local, length, part = hidden_in.shape
    width = 2 * part
    capacity = 2 * s_local // experts
    slots = experts * capacity
    groups = 2 * experts
    rows = slots * length // groups
    tokens = experts * rows
    own = (w_down[0, 0], w_up[0, 0], gain[0])
    rank = own[0].shape[1]
    piece = part // 4
    slab = width // replicas
    bf16, f32 = jnp.bfloat16, jnp.float32
    sizes = (length, capacity, slots)

    other = tuple(across(array, "segment", 1) for array in own)
    packed = call(
        functools.partial(pack_kernel, *sizes),
        "pack",
        [SMEM, VMEM, VMEM],
        [((2, rows, part), bf16)] * groups + [((2 * s_local * length + 16, piece), bf16)] * 4,
    )(cluster_ids, hidden_in, cotangent)
    recvs = exchanged(packed[:groups])
    slabs = [
        lax.ppermute(block, ("dp", "segment"), slab_route(replicas, turn // 2, turn % 2))
        for turn, block in enumerate(packed[groups:])
    ]
    repacked = call(
        functools.partial(repack_kernel, *sizes),
        "repack",
        [VMEM] * 4,
        [((2, replicas, 2 * rows, piece), bf16)] * experts,
    )(*slabs)
    mine = [repacked[0]] + [across(repacked[step], "expert", step) for step in range(1, experts)]
    theirs = [across(block, "segment", 1) for block in mine]

    *outs, small, middle, slope, moments = call(
        functools.partial(forward_kernel, groups),
        "forward",
        [VMEM] * groups + [HBM] * 6,
        [((rows, part), bf16)] * groups
        + [
            ((tokens, 3 * rank + 128), bf16),
            ((tokens, width), bf16),
            ((tokens, rank), f32),
            ((tokens, 256), f32),
        ],
        [
            pltpu.VMEM((2, width, rank), bf16),
            pltpu.VMEM((2, rank, width), bf16),
            pltpu.VMEM((2, 1, width), bf16),
            pltpu.VMEM((tokens, width), bf16),
            pltpu.SemaphoreType.DMA((2, 3, 2)),
        ],
    )(*recvs, *own, *other)

    def gathered(block):
        near = [block] + [across(block, "dp", step) for step in range(1, replicas)]
        return near + [across(piece, "segment", 1) for piece in near]

    firsts = gathered(small)
    (small_back,) = call(
        functools.partial(backward_kernel, groups),
        "backward",
        [VMEM] * groups + [HBM] * 6 + [VMEM] * 4,
        [((tokens, rank + 128), bf16)],
        [
            pltpu.VMEM((width, rank), bf16),
            pltpu.VMEM((rank, width), bf16),
            pltpu.VMEM((1, width), bf16),
            pltpu.VMEM((tokens, width), f32),
            pltpu.SemaphoreType.DMA((3, 2)),
        ],
    )(*recvs, *own, *other, small, middle, slope, moments)
    seconds = gathered(small_back)

    backs = exchanged(outs)
    (out_hidden,) = call(
        functools.partial(unpack_kernel, *sizes),
        "unpack",
        [SMEM] + [VMEM] * groups,
        [(hidden_in.shape, bf16)],
        [pltpu.VMEM((slots * length, part), bf16)],
    )(cluster_ids, *backs)

    all_tokens = 2 * replicas * tokens
    grad_dn, grad_upper = call(
        functools.partial(gradient_kernel, experts, replicas),
        "gradients",
        [VMEM] * (2 * experts + 4 * replicas) + [HBM] * 6,
        [((slab, rank), bf16), ((rank, slab), bf16)],
        [
            pltpu.VMEM((slab, rank), bf16),
            pltpu.VMEM((rank, slab), bf16),
            pltpu.VMEM((2, 1, slab), bf16),
            pltpu.VMEM((all_tokens, 3 * rank + 128), bf16),
            pltpu.VMEM((all_tokens, rank + 128), bf16),
            pltpu.VMEM((all_tokens, slab), bf16),
            pltpu.VMEM((all_tokens, slab), bf16),
            pltpu.VMEM((all_tokens, slab), bf16),
            pltpu.VMEM((all_tokens, 256), f32),
            pltpu.VMEM((all_tokens, 256), f32),
            pltpu.SemaphoreType.DMA((2, 4)),
        ],
    )(*mine, *theirs, *firsts, *seconds, *own, *other)
    return (out_hidden, grad_dn[None, None], grad_upper[None, None])


def solution(mesh):
    two = dict(mesh.shape) == {"expert": 4, "dp": 4, "segment": 2}
    on_device = on_device_two_phases if two else on_device_pipelined
    return jax.shard_map(
        on_device,
        mesh=mesh,
        in_specs=(
            P(("expert", "dp"), None, "segment"),
            P(("expert", "dp"), None, "segment"),
            P(("expert", "dp")),
            P("expert", "segment", None, None),
            P("expert", "segment", None, None),
            P("expert", "segment", None),
        ),
        out_specs=(
            P(("expert", "dp"), None, "segment"),
            P("expert", "segment", "dp", None),
            P("expert", "segment", None, "dp"),
        ),
        check_vma=False,
    )
```

```python
import functools

import jax
import jax.numpy as jnp
from jax import lax
from jax.experimental import pallas as pl
from jax.experimental.pallas import tpu as pltpu
from jax.sharding import PartitionSpec as P

MICRO = 4


EPS = 1e-05
C_ZERO = 0.7978845608028654
C_ONE = 0.044715


def shifted(block, axis, distance):
    devices = range(lax.axis_size(axis))
    route = [(i - distance, i) for i in devices if i - distance in devices]
    return lax.ppermute(block, axis, route)


def from_root(block, axis, holder):
    block = jnp.where(lax.axis_index(axis) == holder, block, jnp.zeros_like(block))
    return lax.psum(block, axis)


def gelu_value(z):
    return 0.5 * z * (1.0 + jnp.tanh(C_ZERO * (z + C_ONE * z * z * z)))


def gelu_slope(z):
    tval = jnp.tanh(C_ZERO * (z + C_ONE * z * z * z))
    return 0.5 * (1.0 + tval) + 0.5 * z * (1.0 - tval * tval) * C_ZERO * (1.0 + 3.0 * C_ONE * z * z)


def normalize(hidden):
    wide = hidden.astype(jnp.float32)
    center = wide - jnp.mean(wide, axis=-1, keepdims=True)
    inverse = lax.rsqrt(jnp.mean(center * center, axis=-1, keepdims=True) + EPS)
    return (wide, center * inverse, inverse)


def phase_forward(hidden, w_dn, w_upper, scale):
    wide, normed, inverse = normalize(hidden)
    lowered = (normed * scale).astype(jnp.bfloat16)
    pre = jnp.dot(lowered, w_dn, preferred_element_type=jnp.float32)
    act = gelu_value(pre).astype(jnp.bfloat16)
    leaving = (wide + jnp.dot(act, w_upper, preferred_element_type=jnp.float32)).astype(
        jnp.bfloat16
    )
    return (leaving, pre)


def phase_backward(hidden, grad_in, pre, w_dn, w_upper, scale):
    wide, normed, inverse = normalize(hidden)
    lowered = (normed * scale).astype(jnp.bfloat16)
    act = gelu_value(pre).astype(jnp.bfloat16)
    d_act = jnp.dot(grad_in, w_upper.T, preferred_element_type=jnp.float32)
    d_pre = (d_act * gelu_slope(pre)).astype(jnp.bfloat16)
    d_low = jnp.dot(d_pre, w_dn.T, preferred_element_type=jnp.float32)
    d_norm = d_low * scale
    d_wide = inverse * (
        d_norm
        - jnp.mean(d_norm, axis=-1, keepdims=True)
        - normed * jnp.mean(d_norm * normed, axis=-1, keepdims=True)
    )
    grad_out = (grad_in.astype(jnp.float32) + d_wide).astype(jnp.bfloat16)
    return (grad_out, lowered, act, d_pre)


def put_slot(buffer, value, slot, valid):
    old_value = lax.dynamic_index_in_dim(buffer, slot, 0, keepdims=False)
    return lax.dynamic_update_index_in_dim(buffer, jnp.where(valid, value, old_value), slot, 0)


def on_device_pipelined(hidden_in, cotangent, cluster_ids, w_down, w_up, gain):
    experts = lax.axis_size("expert")
    phases = lax.axis_size("segment")
    phase = lax.axis_index("segment")
    s_local, length, quarter = hidden_in.shape
    capacity = 2 * s_local // experts
    slots = experts * capacity
    same = (cluster_ids[:, None] == cluster_ids[None, :]).astype(jnp.int32)
    earlier = jnp.sum(jnp.tril(same, -1), axis=1)
    target = cluster_ids * capacity + earlier
    place = (jnp.arange(slots, dtype=jnp.int32)[:, None] == target[None, :]).astype(jnp.bfloat16)

    def to_slots(local):
        flat = local.reshape(s_local, -1)
        moved = jnp.dot(place, flat, preferred_element_type=jnp.float32).astype(jnp.bfloat16)
        return moved.reshape((slots,) + local.shape[1:])

    full_in, full_cot = (
        lax.all_gather(hidden_in, "segment", axis=2, tiled=True),
        lax.all_gather(cotangent, "segment", axis=2, tiled=True),
    )
    slot_in, slot_cot = (
        lax.all_to_all(to_slots(full_in), "expert", split_axis=0, concat_axis=0, tiled=True),
        lax.all_to_all(to_slots(full_cot), "expert", split_axis=0, concat_axis=0, tiled=True),
    )
    width = slot_in.shape[2]
    micro_rows = slots * length // MICRO
    inputs = slot_in.reshape(MICRO, micro_rows, width)
    cots = slot_cot.reshape(MICRO, micro_rows, width)
    w_dn = w_down[0, 0]
    w_upper = w_up[0, 0]
    rank = w_dn.shape[1]
    scale = gain[0, 0].astype(jnp.float32)
    ticks = MICRO + phases - 1

    def forward_tick(tick, carry):
        received, saved, pres, results = carry
        which = tick - phase
        valid = (which >= 0) & (which < MICRO)
        slot = jnp.clip(which, 0, MICRO - 1)
        first = lax.dynamic_index_in_dim(inputs, jnp.minimum(tick, MICRO - 1), 0, keepdims=False)
        entering = jnp.where(phase == 0, first, received)
        leaving, pre = phase_forward(entering, w_dn, w_upper, scale)
        saved = put_slot(saved, entering, slot, valid)
        pres = put_slot(pres, pre, slot, valid)
        results = put_slot(results, leaving, slot, valid & (phase == phases - 1))
        received = shifted(leaving, "segment", 1)
        return (received, saved, pres, results)

    start = (
        jnp.zeros((micro_rows, width), jnp.bfloat16),
        jnp.zeros((MICRO, micro_rows, width), jnp.bfloat16),
        jnp.zeros((MICRO, micro_rows, rank), jnp.float32),
        jnp.zeros((MICRO, micro_rows, width), jnp.bfloat16),
    )
    received, saved, pres, results = lax.fori_loop(0, ticks, forward_tick, start)

    def backward_tick(tick, carry):
        received, lows, acts, dpres, grads = carry
        which = tick - (phases - 1 - phase)
        valid = (which >= 0) & (which < MICRO)
        slot = jnp.clip(which, 0, MICRO - 1)
        last = lax.dynamic_index_in_dim(cots, jnp.minimum(tick, MICRO - 1), 0, keepdims=False)
        grad_in = jnp.where(phase == phases - 1, last, received)
        hidden = lax.dynamic_index_in_dim(saved, slot, 0, keepdims=False)
        pre = lax.dynamic_index_in_dim(pres, slot, 0, keepdims=False)
        grad_out, lowered, act, d_pre = phase_backward(hidden, grad_in, pre, w_dn, w_upper, scale)
        lows = put_slot(lows, lowered, slot, valid)
        acts = put_slot(acts, act, slot, valid)
        dpres = put_slot(dpres, d_pre, slot, valid)
        grads = put_slot(grads, grad_in, slot, valid)
        received = shifted(grad_out, "segment", -1)
        return (received, lows, acts, dpres, grads)

    start_back = (
        jnp.zeros((micro_rows, width), jnp.bfloat16),
        jnp.zeros((MICRO, micro_rows, width), jnp.bfloat16),
        jnp.zeros((MICRO, micro_rows, rank), jnp.bfloat16),
        jnp.zeros((MICRO, micro_rows, rank), jnp.bfloat16),
        jnp.zeros((MICRO, micro_rows, width), jnp.bfloat16),
    )
    received, lows, acts, dpres, grads = lax.fori_loop(0, ticks, backward_tick, start_back)
    contract = (((0,), (0,)), ((), ()))
    grad_dn = lax.dot_general(
        lows.reshape(-1, width),
        dpres.reshape(-1, rank),
        contract,
        preferred_element_type=jnp.float32,
    )
    grad_upper = lax.dot_general(
        acts.reshape(-1, rank),
        grads.reshape(-1, width),
        contract,
        preferred_element_type=jnp.float32,
    )
    summed_dn, summed_upper = (
        lax.psum_scatter(
            grad_dn.astype(jnp.bfloat16), "dp", scatter_dimension=0, tiled=True
        ).astype(jnp.float32),
        lax.psum_scatter(
            grad_upper.astype(jnp.bfloat16), "dp", scatter_dimension=1, tiled=True
        ).astype(jnp.float32),
    )
    returned = from_root(results, "segment", phases - 1)
    returned = returned.reshape(slots, length, width)
    own = lax.dynamic_slice_in_dim(returned, phase * quarter, quarter, 2)
    back = lax.all_to_all(own, "expert", split_axis=0, concat_axis=0, tiled=True)
    out_hidden = jnp.dot(place.T, back.reshape(slots, -1), preferred_element_type=jnp.float32)
    out_hidden = out_hidden.astype(jnp.bfloat16).reshape(s_local, length, quarter)
    return (
        out_hidden,
        summed_dn.astype(jnp.bfloat16)[None, None],
        summed_upper.astype(jnp.bfloat16)[None, None],
    )


CHUNK = 512
VMEM_LIMIT = 56 * 1024 * 1024
TRANS_RHS = (((1,), (1,)), ((), ()))
TRANS_LHS = (((0,), (0,)), ((), ()))


def matmul(left, right, dims=(((1,), (0,)), ((), ()))):
    return lax.dot_general(left, right, dims, preferred_element_type=jnp.float32)


def spread_ids(ids, shape, length):
    lane = lax.broadcasted_iota(jnp.int32, shape, 1)
    spread = jnp.zeros(shape, jnp.int32)
    for n in range(ids.shape[0]):
        spread = jnp.where(lane // length == n, ids[n], spread)
    return spread


def placement(ids_row, length, capacity, slots):
    tokens = ids_row.shape[1]
    kinds = lax.broadcasted_iota(jnp.int32, (8, tokens), 0)
    member = (kinds == ids_row).astype(jnp.float32)
    at_col = lax.broadcasted_iota(jnp.int32, (tokens, tokens), 0)
    at_row = lax.broadcasted_iota(jnp.int32, (tokens, tokens), 1)
    before = (lax.rem(at_col, length) == 0) & (at_col // length < at_row // length)
    counts = matmul(member.astype(jnp.bfloat16), before.astype(jnp.float32).astype(jnp.bfloat16))
    rank = jnp.sum(member * counts, axis=0, keepdims=True).astype(jnp.int32)
    target = (ids_row * capacity + rank) * length + lax.rem(at_row[:1], length)
    packed = lax.broadcasted_iota(jnp.int32, (slots * length, tokens), 0)
    return (packed == target).astype(jnp.float32).astype(jnp.bfloat16)


def pack_kernel(length, capacity, slots, ids, hidden, cot, send):
    groups, _, rows, part = send.shape
    tokens = hidden.shape[0] * length
    ids_row = spread_ids(ids, (8, tokens), length)[:1]
    place = placement(ids_row, length, capacity, slots)
    for which, source in enumerate((hidden, cot)):
        moved = matmul(place, source[...].reshape(tokens, part)).astype(jnp.bfloat16)
        for group in range(groups):
            send[group, which] = moved[group * rows : (group + 1) * rows]


def slice_kernel(recv, *outs):
    experts, _, _, rows, part = recv.shape
    slab = outs[0].shape[2]
    place = lax.axis_index("dp")
    per_half = part // slab
    for step, out in enumerate(outs):
        chip = place ^ step
        half = chip // per_half
        cols = pl.ds(pl.multiple_of((chip - half * per_half) * slab, slab), slab)
        for which in range(2):
            for e in range(experts):
                out[which, e * rows : (e + 1) * rows] = recv[e, half, which, :, cols]


def unpack_kernel(length, capacity, slots, ids, back, out):
    groups, rows, width = back.shape
    s_local = out.shape[0]
    ids_row = spread_ids(ids, (8, s_local * length), length)[:1]
    place = placement(ids_row, length, capacity, slots)
    moved = matmul(place, back[...].reshape(groups * rows, width), TRANS_LHS)
    out[...] = moved.astype(jnp.bfloat16).reshape(s_local, length, width)


def split_three(value):
    top = value.astype(jnp.bfloat16).astype(jnp.float32)
    mid = (value - top).astype(jnp.bfloat16).astype(jnp.float32)
    low = (value - top - mid).astype(jnp.bfloat16).astype(jnp.float32)
    return [top, mid, low]


def side_by_side(columns, tokens):
    lane = lax.broadcasted_iota(jnp.int32, (tokens, 128), 1)
    block = jnp.zeros((tokens, 128), jnp.float32)
    at = 0
    for column in columns:
        for piece in split_three(column):
            block = jnp.where(lane == at, piece, block)
            at += 1
    return block.astype(jnp.bfloat16)


def lanes(value):
    total = value[:, :128]
    for start in range(128, value.shape[1], 128):
        total = total + value[:, start : start + 128]
    return total


def row_sum(parts):
    return jnp.sum(parts, axis=1, keepdims=True)


def chain_kernel(
    recv, own_dn, own_up, own_gain, other_dn, other_up, other_gain,
    out, small,
    dn_buf, up_buf, gain_buf, entering, middle, d_norms, sems,
):
    phase = lax.axis_index("segment")
    experts, phases, _, rows, part = recv.shape
    tokens = experts * rows
    width = phases * part
    rank = dn_buf.shape[2]
    own, other = (own_dn, own_up, own_gain), (other_dn, other_up, other_gain)

    def copies(sources, at):
        return [
            pltpu.make_async_copy(source, buffer.at[at], sems.at[at, which])
            for which, (source, buffer) in enumerate(zip(sources, (dn_buf, up_buf, gain_buf)))
        ]

    for this in range(2):

        @pl.when(phase == this)
        def _():
            for at in range(2):
                for copy in copies(own if at == this else other, at):
                    copy.start()

    waits = [copies(own, at) for at in range(2)]
    cols = range(0, width, CHUNK)

    def block(which, col):
        half, start = col // part, col % part
        return jnp.concatenate(
            [recv[e, half, which, :, start : start + CHUNK] for e in range(experts)], axis=0
        )

    def inverse_of(ref, mean):
        total = jnp.zeros((tokens, 128), jnp.float32)
        for col in cols:
            center = ref[:, col : col + CHUNK].astype(jnp.float32) - mean
            total = total + lanes(center * center)
        return lax.rsqrt(row_sum(total) / width + EPS)

    def down(ref, mean, inverse, at):
        pre = jnp.zeros((tokens, rank), jnp.float32)
        for col in cols:
            here = slice(col, col + CHUNK)
            normed = (ref[:, here].astype(jnp.float32) - mean) * inverse
            lowered = (normed * gain_buf[at, :, here].astype(jnp.float32)).astype(jnp.bfloat16)
            pre = pre + matmul(lowered, dn_buf[at, here, :])
        return pre

    total = jnp.zeros((tokens, 128), jnp.float32)
    for col in cols:
        value = block(0, col)
        entering[:, col : col + CHUNK] = value
        total = total + lanes(value.astype(jnp.float32))
    mean_0 = row_sum(total) / width
    inverse_0 = inverse_of(entering, mean_0)
    waits[0][0].wait()
    waits[0][2].wait()
    pre_0 = down(entering, mean_0, inverse_0, 0)
    act_0 = gelu_value(pre_0).astype(jnp.bfloat16)
    slope_0 = gelu_slope(pre_0)

    waits[0][1].wait()
    total = jnp.zeros((tokens, 128), jnp.float32)
    for col in cols:
        here = slice(col, col + CHUNK)
        value = entering[:, here].astype(jnp.float32) + matmul(act_0, up_buf[0, :, here])
        value = value.astype(jnp.bfloat16)
        middle[:, here] = value
        total = total + lanes(value.astype(jnp.float32))
    mean_1 = row_sum(total) / width
    inverse_1 = inverse_of(middle, mean_1)
    for copy in waits[1]:
        copy.wait()
    d_act = jnp.zeros((tokens, rank), jnp.float32)
    for col in cols:
        d_act = d_act + matmul(block(1, col), up_buf[1, :, col : col + CHUNK], TRANS_RHS)
    pre_1 = down(middle, mean_1, inverse_1, 1)
    act_1 = gelu_value(pre_1).astype(jnp.bfloat16)
    d_pre_1 = (d_act * gelu_slope(pre_1)).astype(jnp.bfloat16)

    total = jnp.zeros((tokens, 128), jnp.float32)
    cross = jnp.zeros((tokens, 128), jnp.float32)
    for col in cols:
        here = slice(col, col + CHUNK)
        wide = middle[:, here].astype(jnp.float32)
        d_norm = matmul(d_pre_1, dn_buf[1, here, :], TRANS_RHS)
        d_norm = d_norm * gain_buf[1, :, here].astype(jnp.float32)
        d_norms[:, here] = d_norm
        total = total + lanes(d_norm)
        cross = cross + lanes(d_norm * ((wide - mean_1) * inverse_1))
        leaving = (wide + matmul(act_1, up_buf[1, :, here])).astype(jnp.bfloat16)
        half, start = col // part, col % part
        for e in range(experts):
            out[e, half, :, start : start + CHUNK] = leaving[e * rows : (e + 1) * rows]
    shift = row_sum(total) / width
    along = row_sum(cross) / width
    d_act = jnp.zeros((tokens, rank), jnp.float32)
    for col in cols:
        here = slice(col, col + CHUNK)
        normed = (middle[:, here].astype(jnp.float32) - mean_1) * inverse_1
        grad = block(1, col).astype(jnp.float32) + inverse_1 * (
            d_norms[:, here] - shift - normed * along
        )
        d_act = d_act + matmul(grad.astype(jnp.bfloat16), up_buf[0, :, here], TRANS_RHS)
    d_pre_0 = (d_act * slope_0).astype(jnp.bfloat16)
    for at, value in enumerate((act_0, act_1, d_pre_0, d_pre_1)):
        small[:, at * rank : (at + 1) * rank] = value
    moments = (mean_0, inverse_0, mean_1, inverse_1, shift, along)
    small[:, 4 * rank :] = side_by_side(moments, tokens)


def gradient_kernel(sources, *refs):
    slices, refs = refs[:sources], refs[sources:]
    smalls, refs = refs[:sources], refs[sources:]
    own, other, refs = refs[:3], refs[3:6], refs[6:]
    (grad_dn, grad_upper, dn_buf, up_buf, gain_buf, small, moments, lows, grads, ups, downs,
     sems) = refs
    core = lax.axis_index("segment")
    place = lax.axis_index("dp")
    _, rows, slab = slices[0].shape
    rank = dn_buf.shape[1]
    features = pl.ds(pl.multiple_of(place * slab, slab), slab)

    def copies(up, gain_first, dn, gain_second):
        moves = (
            (up.at[:, features], up_buf),
            (dn.at[features, :], dn_buf),
            (gain_first.at[:, features], gain_buf.at[0]),
            (gain_second.at[:, features], gain_buf.at[1]),
        )
        return [
            pltpu.make_async_copy(source, target, sems.at[at])
            for at, (source, target) in enumerate(moves)
        ]

    @pl.when(core == 0)
    def _():
        for copy in copies(own[1], own[2], other[0], other[2]):
            copy.start()

    @pl.when(core != 0)
    def _():
        for copy in copies(other[1], other[2], own[0], own[2]):
            copy.start()

    for source in range(sources):
        small[source * rows : (source + 1) * rows] = smalls[source][...]
    held = lax.broadcasted_iota(jnp.int32, (128, 6 * 128), 0)
    wanted = lax.broadcasted_iota(jnp.int32, (128, 6 * 128), 1) // 128
    adds = (held // 3 == wanted).astype(jnp.float32).astype(jnp.bfloat16)
    moments[...] = matmul(small[:, 4 * rank :], adds)
    for copy in copies(own[1], own[2], other[0], other[2]):
        copy.wait()

    columns = 256

    def moment(at, index):
        value = moments[at, index * 128 : (index + 1) * 128]
        return jnp.concatenate([value] * (columns // 128), axis=1)

    for col in range(0, slab, columns):
        here = slice(col, col + columns)
        ups[...] = matmul(small[:, :rank], up_buf[:, here])
        scales = [gain_buf[at, :, here].astype(jnp.float32) for at in range(2)]

        @pl.when(core == 0)
        def _():
            downs[...] = matmul(small[:, 3 * rank : 4 * rank], dn_buf[here, :], TRANS_RHS)
            for source in range(sources):
                at = slice(source * rows, (source + 1) * rows)
                wide = slices[source][0, :, here].astype(jnp.float32)
                normed = (wide - moment(at, 0)) * moment(at, 1)
                lows[at, here] = (normed * scales[0]).astype(jnp.bfloat16)
                middle = (wide + ups[at]).astype(jnp.bfloat16).astype(jnp.float32)
                inverse = moment(at, 3)
                normed = (middle - moment(at, 2)) * inverse
                d_norm = downs[at] * scales[1]
                grads[at, here] = (
                    slices[source][1, :, here].astype(jnp.float32)
                    + inverse * (d_norm - moment(at, 4) - normed * moment(at, 5))
                ).astype(jnp.bfloat16)

        @pl.when(core != 0)
        def _():
            for source in range(sources):
                at = slice(source * rows, (source + 1) * rows)
                wide = slices[source][0, :, here].astype(jnp.float32)
                middle = (wide + ups[at]).astype(jnp.bfloat16).astype(jnp.float32)
                normed = (middle - moment(at, 2)) * moment(at, 3)
                lows[at, here] = (normed * scales[1]).astype(jnp.bfloat16)
                grads[at, here] = slices[source][1, :, here]

    def finish(act, d_pre):
        for col in range(0, slab, columns):
            here = slice(col, col + columns)
            turned = matmul(d_pre, lows[:, here], TRANS_LHS).astype(jnp.bfloat16)
            grad_dn[here, :] = turned.T
            grad_upper[:, here] = matmul(act, grads[:, here], TRANS_LHS).astype(jnp.bfloat16)

    @pl.when(core == 0)
    def _():
        finish(small[:, :rank], small[:, 2 * rank : 3 * rank])

    @pl.when(core != 0)
    def _():
        finish(small[:, rank : 2 * rank], small[:, 3 * rank : 4 * rank])


VMEM = pl.BlockSpec(memory_space=pltpu.VMEM)
SMEM = pl.BlockSpec(memory_space=pltpu.SMEM)
HBM = pl.BlockSpec(memory_space=pl.ANY)


def call(kernel, name, in_specs, outs, scratch=()):
    return pl.pallas_call(
        kernel,
        out_shape=tuple(jax.ShapeDtypeStruct(*out) for out in outs),
        in_specs=in_specs,
        out_specs=tuple(VMEM for _ in outs),
        scratch_shapes=list(scratch),
        compiler_params=pltpu.CompilerParams(vmem_limit_bytes=VMEM_LIMIT),
        name=name,
    )


def across(block, axis, distance):
    size = lax.axis_size(axis)
    return lax.ppermute(block, axis, [(i, i ^ distance) for i in range(size)])


def on_device_two_phases(hidden_in, cotangent, cluster_ids, w_down, w_up, gain):
    experts = lax.axis_size("expert")
    replicas = lax.axis_size("dp")
    s_local, length, part = hidden_in.shape
    width = 2 * part
    capacity = 2 * s_local // experts
    slots = experts * capacity
    groups = 2 * experts
    rows = slots * length // groups
    tokens = experts * rows
    own = (w_down[0, 0], w_up[0, 0], gain[0])
    rank = own[0].shape[1]
    slab = width // replicas
    bf16, f32 = jnp.bfloat16, jnp.float32
    sizes = (length, capacity, slots)
    sections = ("expert", "segment")

    other = tuple(across(array, "segment", 1) for array in own)
    (send,) = call(
        functools.partial(pack_kernel, *sizes),
        "pack",
        [SMEM, VMEM, VMEM],
        [((groups, 2, rows, part), bf16)],
    )(cluster_ids, hidden_in, cotangent)
    recv = lax.all_to_all(send, sections, split_axis=0, concat_axis=0, tiled=True)
    recv = recv.reshape(experts, 2, 2, rows, part)

    def gathered(blocks):
        near = [blocks[0]] + [across(blocks[step], "dp", step) for step in range(1, replicas)]
        return near + [across(piece, "segment", 1) for piece in near]

    slices = gathered(
        call(slice_kernel, "slices", [VMEM], [((2, tokens, slab), bf16)] * replicas)(recv)
    )
    out, small = call(
        chain_kernel,
        "chain",
        [VMEM] + [HBM] * 6,
        [((experts, 2, rows, part), bf16), ((tokens, 4 * rank + 128), bf16)],
        [
            pltpu.VMEM((2, width, rank), bf16),
            pltpu.VMEM((2, rank, width), bf16),
            pltpu.VMEM((2, 1, width), bf16),
            pltpu.VMEM((tokens, width), bf16),
            pltpu.VMEM((tokens, width), bf16),
            pltpu.VMEM((tokens, width), f32),
            pltpu.SemaphoreType.DMA((2, 3)),
        ],
    )(recv, *own, *other)
    smalls = gathered([small] * replicas)

    back = lax.all_to_all(
        out.reshape(groups, rows, part), sections, split_axis=0, concat_axis=0, tiled=True
    )
    (out_hidden,) = call(
        functools.partial(unpack_kernel, *sizes),
        "unpack",
        [SMEM, VMEM],
        [(hidden_in.shape, bf16)],
    )(cluster_ids, back)

    sources = 2 * replicas
    all_tokens = sources * tokens
    grad_dn, grad_upper = call(
        functools.partial(gradient_kernel, sources),
        "gradients",
        [VMEM] * (2 * sources) + [HBM] * 6,
        [((slab, rank), bf16), ((rank, slab), bf16)],
        [
            pltpu.VMEM((slab, rank), bf16),
            pltpu.VMEM((rank, slab), bf16),
            pltpu.VMEM((2, 1, slab), bf16),
            pltpu.VMEM((all_tokens, 4 * rank + 128), bf16),
            pltpu.VMEM((all_tokens, 6 * 128), f32),
            pltpu.VMEM((all_tokens, slab), bf16),
            pltpu.VMEM((all_tokens, slab), bf16),
            pltpu.VMEM((all_tokens, 256), f32),
            pltpu.VMEM((all_tokens, 256), f32),
            pltpu.SemaphoreType.DMA((4,)),
        ],
    )(*slices, *smalls, *own, *other)
    return (out_hidden, grad_dn[None, None], grad_upper[None, None])


def solution(mesh):
    two = dict(mesh.shape) == {"expert": 4, "dp": 4, "segment": 2}
    on_device = on_device_two_phases if two else on_device_pipelined
    return jax.shard_map(
        on_device,
        mesh=mesh,
        in_specs=(
            P(("expert", "dp"), None, "segment"),
            P(("expert", "dp"), None, "segment"),
            P(("expert", "dp")),
            P("expert", "segment", None, None),
            P("expert", "segment", None, None),
            P("expert", "segment", None),
        ),
        out_specs=(
            P(("expert", "dp"), None, "segment"),
            P("expert", "segment", "dp", None),
            P("expert", "segment", None, "dp"),
        ),
        check_vma=False,
    )
```

```python
import functools

import jax
import jax.numpy as jnp
from jax import lax
from jax.experimental import pallas as pl
from jax.experimental.pallas import tpu as pltpu
from jax.sharding import PartitionSpec as P

MICRO = 4


EPS = 1e-05
C_ZERO = 0.7978845608028654
C_ONE = 0.044715


def shifted(block, axis, distance):
    devices = range(lax.axis_size(axis))
    route = [(i - distance, i) for i in devices if i - distance in devices]
    return lax.ppermute(block, axis, route)


def from_root(block, axis, holder):
    block = jnp.where(lax.axis_index(axis) == holder, block, jnp.zeros_like(block))
    return lax.psum(block, axis)


def gelu_value(z):
    return 0.5 * z * (1.0 + jnp.tanh(C_ZERO * (z + C_ONE * z * z * z)))


def gelu_slope(z):
    tval = jnp.tanh(C_ZERO * (z + C_ONE * z * z * z))
    return 0.5 * (1.0 + tval) + 0.5 * z * (1.0 - tval * tval) * C_ZERO * (1.0 + 3.0 * C_ONE * z * z)


def normalize(hidden):
    wide = hidden.astype(jnp.float32)
    center = wide - jnp.mean(wide, axis=-1, keepdims=True)
    inverse = lax.rsqrt(jnp.mean(center * center, axis=-1, keepdims=True) + EPS)
    return (wide, center * inverse, inverse)


def phase_forward(hidden, w_dn, w_upper, scale):
    wide, normed, inverse = normalize(hidden)
    lowered = (normed * scale).astype(jnp.bfloat16)
    pre = jnp.dot(lowered, w_dn, preferred_element_type=jnp.float32)
    act = gelu_value(pre).astype(jnp.bfloat16)
    leaving = (wide + jnp.dot(act, w_upper, preferred_element_type=jnp.float32)).astype(
        jnp.bfloat16
    )
    return (leaving, pre)


def phase_backward(hidden, grad_in, pre, w_dn, w_upper, scale):
    wide, normed, inverse = normalize(hidden)
    lowered = (normed * scale).astype(jnp.bfloat16)
    act = gelu_value(pre).astype(jnp.bfloat16)
    d_act = jnp.dot(grad_in, w_upper.T, preferred_element_type=jnp.float32)
    d_pre = (d_act * gelu_slope(pre)).astype(jnp.bfloat16)
    d_low = jnp.dot(d_pre, w_dn.T, preferred_element_type=jnp.float32)
    d_norm = d_low * scale
    d_wide = inverse * (
        d_norm
        - jnp.mean(d_norm, axis=-1, keepdims=True)
        - normed * jnp.mean(d_norm * normed, axis=-1, keepdims=True)
    )
    grad_out = (grad_in.astype(jnp.float32) + d_wide).astype(jnp.bfloat16)
    return (grad_out, lowered, act, d_pre)


def put_slot(buffer, value, slot, valid):
    old_value = lax.dynamic_index_in_dim(buffer, slot, 0, keepdims=False)
    return lax.dynamic_update_index_in_dim(buffer, jnp.where(valid, value, old_value), slot, 0)


def on_device_pipelined(hidden_in, cotangent, cluster_ids, w_down, w_up, gain):
    experts = lax.axis_size("expert")
    phases = lax.axis_size("segment")
    phase = lax.axis_index("segment")
    s_local, length, quarter = hidden_in.shape
    capacity = 2 * s_local // experts
    slots = experts * capacity
    same = (cluster_ids[:, None] == cluster_ids[None, :]).astype(jnp.int32)
    earlier = jnp.sum(jnp.tril(same, -1), axis=1)
    target = cluster_ids * capacity + earlier
    place = (jnp.arange(slots, dtype=jnp.int32)[:, None] == target[None, :]).astype(jnp.bfloat16)

    def to_slots(local):
        flat = local.reshape(s_local, -1)
        moved = jnp.dot(place, flat, preferred_element_type=jnp.float32).astype(jnp.bfloat16)
        return moved.reshape((slots,) + local.shape[1:])

    full_in, full_cot = (
        lax.all_gather(hidden_in, "segment", axis=2, tiled=True),
        lax.all_gather(cotangent, "segment", axis=2, tiled=True),
    )
    slot_in, slot_cot = (
        lax.all_to_all(to_slots(full_in), "expert", split_axis=0, concat_axis=0, tiled=True),
        lax.all_to_all(to_slots(full_cot), "expert", split_axis=0, concat_axis=0, tiled=True),
    )
    width = slot_in.shape[2]
    micro_rows = slots * length // MICRO
    inputs = slot_in.reshape(MICRO, micro_rows, width)
    cots = slot_cot.reshape(MICRO, micro_rows, width)
    w_dn = w_down[0, 0]
    w_upper = w_up[0, 0]
    rank = w_dn.shape[1]
    scale = gain[0, 0].astype(jnp.float32)
    ticks = MICRO + phases - 1

    def forward_tick(tick, carry):
        received, saved, pres, results = carry
        which = tick - phase
        valid = (which >= 0) & (which < MICRO)
        slot = jnp.clip(which, 0, MICRO - 1)
        first = lax.dynamic_index_in_dim(inputs, jnp.minimum(tick, MICRO - 1), 0, keepdims=False)
        entering = jnp.where(phase == 0, first, received)
        leaving, pre = phase_forward(entering, w_dn, w_upper, scale)
        saved = put_slot(saved, entering, slot, valid)
        pres = put_slot(pres, pre, slot, valid)
        results = put_slot(results, leaving, slot, valid & (phase == phases - 1))
        received = shifted(leaving, "segment", 1)
        return (received, saved, pres, results)

    start = (
        jnp.zeros((micro_rows, width), jnp.bfloat16),
        jnp.zeros((MICRO, micro_rows, width), jnp.bfloat16),
        jnp.zeros((MICRO, micro_rows, rank), jnp.float32),
        jnp.zeros((MICRO, micro_rows, width), jnp.bfloat16),
    )
    received, saved, pres, results = lax.fori_loop(0, ticks, forward_tick, start)

    def backward_tick(tick, carry):
        received, lows, acts, dpres, grads = carry
        which = tick - (phases - 1 - phase)
        valid = (which >= 0) & (which < MICRO)
        slot = jnp.clip(which, 0, MICRO - 1)
        last = lax.dynamic_index_in_dim(cots, jnp.minimum(tick, MICRO - 1), 0, keepdims=False)
        grad_in = jnp.where(phase == phases - 1, last, received)
        hidden = lax.dynamic_index_in_dim(saved, slot, 0, keepdims=False)
        pre = lax.dynamic_index_in_dim(pres, slot, 0, keepdims=False)
        grad_out, lowered, act, d_pre = phase_backward(hidden, grad_in, pre, w_dn, w_upper, scale)
        lows = put_slot(lows, lowered, slot, valid)
        acts = put_slot(acts, act, slot, valid)
        dpres = put_slot(dpres, d_pre, slot, valid)
        grads = put_slot(grads, grad_in, slot, valid)
        received = shifted(grad_out, "segment", -1)
        return (received, lows, acts, dpres, grads)

    start_back = (
        jnp.zeros((micro_rows, width), jnp.bfloat16),
        jnp.zeros((MICRO, micro_rows, width), jnp.bfloat16),
        jnp.zeros((MICRO, micro_rows, rank), jnp.bfloat16),
        jnp.zeros((MICRO, micro_rows, rank), jnp.bfloat16),
        jnp.zeros((MICRO, micro_rows, width), jnp.bfloat16),
    )
    received, lows, acts, dpres, grads = lax.fori_loop(0, ticks, backward_tick, start_back)
    contract = (((0,), (0,)), ((), ()))
    grad_dn = lax.dot_general(
        lows.reshape(-1, width),
        dpres.reshape(-1, rank),
        contract,
        preferred_element_type=jnp.float32,
    )
    grad_upper = lax.dot_general(
        acts.reshape(-1, rank),
        grads.reshape(-1, width),
        contract,
        preferred_element_type=jnp.float32,
    )
    summed_dn, summed_upper = (
        lax.psum_scatter(
            grad_dn.astype(jnp.bfloat16), "dp", scatter_dimension=0, tiled=True
        ).astype(jnp.float32),
        lax.psum_scatter(
            grad_upper.astype(jnp.bfloat16), "dp", scatter_dimension=1, tiled=True
        ).astype(jnp.float32),
    )
    returned = from_root(results, "segment", phases - 1)
    returned = returned.reshape(slots, length, width)
    own = lax.dynamic_slice_in_dim(returned, phase * quarter, quarter, 2)
    back = lax.all_to_all(own, "expert", split_axis=0, concat_axis=0, tiled=True)
    out_hidden = jnp.dot(place.T, back.reshape(slots, -1), preferred_element_type=jnp.float32)
    out_hidden = out_hidden.astype(jnp.bfloat16).reshape(s_local, length, quarter)
    return (
        out_hidden,
        summed_dn.astype(jnp.bfloat16)[None, None],
        summed_upper.astype(jnp.bfloat16)[None, None],
    )


CHUNK = 512
MIB = 1024 * 1024
TRANS_RHS = (((1,), (1,)), ((), ()))
TRANS_LHS = (((0,), (0,)), ((), ()))


def matmul(left, right, dims=(((1,), (0,)), ((), ()))):
    return lax.dot_general(left, right, dims, preferred_element_type=jnp.float32)


def spread_ids(ids, shape, length):
    lane = lax.broadcasted_iota(jnp.int32, shape, 1)
    spread = jnp.zeros(shape, jnp.int32)
    for n in range(ids.shape[0]):
        spread = jnp.where(lane // length == n, ids[n], spread)
    return spread


def placement(ids_row, length, capacity, slots):
    tokens = ids_row.shape[1]
    kinds = lax.broadcasted_iota(jnp.int32, (8, tokens), 0)
    member = (kinds == ids_row).astype(jnp.float32)
    at_col = lax.broadcasted_iota(jnp.int32, (tokens, tokens), 0)
    at_row = lax.broadcasted_iota(jnp.int32, (tokens, tokens), 1)
    before = (lax.rem(at_col, length) == 0) & (at_col // length < at_row // length)
    counts = matmul(member.astype(jnp.bfloat16), before.astype(jnp.float32).astype(jnp.bfloat16))
    rank = jnp.sum(member * counts, axis=0, keepdims=True).astype(jnp.int32)
    target = (ids_row * capacity + rank) * length + lax.rem(at_row[:1], length)
    packed = lax.broadcasted_iota(jnp.int32, (slots * length, tokens), 0)
    return (packed == target).astype(jnp.float32).astype(jnp.bfloat16)


def pack_kernel(length, capacity, slots, ids, hidden, cot, send):
    groups, _, rows, part = send.shape
    tokens = hidden.shape[0] * length
    ids_row = spread_ids(ids, (8, tokens), length)[:1]
    place = placement(ids_row, length, capacity, slots)
    for which, source in enumerate((hidden, cot)):
        moved = matmul(place, source[...].reshape(tokens, part)).astype(jnp.bfloat16)
        for group in range(groups):
            send[group, which] = moved[group * rows : (group + 1) * rows]


def slice_kernel(recv, _dn, _up, _gain, *outs):
    experts, _, _, rows, part = recv.shape
    slab = outs[0].shape[2]
    place = lax.axis_index("dp")
    per_half = part // slab
    for step, out in enumerate(outs):
        chip = place ^ step
        half = chip // per_half
        cols = pl.ds(pl.multiple_of((chip - half * per_half) * slab, slab), slab)
        for which in range(2):
            for e in range(experts):
                out[which, e * rows : (e + 1) * rows] = recv[e, half, which, :, cols]


def unpack_kernel(length, capacity, slots, ids, back, out):
    groups, rows, width = back.shape
    s_local = out.shape[0]
    ids_row = spread_ids(ids, (8, s_local * length), length)[:1]
    place = placement(ids_row, length, capacity, slots)
    moved = matmul(place, back[...].reshape(groups * rows, width), TRANS_LHS)
    out[...] = moved.astype(jnp.bfloat16).reshape(s_local, length, width)


def split_three(value):
    top = value.astype(jnp.bfloat16).astype(jnp.float32)
    mid = (value - top).astype(jnp.bfloat16).astype(jnp.float32)
    low = (value - top - mid).astype(jnp.bfloat16).astype(jnp.float32)
    return [top, mid, low]


def side_by_side(columns, tokens):
    lane = lax.broadcasted_iota(jnp.int32, (tokens, 128), 1)
    block = jnp.zeros((tokens, 128), jnp.float32)
    at = 0
    for column in columns:
        for piece in split_three(column):
            block = jnp.where(lane == at, piece, block)
            at += 1
    return block.astype(jnp.bfloat16)


def lanes(value):
    total = value[:, :128]
    for start in range(128, value.shape[1], 128):
        total = total + value[:, start : start + 128]
    return total


def row_sum(parts):
    return jnp.sum(parts, axis=1, keepdims=True)


def chain_kernel(
    recv, own_dn, own_up, own_gain, other_dn, other_up, other_gain,
    small, middle,
    dn_buf, up_buf, gain_buf, entering, d_norms, sems,
):
    phase = lax.axis_index("segment")
    experts, phases, _, rows, part = recv.shape
    tokens = experts * rows
    width = phases * part
    rank = dn_buf.shape[2]
    own, other = (own_dn, own_up, own_gain), (other_dn, other_up, other_gain)

    def copies(sources, at):
        return [
            pltpu.make_async_copy(source, buffer.at[at], sems.at[at, which])
            for which, (source, buffer) in enumerate(zip(sources, (dn_buf, up_buf, gain_buf)))
        ]

    def fetch(at):
        for this in range(2):

            @pl.when(phase == this)
            def _():
                for copy in copies(own if at == this else other, at):
                    copy.start()

    fetch(0)
    waits = [copies(own, at) for at in range(2)]
    cols = range(0, width, CHUNK)

    def block(which, col):
        half, start = col // part, col % part
        return jnp.concatenate(
            [recv[e, half, which, :, start : start + CHUNK] for e in range(experts)], axis=0
        )

    def inverse_of(ref, mean):
        total = jnp.zeros((tokens, 128), jnp.float32)
        for col in cols:
            center = ref[:, col : col + CHUNK].astype(jnp.float32) - mean
            total = total + lanes(center * center)
        return lax.rsqrt(row_sum(total) / width + EPS)

    def down(ref, mean, inverse, at):
        pre = jnp.zeros((tokens, rank), jnp.float32)
        for col in cols:
            here = slice(col, col + CHUNK)
            normed = (ref[:, here].astype(jnp.float32) - mean) * inverse
            lowered = (normed * gain_buf[at, :, here].astype(jnp.float32)).astype(jnp.bfloat16)
            pre = pre + matmul(lowered, dn_buf[at, here, :])
        return pre

    total = jnp.zeros((tokens, 128), jnp.float32)
    for col in cols:
        value = block(0, col)
        entering[:, col : col + CHUNK] = value
        total = total + lanes(value.astype(jnp.float32))
    mean_0 = row_sum(total) / width
    inverse_0 = inverse_of(entering, mean_0)
    waits[0][0].wait()
    waits[0][2].wait()
    fetch(1)
    pre_0 = down(entering, mean_0, inverse_0, 0)
    act_0 = gelu_value(pre_0).astype(jnp.bfloat16)
    slope_0 = gelu_slope(pre_0)

    waits[0][1].wait()
    total = jnp.zeros((tokens, 128), jnp.float32)
    for col in cols:
        here = slice(col, col + CHUNK)
        value = entering[:, here].astype(jnp.float32) + matmul(act_0, up_buf[0, :, here])
        value = value.astype(jnp.bfloat16)
        middle[:, here] = value
        total = total + lanes(value.astype(jnp.float32))
    mean_1 = row_sum(total) / width
    inverse_1 = inverse_of(middle, mean_1)
    for copy in waits[1]:
        copy.wait()
    d_act = jnp.zeros((tokens, rank), jnp.float32)
    for col in cols:
        d_act = d_act + matmul(block(1, col), up_buf[1, :, col : col + CHUNK], TRANS_RHS)
    pre_1 = down(middle, mean_1, inverse_1, 1)
    act_1 = gelu_value(pre_1).astype(jnp.bfloat16)
    d_pre_1 = (d_act * gelu_slope(pre_1)).astype(jnp.bfloat16)

    total = jnp.zeros((tokens, 128), jnp.float32)
    cross = jnp.zeros((tokens, 128), jnp.float32)
    for col in cols:
        here = slice(col, col + CHUNK)
        wide = middle[:, here].astype(jnp.float32)
        d_norm = matmul(d_pre_1, dn_buf[1, here, :], TRANS_RHS)
        d_norm = d_norm * gain_buf[1, :, here].astype(jnp.float32)
        d_norms[:, here] = d_norm
        total = total + lanes(d_norm)
        cross = cross + lanes(d_norm * ((wide - mean_1) * inverse_1))
    shift = row_sum(total) / width
    along = row_sum(cross) / width
    d_act = jnp.zeros((tokens, rank), jnp.float32)
    for col in cols:
        here = slice(col, col + CHUNK)
        normed = (middle[:, here].astype(jnp.float32) - mean_1) * inverse_1
        grad = block(1, col).astype(jnp.float32) + inverse_1 * (
            d_norms[:, here] - shift - normed * along
        )
        d_act = d_act + matmul(grad.astype(jnp.bfloat16), up_buf[0, :, here], TRANS_RHS)
    d_pre_0 = (d_act * slope_0).astype(jnp.bfloat16)
    for at, value in enumerate((act_0, act_1, d_pre_0, d_pre_1)):
        small[:, at * rank : (at + 1) * rank] = value
    moments = (mean_0, inverse_0, mean_1, inverse_1, shift, along)
    small[:, 4 * rank :] = side_by_side(moments, tokens)


def result_kernel(middle, small, own_up, other_up, out, up_buf, sem):
    phase = lax.axis_index("segment")
    experts, _, rows, part = out.shape
    rank, width = up_buf.shape
    copies = [pltpu.make_async_copy(source, up_buf, sem) for source in (own_up, other_up)]

    @pl.when(phase == 1)
    def _():
        copies[0].start()

    @pl.when(phase != 1)
    def _():
        copies[1].start()

    copies[0].wait()
    act = small[:, rank : 2 * rank]
    for col in range(0, width, CHUNK):
        here = slice(col, col + CHUNK)
        leaving = middle[:, here].astype(jnp.float32) + matmul(act, up_buf[:, here])
        leaving = leaving.astype(jnp.bfloat16)
        half, start = col // part, col % part
        for e in range(experts):
            out[e, half, :, start : start + CHUNK] = leaving[e * rows : (e + 1) * rows]


def gradient_kernel(sources, *refs):
    slices, refs = refs[:sources], refs[sources:]
    smalls, refs = refs[:sources], refs[sources:]
    own, other, refs = refs[:3], refs[3:6], refs[7:]
    (grad_dn, grad_upper, dn_buf, up_buf, gain_buf, small, moments, lows, grads, ups, downs,
     sems) = refs
    core = lax.axis_index("segment")
    place = lax.axis_index("dp")
    _, rows, slab = slices[0].shape
    rank = dn_buf.shape[1]
    features = pl.ds(pl.multiple_of(place * slab, slab), slab)

    def copies(up, gain_first, dn, gain_second):
        moves = (
            (up.at[:, features], up_buf),
            (dn.at[features, :], dn_buf),
            (gain_first.at[:, features], gain_buf.at[0]),
            (gain_second.at[:, features], gain_buf.at[1]),
        )
        return [
            pltpu.make_async_copy(source, target, sems.at[at])
            for at, (source, target) in enumerate(moves)
        ]

    @pl.when(core == 0)
    def _():
        for copy in copies(own[1], own[2], other[0], other[2]):
            copy.start()

    @pl.when(core != 0)
    def _():
        for copy in copies(other[1], other[2], own[0], own[2]):
            copy.start()

    for source in range(sources):
        small[source * rows : (source + 1) * rows] = smalls[source][...]
    held = lax.broadcasted_iota(jnp.int32, (128, 6 * 128), 0)
    wanted = lax.broadcasted_iota(jnp.int32, (128, 6 * 128), 1) // 128
    adds = (held // 3 == wanted).astype(jnp.float32).astype(jnp.bfloat16)
    moments[...] = matmul(small[:, 4 * rank :], adds)
    for copy in copies(own[1], own[2], other[0], other[2]):
        copy.wait()

    columns = 256

    def moment(at, index):
        value = moments[at, index * 128 : (index + 1) * 128]
        return jnp.concatenate([value] * (columns // 128), axis=1)

    for col in range(0, slab, columns):
        here = slice(col, col + columns)
        ups[...] = matmul(small[:, :rank], up_buf[:, here])
        scales = [gain_buf[at, :, here].astype(jnp.float32) for at in range(2)]

        @pl.when(core == 0)
        def _():
            downs[...] = matmul(small[:, 3 * rank : 4 * rank], dn_buf[here, :], TRANS_RHS)
            for source in range(sources):
                at = slice(source * rows, (source + 1) * rows)
                wide = slices[source][0, :, here].astype(jnp.float32)
                normed = (wide - moment(at, 0)) * moment(at, 1)
                lows[at, here] = (normed * scales[0]).astype(jnp.bfloat16)
                middle = (wide + ups[at]).astype(jnp.bfloat16).astype(jnp.float32)
                inverse = moment(at, 3)
                normed = (middle - moment(at, 2)) * inverse
                d_norm = downs[at] * scales[1]
                grads[at, here] = (
                    slices[source][1, :, here].astype(jnp.float32)
                    + inverse * (d_norm - moment(at, 4) - normed * moment(at, 5))
                ).astype(jnp.bfloat16)

        @pl.when(core != 0)
        def _():
            for source in range(sources):
                at = slice(source * rows, (source + 1) * rows)
                wide = slices[source][0, :, here].astype(jnp.float32)
                middle = (wide + ups[at]).astype(jnp.bfloat16).astype(jnp.float32)
                normed = (middle - moment(at, 2)) * moment(at, 3)
                lows[at, here] = (normed * scales[1]).astype(jnp.bfloat16)
                grads[at, here] = slices[source][1, :, here]

    def finish(act, d_pre):
        for col in range(0, slab, columns):
            here = slice(col, col + columns)
            turned = matmul(d_pre, lows[:, here], TRANS_LHS).astype(jnp.bfloat16)
            grad_dn[here, :] = turned.T
            grad_upper[:, here] = matmul(act, grads[:, here], TRANS_LHS).astype(jnp.bfloat16)

    @pl.when(core == 0)
    def _():
        finish(small[:, :rank], small[:, 2 * rank : 3 * rank])

    @pl.when(core != 0)
    def _():
        finish(small[:, rank : 2 * rank], small[:, 3 * rank : 4 * rank])


VMEM = pl.BlockSpec(memory_space=pltpu.VMEM)
SMEM = pl.BlockSpec(memory_space=pltpu.SMEM)
HBM = pl.BlockSpec(memory_space=pl.ANY)


def call(kernel, name, grant, in_specs, outs, scratch=()):
    return pl.pallas_call(
        kernel,
        out_shape=tuple(jax.ShapeDtypeStruct(*out) for out in outs),
        in_specs=in_specs,
        out_specs=tuple(VMEM for _ in outs),
        scratch_shapes=list(scratch),
        compiler_params=pltpu.CompilerParams(vmem_limit_bytes=grant * MIB),
        name=name,
    )


def across(block, axis, distance):
    size = lax.axis_size(axis)
    return lax.ppermute(block, axis, [(i, i ^ distance) for i in range(size)])


def on_device_two_phases(hidden_in, cotangent, cluster_ids, w_down, w_up, gain):
    experts = lax.axis_size("expert")
    replicas = lax.axis_size("dp")
    s_local, length, part = hidden_in.shape
    width = 2 * part
    capacity = 2 * s_local // experts
    slots = experts * capacity
    groups = 2 * experts
    rows = slots * length // groups
    tokens = experts * rows
    own = (w_down[0, 0], w_up[0, 0], gain[0])
    rank = own[0].shape[1]
    slab = width // replicas
    bf16, f32 = jnp.bfloat16, jnp.float32
    sizes = (length, capacity, slots)
    sections = ("expert", "segment")

    other = tuple(across(array, "segment", 1) for array in own)
    (send,) = call(
        functools.partial(pack_kernel, *sizes),
        "pack",
        8,
        [SMEM, VMEM, VMEM],
        [((groups, 2, rows, part), bf16)],
    )(cluster_ids, hidden_in, cotangent)
    recv = lax.all_to_all(send, sections, split_axis=0, concat_axis=0, tiled=True)
    recv = recv.reshape(experts, 2, 2, rows, part)

    def gathered(blocks):
        near = [blocks[0]] + [across(blocks[step], "dp", step) for step in range(1, replicas)]
        return near + [across(piece, "segment", 1) for piece in near]

    slices = gathered(
        call(
            slice_kernel, "slices", 8, [VMEM] + [HBM] * 3, [((2, tokens, slab), bf16)] * replicas
        )(recv, *other)
    )
    small, middle = call(
        chain_kernel,
        "chain",
        24,
        [VMEM] + [HBM] * 6,
        [((tokens, 4 * rank + 128), bf16), ((tokens, width), bf16)],
        [
            pltpu.VMEM((2, width, rank), bf16),
            pltpu.VMEM((2, rank, width), bf16),
            pltpu.VMEM((2, 1, width), bf16),
            pltpu.VMEM((tokens, width), bf16),
            pltpu.VMEM((tokens, width), f32),
            pltpu.SemaphoreType.DMA((2, 3)),
        ],
    )(recv, *own, *other)
    smalls = gathered([small] * replicas)

    (out,) = call(
        result_kernel,
        "results",
        12,
        [VMEM] * 2 + [HBM] * 2,
        [((experts, 2, rows, part), bf16)],
        [pltpu.VMEM((rank, width), bf16), pltpu.SemaphoreType.DMA],
    )(middle, small, own[1], other[1])
    back = lax.all_to_all(
        out.reshape(groups, rows, part), sections, split_axis=0, concat_axis=0, tiled=True
    )
    (out_hidden,) = call(
        functools.partial(unpack_kernel, *sizes),
        "unpack",
        8,
        [SMEM, VMEM],
        [(hidden_in.shape, bf16)],
    )(cluster_ids, back)

    sources = 2 * replicas
    all_tokens = sources * tokens
    grad_dn, grad_upper = call(
        functools.partial(gradient_kernel, sources),
        "gradients",
        24,
        [VMEM] * (2 * sources) + [HBM] * 7,
        [((slab, rank), bf16), ((rank, slab), bf16)],
        [
            pltpu.VMEM((slab, rank), bf16),
            pltpu.VMEM((rank, slab), bf16),
            pltpu.VMEM((2, 1, slab), bf16),
            pltpu.VMEM((all_tokens, 4 * rank + 128), bf16),
            pltpu.VMEM((all_tokens, 6 * 128), f32),
            pltpu.VMEM((all_tokens, slab), bf16),
            pltpu.VMEM((all_tokens, slab), bf16),
            pltpu.VMEM((all_tokens, 256), f32),
            pltpu.VMEM((all_tokens, 256), f32),
            pltpu.SemaphoreType.DMA((4,)),
        ],
    )(*slices, *smalls, *own, *other, out_hidden)
    return (out_hidden, grad_dn[None, None], grad_upper[None, None])


def solution(mesh):
    two = dict(mesh.shape) == {"expert": 4, "dp": 4, "segment": 2}
    on_device = on_device_two_phases if two else on_device_pipelined
    return jax.shard_map(
        on_device,
        mesh=mesh,
        in_specs=(
            P(("expert", "dp"), None, "segment"),
            P(("expert", "dp"), None, "segment"),
            P(("expert", "dp")),
            P("expert", "segment", None, None),
            P("expert", "segment", None, None),
            P("expert", "segment", None),
        ),
        out_specs=(
            P(("expert", "dp"), None, "segment"),
            P("expert", "segment", "dp", None),
            P("expert", "segment", None, "dp"),
        ),
        check_vma=False,
    )
```

```python
import functools

import jax
import jax.numpy as jnp
from jax import lax
from jax.experimental import pallas as pl
from jax.experimental.pallas import tpu as pltpu
from jax.sharding import PartitionSpec as P

MICRO = 4


EPS = 1e-05
C_ZERO = 0.7978845608028654
C_ONE = 0.044715


def shifted(block, axis, distance):
    devices = range(lax.axis_size(axis))
    route = [(i - distance, i) for i in devices if i - distance in devices]
    return lax.ppermute(block, axis, route)


def from_root(block, axis, holder):
    block = jnp.where(lax.axis_index(axis) == holder, block, jnp.zeros_like(block))
    return lax.psum(block, axis)


def gelu_value(z):
    return 0.5 * z * (1.0 + jnp.tanh(C_ZERO * (z + C_ONE * z * z * z)))


def gelu_slope(z):
    tval = jnp.tanh(C_ZERO * (z + C_ONE * z * z * z))
    return 0.5 * (1.0 + tval) + 0.5 * z * (1.0 - tval * tval) * C_ZERO * (1.0 + 3.0 * C_ONE * z * z)


def normalize(hidden):
    wide = hidden.astype(jnp.float32)
    center = wide - jnp.mean(wide, axis=-1, keepdims=True)
    inverse = lax.rsqrt(jnp.mean(center * center, axis=-1, keepdims=True) + EPS)
    return (wide, center * inverse, inverse)


def phase_forward(hidden, w_dn, w_upper, scale):
    wide, normed, inverse = normalize(hidden)
    lowered = (normed * scale).astype(jnp.bfloat16)
    pre = jnp.dot(lowered, w_dn, preferred_element_type=jnp.float32)
    act = gelu_value(pre).astype(jnp.bfloat16)
    leaving = (wide + jnp.dot(act, w_upper, preferred_element_type=jnp.float32)).astype(
        jnp.bfloat16
    )
    return (leaving, pre)


def phase_backward(hidden, grad_in, pre, w_dn, w_upper, scale):
    wide, normed, inverse = normalize(hidden)
    lowered = (normed * scale).astype(jnp.bfloat16)
    act = gelu_value(pre).astype(jnp.bfloat16)
    d_act = jnp.dot(grad_in, w_upper.T, preferred_element_type=jnp.float32)
    d_pre = (d_act * gelu_slope(pre)).astype(jnp.bfloat16)
    d_low = jnp.dot(d_pre, w_dn.T, preferred_element_type=jnp.float32)
    d_norm = d_low * scale
    d_wide = inverse * (
        d_norm
        - jnp.mean(d_norm, axis=-1, keepdims=True)
        - normed * jnp.mean(d_norm * normed, axis=-1, keepdims=True)
    )
    grad_out = (grad_in.astype(jnp.float32) + d_wide).astype(jnp.bfloat16)
    return (grad_out, lowered, act, d_pre)


def put_slot(buffer, value, slot, valid):
    old_value = lax.dynamic_index_in_dim(buffer, slot, 0, keepdims=False)
    return lax.dynamic_update_index_in_dim(buffer, jnp.where(valid, value, old_value), slot, 0)


def on_device_pipelined(hidden_in, cotangent, cluster_ids, w_down, w_up, gain):
    experts = lax.axis_size("expert")
    phases = lax.axis_size("segment")
    phase = lax.axis_index("segment")
    s_local, length, quarter = hidden_in.shape
    capacity = 2 * s_local // experts
    slots = experts * capacity
    same = (cluster_ids[:, None] == cluster_ids[None, :]).astype(jnp.int32)
    earlier = jnp.sum(jnp.tril(same, -1), axis=1)
    target = cluster_ids * capacity + earlier
    place = (jnp.arange(slots, dtype=jnp.int32)[:, None] == target[None, :]).astype(jnp.bfloat16)

    def to_slots(local):
        flat = local.reshape(s_local, -1)
        moved = jnp.dot(place, flat, preferred_element_type=jnp.float32).astype(jnp.bfloat16)
        return moved.reshape((slots,) + local.shape[1:])

    full_in, full_cot = (
        lax.all_gather(hidden_in, "segment", axis=2, tiled=True),
        lax.all_gather(cotangent, "segment", axis=2, tiled=True),
    )
    slot_in, slot_cot = (
        lax.all_to_all(to_slots(full_in), "expert", split_axis=0, concat_axis=0, tiled=True),
        lax.all_to_all(to_slots(full_cot), "expert", split_axis=0, concat_axis=0, tiled=True),
    )
    width = slot_in.shape[2]
    micro_rows = slots * length // MICRO
    inputs = slot_in.reshape(MICRO, micro_rows, width)
    cots = slot_cot.reshape(MICRO, micro_rows, width)
    w_dn = w_down[0, 0]
    w_upper = w_up[0, 0]
    rank = w_dn.shape[1]
    scale = gain[0, 0].astype(jnp.float32)
    ticks = MICRO + phases - 1

    def forward_tick(tick, carry):
        received, saved, pres, results = carry
        which = tick - phase
        valid = (which >= 0) & (which < MICRO)
        slot = jnp.clip(which, 0, MICRO - 1)
        first = lax.dynamic_index_in_dim(inputs, jnp.minimum(tick, MICRO - 1), 0, keepdims=False)
        entering = jnp.where(phase == 0, first, received)
        leaving, pre = phase_forward(entering, w_dn, w_upper, scale)
        saved = put_slot(saved, entering, slot, valid)
        pres = put_slot(pres, pre, slot, valid)
        results = put_slot(results, leaving, slot, valid & (phase == phases - 1))
        received = shifted(leaving, "segment", 1)
        return (received, saved, pres, results)

    start = (
        jnp.zeros((micro_rows, width), jnp.bfloat16),
        jnp.zeros((MICRO, micro_rows, width), jnp.bfloat16),
        jnp.zeros((MICRO, micro_rows, rank), jnp.float32),
        jnp.zeros((MICRO, micro_rows, width), jnp.bfloat16),
    )
    received, saved, pres, results = lax.fori_loop(0, ticks, forward_tick, start)

    def backward_tick(tick, carry):
        received, lows, acts, dpres, grads = carry
        which = tick - (phases - 1 - phase)
        valid = (which >= 0) & (which < MICRO)
        slot = jnp.clip(which, 0, MICRO - 1)
        last = lax.dynamic_index_in_dim(cots, jnp.minimum(tick, MICRO - 1), 0, keepdims=False)
        grad_in = jnp.where(phase == phases - 1, last, received)
        hidden = lax.dynamic_index_in_dim(saved, slot, 0, keepdims=False)
        pre = lax.dynamic_index_in_dim(pres, slot, 0, keepdims=False)
        grad_out, lowered, act, d_pre = phase_backward(hidden, grad_in, pre, w_dn, w_upper, scale)
        lows = put_slot(lows, lowered, slot, valid)
        acts = put_slot(acts, act, slot, valid)
        dpres = put_slot(dpres, d_pre, slot, valid)
        grads = put_slot(grads, grad_in, slot, valid)
        received = shifted(grad_out, "segment", -1)
        return (received, lows, acts, dpres, grads)

    start_back = (
        jnp.zeros((micro_rows, width), jnp.bfloat16),
        jnp.zeros((MICRO, micro_rows, width), jnp.bfloat16),
        jnp.zeros((MICRO, micro_rows, rank), jnp.bfloat16),
        jnp.zeros((MICRO, micro_rows, rank), jnp.bfloat16),
        jnp.zeros((MICRO, micro_rows, width), jnp.bfloat16),
    )
    received, lows, acts, dpres, grads = lax.fori_loop(0, ticks, backward_tick, start_back)
    contract = (((0,), (0,)), ((), ()))
    grad_dn = lax.dot_general(
        lows.reshape(-1, width),
        dpres.reshape(-1, rank),
        contract,
        preferred_element_type=jnp.float32,
    )
    grad_upper = lax.dot_general(
        acts.reshape(-1, rank),
        grads.reshape(-1, width),
        contract,
        preferred_element_type=jnp.float32,
    )
    summed_dn, summed_upper = (
        lax.psum_scatter(
            grad_dn.astype(jnp.bfloat16), "dp", scatter_dimension=0, tiled=True
        ).astype(jnp.float32),
        lax.psum_scatter(
            grad_upper.astype(jnp.bfloat16), "dp", scatter_dimension=1, tiled=True
        ).astype(jnp.float32),
    )
    returned = from_root(results, "segment", phases - 1)
    returned = returned.reshape(slots, length, width)
    own = lax.dynamic_slice_in_dim(returned, phase * quarter, quarter, 2)
    back = lax.all_to_all(own, "expert", split_axis=0, concat_axis=0, tiled=True)
    out_hidden = jnp.dot(place.T, back.reshape(slots, -1), preferred_element_type=jnp.float32)
    out_hidden = out_hidden.astype(jnp.bfloat16).reshape(s_local, length, quarter)
    return (
        out_hidden,
        summed_dn.astype(jnp.bfloat16)[None, None],
        summed_upper.astype(jnp.bfloat16)[None, None],
    )


CHUNK = 512
MIB = 1024 * 1024
TRANS_RHS = (((1,), (1,)), ((), ()))
TRANS_LHS = (((0,), (0,)), ((), ()))


def matmul(left, right, dims=(((1,), (0,)), ((), ()))):
    return lax.dot_general(left, right, dims, preferred_element_type=jnp.float32)


def spread_ids(ids, shape, length):
    lane = lax.broadcasted_iota(jnp.int32, shape, 1)
    spread = jnp.zeros(shape, jnp.int32)
    for n in range(ids.shape[0]):
        spread = jnp.where(lane // length == n, ids[n], spread)
    return spread


def placement(ids_row, length, capacity, slots):
    tokens = ids_row.shape[1]
    kinds = lax.broadcasted_iota(jnp.int32, (8, tokens), 0)
    member = (kinds == ids_row).astype(jnp.float32)
    at_col = lax.broadcasted_iota(jnp.int32, (tokens, tokens), 0)
    at_row = lax.broadcasted_iota(jnp.int32, (tokens, tokens), 1)
    before = (lax.rem(at_col, length) == 0) & (at_col // length < at_row // length)
    counts = matmul(member.astype(jnp.bfloat16), before.astype(jnp.float32).astype(jnp.bfloat16))
    rank = jnp.sum(member * counts, axis=0, keepdims=True).astype(jnp.int32)
    target = (ids_row * capacity + rank) * length + lax.rem(at_row[:1], length)
    packed = lax.broadcasted_iota(jnp.int32, (slots * length, tokens), 0)
    return (packed == target).astype(jnp.float32).astype(jnp.bfloat16)


def pack_kernel(length, capacity, slots, ids, hidden, cot, send, id_buf, buf, packed, sems):
    groups, _, rows, part = send.shape
    tokens = hidden.shape[0] * length
    arriving = [
        pltpu.make_async_copy(source, target, sems.at[at])
        for at, (source, target) in enumerate(
            ((ids, id_buf), (hidden, buf.at[0]), (cot, buf.at[1]))
        )
    ]
    leaving = [
        pltpu.make_async_copy(packed.at[:, at], send.at[:, at], sems.at[3 + at]) for at in range(2)
    ]
    for copy in arriving:
        copy.start()
    arriving[0].wait()
    ids_row = spread_ids(id_buf, (8, tokens), length)[:1]
    place = placement(ids_row, length, capacity, slots)
    for which in range(2):
        arriving[1 + which].wait()
        moved = matmul(place, buf[which].reshape(tokens, part)).astype(jnp.bfloat16)
        for group in range(groups):
            packed[group, which] = moved[group * rows : (group + 1) * rows]
        leaving[which].start()
    for copy in leaving:
        copy.wait()


def slice_kernel(recv, _dn, _up, _gain, *outs):
    experts, _, _, rows, part = recv.shape
    slab = outs[0].shape[2]
    place = lax.axis_index("dp")
    per_half = part // slab
    for step, out in enumerate(outs):
        chip = place ^ step
        half = chip // per_half
        cols = pl.ds(pl.multiple_of((chip - half * per_half) * slab, slab), slab)
        for which in range(2):
            for e in range(experts):
                out[which, e * rows : (e + 1) * rows] = recv[e, half, which, :, cols]


def unpack(sizes, id_buf, back, out):
    length, capacity, slots = sizes
    groups, rows, width = back.shape
    s_local = out.shape[0]
    ids_row = spread_ids(id_buf, (8, s_local * length), length)[:1]
    place = placement(ids_row, length, capacity, slots)
    moved = matmul(place, back[...].reshape(groups * rows, width), TRANS_LHS)
    out[...] = moved.astype(jnp.bfloat16).reshape(s_local, length, width)


def split_three(value):
    top = value.astype(jnp.bfloat16).astype(jnp.float32)
    mid = (value - top).astype(jnp.bfloat16).astype(jnp.float32)
    low = (value - top - mid).astype(jnp.bfloat16).astype(jnp.float32)
    return [top, mid, low]


def side_by_side(columns, tokens):
    lane = lax.broadcasted_iota(jnp.int32, (tokens, 128), 1)
    block = jnp.zeros((tokens, 128), jnp.float32)
    at = 0
    for column in columns:
        for piece in split_three(column):
            block = jnp.where(lane == at, piece, block)
            at += 1
    return block.astype(jnp.bfloat16)


def lanes(value):
    total = value[:, :128]
    for start in range(128, value.shape[1], 128):
        total = total + value[:, start : start + 128]
    return total


def row_sum(parts):
    return jnp.sum(parts, axis=1, keepdims=True)


def chain_kernel(
    recv, own_dn, own_up, own_gain, other_dn, other_up, other_gain, _slice,
    out, small,
    dn_buf, up_buf, gain_buf, entering, middle, d_norms, sems,
):
    phase = lax.axis_index("segment")
    experts, phases, _, rows, part = recv.shape
    tokens = experts * rows
    width = phases * part
    rank = dn_buf.shape[2]
    own, other = (own_dn, own_up, own_gain), (other_dn, other_up, other_gain)

    def copies(sources, at):
        return [
            pltpu.make_async_copy(source, buffer.at[at], sems.at[at, which])
            for which, (source, buffer) in enumerate(zip(sources, (dn_buf, up_buf, gain_buf)))
        ]

    def fetch(at):
        for this in range(2):

            @pl.when(phase == this)
            def _():
                for copy in copies(own if at == this else other, at):
                    copy.start()

    fetch(0)
    waits = [copies(own, at) for at in range(2)]
    cols = range(0, width, CHUNK)

    def block(which, col):
        half, start = col // part, col % part
        return jnp.concatenate(
            [recv[e, half, which, :, start : start + CHUNK] for e in range(experts)], axis=0
        )

    def inverse_of(ref, mean):
        total = jnp.zeros((tokens, 128), jnp.float32)
        for col in cols:
            center = ref[:, col : col + CHUNK].astype(jnp.float32) - mean
            total = total + lanes(center * center)
        return lax.rsqrt(row_sum(total) / width + EPS)

    def down(ref, mean, inverse, at):
        pre = jnp.zeros((tokens, rank), jnp.float32)
        for col in cols:
            here = slice(col, col + CHUNK)
            normed = (ref[:, here].astype(jnp.float32) - mean) * inverse
            lowered = (normed * gain_buf[at, :, here].astype(jnp.float32)).astype(jnp.bfloat16)
            pre = pre + matmul(lowered, dn_buf[at, here, :])
        return pre

    total = jnp.zeros((tokens, 128), jnp.float32)
    for col in cols:
        value = block(0, col)
        entering[:, col : col + CHUNK] = value
        total = total + lanes(value.astype(jnp.float32))
    mean_0 = row_sum(total) / width
    inverse_0 = inverse_of(entering, mean_0)
    waits[0][0].wait()
    waits[0][2].wait()
    fetch(1)
    pre_0 = down(entering, mean_0, inverse_0, 0)
    act_0 = gelu_value(pre_0).astype(jnp.bfloat16)
    slope_0 = gelu_slope(pre_0)

    waits[0][1].wait()
    total = jnp.zeros((tokens, 128), jnp.float32)
    for col in cols:
        here = slice(col, col + CHUNK)
        value = entering[:, here].astype(jnp.float32) + matmul(act_0, up_buf[0, :, here])
        value = value.astype(jnp.bfloat16)
        middle[:, here] = value
        total = total + lanes(value.astype(jnp.float32))
    mean_1 = row_sum(total) / width
    inverse_1 = inverse_of(middle, mean_1)
    for copy in waits[1]:
        copy.wait()
    d_act = jnp.zeros((tokens, rank), jnp.float32)
    for col in cols:
        d_act = d_act + matmul(block(1, col), up_buf[1, :, col : col + CHUNK], TRANS_RHS)
    pre_1 = down(middle, mean_1, inverse_1, 1)
    act_1 = gelu_value(pre_1).astype(jnp.bfloat16)
    d_pre_1 = (d_act * gelu_slope(pre_1)).astype(jnp.bfloat16)

    total = jnp.zeros((tokens, 128), jnp.float32)
    cross = jnp.zeros((tokens, 128), jnp.float32)
    for col in cols:
        here = slice(col, col + CHUNK)
        wide = middle[:, here].astype(jnp.float32)
        d_norm = matmul(d_pre_1, dn_buf[1, here, :], TRANS_RHS)
        d_norm = d_norm * gain_buf[1, :, here].astype(jnp.float32)
        d_norms[:, here] = d_norm
        total = total + lanes(d_norm)
        cross = cross + lanes(d_norm * ((wide - mean_1) * inverse_1))
        leaving = (wide + matmul(act_1, up_buf[1, :, here])).astype(jnp.bfloat16)
        half, start = col // part, col % part
        for e in range(experts):
            out[e, half, :, start : start + CHUNK] = leaving[e * rows : (e + 1) * rows]
    shift = row_sum(total) / width
    along = row_sum(cross) / width
    d_act = jnp.zeros((tokens, rank), jnp.float32)
    for col in cols:
        here = slice(col, col + CHUNK)
        normed = (middle[:, here].astype(jnp.float32) - mean_1) * inverse_1
        grad = block(1, col).astype(jnp.float32) + inverse_1 * (
            d_norms[:, here] - shift - normed * along
        )
        d_act = d_act + matmul(grad.astype(jnp.bfloat16), up_buf[0, :, here], TRANS_RHS)
    d_pre_0 = (d_act * slope_0).astype(jnp.bfloat16)
    for at, value in enumerate((act_0, act_1, d_pre_0, d_pre_1)):
        small[:, at * rank : (at + 1) * rank] = value
    moments = (mean_0, inverse_0, mean_1, inverse_1, shift, along)
    small[:, 4 * rank :] = side_by_side(moments, tokens)


def join_kernel(pieces, *refs):
    rows = refs[0].shape[0]
    for at, piece in enumerate(refs[:pieces]):
        refs[-1][at * rows : (at + 1) * rows] = piece[...]


def gradient_kernel(sources, sizes, *refs):
    slices, refs = refs[:sources], refs[sources:]
    smalls, refs = refs[:2], refs[2:]
    own, other, refs = refs[:3], refs[3:6], refs[6:]
    (ids, back, out_hidden, grad_dn, grad_upper, id_buf, dn_buf, up_buf, gain_buf, small, moments,
     lows, grads, ups, downs, sems) = refs
    id_copy = pltpu.make_async_copy(ids, id_buf, sems.at[4])
    id_copy.start()
    core = lax.axis_index("segment")
    place = lax.axis_index("dp")
    _, rows, slab = slices[0].shape
    rank = dn_buf.shape[1]
    features = pl.ds(pl.multiple_of(place * slab, slab), slab)

    def copies(up, gain_first, dn, gain_second):
        moves = (
            (up.at[:, features], up_buf),
            (dn.at[features, :], dn_buf),
            (gain_first.at[:, features], gain_buf.at[0]),
            (gain_second.at[:, features], gain_buf.at[1]),
        )
        return [
            pltpu.make_async_copy(source, target, sems.at[at])
            for at, (source, target) in enumerate(moves)
        ]

    @pl.when(core == 0)
    def _():
        for copy in copies(own[1], own[2], other[0], other[2]):
            copy.start()

    @pl.when(core != 0)
    def _():
        for copy in copies(other[1], other[2], own[0], own[2]):
            copy.start()

    for core_at, source in enumerate(smalls):
        small[core_at * source.shape[0] : (core_at + 1) * source.shape[0]] = source[...]
    id_copy.wait()
    unpack(sizes, id_buf, back, out_hidden)
    held = lax.broadcasted_iota(jnp.int32, (128, 6 * 128), 0)
    wanted = lax.broadcasted_iota(jnp.int32, (128, 6 * 128), 1) // 128
    adds = (held // 3 == wanted).astype(jnp.float32).astype(jnp.bfloat16)
    moments[...] = matmul(small[:, 4 * rank :], adds)
    for copy in copies(own[1], own[2], other[0], other[2]):
        copy.wait()

    columns = 256

    def moment(at, index):
        value = moments[at, index * 128 : (index + 1) * 128]
        return jnp.concatenate([value] * (columns // 128), axis=1)

    for col in range(0, slab, columns):
        here = slice(col, col + columns)
        ups[...] = matmul(small[:, :rank], up_buf[:, here])
        scales = [gain_buf[at, :, here].astype(jnp.float32) for at in range(2)]

        @pl.when(core == 0)
        def _():
            downs[...] = matmul(small[:, 3 * rank : 4 * rank], dn_buf[here, :], TRANS_RHS)
            for source in range(sources):
                at = slice(source * rows, (source + 1) * rows)
                wide = slices[source][0, :, here].astype(jnp.float32)
                normed = (wide - moment(at, 0)) * moment(at, 1)
                lows[at, here] = (normed * scales[0]).astype(jnp.bfloat16)
                middle = (wide + ups[at]).astype(jnp.bfloat16).astype(jnp.float32)
                inverse = moment(at, 3)
                normed = (middle - moment(at, 2)) * inverse
                d_norm = downs[at] * scales[1]
                grads[at, here] = (
                    slices[source][1, :, here].astype(jnp.float32)
                    + inverse * (d_norm - moment(at, 4) - normed * moment(at, 5))
                ).astype(jnp.bfloat16)

        @pl.when(core != 0)
        def _():
            for source in range(sources):
                at = slice(source * rows, (source + 1) * rows)
                wide = slices[source][0, :, here].astype(jnp.float32)
                middle = (wide + ups[at]).astype(jnp.bfloat16).astype(jnp.float32)
                normed = (middle - moment(at, 2)) * moment(at, 3)
                lows[at, here] = (normed * scales[1]).astype(jnp.bfloat16)
                grads[at, here] = slices[source][1, :, here]

    def finish(act, d_pre):
        for col in range(0, slab, columns):
            here = slice(col, col + columns)
            turned = matmul(d_pre, lows[:, here], TRANS_LHS).astype(jnp.bfloat16)
            grad_dn[here, :] = turned.T
            grad_upper[:, here] = matmul(act, grads[:, here], TRANS_LHS).astype(jnp.bfloat16)

    @pl.when(core == 0)
    def _():
        finish(small[:, :rank], small[:, 2 * rank : 3 * rank])

    @pl.when(core != 0)
    def _():
        finish(small[:, rank : 2 * rank], small[:, 3 * rank : 4 * rank])


VMEM = pl.BlockSpec(memory_space=pltpu.VMEM)
HBM = pl.BlockSpec(memory_space=pltpu.HBM)


def call(kernel, name, grant, in_specs, outs, scratch=(), outs_in=VMEM, flops=0, moved=MIB):
    return pl.pallas_call(
        kernel,
        out_shape=tuple(jax.ShapeDtypeStruct(*out) for out in outs),
        in_specs=in_specs,
        out_specs=tuple(outs_in for _ in outs),
        scratch_shapes=list(scratch),
        compiler_params=pltpu.CompilerParams(vmem_limit_bytes=grant * MIB),
        cost_estimate=pl.CostEstimate(flops=flops, bytes_accessed=moved, transcendentals=0),
        name=name,
    )


def across(block, axis, distance):
    size = lax.axis_size(axis)
    return lax.ppermute(block, axis, [(i, i ^ distance) for i in range(size)])


def on_device_two_phases(hidden_in, cotangent, cluster_ids, w_down, w_up, gain):
    experts = lax.axis_size("expert")
    replicas = lax.axis_size("dp")
    s_local, length, part = hidden_in.shape
    width = 2 * part
    capacity = 2 * s_local // experts
    slots = experts * capacity
    groups = 2 * experts
    rows = slots * length // groups
    tokens = experts * rows
    own = (w_down[0, 0], w_up[0, 0], gain[0])
    rank = own[0].shape[1]
    slab = width // replicas
    bf16, f32 = jnp.bfloat16, jnp.float32
    sizes = (length, capacity, slots)
    sections = ("expert", "segment")

    other = tuple(across(array, "segment", 1) for array in own)
    (send,) = call(
        functools.partial(pack_kernel, *sizes),
        "pack",
        56,
        [HBM] * 3,
        [((groups, 2, rows, part), bf16)],
        [
            pltpu.SMEM(cluster_ids.shape, jnp.int32),
            pltpu.VMEM((2,) + hidden_in.shape, bf16),
            pltpu.VMEM((groups, 2, rows, part), bf16),
            pltpu.SemaphoreType.DMA((5,)),
        ],
        outs_in=HBM,
    )(cluster_ids, hidden_in, cotangent)
    recv = lax.all_to_all(send, sections, split_axis=0, concat_axis=0, tiled=True)
    recv = recv.reshape(experts, 2, 2, rows, part)

    def gathered(blocks):
        near = [blocks[0]] + [across(blocks[step], "dp", step) for step in range(1, replicas)]
        return near + [across(piece, "segment", 1) for piece in near]

    slices = gathered(
        call(
            slice_kernel, "slices", 8, [VMEM] + [HBM] * 3, [((2, tokens, slab), bf16)] * replicas
        )(recv, *other)
    )
    out, small = call(
        chain_kernel,
        "chain",
        24,
        [VMEM] + [HBM] * 6 + [pl.BlockSpec(memory_space=pl.ANY)],
        [((experts, 2, rows, part), bf16), ((tokens, 4 * rank + 128), bf16)],
        [
            pltpu.VMEM((2, width, rank), bf16),
            pltpu.VMEM((2, rank, width), bf16),
            pltpu.VMEM((2, 1, width), bf16),
            pltpu.VMEM((tokens, width), bf16),
            pltpu.VMEM((tokens, width), bf16),
            pltpu.VMEM((tokens, width), f32),
            pltpu.SemaphoreType.DMA((2, 3)),
        ],
        flops=7 * 2 * tokens * width * rank,
        moved=10 * MIB,
    )(recv, *own, *other, slices[0])
    back = lax.all_to_all(
        out.reshape(groups, rows, part), sections, split_axis=0, concat_axis=0, tiled=True
    )
    near = [small] + [across(small, "dp", step) for step in range(1, replicas)]
    waited = slices[replicas:] + [back]
    (joined,) = call(
        functools.partial(join_kernel, replicas),
        "join",
        8,
        [VMEM] * replicas + [HBM] * len(waited),
        [((replicas * tokens, 4 * rank + 128), bf16)],
    )(*near, *waited)
    smalls = (joined, across(joined, "segment", 1))
    sources = 2 * replicas
    all_tokens = sources * tokens
    out_hidden, grad_dn, grad_upper = call(
        functools.partial(gradient_kernel, sources, sizes),
        "gradients",
        24,
        [VMEM] * (sources + 2) + [HBM] * 7 + [VMEM],
        [(hidden_in.shape, bf16), ((slab, rank), bf16), ((rank, slab), bf16)],
        [
            pltpu.SMEM(cluster_ids.shape, jnp.int32),
            pltpu.VMEM((slab, rank), bf16),
            pltpu.VMEM((rank, slab), bf16),
            pltpu.VMEM((2, 1, slab), bf16),
            pltpu.VMEM((all_tokens, 4 * rank + 128), bf16),
            pltpu.VMEM((all_tokens, 6 * 128), f32),
            pltpu.VMEM((all_tokens, slab), bf16),
            pltpu.VMEM((all_tokens, slab), bf16),
            pltpu.VMEM((all_tokens, 256), f32),
            pltpu.VMEM((all_tokens, 256), f32),
            pltpu.SemaphoreType.DMA((5,)),
        ],
    )(*slices, *smalls, *own, *other, cluster_ids, back)
    return (out_hidden, grad_dn[None, None], grad_upper[None, None])


def solution(mesh):
    two = dict(mesh.shape) == {"expert": 4, "dp": 4, "segment": 2}
    on_device = on_device_two_phases if two else on_device_pipelined
    return jax.shard_map(
        on_device,
        mesh=mesh,
        in_specs=(
            P(("expert", "dp"), None, "segment"),
            P(("expert", "dp"), None, "segment"),
            P(("expert", "dp")),
            P("expert", "segment", None, None),
            P("expert", "segment", None, None),
            P("expert", "segment", None),
        ),
        out_specs=(
            P(("expert", "dp"), None, "segment"),
            P("expert", "segment", "dp", None),
            P("expert", "segment", None, "dp"),
        ),
        check_vma=False,
    )
```

```python
import functools

import jax
import jax.numpy as jnp
from jax import lax
from jax.experimental import pallas as pl
from jax.experimental.pallas import tpu as pltpu
from jax.sharding import PartitionSpec as P

MICRO = 4


EPS = 1e-05
C_ZERO = 0.7978845608028654
C_ONE = 0.044715


def shifted(block, axis, distance):
    devices = range(lax.axis_size(axis))
    route = [(i - distance, i) for i in devices if i - distance in devices]
    return lax.ppermute(block, axis, route)


def from_root(block, axis, holder):
    block = jnp.where(lax.axis_index(axis) == holder, block, jnp.zeros_like(block))
    return lax.psum(block, axis)


def gelu_value(z):
    return 0.5 * z * (1.0 + jnp.tanh(C_ZERO * (z + C_ONE * z * z * z)))


def gelu_slope(z):
    tval = jnp.tanh(C_ZERO * (z + C_ONE * z * z * z))
    return 0.5 * (1.0 + tval) + 0.5 * z * (1.0 - tval * tval) * C_ZERO * (1.0 + 3.0 * C_ONE * z * z)


def normalize(hidden):
    wide = hidden.astype(jnp.float32)
    center = wide - jnp.mean(wide, axis=-1, keepdims=True)
    inverse = lax.rsqrt(jnp.mean(center * center, axis=-1, keepdims=True) + EPS)
    return (wide, center * inverse, inverse)


def phase_forward(hidden, w_dn, w_upper, scale):
    wide, normed, inverse = normalize(hidden)
    lowered = (normed * scale).astype(jnp.bfloat16)
    pre = jnp.dot(lowered, w_dn, preferred_element_type=jnp.float32)
    act = gelu_value(pre).astype(jnp.bfloat16)
    leaving = (wide + jnp.dot(act, w_upper, preferred_element_type=jnp.float32)).astype(
        jnp.bfloat16
    )
    return (leaving, pre)


def phase_backward(hidden, grad_in, pre, w_dn, w_upper, scale):
    wide, normed, inverse = normalize(hidden)
    lowered = (normed * scale).astype(jnp.bfloat16)
    act = gelu_value(pre).astype(jnp.bfloat16)
    d_act = jnp.dot(grad_in, w_upper.T, preferred_element_type=jnp.float32)
    d_pre = (d_act * gelu_slope(pre)).astype(jnp.bfloat16)
    d_low = jnp.dot(d_pre, w_dn.T, preferred_element_type=jnp.float32)
    d_norm = d_low * scale
    d_wide = inverse * (
        d_norm
        - jnp.mean(d_norm, axis=-1, keepdims=True)
        - normed * jnp.mean(d_norm * normed, axis=-1, keepdims=True)
    )
    grad_out = (grad_in.astype(jnp.float32) + d_wide).astype(jnp.bfloat16)
    return (grad_out, lowered, act, d_pre)


def put_slot(buffer, value, slot, valid):
    old_value = lax.dynamic_index_in_dim(buffer, slot, 0, keepdims=False)
    return lax.dynamic_update_index_in_dim(buffer, jnp.where(valid, value, old_value), slot, 0)


def on_device_pipelined(hidden_in, cotangent, cluster_ids, w_down, w_up, gain):
    experts = lax.axis_size("expert")
    phases = lax.axis_size("segment")
    phase = lax.axis_index("segment")
    s_local, length, quarter = hidden_in.shape
    capacity = 2 * s_local // experts
    slots = experts * capacity
    same = (cluster_ids[:, None] == cluster_ids[None, :]).astype(jnp.int32)
    earlier = jnp.sum(jnp.tril(same, -1), axis=1)
    target = cluster_ids * capacity + earlier
    place = (jnp.arange(slots, dtype=jnp.int32)[:, None] == target[None, :]).astype(jnp.bfloat16)

    def to_slots(local):
        flat = local.reshape(s_local, -1)
        moved = jnp.dot(place, flat, preferred_element_type=jnp.float32).astype(jnp.bfloat16)
        return moved.reshape((slots,) + local.shape[1:])

    full_in, full_cot = (
        lax.all_gather(hidden_in, "segment", axis=2, tiled=True),
        lax.all_gather(cotangent, "segment", axis=2, tiled=True),
    )
    slot_in, slot_cot = (
        lax.all_to_all(to_slots(full_in), "expert", split_axis=0, concat_axis=0, tiled=True),
        lax.all_to_all(to_slots(full_cot), "expert", split_axis=0, concat_axis=0, tiled=True),
    )
    width = slot_in.shape[2]
    micro_rows = slots * length // MICRO
    inputs = slot_in.reshape(MICRO, micro_rows, width)
    cots = slot_cot.reshape(MICRO, micro_rows, width)
    w_dn = w_down[0, 0]
    w_upper = w_up[0, 0]
    rank = w_dn.shape[1]
    scale = gain[0, 0].astype(jnp.float32)
    ticks = MICRO + phases - 1

    def forward_tick(tick, carry):
        received, saved, pres, results = carry
        which = tick - phase
        valid = (which >= 0) & (which < MICRO)
        slot = jnp.clip(which, 0, MICRO - 1)
        first = lax.dynamic_index_in_dim(inputs, jnp.minimum(tick, MICRO - 1), 0, keepdims=False)
        entering = jnp.where(phase == 0, first, received)
        leaving, pre = phase_forward(entering, w_dn, w_upper, scale)
        saved = put_slot(saved, entering, slot, valid)
        pres = put_slot(pres, pre, slot, valid)
        results = put_slot(results, leaving, slot, valid & (phase == phases - 1))
        received = shifted(leaving, "segment", 1)
        return (received, saved, pres, results)

    start = (
        jnp.zeros((micro_rows, width), jnp.bfloat16),
        jnp.zeros((MICRO, micro_rows, width), jnp.bfloat16),
        jnp.zeros((MICRO, micro_rows, rank), jnp.float32),
        jnp.zeros((MICRO, micro_rows, width), jnp.bfloat16),
    )
    received, saved, pres, results = lax.fori_loop(0, ticks, forward_tick, start)

    def backward_tick(tick, carry):
        received, lows, acts, dpres, grads = carry
        which = tick - (phases - 1 - phase)
        valid = (which >= 0) & (which < MICRO)
        slot = jnp.clip(which, 0, MICRO - 1)
        last = lax.dynamic_index_in_dim(cots, jnp.minimum(tick, MICRO - 1), 0, keepdims=False)
        grad_in = jnp.where(phase == phases - 1, last, received)
        hidden = lax.dynamic_index_in_dim(saved, slot, 0, keepdims=False)
        pre = lax.dynamic_index_in_dim(pres, slot, 0, keepdims=False)
        grad_out, lowered, act, d_pre = phase_backward(hidden, grad_in, pre, w_dn, w_upper, scale)
        lows = put_slot(lows, lowered, slot, valid)
        acts = put_slot(acts, act, slot, valid)
        dpres = put_slot(dpres, d_pre, slot, valid)
        grads = put_slot(grads, grad_in, slot, valid)
        received = shifted(grad_out, "segment", -1)
        return (received, lows, acts, dpres, grads)

    start_back = (
        jnp.zeros((micro_rows, width), jnp.bfloat16),
        jnp.zeros((MICRO, micro_rows, width), jnp.bfloat16),
        jnp.zeros((MICRO, micro_rows, rank), jnp.bfloat16),
        jnp.zeros((MICRO, micro_rows, rank), jnp.bfloat16),
        jnp.zeros((MICRO, micro_rows, width), jnp.bfloat16),
    )
    received, lows, acts, dpres, grads = lax.fori_loop(0, ticks, backward_tick, start_back)
    contract = (((0,), (0,)), ((), ()))
    grad_dn = lax.dot_general(
        lows.reshape(-1, width),
        dpres.reshape(-1, rank),
        contract,
        preferred_element_type=jnp.float32,
    )
    grad_upper = lax.dot_general(
        acts.reshape(-1, rank),
        grads.reshape(-1, width),
        contract,
        preferred_element_type=jnp.float32,
    )
    summed_dn, summed_upper = (
        lax.psum_scatter(
            grad_dn.astype(jnp.bfloat16), "dp", scatter_dimension=0, tiled=True
        ).astype(jnp.float32),
        lax.psum_scatter(
            grad_upper.astype(jnp.bfloat16), "dp", scatter_dimension=1, tiled=True
        ).astype(jnp.float32),
    )
    returned = from_root(results, "segment", phases - 1)
    returned = returned.reshape(slots, length, width)
    own = lax.dynamic_slice_in_dim(returned, phase * quarter, quarter, 2)
    back = lax.all_to_all(own, "expert", split_axis=0, concat_axis=0, tiled=True)
    out_hidden = jnp.dot(place.T, back.reshape(slots, -1), preferred_element_type=jnp.float32)
    out_hidden = out_hidden.astype(jnp.bfloat16).reshape(s_local, length, quarter)
    return (
        out_hidden,
        summed_dn.astype(jnp.bfloat16)[None, None],
        summed_upper.astype(jnp.bfloat16)[None, None],
    )


CHUNK = 512
MIB = 1024 * 1024
TRANS_RHS = (((1,), (1,)), ((), ()))
TRANS_LHS = (((0,), (0,)), ((), ()))


def matmul(left, right, dims=(((1,), (0,)), ((), ()))):
    return lax.dot_general(left, right, dims, preferred_element_type=jnp.float32)


def spread_ids(ids, shape, length):
    lane = lax.broadcasted_iota(jnp.int32, shape, 1)
    spread = jnp.zeros(shape, jnp.int32)
    for n in range(ids.shape[0]):
        spread = jnp.where(lane // length == n, ids[n], spread)
    return spread


def placement(ids_row, length, capacity, slots):
    tokens = ids_row.shape[1]
    kinds = lax.broadcasted_iota(jnp.int32, (8, tokens), 0)
    member = (kinds == ids_row).astype(jnp.float32)
    at_col = lax.broadcasted_iota(jnp.int32, (tokens, tokens), 0)
    at_row = lax.broadcasted_iota(jnp.int32, (tokens, tokens), 1)
    before = (lax.rem(at_col, length) == 0) & (at_col // length < at_row // length)
    counts = matmul(member.astype(jnp.bfloat16), before.astype(jnp.float32).astype(jnp.bfloat16))
    rank = jnp.sum(member * counts, axis=0, keepdims=True).astype(jnp.int32)
    target = (ids_row * capacity + rank) * length + lax.rem(at_row[:1], length)
    packed = lax.broadcasted_iota(jnp.int32, (slots * length, tokens), 0)
    return (packed == target).astype(jnp.float32).astype(jnp.bfloat16)


def pack_kernel(length, capacity, slots, ids, hidden, cot, send, id_buf, buf, packed, sems):
    groups, _, rows, part = send.shape
    tokens = hidden.shape[0] * length
    arriving = [
        pltpu.make_async_copy(source, target, sems.at[at])
        for at, (source, target) in enumerate(
            ((ids, id_buf), (hidden, buf.at[0]), (cot, buf.at[1]))
        )
    ]
    leaving = [
        pltpu.make_async_copy(packed.at[:, at], send.at[:, at], sems.at[3 + at]) for at in range(2)
    ]
    for copy in arriving:
        copy.start()
    arriving[0].wait()
    ids_row = spread_ids(id_buf, (8, tokens), length)[:1]
    place = placement(ids_row, length, capacity, slots)
    for which in range(2):
        arriving[1 + which].wait()
        moved = matmul(place, buf[which].reshape(tokens, part)).astype(jnp.bfloat16)
        for group in range(groups):
            packed[group, which] = moved[group * rows : (group + 1) * rows]
        leaving[which].start()
    for copy in leaving:
        copy.wait()


def slice_kernel(recv, _dn, _up, _gain, *outs):
    experts, _, _, rows, part = recv.shape
    slab = outs[0].shape[2]
    place = lax.axis_index("dp")
    per_half = part // slab
    for step, out in enumerate(outs):
        chip = place ^ step
        half = chip // per_half
        cols = pl.ds(pl.multiple_of((chip - half * per_half) * slab, slab), slab)
        for which in range(2):
            for e in range(experts):
                out[which, e * rows : (e + 1) * rows] = recv[e, half, which, :, cols]


def unpack(sizes, id_buf, back, out):
    length, capacity, slots = sizes
    groups, rows, width = back.shape
    s_local = out.shape[0]
    ids_row = spread_ids(id_buf, (8, s_local * length), length)[:1]
    place = placement(ids_row, length, capacity, slots)
    moved = matmul(place, back[...].reshape(groups * rows, width), TRANS_LHS)
    out[...] = moved.astype(jnp.bfloat16).reshape(s_local, length, width)


def split_three(value):
    top = value.astype(jnp.bfloat16).astype(jnp.float32)
    mid = (value - top).astype(jnp.bfloat16).astype(jnp.float32)
    low = (value - top - mid).astype(jnp.bfloat16).astype(jnp.float32)
    return [top, mid, low]


def side_by_side(columns, tokens):
    lane = lax.broadcasted_iota(jnp.int32, (tokens, 128), 1)
    block = jnp.zeros((tokens, 128), jnp.float32)
    at = 0
    for column in columns:
        for piece in split_three(column):
            block = jnp.where(lane == at, piece, block)
            at += 1
    return block.astype(jnp.bfloat16)


def lanes(value):
    total = value[:, :128]
    for start in range(128, value.shape[1], 128):
        total = total + value[:, start : start + 128]
    return total


def row_sum(parts):
    return jnp.sum(parts, axis=1, keepdims=True)


def chain_kernel(
    recv_in, own_dn, own_up, own_gain, other_dn, other_up, other_gain,
    out, small,
    recv, dn_buf, up_buf, gain_buf, entering, middle, d_norms, sems,
):
    phase = lax.axis_index("segment")
    experts, phases, _, rows, part = recv.shape
    tokens = experts * rows
    width = phases * part
    rank = dn_buf.shape[2]
    own, other = (own_dn, own_up, own_gain), (other_dn, other_up, other_gain)

    def copies(sources, at):
        return [
            pltpu.make_async_copy(source, buffer.at[at], sems.at[at, which])
            for which, (source, buffer) in enumerate(zip(sources, (dn_buf, up_buf, gain_buf)))
        ]

    def fetch(at):
        for this in range(2):

            @pl.when(phase == this)
            def _():
                for copy in copies(own if at == this else other, at):
                    copy.start()

    arriving = [
        pltpu.make_async_copy(recv_in.at[:, :, at], recv.at[:, :, at], sems.at[2, at])
        for at in range(2)
    ]
    arriving[0].start()
    fetch(0)
    waits = [copies(own, at) for at in range(2)]
    cols = range(0, width, CHUNK)

    def block(which, col):
        half, start = col // part, col % part
        return jnp.concatenate(
            [recv[e, half, which, :, start : start + CHUNK] for e in range(experts)], axis=0
        )

    def inverse_of(ref, mean):
        total = jnp.zeros((tokens, 128), jnp.float32)
        for col in cols:
            center = ref[:, col : col + CHUNK].astype(jnp.float32) - mean
            total = total + lanes(center * center)
        return lax.rsqrt(row_sum(total) / width + EPS)

    def down(ref, mean, inverse, at):
        pre = jnp.zeros((tokens, rank), jnp.float32)
        for col in cols:
            here = slice(col, col + CHUNK)
            normed = (ref[:, here].astype(jnp.float32) - mean) * inverse
            lowered = (normed * gain_buf[at, :, here].astype(jnp.float32)).astype(jnp.bfloat16)
            pre = pre + matmul(lowered, dn_buf[at, here, :])
        return pre

    total = jnp.zeros((tokens, 128), jnp.float32)
    arriving[0].wait()
    for col in cols:
        value = block(0, col)
        entering[:, col : col + CHUNK] = value
        total = total + lanes(value.astype(jnp.float32))
    mean_0 = row_sum(total) / width
    inverse_0 = inverse_of(entering, mean_0)
    waits[0][0].wait()
    waits[0][2].wait()
    arriving[1].start()
    fetch(1)
    pre_0 = down(entering, mean_0, inverse_0, 0)
    act_0 = gelu_value(pre_0).astype(jnp.bfloat16)
    slope_0 = gelu_slope(pre_0)

    waits[0][1].wait()
    total = jnp.zeros((tokens, 128), jnp.float32)
    for col in cols:
        here = slice(col, col + CHUNK)
        value = entering[:, here].astype(jnp.float32) + matmul(act_0, up_buf[0, :, here])
        value = value.astype(jnp.bfloat16)
        middle[:, here] = value
        total = total + lanes(value.astype(jnp.float32))
    mean_1 = row_sum(total) / width
    inverse_1 = inverse_of(middle, mean_1)
    for copy in waits[1] + arriving[1:]:
        copy.wait()
    d_act = jnp.zeros((tokens, rank), jnp.float32)
    for col in cols:
        d_act = d_act + matmul(block(1, col), up_buf[1, :, col : col + CHUNK], TRANS_RHS)
    pre_1 = down(middle, mean_1, inverse_1, 1)
    act_1 = gelu_value(pre_1).astype(jnp.bfloat16)
    d_pre_1 = (d_act * gelu_slope(pre_1)).astype(jnp.bfloat16)

    total = jnp.zeros((tokens, 128), jnp.float32)
    cross = jnp.zeros((tokens, 128), jnp.float32)
    for col in cols:
        here = slice(col, col + CHUNK)
        wide = middle[:, here].astype(jnp.float32)
        d_norm = matmul(d_pre_1, dn_buf[1, here, :], TRANS_RHS)
        d_norm = d_norm * gain_buf[1, :, here].astype(jnp.float32)
        d_norms[:, here] = d_norm
        total = total + lanes(d_norm)
        cross = cross + lanes(d_norm * ((wide - mean_1) * inverse_1))
        leaving = (wide + matmul(act_1, up_buf[1, :, here])).astype(jnp.bfloat16)
        half, start = col // part, col % part
        for e in range(experts):
            out[e, half, :, start : start + CHUNK] = leaving[e * rows : (e + 1) * rows]
    shift = row_sum(total) / width
    along = row_sum(cross) / width
    d_act = jnp.zeros((tokens, rank), jnp.float32)
    for col in cols:
        here = slice(col, col + CHUNK)
        normed = (middle[:, here].astype(jnp.float32) - mean_1) * inverse_1
        grad = block(1, col).astype(jnp.float32) + inverse_1 * (
            d_norms[:, here] - shift - normed * along
        )
        d_act = d_act + matmul(grad.astype(jnp.bfloat16), up_buf[0, :, here], TRANS_RHS)
    d_pre_0 = (d_act * slope_0).astype(jnp.bfloat16)
    for at, value in enumerate((act_0, act_1, d_pre_0, d_pre_1)):
        small[:, at * rank : (at + 1) * rank] = value
    moments = (mean_0, inverse_0, mean_1, inverse_1, shift, along)
    small[:, 4 * rank :] = side_by_side(moments, tokens)


def join_kernel(pieces, *refs):
    rows = refs[0].shape[0]
    for at, piece in enumerate(refs[:pieces]):
        refs[-1][at * rows : (at + 1) * rows] = piece[...]


def gradient_kernel(sources, sizes, *refs):
    slices, refs = refs[:sources], refs[sources:]
    smalls, refs = refs[:2], refs[2:]
    own, other, refs = refs[:3], refs[3:6], refs[6:]
    (ids, back, out_hidden, grad_dn, grad_upper, id_buf, dn_buf, up_buf, gain_buf, small, moments,
     lows, grads, ups, downs, sems) = refs
    id_copy = pltpu.make_async_copy(ids, id_buf, sems.at[4])
    id_copy.start()
    core = lax.axis_index("segment")
    place = lax.axis_index("dp")
    _, rows, slab = slices[0].shape
    rank = dn_buf.shape[1]
    features = pl.ds(pl.multiple_of(place * slab, slab), slab)

    def copies(up, gain_first, dn, gain_second):
        moves = (
            (up.at[:, features], up_buf),
            (dn.at[features, :], dn_buf),
            (gain_first.at[:, features], gain_buf.at[0]),
            (gain_second.at[:, features], gain_buf.at[1]),
        )
        return [
            pltpu.make_async_copy(source, target, sems.at[at])
            for at, (source, target) in enumerate(moves)
        ]

    @pl.when(core == 0)
    def _():
        for copy in copies(own[1], own[2], other[0], other[2]):
            copy.start()

    @pl.when(core != 0)
    def _():
        for copy in copies(other[1], other[2], own[0], own[2]):
            copy.start()

    for core_at, source in enumerate(smalls):
        small[core_at * source.shape[0] : (core_at + 1) * source.shape[0]] = source[...]
    id_copy.wait()
    unpack(sizes, id_buf, back, out_hidden)
    held = lax.broadcasted_iota(jnp.int32, (128, 6 * 128), 0)
    wanted = lax.broadcasted_iota(jnp.int32, (128, 6 * 128), 1) // 128
    adds = (held // 3 == wanted).astype(jnp.float32).astype(jnp.bfloat16)
    moments[...] = matmul(small[:, 4 * rank :], adds)
    for copy in copies(own[1], own[2], other[0], other[2]):
        copy.wait()

    columns = 256

    def moment(at, index):
        value = moments[at, index * 128 : (index + 1) * 128]
        return jnp.concatenate([value] * (columns // 128), axis=1)

    for col in range(0, slab, columns):
        here = slice(col, col + columns)
        ups[...] = matmul(small[:, :rank], up_buf[:, here])
        scales = [gain_buf[at, :, here].astype(jnp.float32) for at in range(2)]

        @pl.when(core == 0)
        def _():
            downs[...] = matmul(small[:, 3 * rank : 4 * rank], dn_buf[here, :], TRANS_RHS)
            for source in range(sources):
                at = slice(source * rows, (source + 1) * rows)
                wide = slices[source][0, :, here].astype(jnp.float32)
                normed = (wide - moment(at, 0)) * moment(at, 1)
                lows[at, here] = (normed * scales[0]).astype(jnp.bfloat16)
                middle = (wide + ups[at]).astype(jnp.bfloat16).astype(jnp.float32)
                inverse = moment(at, 3)
                normed = (middle - moment(at, 2)) * inverse
                d_norm = downs[at] * scales[1]
                grads[at, here] = (
                    slices[source][1, :, here].astype(jnp.float32)
                    + inverse * (d_norm - moment(at, 4) - normed * moment(at, 5))
                ).astype(jnp.bfloat16)

        @pl.when(core != 0)
        def _():
            for source in range(sources):
                at = slice(source * rows, (source + 1) * rows)
                wide = slices[source][0, :, here].astype(jnp.float32)
                middle = (wide + ups[at]).astype(jnp.bfloat16).astype(jnp.float32)
                normed = (middle - moment(at, 2)) * moment(at, 3)
                lows[at, here] = (normed * scales[1]).astype(jnp.bfloat16)
                grads[at, here] = slices[source][1, :, here]

    def finish(act, d_pre):
        for col in range(0, slab, columns):
            here = slice(col, col + columns)
            turned = matmul(d_pre, lows[:, here], TRANS_LHS).astype(jnp.bfloat16)
            grad_dn[here, :] = turned.T
            grad_upper[:, here] = matmul(act, grads[:, here], TRANS_LHS).astype(jnp.bfloat16)

    @pl.when(core == 0)
    def _():
        finish(small[:, :rank], small[:, 2 * rank : 3 * rank])

    @pl.when(core != 0)
    def _():
        finish(small[:, rank : 2 * rank], small[:, 3 * rank : 4 * rank])


VMEM = pl.BlockSpec(memory_space=pltpu.VMEM)
HBM = pl.BlockSpec(memory_space=pltpu.HBM)


def call(kernel, name, grant, in_specs, outs, scratch=(), outs_in=VMEM, flops=0, moved=MIB):
    return pl.pallas_call(
        kernel,
        out_shape=tuple(jax.ShapeDtypeStruct(*out) for out in outs),
        in_specs=in_specs,
        out_specs=tuple(outs_in for _ in outs),
        scratch_shapes=list(scratch),
        compiler_params=pltpu.CompilerParams(vmem_limit_bytes=grant * MIB),
        cost_estimate=pl.CostEstimate(flops=flops, bytes_accessed=moved, transcendentals=0),
        name=name,
    )


def across(block, axis, distance):
    size = lax.axis_size(axis)
    return lax.ppermute(block, axis, [(i, i ^ distance) for i in range(size)])


def on_device_two_phases(hidden_in, cotangent, cluster_ids, w_down, w_up, gain):
    experts = lax.axis_size("expert")
    replicas = lax.axis_size("dp")
    s_local, length, part = hidden_in.shape
    width = 2 * part
    capacity = 2 * s_local // experts
    slots = experts * capacity
    groups = 2 * experts
    rows = slots * length // groups
    tokens = experts * rows
    own = (w_down[0, 0], w_up[0, 0], gain[0])
    rank = own[0].shape[1]
    slab = width // replicas
    bf16, f32 = jnp.bfloat16, jnp.float32
    sizes = (length, capacity, slots)
    sections = ("expert", "segment")

    other = tuple(across(array, "segment", 1) for array in own)
    (send,) = call(
        functools.partial(pack_kernel, *sizes),
        "pack",
        56,
        [HBM] * 3,
        [((groups, 2, rows, part), bf16)],
        [
            pltpu.SMEM(cluster_ids.shape, jnp.int32),
            pltpu.VMEM((2,) + hidden_in.shape, bf16),
            pltpu.VMEM((groups, 2, rows, part), bf16),
            pltpu.SemaphoreType.DMA((5,)),
        ],
        outs_in=HBM,
    )(cluster_ids, hidden_in, cotangent)
    recv = lax.all_to_all(send, sections, split_axis=0, concat_axis=0, tiled=True)
    recv = recv.reshape(experts, 2, 2, rows, part)

    def gathered(blocks):
        near = [blocks[0]] + [across(blocks[step], "dp", step) for step in range(1, replicas)]
        return near + [across(piece, "segment", 1) for piece in near]

    slices = gathered(
        call(
            slice_kernel, "slices", 8, [VMEM] + [HBM] * 3, [((2, tokens, slab), bf16)] * replicas
        )(recv, *other)
    )
    out, small = call(
        chain_kernel,
        "chain",
        60,
        [HBM] * 7,
        [((experts, 2, rows, part), bf16), ((tokens, 4 * rank + 128), bf16)],
        [
            pltpu.VMEM(recv.shape, bf16),
            pltpu.VMEM((2, width, rank), bf16),
            pltpu.VMEM((2, rank, width), bf16),
            pltpu.VMEM((2, 1, width), bf16),
            pltpu.VMEM((tokens, width), bf16),
            pltpu.VMEM((tokens, width), bf16),
            pltpu.VMEM((tokens, width), f32),
            pltpu.SemaphoreType.DMA((3, 3)),
        ],
        flops=7 * 2 * tokens * width * rank,
        moved=10 * MIB,
    )(recv, *own, *other)
    back = lax.all_to_all(
        out.reshape(groups, rows, part), sections, split_axis=0, concat_axis=0, tiled=True
    )
    two_away = across(small, "dp", 2)
    near = [small, across(small, "dp", 1), two_away, across(two_away, "dp", 1)]
    waited = slices[replicas:] + [back]
    (joined,) = call(
        functools.partial(join_kernel, replicas),
        "join",
        60,
        [VMEM] * replicas + [HBM] * len(waited),
        [((replicas * tokens, 4 * rank + 128), bf16)],
    )(*near, *waited)
    smalls = (joined, across(joined, "segment", 1))
    sources = 2 * replicas
    all_tokens = sources * tokens
    out_hidden, grad_dn, grad_upper = call(
        functools.partial(gradient_kernel, sources, sizes),
        "gradients",
        60,
        [VMEM] * (sources + 2) + [HBM] * 7 + [VMEM],
        [(hidden_in.shape, bf16), ((slab, rank), bf16), ((rank, slab), bf16)],
        [
            pltpu.SMEM(cluster_ids.shape, jnp.int32),
            pltpu.VMEM((slab, rank), bf16),
            pltpu.VMEM((rank, slab), bf16),
            pltpu.VMEM((2, 1, slab), bf16),
            pltpu.VMEM((all_tokens, 4 * rank + 128), bf16),
            pltpu.VMEM((all_tokens, 6 * 128), f32),
            pltpu.VMEM((all_tokens, slab), bf16),
            pltpu.VMEM((all_tokens, slab), bf16),
            pltpu.VMEM((all_tokens, 256), f32),
            pltpu.VMEM((all_tokens, 256), f32),
            pltpu.SemaphoreType.DMA((5,)),
        ],
    )(*slices, *smalls, *own, *other, cluster_ids, back)
    return (out_hidden, grad_dn[None, None], grad_upper[None, None])


def solution(mesh):
    two = dict(mesh.shape) == {"expert": 4, "dp": 4, "segment": 2}
    on_device = on_device_two_phases if two else on_device_pipelined
    return jax.shard_map(
        on_device,
        mesh=mesh,
        in_specs=(
            P(("expert", "dp"), None, "segment"),
            P(("expert", "dp"), None, "segment"),
            P(("expert", "dp")),
            P("expert", "segment", None, None),
            P("expert", "segment", None, None),
            P("expert", "segment", None),
        ),
        out_specs=(
            P(("expert", "dp"), None, "segment"),
            P("expert", "segment", "dp", None),
            P("expert", "segment", None, "dp"),
        ),
        check_vma=False,
    )
```

```python
import functools

import jax
import jax.numpy as jnp
from jax import lax
from jax.experimental import pallas as pl
from jax.experimental.pallas import tpu as pltpu
from jax.sharding import PartitionSpec as P

MICRO = 4


EPS = 1e-05
C_ZERO = 0.7978845608028654
C_ONE = 0.044715


def shifted(block, axis, distance):
    devices = range(lax.axis_size(axis))
    route = [(i - distance, i) for i in devices if i - distance in devices]
    return lax.ppermute(block, axis, route)


def from_root(block, axis, holder):
    block = jnp.where(lax.axis_index(axis) == holder, block, jnp.zeros_like(block))
    return lax.psum(block, axis)


def gelu_value(z):
    return 0.5 * z * (1.0 + jnp.tanh(C_ZERO * (z + C_ONE * z * z * z)))


def gelu_slope(z):
    tval = jnp.tanh(C_ZERO * (z + C_ONE * z * z * z))
    return 0.5 * (1.0 + tval) + 0.5 * z * (1.0 - tval * tval) * C_ZERO * (1.0 + 3.0 * C_ONE * z * z)


def normalize(hidden):
    wide = hidden.astype(jnp.float32)
    center = wide - jnp.mean(wide, axis=-1, keepdims=True)
    inverse = lax.rsqrt(jnp.mean(center * center, axis=-1, keepdims=True) + EPS)
    return (wide, center * inverse, inverse)


def phase_forward(hidden, w_dn, w_upper, scale):
    wide, normed, inverse = normalize(hidden)
    lowered = (normed * scale).astype(jnp.bfloat16)
    pre = jnp.dot(lowered, w_dn, preferred_element_type=jnp.float32)
    act = gelu_value(pre).astype(jnp.bfloat16)
    leaving = (wide + jnp.dot(act, w_upper, preferred_element_type=jnp.float32)).astype(
        jnp.bfloat16
    )
    return (leaving, pre)


def phase_backward(hidden, grad_in, pre, w_dn, w_upper, scale):
    wide, normed, inverse = normalize(hidden)
    lowered = (normed * scale).astype(jnp.bfloat16)
    act = gelu_value(pre).astype(jnp.bfloat16)
    d_act = jnp.dot(grad_in, w_upper.T, preferred_element_type=jnp.float32)
    d_pre = (d_act * gelu_slope(pre)).astype(jnp.bfloat16)
    d_low = jnp.dot(d_pre, w_dn.T, preferred_element_type=jnp.float32)
    d_norm = d_low * scale
    d_wide = inverse * (
        d_norm
        - jnp.mean(d_norm, axis=-1, keepdims=True)
        - normed * jnp.mean(d_norm * normed, axis=-1, keepdims=True)
    )
    grad_out = (grad_in.astype(jnp.float32) + d_wide).astype(jnp.bfloat16)
    return (grad_out, lowered, act, d_pre)


def put_slot(buffer, value, slot, valid):
    old_value = lax.dynamic_index_in_dim(buffer, slot, 0, keepdims=False)
    return lax.dynamic_update_index_in_dim(buffer, jnp.where(valid, value, old_value), slot, 0)


def on_device_pipelined(hidden_in, cotangent, cluster_ids, w_down, w_up, gain):
    experts = lax.axis_size("expert")
    phases = lax.axis_size("segment")
    phase = lax.axis_index("segment")
    s_local, length, quarter = hidden_in.shape
    capacity = 2 * s_local // experts
    slots = experts * capacity
    same = (cluster_ids[:, None] == cluster_ids[None, :]).astype(jnp.int32)
    earlier = jnp.sum(jnp.tril(same, -1), axis=1)
    target = cluster_ids * capacity + earlier
    place = (jnp.arange(slots, dtype=jnp.int32)[:, None] == target[None, :]).astype(jnp.bfloat16)

    def to_slots(local):
        flat = local.reshape(s_local, -1)
        moved = jnp.dot(place, flat, preferred_element_type=jnp.float32).astype(jnp.bfloat16)
        return moved.reshape((slots,) + local.shape[1:])

    full_in, full_cot = (
        lax.all_gather(hidden_in, "segment", axis=2, tiled=True),
        lax.all_gather(cotangent, "segment", axis=2, tiled=True),
    )
    slot_in, slot_cot = (
        lax.all_to_all(to_slots(full_in), "expert", split_axis=0, concat_axis=0, tiled=True),
        lax.all_to_all(to_slots(full_cot), "expert", split_axis=0, concat_axis=0, tiled=True),
    )
    width = slot_in.shape[2]
    micro_rows = slots * length // MICRO
    inputs = slot_in.reshape(MICRO, micro_rows, width)
    cots = slot_cot.reshape(MICRO, micro_rows, width)
    w_dn = w_down[0, 0]
    w_upper = w_up[0, 0]
    rank = w_dn.shape[1]
    scale = gain[0, 0].astype(jnp.float32)
    ticks = MICRO + phases - 1

    def forward_tick(tick, carry):
        received, saved, pres, results = carry
        which = tick - phase
        valid = (which >= 0) & (which < MICRO)
        slot = jnp.clip(which, 0, MICRO - 1)
        first = lax.dynamic_index_in_dim(inputs, jnp.minimum(tick, MICRO - 1), 0, keepdims=False)
        entering = jnp.where(phase == 0, first, received)
        leaving, pre = phase_forward(entering, w_dn, w_upper, scale)
        saved = put_slot(saved, entering, slot, valid)
        pres = put_slot(pres, pre, slot, valid)
        results = put_slot(results, leaving, slot, valid & (phase == phases - 1))
        received = shifted(leaving, "segment", 1)
        return (received, saved, pres, results)

    start = (
        jnp.zeros((micro_rows, width), jnp.bfloat16),
        jnp.zeros((MICRO, micro_rows, width), jnp.bfloat16),
        jnp.zeros((MICRO, micro_rows, rank), jnp.float32),
        jnp.zeros((MICRO, micro_rows, width), jnp.bfloat16),
    )
    received, saved, pres, results = lax.fori_loop(0, ticks, forward_tick, start)

    def backward_tick(tick, carry):
        received, lows, acts, dpres, grads = carry
        which = tick - (phases - 1 - phase)
        valid = (which >= 0) & (which < MICRO)
        slot = jnp.clip(which, 0, MICRO - 1)
        last = lax.dynamic_index_in_dim(cots, jnp.minimum(tick, MICRO - 1), 0, keepdims=False)
        grad_in = jnp.where(phase == phases - 1, last, received)
        hidden = lax.dynamic_index_in_dim(saved, slot, 0, keepdims=False)
        pre = lax.dynamic_index_in_dim(pres, slot, 0, keepdims=False)
        grad_out, lowered, act, d_pre = phase_backward(hidden, grad_in, pre, w_dn, w_upper, scale)
        lows = put_slot(lows, lowered, slot, valid)
        acts = put_slot(acts, act, slot, valid)
        dpres = put_slot(dpres, d_pre, slot, valid)
        grads = put_slot(grads, grad_in, slot, valid)
        received = shifted(grad_out, "segment", -1)
        return (received, lows, acts, dpres, grads)

    start_back = (
        jnp.zeros((micro_rows, width), jnp.bfloat16),
        jnp.zeros((MICRO, micro_rows, width), jnp.bfloat16),
        jnp.zeros((MICRO, micro_rows, rank), jnp.bfloat16),
        jnp.zeros((MICRO, micro_rows, rank), jnp.bfloat16),
        jnp.zeros((MICRO, micro_rows, width), jnp.bfloat16),
    )
    received, lows, acts, dpres, grads = lax.fori_loop(0, ticks, backward_tick, start_back)
    contract = (((0,), (0,)), ((), ()))
    grad_dn = lax.dot_general(
        lows.reshape(-1, width),
        dpres.reshape(-1, rank),
        contract,
        preferred_element_type=jnp.float32,
    )
    grad_upper = lax.dot_general(
        acts.reshape(-1, rank),
        grads.reshape(-1, width),
        contract,
        preferred_element_type=jnp.float32,
    )
    summed_dn, summed_upper = (
        lax.psum_scatter(
            grad_dn.astype(jnp.bfloat16), "dp", scatter_dimension=0, tiled=True
        ).astype(jnp.float32),
        lax.psum_scatter(
            grad_upper.astype(jnp.bfloat16), "dp", scatter_dimension=1, tiled=True
        ).astype(jnp.float32),
    )
    returned = from_root(results, "segment", phases - 1)
    returned = returned.reshape(slots, length, width)
    own = lax.dynamic_slice_in_dim(returned, phase * quarter, quarter, 2)
    back = lax.all_to_all(own, "expert", split_axis=0, concat_axis=0, tiled=True)
    out_hidden = jnp.dot(place.T, back.reshape(slots, -1), preferred_element_type=jnp.float32)
    out_hidden = out_hidden.astype(jnp.bfloat16).reshape(s_local, length, quarter)
    return (
        out_hidden,
        summed_dn.astype(jnp.bfloat16)[None, None],
        summed_upper.astype(jnp.bfloat16)[None, None],
    )


CHUNK = 512
MIB = 1024 * 1024
TRANS_RHS = (((1,), (1,)), ((), ()))
TRANS_LHS = (((0,), (0,)), ((), ()))


def matmul(left, right, dims=(((1,), (0,)), ((), ()))):
    return lax.dot_general(left, right, dims, preferred_element_type=jnp.float32)


def spread_ids(ids, shape, length):
    lane = lax.broadcasted_iota(jnp.int32, shape, 1)
    spread = jnp.zeros(shape, jnp.int32)
    for n in range(ids.shape[0]):
        spread = jnp.where(lane // length == n, ids[n], spread)
    return spread


def ranked(ids_row, length):
    tokens = ids_row.shape[1]
    kinds = lax.broadcasted_iota(jnp.int32, (8, tokens), 0)
    member = (kinds == ids_row).astype(jnp.float32)
    at_col = lax.broadcasted_iota(jnp.int32, (tokens, tokens), 0)
    at_row = lax.broadcasted_iota(jnp.int32, (tokens, tokens), 1)
    before = (lax.rem(at_col, length) == 0) & (at_col // length < at_row // length)
    counts = matmul(member.astype(jnp.bfloat16), before.astype(jnp.float32).astype(jnp.bfloat16))
    rank = jnp.sum(member * counts, axis=0, keepdims=True)
    total = jnp.sum(member, axis=1, keepdims=True) * (1.0 / length)
    lower = jnp.sum(jnp.where(kinds < ids_row, total, 0.0), axis=0, keepdims=True)
    return rank.astype(jnp.int32), lower.astype(jnp.int32)


def one_hot(target, rows):
    wanted = lax.broadcasted_iota(jnp.int32, (rows, target.shape[1]), 0)
    return (wanted == target).astype(jnp.float32).astype(jnp.bfloat16)


def placements(ids_row, length, capacity, slots):
    rank, lower = ranked(ids_row, length)
    token = lax.rem(lax.broadcasted_iota(jnp.int32, ids_row.shape, 1), length)
    place = rank + lower
    group = lax.rem(place, 2)
    per_core = capacity // 2
    packed = ((ids_row * 2 + group) * per_core + rank // 2) * length + token
    tokens = ids_row.shape[1]
    ordered = group * (tokens // 2) + (place // 2) * length + token
    return one_hot(packed, slots * length), one_hot(ordered, tokens)


def pack_kernel(length, capacity, slots, ids, hidden, cot, *refs):
    send, slabs, refs = refs[0], refs[1:5], refs[5:]
    id_buf, buf, packed, ordered, turned, out_slabs, sems = refs
    groups, _, rows, part = send.shape
    tokens = hidden.shape[0] * length
    slab = part // 2
    half = tokens // 2
    replica = lax.axis_index("dp")
    arriving = [
        pltpu.make_async_copy(source, target, sems.at[at])
        for at, (source, target) in enumerate(
            ((ids, id_buf), (hidden, buf.at[0]), (cot, buf.at[1]))
        )
    ]
    leaving = [
        pltpu.make_async_copy(packed.at[:, at], send.at[:, at], sems.at[3 + at]) for at in range(2)
    ]
    sliding = [
        pltpu.make_async_copy(out_slabs.at[at], slabs[at], sems.at[5 + at]) for at in range(4)
    ]
    for copy in arriving:
        copy.start()
    arriving[0].wait()
    ids_row = spread_ids(id_buf, (16, tokens), length)
    by_slot, by_group = placements(ids_row[:1], length, capacity, slots)
    for group in range(2):
        mine = by_group[group * half : (group + 1) * half]
        clusters = matmul(ids_row.astype(jnp.float32).astype(jnp.bfloat16), mine, TRANS_RHS)
        turned[group] = jnp.concatenate(
            [clusters.astype(jnp.bfloat16), jnp.zeros((16, 128 - half), jnp.bfloat16)], axis=1
        )
    for which in range(2):
        arriving[1 + which].wait()
        flat = buf[which].reshape(tokens, part)
        moved = matmul(by_slot, flat).astype(jnp.bfloat16)
        for group in range(groups):
            packed[group, which] = moved[group * rows : (group + 1) * rows]
        leaving[which].start()
        ordered[which] = matmul(by_group, flat).astype(jnp.bfloat16)
    for turn in range(4):
        pair = (turn // 2) ^ (replica & 1)
        group = (turn % 2) ^ (replica >> 1)
        cols = pl.ds(pl.multiple_of(pair * slab, slab), slab)
        at = pl.ds(pl.multiple_of(group * half, half), half)
        for which in range(2):
            out_slabs[turn, which * half : (which + 1) * half] = ordered[which, at, cols]
        out_slabs[turn, tokens:] = jnp.zeros((16, slab), jnp.bfloat16)
        out_slabs[turn, tokens:, :128] = turned[group]
        sliding[turn].start()
    for copy in leaving + sliding:
        copy.wait()


def repack_kernel(length, capacity, *refs):
    slabs, outs = refs[:4], refs[5:]
    experts, rows = len(outs), outs[0].shape[2]
    half = (slabs[0].shape[0] - 16) // 2
    core, replica = lax.axis_index("segment"), lax.axis_index("dp")
    for turn, slab in enumerate(slabs):
        near = turn // 2 + 2 * ((turn % 2) ^ (replica >> 1) ^ core)
        ids_row = slab[2 * half :, :128].astype(jnp.float32)[:1, :half].astype(jnp.int32)
        rank, _ = ranked(ids_row, length)
        token = lax.rem(lax.broadcasted_iota(jnp.int32, ids_row.shape, 1), length)
        step = ids_row ^ lax.axis_index("expert")
        place = one_hot((step * (capacity // 2) + rank) * length + token, experts * rows)
        for which in range(2):
            moved = matmul(place, slab[which * half : (which + 1) * half]).astype(jnp.bfloat16)
            for e in range(experts):
                outs[e][which, near] = moved[e * rows : (e + 1) * rows]


def unpack(sizes, id_buf, back, out):
    length, capacity, slots = sizes
    groups, rows, width = back.shape
    s_local = out.shape[0]
    ids_row = spread_ids(id_buf, (8, s_local * length), length)[:1]
    place, _ = placements(ids_row, length, capacity, slots)
    moved = matmul(place, back[...].reshape(groups * rows, width), TRANS_LHS)
    out[...] = moved.astype(jnp.bfloat16).reshape(s_local, length, width)


def split_three(value):
    top = value.astype(jnp.bfloat16).astype(jnp.float32)
    mid = (value - top).astype(jnp.bfloat16).astype(jnp.float32)
    low = (value - top - mid).astype(jnp.bfloat16).astype(jnp.float32)
    return [top, mid, low]


def side_by_side(columns, tokens):
    lane = lax.broadcasted_iota(jnp.int32, (tokens, 128), 1)
    block = jnp.zeros((tokens, 128), jnp.float32)
    at = 0
    for column in columns:
        for piece in split_three(column):
            block = jnp.where(lane == at, piece, block)
            at += 1
    return block.astype(jnp.bfloat16)


def lanes(value):
    total = value[:, :128]
    for start in range(128, value.shape[1], 128):
        total = total + value[:, start : start + 128]
    return total


def row_sum(parts):
    return jnp.sum(parts, axis=1, keepdims=True)


def chain_kernel(
    recv_in, own_dn, own_up, own_gain, other_dn, other_up, other_gain,
    small, middle,
    recv, dn_buf, up_buf, gain_buf, entering, d_norms, sems,
):
    phase = lax.axis_index("segment")
    experts, phases, _, rows, part = recv.shape
    tokens = experts * rows
    width = phases * part
    rank = dn_buf.shape[2]
    own, other = (own_dn, own_up, own_gain), (other_dn, other_up, other_gain)

    def copies(sources, at):
        return [
            pltpu.make_async_copy(source, buffer.at[at], sems.at[at, which])
            for which, (source, buffer) in enumerate(zip(sources, (dn_buf, up_buf, gain_buf)))
        ]

    def fetch(at):
        for this in range(2):

            @pl.when(phase == this)
            def _():
                for copy in copies(own if at == this else other, at):
                    copy.start()

    arriving = [
        pltpu.make_async_copy(recv_in.at[:, :, at], recv.at[:, :, at], sems.at[2, at])
        for at in range(2)
    ]
    arriving[0].start()
    fetch(0)
    waits = [copies(own, at) for at in range(2)]
    cols = range(0, width, CHUNK)

    def block(which, col):
        half, start = col // part, col % part
        return jnp.concatenate(
            [recv[e, half, which, :, start : start + CHUNK] for e in range(experts)], axis=0
        )

    def inverse_of(ref, mean):
        total = jnp.zeros((tokens, 128), jnp.float32)
        for col in cols:
            center = ref[:, col : col + CHUNK].astype(jnp.float32) - mean
            total = total + lanes(center * center)
        return lax.rsqrt(row_sum(total) / width + EPS)

    def down(ref, mean, inverse, at):
        pre = jnp.zeros((tokens, rank), jnp.float32)
        for col in cols:
            here = slice(col, col + CHUNK)
            normed = (ref[:, here].astype(jnp.float32) - mean) * inverse
            lowered = (normed * gain_buf[at, :, here].astype(jnp.float32)).astype(jnp.bfloat16)
            pre = pre + matmul(lowered, dn_buf[at, here, :])
        return pre

    total = jnp.zeros((tokens, 128), jnp.float32)
    arriving[0].wait()
    for col in cols:
        value = block(0, col)
        entering[:, col : col + CHUNK] = value
        total = total + lanes(value.astype(jnp.float32))
    mean_0 = row_sum(total) / width
    inverse_0 = inverse_of(entering, mean_0)
    waits[0][0].wait()
    waits[0][2].wait()
    arriving[1].start()
    fetch(1)
    pre_0 = down(entering, mean_0, inverse_0, 0)
    act_0 = gelu_value(pre_0).astype(jnp.bfloat16)
    slope_0 = gelu_slope(pre_0)

    waits[0][1].wait()
    total = jnp.zeros((tokens, 128), jnp.float32)
    for col in cols:
        here = slice(col, col + CHUNK)
        value = entering[:, here].astype(jnp.float32) + matmul(act_0, up_buf[0, :, here])
        value = value.astype(jnp.bfloat16)
        middle[:, here] = value
        total = total + lanes(value.astype(jnp.float32))
    mean_1 = row_sum(total) / width
    inverse_1 = inverse_of(middle, mean_1)
    for copy in waits[1] + arriving[1:]:
        copy.wait()
    d_act = jnp.zeros((tokens, rank), jnp.float32)
    for col in cols:
        d_act = d_act + matmul(block(1, col), up_buf[1, :, col : col + CHUNK], TRANS_RHS)
    pre_1 = down(middle, mean_1, inverse_1, 1)
    act_1 = gelu_value(pre_1).astype(jnp.bfloat16)
    d_pre_1 = (d_act * gelu_slope(pre_1)).astype(jnp.bfloat16)

    total = jnp.zeros((tokens, 128), jnp.float32)
    cross = jnp.zeros((tokens, 128), jnp.float32)
    for col in cols:
        here = slice(col, col + CHUNK)
        wide = middle[:, here].astype(jnp.float32)
        d_norm = matmul(d_pre_1, dn_buf[1, here, :], TRANS_RHS)
        d_norm = d_norm * gain_buf[1, :, here].astype(jnp.float32)
        d_norms[:, here] = d_norm
        total = total + lanes(d_norm)
        cross = cross + lanes(d_norm * ((wide - mean_1) * inverse_1))
    shift = row_sum(total) / width
    along = row_sum(cross) / width
    d_act = jnp.zeros((tokens, rank), jnp.float32)
    for col in cols:
        here = slice(col, col + CHUNK)
        normed = (middle[:, here].astype(jnp.float32) - mean_1) * inverse_1
        grad = block(1, col).astype(jnp.float32) + inverse_1 * (
            d_norms[:, here] - shift - normed * along
        )
        d_act = d_act + matmul(grad.astype(jnp.bfloat16), up_buf[0, :, here], TRANS_RHS)
    d_pre_0 = (d_act * slope_0).astype(jnp.bfloat16)
    for at, value in enumerate((act_0, act_1, d_pre_0, d_pre_1)):
        small[:, at * rank : (at + 1) * rank] = value
    moments = (mean_0, inverse_0, mean_1, inverse_1, shift, along)
    small[:, 4 * rank :] = side_by_side(moments, tokens)


def result_kernel(middle, small, own_up, other_up, out, up_buf, sem):
    phase = lax.axis_index("segment")
    experts, _, rows, part = out.shape
    rank, width = up_buf.shape
    copies = [pltpu.make_async_copy(source, up_buf, sem) for source in (own_up, other_up)]

    @pl.when(phase == 1)
    def _():
        copies[0].start()

    @pl.when(phase != 1)
    def _():
        copies[1].start()

    copies[0].wait()
    act = small[:, rank : 2 * rank]
    for col in range(0, width, CHUNK):
        here = slice(col, col + CHUNK)
        leaving = middle[:, here].astype(jnp.float32) + matmul(act, up_buf[:, here])
        leaving = leaving.astype(jnp.bfloat16)
        half, start = col // part, col % part
        for e in range(experts):
            out[e, half, :, start : start + CHUNK] = leaving[e * rows : (e + 1) * rows]


def gradient_kernel(experts, sources, sizes, *refs):
    sides, refs = (refs[:experts], refs[experts : 2 * experts]), refs[2 * experts :]
    smalls, refs = refs[:sources], refs[sources:]
    own, other, refs = refs[:3], refs[3:6], refs[6:]
    (ids, back, out_hidden, grad_dn, grad_upper, id_buf, dn_buf, up_buf, gain_buf, small, moments,
     lows, grads, ups, downs, sems) = refs
    id_copy = pltpu.make_async_copy(ids, id_buf, sems.at[4])
    id_copy.start()
    core = lax.axis_index("segment")
    place = lax.axis_index("dp")
    _, replicas, _, slab = sides[0][0].shape
    rows = smalls[0].shape[0]
    rank = dn_buf.shape[1]
    features = pl.ds(pl.multiple_of(place * slab, slab), slab)

    def copies(up, gain_first, dn, gain_second):
        moves = (
            (up.at[:, features], up_buf),
            (dn.at[features, :], dn_buf),
            (gain_first.at[:, features], gain_buf.at[0]),
            (gain_second.at[:, features], gain_buf.at[1]),
        )
        return [
            pltpu.make_async_copy(source, target, sems.at[at])
            for at, (source, target) in enumerate(moves)
        ]

    @pl.when(core == 0)
    def _():
        for copy in copies(own[1], own[2], other[0], other[2]):
            copy.start()

    @pl.when(core != 0)
    def _():
        for copy in copies(other[1], other[2], own[0], own[2]):
            copy.start()

    per_expert = rows // experts
    for source in range(sources):
        for step in range(experts):
            to = source * rows + step * per_expert
            start = (lax.axis_index("expert") ^ step) * per_expert
            small[to : to + per_expert] = smalls[source][
                pl.ds(pl.multiple_of(start, per_expert), per_expert)
            ]

    def sliced(source, which, here):
        side, near = sides[source // replicas], source % replicas
        return jnp.concatenate([side[e][which, near, :, here] for e in range(experts)], axis=0)

    id_copy.wait()
    unpack(sizes, id_buf, back, out_hidden)
    held = lax.broadcasted_iota(jnp.int32, (128, 6 * 128), 0)
    wanted = lax.broadcasted_iota(jnp.int32, (128, 6 * 128), 1) // 128
    adds = (held // 3 == wanted).astype(jnp.float32).astype(jnp.bfloat16)
    moments[...] = matmul(small[:, 4 * rank :], adds)
    for copy in copies(own[1], own[2], other[0], other[2]):
        copy.wait()

    columns = 256

    def moment(at, index):
        value = moments[at, index * 128 : (index + 1) * 128]
        return jnp.concatenate([value] * (columns // 128), axis=1)

    for col in range(0, slab, columns):
        here = slice(col, col + columns)
        ups[...] = matmul(small[:, :rank], up_buf[:, here])
        scales = [gain_buf[at, :, here].astype(jnp.float32) for at in range(2)]

        @pl.when(core == 0)
        def _():
            downs[...] = matmul(small[:, 3 * rank : 4 * rank], dn_buf[here, :], TRANS_RHS)
            for source in range(sources):
                at = slice(source * rows, (source + 1) * rows)
                wide = sliced(source, 0, here).astype(jnp.float32)
                normed = (wide - moment(at, 0)) * moment(at, 1)
                lows[at, here] = (normed * scales[0]).astype(jnp.bfloat16)
                middle = (wide + ups[at]).astype(jnp.bfloat16).astype(jnp.float32)
                inverse = moment(at, 3)
                normed = (middle - moment(at, 2)) * inverse
                d_norm = downs[at] * scales[1]
                grads[at, here] = (
                    sliced(source, 1, here).astype(jnp.float32)
                    + inverse * (d_norm - moment(at, 4) - normed * moment(at, 5))
                ).astype(jnp.bfloat16)

        @pl.when(core != 0)
        def _():
            for source in range(sources):
                at = slice(source * rows, (source + 1) * rows)
                wide = sliced(source, 0, here).astype(jnp.float32)
                middle = (wide + ups[at]).astype(jnp.bfloat16).astype(jnp.float32)
                normed = (middle - moment(at, 2)) * moment(at, 3)
                lows[at, here] = (normed * scales[1]).astype(jnp.bfloat16)
                grads[at, here] = sliced(source, 1, here)

    def finish(act, d_pre):
        for col in range(0, slab, columns):
            here = slice(col, col + columns)
            turned = matmul(d_pre, lows[:, here], TRANS_LHS).astype(jnp.bfloat16)
            grad_dn[here, :] = turned.T
            grad_upper[:, here] = matmul(act, grads[:, here], TRANS_LHS).astype(jnp.bfloat16)

    @pl.when(core == 0)
    def _():
        finish(small[:, :rank], small[:, 2 * rank : 3 * rank])

    @pl.when(core != 0)
    def _():
        finish(small[:, rank : 2 * rank], small[:, 3 * rank : 4 * rank])


VMEM = pl.BlockSpec(memory_space=pltpu.VMEM)
HBM = pl.BlockSpec(memory_space=pltpu.HBM)


def call(kernel, name, grant, in_specs, outs, scratch=(), outs_in=VMEM, flops=0, moved=MIB):
    return pl.pallas_call(
        kernel,
        out_shape=tuple(jax.ShapeDtypeStruct(*out) for out in outs),
        in_specs=in_specs,
        out_specs=tuple(outs_in for _ in outs),
        scratch_shapes=list(scratch),
        compiler_params=pltpu.CompilerParams(vmem_limit_bytes=grant * MIB),
        cost_estimate=pl.CostEstimate(flops=flops, bytes_accessed=moved, transcendentals=0),
        name=name,
    )


def across(block, axis, distance):
    size = lax.axis_size(axis)
    return lax.ppermute(block, axis, [(i, i ^ distance) for i in range(size)])


def slab_route(replicas, pair, low):
    route = []
    for replica in range(replicas):
        for core in range(2):
            chip = 2 * core + ((replica & 1) ^ pair)
            route.append((2 * replica + core, 2 * chip + ((replica >> 1) ^ low)))
    return route


def on_device_two_phases(hidden_in, cotangent, cluster_ids, w_down, w_up, gain):
    experts = lax.axis_size("expert")
    replicas = lax.axis_size("dp")
    s_local, length, part = hidden_in.shape
    width = 2 * part
    capacity = 2 * s_local // experts
    slots = experts * capacity
    groups = 2 * experts
    rows = slots * length // groups
    tokens = experts * rows
    own = (w_down[0, 0], w_up[0, 0], gain[0])
    rank = own[0].shape[1]
    slab = width // replicas
    bf16, f32 = jnp.bfloat16, jnp.float32
    sizes = (length, capacity, slots)
    sections = ("expert", "segment")

    other_dn = across(own[0], "segment", 1)
    half = s_local * length // 2
    send, *slabs = call(
        functools.partial(pack_kernel, *sizes),
        "pack",
        60,
        [HBM] * 3,
        [((groups, 2, rows, part), bf16)] + [((2 * half + 16, slab), bf16)] * 4,
        [
            pltpu.SMEM(cluster_ids.shape, jnp.int32),
            pltpu.VMEM((2,) + hidden_in.shape, bf16),
            pltpu.VMEM((groups, 2, rows, part), bf16),
            pltpu.VMEM((2, 2 * half, part), bf16),
            pltpu.VMEM((2, 16, 128), bf16),
            pltpu.VMEM((4, 2 * half + 16, slab), bf16),
            pltpu.SemaphoreType.DMA((9,)),
        ],
        outs_in=HBM,
    )(cluster_ids, hidden_in, cotangent)
    recv = lax.all_to_all(send, sections, split_axis=0, concat_axis=0, tiled=True)
    recv = recv.reshape(experts, 2, 2, rows, part)
    recv, up, scale = lax.optimization_barrier((recv, own[1], own[2]))
    other = (other_dn, across(up, "segment", 1), across(scale, "segment", 1))
    slabs = [
        lax.ppermute(block, ("dp", "segment"), slab_route(replicas, turn // 2, turn % 2))
        for turn, block in enumerate(slabs)
    ]
    slices = call(
        functools.partial(repack_kernel, length, capacity),
        "repack",
        60,
        [VMEM] * 4 + [HBM],
        [((2, replicas, rows, slab), bf16)] * experts,
    )(*slabs, recv)
    mine = [slices[0]] + [across(slices[step], "expert", step) for step in range(1, experts)]

    small, middle = call(
        chain_kernel,
        "chain",
        60,
        [HBM] * 7,
        [((tokens, 4 * rank + 128), bf16), ((tokens, width), bf16)],
        [
            pltpu.VMEM(recv.shape, bf16),
            pltpu.VMEM((2, width, rank), bf16),
            pltpu.VMEM((2, rank, width), bf16),
            pltpu.VMEM((2, 1, width), bf16),
            pltpu.VMEM((tokens, width), bf16),
            pltpu.VMEM((tokens, width), f32),
            pltpu.SemaphoreType.DMA((3, 3)),
        ],
        flops=7 * 2 * tokens * width * rank,
        moved=10 * MIB,
    )(recv, *own, *other)
    mine, small, middle = lax.optimization_barrier((mine, small, middle))
    theirs = [across(block, "segment", 1) for block in mine]
    near = [small] + [across(small, "dp", step) for step in range(1, replicas)]
    smalls = near + [across(piece, "segment", 1) for piece in near]

    (out,) = call(
        result_kernel,
        "results",
        60,
        [VMEM] * 2 + [HBM] * 2,
        [((experts, 2, rows, part), bf16)],
        [pltpu.VMEM((rank, width), bf16), pltpu.SemaphoreType.DMA],
    )(middle, small, own[1], other[1])
    back = lax.all_to_all(
        out.reshape(groups, rows, part), sections, split_axis=0, concat_axis=0, tiled=True
    )

    sources = 2 * replicas
    all_tokens = sources * tokens
    out_hidden, grad_dn, grad_upper = call(
        functools.partial(gradient_kernel, experts, sources, sizes),
        "gradients",
        60,
        [VMEM] * (2 * experts + sources) + [HBM] * 7 + [VMEM],
        [(hidden_in.shape, bf16), ((slab, rank), bf16), ((rank, slab), bf16)],
        [
            pltpu.SMEM(cluster_ids.shape, jnp.int32),
            pltpu.VMEM((slab, rank), bf16),
            pltpu.VMEM((rank, slab), bf16),
            pltpu.VMEM((2, 1, slab), bf16),
            pltpu.VMEM((all_tokens, 4 * rank + 128), bf16),
            pltpu.VMEM((all_tokens, 6 * 128), f32),
            pltpu.VMEM((all_tokens, slab), bf16),
            pltpu.VMEM((all_tokens, slab), bf16),
            pltpu.VMEM((all_tokens, 256), f32),
            pltpu.VMEM((all_tokens, 256), f32),
            pltpu.SemaphoreType.DMA((5,)),
        ],
    )(*mine, *theirs, *smalls, *own, *other, cluster_ids, back)
    return (out_hidden, grad_dn[None, None], grad_upper[None, None])


def solution(mesh):
    two = dict(mesh.shape) == {"expert": 4, "dp": 4, "segment": 2}
    on_device = on_device_two_phases if two else on_device_pipelined
    return jax.shard_map(
        on_device,
        mesh=mesh,
        in_specs=(
            P(("expert", "dp"), None, "segment"),
            P(("expert", "dp"), None, "segment"),
            P(("expert", "dp")),
            P("expert", "segment", None, None),
            P("expert", "segment", None, None),
            P("expert", "segment", None),
        ),
        out_specs=(
            P(("expert", "dp"), None, "segment"),
            P("expert", "segment", "dp", None),
            P("expert", "segment", None, "dp"),
        ),
        check_vma=False,
    )
```

```python
import functools

import jax
import jax.numpy as jnp
from jax import lax
from jax.experimental import pallas as pl
from jax.experimental.pallas import tpu as pltpu
from jax.sharding import PartitionSpec as P

MICRO = 4


EPS = 1e-05
C_ZERO = 0.7978845608028654
C_ONE = 0.044715


def shifted(block, axis, distance):
    devices = range(lax.axis_size(axis))
    route = [(i - distance, i) for i in devices if i - distance in devices]
    return lax.ppermute(block, axis, route)


def from_root(block, axis, holder):
    block = jnp.where(lax.axis_index(axis) == holder, block, jnp.zeros_like(block))
    return lax.psum(block, axis)


def gelu_value(z):
    return 0.5 * z * (1.0 + jnp.tanh(C_ZERO * (z + C_ONE * z * z * z)))


def gelu_slope(z):
    tval = jnp.tanh(C_ZERO * (z + C_ONE * z * z * z))
    return 0.5 * (1.0 + tval) + 0.5 * z * (1.0 - tval * tval) * C_ZERO * (1.0 + 3.0 * C_ONE * z * z)


def normalize(hidden):
    wide = hidden.astype(jnp.float32)
    center = wide - jnp.mean(wide, axis=-1, keepdims=True)
    inverse = lax.rsqrt(jnp.mean(center * center, axis=-1, keepdims=True) + EPS)
    return (wide, center * inverse, inverse)


def phase_forward(hidden, w_dn, w_upper, scale):
    wide, normed, inverse = normalize(hidden)
    lowered = (normed * scale).astype(jnp.bfloat16)
    pre = jnp.dot(lowered, w_dn, preferred_element_type=jnp.float32)
    act = gelu_value(pre).astype(jnp.bfloat16)
    leaving = (wide + jnp.dot(act, w_upper, preferred_element_type=jnp.float32)).astype(
        jnp.bfloat16
    )
    return (leaving, pre)


def phase_backward(hidden, grad_in, pre, w_dn, w_upper, scale):
    wide, normed, inverse = normalize(hidden)
    lowered = (normed * scale).astype(jnp.bfloat16)
    act = gelu_value(pre).astype(jnp.bfloat16)
    d_act = jnp.dot(grad_in, w_upper.T, preferred_element_type=jnp.float32)
    d_pre = (d_act * gelu_slope(pre)).astype(jnp.bfloat16)
    d_low = jnp.dot(d_pre, w_dn.T, preferred_element_type=jnp.float32)
    d_norm = d_low * scale
    d_wide = inverse * (
        d_norm
        - jnp.mean(d_norm, axis=-1, keepdims=True)
        - normed * jnp.mean(d_norm * normed, axis=-1, keepdims=True)
    )
    grad_out = (grad_in.astype(jnp.float32) + d_wide).astype(jnp.bfloat16)
    return (grad_out, lowered, act, d_pre)


def put_slot(buffer, value, slot, valid):
    old_value = lax.dynamic_index_in_dim(buffer, slot, 0, keepdims=False)
    return lax.dynamic_update_index_in_dim(buffer, jnp.where(valid, value, old_value), slot, 0)


def on_device_pipelined(hidden_in, cotangent, cluster_ids, w_down, w_up, gain):
    experts = lax.axis_size("expert")
    phases = lax.axis_size("segment")
    phase = lax.axis_index("segment")
    s_local, length, quarter = hidden_in.shape
    capacity = 2 * s_local // experts
    slots = experts * capacity
    same = (cluster_ids[:, None] == cluster_ids[None, :]).astype(jnp.int32)
    earlier = jnp.sum(jnp.tril(same, -1), axis=1)
    target = cluster_ids * capacity + earlier
    place = (jnp.arange(slots, dtype=jnp.int32)[:, None] == target[None, :]).astype(jnp.bfloat16)

    def to_slots(local):
        flat = local.reshape(s_local, -1)
        moved = jnp.dot(place, flat, preferred_element_type=jnp.float32).astype(jnp.bfloat16)
        return moved.reshape((slots,) + local.shape[1:])

    full_in, full_cot = (
        lax.all_gather(hidden_in, "segment", axis=2, tiled=True),
        lax.all_gather(cotangent, "segment", axis=2, tiled=True),
    )
    slot_in, slot_cot = (
        lax.all_to_all(to_slots(full_in), "expert", split_axis=0, concat_axis=0, tiled=True),
        lax.all_to_all(to_slots(full_cot), "expert", split_axis=0, concat_axis=0, tiled=True),
    )
    width = slot_in.shape[2]
    micro_rows = slots * length // MICRO
    inputs = slot_in.reshape(MICRO, micro_rows, width)
    cots = slot_cot.reshape(MICRO, micro_rows, width)
    w_dn = w_down[0, 0]
    w_upper = w_up[0, 0]
    rank = w_dn.shape[1]
    scale = gain[0, 0].astype(jnp.float32)
    ticks = MICRO + phases - 1

    def forward_tick(tick, carry):
        received, saved, pres, results = carry
        which = tick - phase
        valid = (which >= 0) & (which < MICRO)
        slot = jnp.clip(which, 0, MICRO - 1)
        first = lax.dynamic_index_in_dim(inputs, jnp.minimum(tick, MICRO - 1), 0, keepdims=False)
        entering = jnp.where(phase == 0, first, received)
        leaving, pre = phase_forward(entering, w_dn, w_upper, scale)
        saved = put_slot(saved, entering, slot, valid)
        pres = put_slot(pres, pre, slot, valid)
        results = put_slot(results, leaving, slot, valid & (phase == phases - 1))
        received = shifted(leaving, "segment", 1)
        return (received, saved, pres, results)

    start = (
        jnp.zeros((micro_rows, width), jnp.bfloat16),
        jnp.zeros((MICRO, micro_rows, width), jnp.bfloat16),
        jnp.zeros((MICRO, micro_rows, rank), jnp.float32),
        jnp.zeros((MICRO, micro_rows, width), jnp.bfloat16),
    )
    received, saved, pres, results = lax.fori_loop(0, ticks, forward_tick, start)

    def backward_tick(tick, carry):
        received, lows, acts, dpres, grads = carry
        which = tick - (phases - 1 - phase)
        valid = (which >= 0) & (which < MICRO)
        slot = jnp.clip(which, 0, MICRO - 1)
        last = lax.dynamic_index_in_dim(cots, jnp.minimum(tick, MICRO - 1), 0, keepdims=False)
        grad_in = jnp.where(phase == phases - 1, last, received)
        hidden = lax.dynamic_index_in_dim(saved, slot, 0, keepdims=False)
        pre = lax.dynamic_index_in_dim(pres, slot, 0, keepdims=False)
        grad_out, lowered, act, d_pre = phase_backward(hidden, grad_in, pre, w_dn, w_upper, scale)
        lows = put_slot(lows, lowered, slot, valid)
        acts = put_slot(acts, act, slot, valid)
        dpres = put_slot(dpres, d_pre, slot, valid)
        grads = put_slot(grads, grad_in, slot, valid)
        received = shifted(grad_out, "segment", -1)
        return (received, lows, acts, dpres, grads)

    start_back = (
        jnp.zeros((micro_rows, width), jnp.bfloat16),
        jnp.zeros((MICRO, micro_rows, width), jnp.bfloat16),
        jnp.zeros((MICRO, micro_rows, rank), jnp.bfloat16),
        jnp.zeros((MICRO, micro_rows, rank), jnp.bfloat16),
        jnp.zeros((MICRO, micro_rows, width), jnp.bfloat16),
    )
    received, lows, acts, dpres, grads = lax.fori_loop(0, ticks, backward_tick, start_back)
    contract = (((0,), (0,)), ((), ()))
    grad_dn = lax.dot_general(
        lows.reshape(-1, width),
        dpres.reshape(-1, rank),
        contract,
        preferred_element_type=jnp.float32,
    )
    grad_upper = lax.dot_general(
        acts.reshape(-1, rank),
        grads.reshape(-1, width),
        contract,
        preferred_element_type=jnp.float32,
    )
    summed_dn, summed_upper = (
        lax.psum_scatter(
            grad_dn.astype(jnp.bfloat16), "dp", scatter_dimension=0, tiled=True
        ).astype(jnp.float32),
        lax.psum_scatter(
            grad_upper.astype(jnp.bfloat16), "dp", scatter_dimension=1, tiled=True
        ).astype(jnp.float32),
    )
    returned = from_root(results, "segment", phases - 1)
    returned = returned.reshape(slots, length, width)
    own = lax.dynamic_slice_in_dim(returned, phase * quarter, quarter, 2)
    back = lax.all_to_all(own, "expert", split_axis=0, concat_axis=0, tiled=True)
    out_hidden = jnp.dot(place.T, back.reshape(slots, -1), preferred_element_type=jnp.float32)
    out_hidden = out_hidden.astype(jnp.bfloat16).reshape(s_local, length, quarter)
    return (
        out_hidden,
        summed_dn.astype(jnp.bfloat16)[None, None],
        summed_upper.astype(jnp.bfloat16)[None, None],
    )


CHUNK = 512
MIB = 1024 * 1024
TRANS_RHS = (((1,), (1,)), ((), ()))
TRANS_LHS = (((0,), (0,)), ((), ()))


def matmul(left, right, dims=(((1,), (0,)), ((), ()))):
    return lax.dot_general(left, right, dims, preferred_element_type=jnp.float32)


def spread_ids(ids, shape, length):
    lane = lax.broadcasted_iota(jnp.int32, shape, 1)
    spread = jnp.zeros(shape, jnp.int32)
    for n in range(ids.shape[0]):
        spread = jnp.where(lane // length == n, ids[n], spread)
    return spread


def ranked(ids_row, length):
    tokens = ids_row.shape[1]
    kinds = lax.broadcasted_iota(jnp.int32, (8, tokens), 0)
    member = (kinds == ids_row).astype(jnp.float32)
    at_col = lax.broadcasted_iota(jnp.int32, (tokens, tokens), 0)
    at_row = lax.broadcasted_iota(jnp.int32, (tokens, tokens), 1)
    before = (lax.rem(at_col, length) == 0) & (at_col // length < at_row // length)
    counts = matmul(member.astype(jnp.bfloat16), before.astype(jnp.float32).astype(jnp.bfloat16))
    rank = jnp.sum(member * counts, axis=0, keepdims=True)
    total = jnp.sum(member, axis=1, keepdims=True) * (1.0 / length)
    lower = jnp.sum(jnp.where(kinds < ids_row, total, 0.0), axis=0, keepdims=True)
    return rank.astype(jnp.int32), lower.astype(jnp.int32)


def one_hot(target, rows):
    wanted = lax.broadcasted_iota(jnp.int32, (rows, target.shape[1]), 0)
    return (wanted == target).astype(jnp.float32).astype(jnp.bfloat16)


def placements(ids_row, length, capacity, slots):
    rank, lower = ranked(ids_row, length)
    token = lax.rem(lax.broadcasted_iota(jnp.int32, ids_row.shape, 1), length)
    place = rank + lower
    group = lax.rem(place, 2)
    per_core = capacity // 2
    packed = ((ids_row * 2 + group) * per_core + rank // 2) * length + token
    tokens = ids_row.shape[1]
    ordered = group * (tokens // 2) + (place // 2) * length + token
    return one_hot(packed, slots * length), one_hot(ordered, tokens)


def pack_kernel(length, capacity, slots, ids, hidden, cot, send, id_buf, buf, packed, sems):
    groups, _, rows, part = send.shape
    tokens = hidden.shape[0] * length
    arriving = [
        pltpu.make_async_copy(source, target, sems.at[at])
        for at, (source, target) in enumerate(
            ((ids, id_buf), (hidden, buf.at[0]), (cot, buf.at[1]))
        )
    ]
    leaving = [
        pltpu.make_async_copy(packed.at[:, at], send.at[:, at], sems.at[3 + at]) for at in range(2)
    ]
    for copy in arriving:
        copy.start()
    arriving[0].wait()
    ids_row = spread_ids(id_buf, (8, tokens), length)[:1]
    place, _ = placements(ids_row, length, capacity, slots)
    for which in range(2):
        arriving[1 + which].wait()
        moved = matmul(place, buf[which].reshape(tokens, part)).astype(jnp.bfloat16)
        for group in range(groups):
            packed[group, which] = moved[group * rows : (group + 1) * rows]
        leaving[which].start()
    for copy in leaving:
        copy.wait()


def slab_kernel(length, capacity, slots, ids, hidden, cot, _, *refs):
    slabs, refs = refs[:4], refs[4:]
    id_buf, buf, ordered, turned, out_slabs, sems = refs
    s_local, _, part = hidden.shape
    tokens = s_local * length
    slab = part // 2
    half = tokens // 2
    replica = lax.axis_index("dp")
    arriving = [
        pltpu.make_async_copy(source, target, sems.at[at])
        for at, (source, target) in enumerate(
            ((ids, id_buf), (hidden, buf.at[0]), (cot, buf.at[1]))
        )
    ]
    leaving = [
        pltpu.make_async_copy(out_slabs.at[at], slabs[at], sems.at[3 + at]) for at in range(4)
    ]
    for copy in arriving:
        copy.start()
    arriving[0].wait()
    ids_row = spread_ids(id_buf, (16, tokens), length)
    _, by_group = placements(ids_row[:1], length, capacity, slots)
    for group in range(2):
        mine = by_group[group * half : (group + 1) * half]
        clusters = matmul(ids_row.astype(jnp.float32).astype(jnp.bfloat16), mine, TRANS_RHS)
        turned[group] = jnp.concatenate(
            [clusters.astype(jnp.bfloat16), jnp.zeros((16, 128 - half), jnp.bfloat16)], axis=1
        )
    for which in range(2):
        arriving[1 + which].wait()
        flat = buf[which].reshape(tokens, part)
        ordered[which] = matmul(by_group, flat).astype(jnp.bfloat16)
    for turn in range(4):
        pair = (turn // 2) ^ (replica & 1)
        group = (turn % 2) ^ (replica >> 1)
        cols = pl.ds(pl.multiple_of(pair * slab, slab), slab)
        at = pl.ds(pl.multiple_of(group * half, half), half)
        for which in range(2):
            out_slabs[turn, which * half : (which + 1) * half] = ordered[which, at, cols]
        out_slabs[turn, tokens:] = jnp.zeros((16, slab), jnp.bfloat16)
        out_slabs[turn, tokens:, :128] = turned[group]
        leaving[turn].start()
    for copy in leaving:
        copy.wait()


def repack_kernel(length, capacity, *refs):
    slabs, outs = refs[:4], refs[4:]
    experts, rows = len(outs), outs[0].shape[2]
    half = (slabs[0].shape[0] - 16) // 2
    core, replica = lax.axis_index("segment"), lax.axis_index("dp")
    for turn, slab in enumerate(slabs):
        near = turn // 2 + 2 * ((turn % 2) ^ (replica >> 1) ^ core)
        ids_row = slab[2 * half :, :128].astype(jnp.float32)[:1, :half].astype(jnp.int32)
        rank, _ = ranked(ids_row, length)
        token = lax.rem(lax.broadcasted_iota(jnp.int32, ids_row.shape, 1), length)
        step = ids_row ^ lax.axis_index("expert")
        place = one_hot((step * (capacity // 2) + rank) * length + token, experts * rows)
        for which in range(2):
            moved = matmul(place, slab[which * half : (which + 1) * half]).astype(jnp.bfloat16)
            for e in range(experts):
                outs[e][which, near] = moved[e * rows : (e + 1) * rows]


def unpack(sizes, id_buf, back, out):
    length, capacity, slots = sizes
    groups, rows, width = back.shape
    s_local = out.shape[0]
    ids_row = spread_ids(id_buf, (8, s_local * length), length)[:1]
    place, _ = placements(ids_row, length, capacity, slots)
    moved = matmul(place, back[...].reshape(groups * rows, width), TRANS_LHS)
    out[...] = moved.astype(jnp.bfloat16).reshape(s_local, length, width)


def split_three(value):
    top = value.astype(jnp.bfloat16).astype(jnp.float32)
    mid = (value - top).astype(jnp.bfloat16).astype(jnp.float32)
    low = (value - top - mid).astype(jnp.bfloat16).astype(jnp.float32)
    return [top, mid, low]


def side_by_side(columns, tokens):
    lane = lax.broadcasted_iota(jnp.int32, (tokens, 128), 1)
    block = jnp.zeros((tokens, 128), jnp.float32)
    at = 0
    for column in columns:
        for piece in split_three(column):
            block = jnp.where(lane == at, piece, block)
            at += 1
    return block.astype(jnp.bfloat16)


def lanes(value):
    total = value[:, :128]
    for start in range(128, value.shape[1], 128):
        total = total + value[:, start : start + 128]
    return total


def row_sum(parts):
    return jnp.sum(parts, axis=1, keepdims=True)


def chain_kernel(
    recv_in, own_dn, own_up, own_gain, other_dn, other_up, other_gain,
    out, small,
    recv, dn_buf, up_buf, gain_buf, entering, middle, d_norms, sems,
):
    phase = lax.axis_index("segment")
    experts, phases, _, rows, part = recv.shape
    tokens = experts * rows
    width = phases * part
    rank = dn_buf.shape[2]
    own, other = (own_dn, own_up, own_gain), (other_dn, other_up, other_gain)

    def copies(sources, at):
        return [
            pltpu.make_async_copy(source, buffer.at[at], sems.at[at, which])
            for which, (source, buffer) in enumerate(zip(sources, (dn_buf, up_buf, gain_buf)))
        ]

    def fetch(at):
        for this in range(2):

            @pl.when(phase == this)
            def _():
                for copy in copies(own if at == this else other, at):
                    copy.start()

    arriving = [
        pltpu.make_async_copy(recv_in.at[:, :, at], recv.at[:, :, at], sems.at[2, at])
        for at in range(2)
    ]
    arriving[0].start()
    fetch(0)
    waits = [copies(own, at) for at in range(2)]
    cols = range(0, width, CHUNK)

    def block(which, col):
        half, start = col // part, col % part
        return jnp.concatenate(
            [recv[e, half, which, :, start : start + CHUNK] for e in range(experts)], axis=0
        )

    def inverse_of(ref, mean):
        total = jnp.zeros((tokens, 128), jnp.float32)
        for col in cols:
            center = ref[:, col : col + CHUNK].astype(jnp.float32) - mean
            total = total + lanes(center * center)
        return lax.rsqrt(row_sum(total) / width + EPS)

    def down(ref, mean, inverse, at):
        pre = jnp.zeros((tokens, rank), jnp.float32)
        for col in cols:
            here = slice(col, col + CHUNK)
            normed = (ref[:, here].astype(jnp.float32) - mean) * inverse
            lowered = (normed * gain_buf[at, :, here].astype(jnp.float32)).astype(jnp.bfloat16)
            pre = pre + matmul(lowered, dn_buf[at, here, :])
        return pre

    total = jnp.zeros((tokens, 128), jnp.float32)
    arriving[0].wait()
    for col in cols:
        value = block(0, col)
        entering[:, col : col + CHUNK] = value
        total = total + lanes(value.astype(jnp.float32))
    mean_0 = row_sum(total) / width
    inverse_0 = inverse_of(entering, mean_0)
    waits[0][0].wait()
    waits[0][2].wait()
    arriving[1].start()
    fetch(1)
    pre_0 = down(entering, mean_0, inverse_0, 0)
    act_0 = gelu_value(pre_0).astype(jnp.bfloat16)
    slope_0 = gelu_slope(pre_0)

    waits[0][1].wait()
    total = jnp.zeros((tokens, 128), jnp.float32)
    for col in cols:
        here = slice(col, col + CHUNK)
        value = entering[:, here].astype(jnp.float32) + matmul(act_0, up_buf[0, :, here])
        value = value.astype(jnp.bfloat16)
        middle[:, here] = value
        total = total + lanes(value.astype(jnp.float32))
    mean_1 = row_sum(total) / width
    inverse_1 = inverse_of(middle, mean_1)
    for copy in waits[1] + arriving[1:]:
        copy.wait()
    d_act = jnp.zeros((tokens, rank), jnp.float32)
    for col in cols:
        d_act = d_act + matmul(block(1, col), up_buf[1, :, col : col + CHUNK], TRANS_RHS)
    pre_1 = down(middle, mean_1, inverse_1, 1)
    act_1 = gelu_value(pre_1).astype(jnp.bfloat16)
    d_pre_1 = (d_act * gelu_slope(pre_1)).astype(jnp.bfloat16)

    total = jnp.zeros((tokens, 128), jnp.float32)
    cross = jnp.zeros((tokens, 128), jnp.float32)
    for col in cols:
        here = slice(col, col + CHUNK)
        wide = middle[:, here].astype(jnp.float32)
        d_norm = matmul(d_pre_1, dn_buf[1, here, :], TRANS_RHS)
        d_norm = d_norm * gain_buf[1, :, here].astype(jnp.float32)
        d_norms[:, here] = d_norm
        total = total + lanes(d_norm)
        cross = cross + lanes(d_norm * ((wide - mean_1) * inverse_1))
        leaving = (wide + matmul(act_1, up_buf[1, :, here])).astype(jnp.bfloat16)
        half, start = col // part, col % part
        for e in range(experts):
            out[e, half, :, start : start + CHUNK] = leaving[e * rows : (e + 1) * rows]
    shift = row_sum(total) / width
    along = row_sum(cross) / width
    d_act = jnp.zeros((tokens, rank), jnp.float32)
    for col in cols:
        here = slice(col, col + CHUNK)
        normed = (middle[:, here].astype(jnp.float32) - mean_1) * inverse_1
        grad = block(1, col).astype(jnp.float32) + inverse_1 * (
            d_norms[:, here] - shift - normed * along
        )
        d_act = d_act + matmul(grad.astype(jnp.bfloat16), up_buf[0, :, here], TRANS_RHS)
    d_pre_0 = (d_act * slope_0).astype(jnp.bfloat16)
    for at, value in enumerate((act_0, act_1, d_pre_0, d_pre_1)):
        small[:, at * rank : (at + 1) * rank] = value
    moments = (mean_0, inverse_0, mean_1, inverse_1, shift, along)
    small[:, 4 * rank :] = side_by_side(moments, tokens)


def gradient_kernel(experts, sources, sizes, *refs):
    sides, refs = (refs[:experts], refs[experts : 2 * experts]), refs[2 * experts :]
    smalls, refs = refs[:sources], refs[sources:]
    own, other, refs = refs[:3], refs[3:6], refs[6:]
    (ids, back, out_hidden, grad_dn, grad_upper, id_buf, dn_buf, up_buf, gain_buf, small, moments,
     lows, grads, ups, downs, sems) = refs
    id_copy = pltpu.make_async_copy(ids, id_buf, sems.at[4])
    id_copy.start()
    core = lax.axis_index("segment")
    place = lax.axis_index("dp")
    _, replicas, _, slab = sides[0][0].shape
    rows = smalls[0].shape[0]
    rank = dn_buf.shape[1]
    features = pl.ds(pl.multiple_of(place * slab, slab), slab)

    def copies(up, gain_first, dn, gain_second):
        moves = (
            (up.at[:, features], up_buf),
            (dn.at[features, :], dn_buf),
            (gain_first.at[:, features], gain_buf.at[0]),
            (gain_second.at[:, features], gain_buf.at[1]),
        )
        return [
            pltpu.make_async_copy(source, target, sems.at[at])
            for at, (source, target) in enumerate(moves)
        ]

    @pl.when(core == 0)
    def _():
        for copy in copies(own[1], own[2], other[0], other[2]):
            copy.start()

    @pl.when(core != 0)
    def _():
        for copy in copies(other[1], other[2], own[0], own[2]):
            copy.start()

    per_expert = rows // experts
    for source in range(sources):
        for step in range(experts):
            to = source * rows + step * per_expert
            start = (lax.axis_index("expert") ^ step) * per_expert
            small[to : to + per_expert] = smalls[source][
                pl.ds(pl.multiple_of(start, per_expert), per_expert)
            ]

    def sliced(source, which, here):
        side, near = sides[source // replicas], source % replicas
        return jnp.concatenate([side[e][which, near, :, here] for e in range(experts)], axis=0)

    id_copy.wait()
    unpack(sizes, id_buf, back, out_hidden)
    held = lax.broadcasted_iota(jnp.int32, (128, 6 * 128), 0)
    wanted = lax.broadcasted_iota(jnp.int32, (128, 6 * 128), 1) // 128
    adds = (held // 3 == wanted).astype(jnp.float32).astype(jnp.bfloat16)
    moments[...] = matmul(small[:, 4 * rank :], adds)
    for copy in copies(own[1], own[2], other[0], other[2]):
        copy.wait()

    columns = 256

    def moment(at, index):
        value = moments[at, index * 128 : (index + 1) * 128]
        return jnp.concatenate([value] * (columns // 128), axis=1)

    for col in range(0, slab, columns):
        here = slice(col, col + columns)
        ups[...] = matmul(small[:, :rank], up_buf[:, here])
        scales = [gain_buf[at, :, here].astype(jnp.float32) for at in range(2)]

        @pl.when(core == 0)
        def _():
            downs[...] = matmul(small[:, 3 * rank : 4 * rank], dn_buf[here, :], TRANS_RHS)
            for source in range(sources):
                at = slice(source * rows, (source + 1) * rows)
                wide = sliced(source, 0, here).astype(jnp.float32)
                normed = (wide - moment(at, 0)) * moment(at, 1)
                lows[at, here] = (normed * scales[0]).astype(jnp.bfloat16)
                middle = (wide + ups[at]).astype(jnp.bfloat16).astype(jnp.float32)
                inverse = moment(at, 3)
                normed = (middle - moment(at, 2)) * inverse
                d_norm = downs[at] * scales[1]
                grads[at, here] = (
                    sliced(source, 1, here).astype(jnp.float32)
                    + inverse * (d_norm - moment(at, 4) - normed * moment(at, 5))
                ).astype(jnp.bfloat16)

        @pl.when(core != 0)
        def _():
            for source in range(sources):
                at = slice(source * rows, (source + 1) * rows)
                wide = sliced(source, 0, here).astype(jnp.float32)
                middle = (wide + ups[at]).astype(jnp.bfloat16).astype(jnp.float32)
                normed = (middle - moment(at, 2)) * moment(at, 3)
                lows[at, here] = (normed * scales[1]).astype(jnp.bfloat16)
                grads[at, here] = sliced(source, 1, here)

    def finish(act, d_pre):
        for col in range(0, slab, columns):
            here = slice(col, col + columns)
            turned = matmul(d_pre, lows[:, here], TRANS_LHS).astype(jnp.bfloat16)
            grad_dn[here, :] = turned.T
            grad_upper[:, here] = matmul(act, grads[:, here], TRANS_LHS).astype(jnp.bfloat16)

    @pl.when(core == 0)
    def _():
        finish(small[:, :rank], small[:, 2 * rank : 3 * rank])

    @pl.when(core != 0)
    def _():
        finish(small[:, rank : 2 * rank], small[:, 3 * rank : 4 * rank])


VMEM = pl.BlockSpec(memory_space=pltpu.VMEM)
HBM = pl.BlockSpec(memory_space=pltpu.HBM)


def call(kernel, name, grant, in_specs, outs, scratch=(), outs_in=VMEM, flops=0, moved=MIB):
    return pl.pallas_call(
        kernel,
        out_shape=tuple(jax.ShapeDtypeStruct(*out) for out in outs),
        in_specs=in_specs,
        out_specs=tuple(outs_in for _ in outs),
        scratch_shapes=list(scratch),
        compiler_params=pltpu.CompilerParams(vmem_limit_bytes=grant * MIB),
        cost_estimate=pl.CostEstimate(flops=flops, bytes_accessed=moved, transcendentals=0),
        name=name,
    )


def across(block, axis, distance):
    size = lax.axis_size(axis)
    return lax.ppermute(block, axis, [(i, i ^ distance) for i in range(size)])


def slab_route(replicas, pair, low):
    route = []
    for replica in range(replicas):
        for core in range(2):
            chip = 2 * core + ((replica & 1) ^ pair)
            route.append((2 * replica + core, 2 * chip + ((replica >> 1) ^ low)))
    return route


def on_device_two_phases(hidden_in, cotangent, cluster_ids, w_down, w_up, gain):
    experts = lax.axis_size("expert")
    replicas = lax.axis_size("dp")
    s_local, length, part = hidden_in.shape
    width = 2 * part
    capacity = 2 * s_local // experts
    slots = experts * capacity
    groups = 2 * experts
    rows = slots * length // groups
    tokens = experts * rows
    own = (w_down[0, 0], w_up[0, 0], gain[0])
    rank = own[0].shape[1]
    slab = width // replicas
    bf16, f32 = jnp.bfloat16, jnp.float32
    sizes = (length, capacity, slots)
    sections = ("expert", "segment")

    other = tuple(across(array, "segment", 1) for array in own)
    half = s_local * length // 2
    (send,) = call(
        functools.partial(pack_kernel, *sizes),
        "pack",
        60,
        [HBM] * 3,
        [((groups, 2, rows, part), bf16)],
        [
            pltpu.SMEM(cluster_ids.shape, jnp.int32),
            pltpu.VMEM((2,) + hidden_in.shape, bf16),
            pltpu.VMEM((groups, 2, rows, part), bf16),
            pltpu.SemaphoreType.DMA((5,)),
        ],
        outs_in=HBM,
    )(cluster_ids, hidden_in, cotangent)
    slabs = call(
        functools.partial(slab_kernel, *sizes),
        "slabs",
        60,
        [HBM] * 4,
        [((2 * half + 16, slab), bf16)] * 4,
        [
            pltpu.SMEM(cluster_ids.shape, jnp.int32),
            pltpu.VMEM((2,) + hidden_in.shape, bf16),
            pltpu.VMEM((2, 2 * half, part), bf16),
            pltpu.VMEM((2, 16, 128), bf16),
            pltpu.VMEM((4, 2 * half + 16, slab), bf16),
            pltpu.SemaphoreType.DMA((7,)),
        ],
        outs_in=HBM,
    )(cluster_ids, hidden_in, cotangent, send)
    recv = lax.all_to_all(send, sections, split_axis=0, concat_axis=0, tiled=True)
    recv = recv.reshape(experts, 2, 2, rows, part)
    slabs = [
        lax.ppermute(block, ("dp", "segment"), slab_route(replicas, turn // 2, turn % 2))
        for turn, block in enumerate(slabs)
    ]
    slices = call(
        functools.partial(repack_kernel, length, capacity),
        "repack",
        60,
        [VMEM] * 4,
        [((2, replicas, rows, slab), bf16)] * experts,
    )(*slabs)
    mine = [slices[0]] + [across(slices[step], "expert", step) for step in range(1, experts)]

    out, small = call(
        chain_kernel,
        "chain",
        60,
        [HBM] * 7,
        [((experts, 2, rows, part), bf16), ((tokens, 4 * rank + 128), bf16)],
        [
            pltpu.VMEM(recv.shape, bf16),
            pltpu.VMEM((2, width, rank), bf16),
            pltpu.VMEM((2, rank, width), bf16),
            pltpu.VMEM((2, 1, width), bf16),
            pltpu.VMEM((tokens, width), bf16),
            pltpu.VMEM((tokens, width), bf16),
            pltpu.VMEM((tokens, width), f32),
            pltpu.SemaphoreType.DMA((3, 3)),
        ],
        flops=7 * 2 * tokens * width * rank,
        moved=10 * MIB,
    )(recv, *own, *other)
    mine, small = lax.optimization_barrier((mine, small))
    theirs = [across(block, "segment", 1) for block in mine]
    near = [small] + [across(small, "dp", step) for step in range(1, replicas)]
    smalls = near + [across(piece, "segment", 1) for piece in near]

    back = lax.all_to_all(
        out.reshape(groups, rows, part), sections, split_axis=0, concat_axis=0, tiled=True
    )

    sources = 2 * replicas
    all_tokens = sources * tokens
    out_hidden, grad_dn, grad_upper = call(
        functools.partial(gradient_kernel, experts, sources, sizes),
        "gradients",
        60,
        [VMEM] * (2 * experts + sources) + [HBM] * 7 + [VMEM],
        [(hidden_in.shape, bf16), ((slab, rank), bf16), ((rank, slab), bf16)],
        [
            pltpu.SMEM(cluster_ids.shape, jnp.int32),
            pltpu.VMEM((slab, rank), bf16),
            pltpu.VMEM((rank, slab), bf16),
            pltpu.VMEM((2, 1, slab), bf16),
            pltpu.VMEM((all_tokens, 4 * rank + 128), bf16),
            pltpu.VMEM((all_tokens, 6 * 128), f32),
            pltpu.VMEM((all_tokens, slab), bf16),
            pltpu.VMEM((all_tokens, slab), bf16),
            pltpu.VMEM((all_tokens, 256), f32),
            pltpu.VMEM((all_tokens, 256), f32),
            pltpu.SemaphoreType.DMA((5,)),
        ],
    )(*mine, *theirs, *smalls, *own, *other, cluster_ids, back)
    return (out_hidden, grad_dn[None, None], grad_upper[None, None])


def solution(mesh):
    two = dict(mesh.shape) == {"expert": 4, "dp": 4, "segment": 2}
    on_device = on_device_two_phases if two else on_device_pipelined
    return jax.shard_map(
        on_device,
        mesh=mesh,
        in_specs=(
            P(("expert", "dp"), None, "segment"),
            P(("expert", "dp"), None, "segment"),
            P(("expert", "dp")),
            P("expert", "segment", None, None),
            P("expert", "segment", None, None),
            P("expert", "segment", None),
        ),
        out_specs=(
            P(("expert", "dp"), None, "segment"),
            P("expert", "segment", "dp", None),
            P("expert", "segment", None, "dp"),
        ),
        check_vma=False,
    )
```

```python
import functools

import jax
import jax.numpy as jnp
from jax import lax
from jax.experimental import pallas as pl
from jax.experimental.pallas import tpu as pltpu
from jax.sharding import PartitionSpec as P

MICRO = 4


EPS = 1e-05
C_ZERO = 0.7978845608028654
C_ONE = 0.044715


def shifted(block, axis, distance):
    devices = range(lax.axis_size(axis))
    route = [(i - distance, i) for i in devices if i - distance in devices]
    return lax.ppermute(block, axis, route)


def from_root(block, axis, holder):
    block = jnp.where(lax.axis_index(axis) == holder, block, jnp.zeros_like(block))
    return lax.psum(block, axis)


def gelu_value(z):
    return 0.5 * z * (1.0 + jnp.tanh(C_ZERO * (z + C_ONE * z * z * z)))


def gelu_slope(z):
    tval = jnp.tanh(C_ZERO * (z + C_ONE * z * z * z))
    return 0.5 * (1.0 + tval) + 0.5 * z * (1.0 - tval * tval) * C_ZERO * (1.0 + 3.0 * C_ONE * z * z)


def normalize(hidden):
    wide = hidden.astype(jnp.float32)
    center = wide - jnp.mean(wide, axis=-1, keepdims=True)
    inverse = lax.rsqrt(jnp.mean(center * center, axis=-1, keepdims=True) + EPS)
    return (wide, center * inverse, inverse)


def phase_forward(hidden, w_dn, w_upper, scale):
    wide, normed, inverse = normalize(hidden)
    lowered = (normed * scale).astype(jnp.bfloat16)
    pre = jnp.dot(lowered, w_dn, preferred_element_type=jnp.float32)
    act = gelu_value(pre).astype(jnp.bfloat16)
    leaving = (wide + jnp.dot(act, w_upper, preferred_element_type=jnp.float32)).astype(
        jnp.bfloat16
    )
    return (leaving, pre)


def phase_backward(hidden, grad_in, pre, w_dn, w_upper, scale):
    wide, normed, inverse = normalize(hidden)
    lowered = (normed * scale).astype(jnp.bfloat16)
    act = gelu_value(pre).astype(jnp.bfloat16)
    d_act = jnp.dot(grad_in, w_upper.T, preferred_element_type=jnp.float32)
    d_pre = (d_act * gelu_slope(pre)).astype(jnp.bfloat16)
    d_low = jnp.dot(d_pre, w_dn.T, preferred_element_type=jnp.float32)
    d_norm = d_low * scale
    d_wide = inverse * (
        d_norm
        - jnp.mean(d_norm, axis=-1, keepdims=True)
        - normed * jnp.mean(d_norm * normed, axis=-1, keepdims=True)
    )
    grad_out = (grad_in.astype(jnp.float32) + d_wide).astype(jnp.bfloat16)
    return (grad_out, lowered, act, d_pre)


def put_slot(buffer, value, slot, valid):
    old_value = lax.dynamic_index_in_dim(buffer, slot, 0, keepdims=False)
    return lax.dynamic_update_index_in_dim(buffer, jnp.where(valid, value, old_value), slot, 0)


def on_device_pipelined(hidden_in, cotangent, cluster_ids, w_down, w_up, gain):
    experts = lax.axis_size("expert")
    phases = lax.axis_size("segment")
    phase = lax.axis_index("segment")
    s_local, length, quarter = hidden_in.shape
    capacity = 2 * s_local // experts
    slots = experts * capacity
    same = (cluster_ids[:, None] == cluster_ids[None, :]).astype(jnp.int32)
    earlier = jnp.sum(jnp.tril(same, -1), axis=1)
    target = cluster_ids * capacity + earlier
    place = (jnp.arange(slots, dtype=jnp.int32)[:, None] == target[None, :]).astype(jnp.bfloat16)

    def to_slots(local):
        flat = local.reshape(s_local, -1)
        moved = jnp.dot(place, flat, preferred_element_type=jnp.float32).astype(jnp.bfloat16)
        return moved.reshape((slots,) + local.shape[1:])

    full_in, full_cot = (
        lax.all_gather(hidden_in, "segment", axis=2, tiled=True),
        lax.all_gather(cotangent, "segment", axis=2, tiled=True),
    )
    slot_in, slot_cot = (
        lax.all_to_all(to_slots(full_in), "expert", split_axis=0, concat_axis=0, tiled=True),
        lax.all_to_all(to_slots(full_cot), "expert", split_axis=0, concat_axis=0, tiled=True),
    )
    width = slot_in.shape[2]
    micro_rows = slots * length // MICRO
    inputs = slot_in.reshape(MICRO, micro_rows, width)
    cots = slot_cot.reshape(MICRO, micro_rows, width)
    w_dn = w_down[0, 0]
    w_upper = w_up[0, 0]
    rank = w_dn.shape[1]
    scale = gain[0, 0].astype(jnp.float32)
    ticks = MICRO + phases - 1

    def forward_tick(tick, carry):
        received, saved, pres, results = carry
        which = tick - phase
        valid = (which >= 0) & (which < MICRO)
        slot = jnp.clip(which, 0, MICRO - 1)
        first = lax.dynamic_index_in_dim(inputs, jnp.minimum(tick, MICRO - 1), 0, keepdims=False)
        entering = jnp.where(phase == 0, first, received)
        leaving, pre = phase_forward(entering, w_dn, w_upper, scale)
        saved = put_slot(saved, entering, slot, valid)
        pres = put_slot(pres, pre, slot, valid)
        results = put_slot(results, leaving, slot, valid & (phase == phases - 1))
        received = shifted(leaving, "segment", 1)
        return (received, saved, pres, results)

    start = (
        jnp.zeros((micro_rows, width), jnp.bfloat16),
        jnp.zeros((MICRO, micro_rows, width), jnp.bfloat16),
        jnp.zeros((MICRO, micro_rows, rank), jnp.float32),
        jnp.zeros((MICRO, micro_rows, width), jnp.bfloat16),
    )
    received, saved, pres, results = lax.fori_loop(0, ticks, forward_tick, start)

    def backward_tick(tick, carry):
        received, lows, acts, dpres, grads = carry
        which = tick - (phases - 1 - phase)
        valid = (which >= 0) & (which < MICRO)
        slot = jnp.clip(which, 0, MICRO - 1)
        last = lax.dynamic_index_in_dim(cots, jnp.minimum(tick, MICRO - 1), 0, keepdims=False)
        grad_in = jnp.where(phase == phases - 1, last, received)
        hidden = lax.dynamic_index_in_dim(saved, slot, 0, keepdims=False)
        pre = lax.dynamic_index_in_dim(pres, slot, 0, keepdims=False)
        grad_out, lowered, act, d_pre = phase_backward(hidden, grad_in, pre, w_dn, w_upper, scale)
        lows = put_slot(lows, lowered, slot, valid)
        acts = put_slot(acts, act, slot, valid)
        dpres = put_slot(dpres, d_pre, slot, valid)
        grads = put_slot(grads, grad_in, slot, valid)
        received = shifted(grad_out, "segment", -1)
        return (received, lows, acts, dpres, grads)

    start_back = (
        jnp.zeros((micro_rows, width), jnp.bfloat16),
        jnp.zeros((MICRO, micro_rows, width), jnp.bfloat16),
        jnp.zeros((MICRO, micro_rows, rank), jnp.bfloat16),
        jnp.zeros((MICRO, micro_rows, rank), jnp.bfloat16),
        jnp.zeros((MICRO, micro_rows, width), jnp.bfloat16),
    )
    received, lows, acts, dpres, grads = lax.fori_loop(0, ticks, backward_tick, start_back)
    contract = (((0,), (0,)), ((), ()))
    grad_dn = lax.dot_general(
        lows.reshape(-1, width),
        dpres.reshape(-1, rank),
        contract,
        preferred_element_type=jnp.float32,
    )
    grad_upper = lax.dot_general(
        acts.reshape(-1, rank),
        grads.reshape(-1, width),
        contract,
        preferred_element_type=jnp.float32,
    )
    summed_dn, summed_upper = (
        lax.psum_scatter(
            grad_dn.astype(jnp.bfloat16), "dp", scatter_dimension=0, tiled=True
        ).astype(jnp.float32),
        lax.psum_scatter(
            grad_upper.astype(jnp.bfloat16), "dp", scatter_dimension=1, tiled=True
        ).astype(jnp.float32),
    )
    returned = from_root(results, "segment", phases - 1)
    returned = returned.reshape(slots, length, width)
    own = lax.dynamic_slice_in_dim(returned, phase * quarter, quarter, 2)
    back = lax.all_to_all(own, "expert", split_axis=0, concat_axis=0, tiled=True)
    out_hidden = jnp.dot(place.T, back.reshape(slots, -1), preferred_element_type=jnp.float32)
    out_hidden = out_hidden.astype(jnp.bfloat16).reshape(s_local, length, quarter)
    return (
        out_hidden,
        summed_dn.astype(jnp.bfloat16)[None, None],
        summed_upper.astype(jnp.bfloat16)[None, None],
    )


CHUNK = 512
MIB = 1024 * 1024
TRANS_RHS = (((1,), (1,)), ((), ()))
TRANS_LHS = (((0,), (0,)), ((), ()))


def matmul(left, right, dims=(((1,), (0,)), ((), ()))):
    return lax.dot_general(left, right, dims, preferred_element_type=jnp.float32)


def spread_ids(ids, shape, length):
    lane = lax.broadcasted_iota(jnp.int32, shape, 1)
    spread = jnp.zeros(shape, jnp.int32)
    for n in range(ids.shape[0]):
        spread = jnp.where(lane // length == n, ids[n], spread)
    return spread


def ranked(ids_row, length):
    tokens = ids_row.shape[1]
    kinds = lax.broadcasted_iota(jnp.int32, (8, tokens), 0)
    member = (kinds == ids_row).astype(jnp.float32)
    at_col = lax.broadcasted_iota(jnp.int32, (tokens, tokens), 0)
    at_row = lax.broadcasted_iota(jnp.int32, (tokens, tokens), 1)
    before = (lax.rem(at_col, length) == 0) & (at_col // length < at_row // length)
    counts = matmul(member.astype(jnp.bfloat16), before.astype(jnp.float32).astype(jnp.bfloat16))
    rank = jnp.sum(member * counts, axis=0, keepdims=True)
    total = jnp.sum(member, axis=1, keepdims=True) * (1.0 / length)
    lower = jnp.sum(jnp.where(kinds < ids_row, total, 0.0), axis=0, keepdims=True)
    return rank.astype(jnp.int32), lower.astype(jnp.int32)


def one_hot(target, rows):
    wanted = lax.broadcasted_iota(jnp.int32, (rows, target.shape[1]), 0)
    return (wanted == target).astype(jnp.float32).astype(jnp.bfloat16)


def placements(ids_row, length, capacity, slots):
    rank, lower = ranked(ids_row, length)
    token = lax.rem(lax.broadcasted_iota(jnp.int32, ids_row.shape, 1), length)
    place = rank + lower
    group = lax.rem(place, 2)
    per_core = capacity // 2
    packed = ((ids_row * 2 + group) * per_core + rank // 2) * length + token
    tokens = ids_row.shape[1]
    ordered = group * (tokens // 2) + (place // 2) * length + token
    return one_hot(packed, slots * length), one_hot(ordered, tokens)


def pack_kernel(length, capacity, slots, ids, hidden, cot, send, id_buf, buf, packed, sems):
    groups, _, rows, part = send.shape
    tokens = hidden.shape[0] * length
    arriving = [
        pltpu.make_async_copy(source, target, sems.at[at])
        for at, (source, target) in enumerate(
            ((ids, id_buf), (hidden, buf.at[0]), (cot, buf.at[1]))
        )
    ]
    leaving = [
        pltpu.make_async_copy(packed.at[:, at], send.at[:, at], sems.at[3 + at]) for at in range(2)
    ]
    for copy in arriving:
        copy.start()
    arriving[0].wait()
    ids_row = spread_ids(id_buf, (8, tokens), length)[:1]
    place, _ = placements(ids_row, length, capacity, slots)
    for which in range(2):
        arriving[1 + which].wait()
        moved = matmul(place, buf[which].reshape(tokens, part)).astype(jnp.bfloat16)
        for group in range(groups):
            packed[group, which] = moved[group * rows : (group + 1) * rows]
        leaving[which].start()
    for copy in leaving:
        copy.wait()


def slab_kernel(length, capacity, slots, ids, hidden, cot, _, *refs):
    slabs, refs = refs[:4], refs[4:]
    id_buf, buf, ordered, turned, out_slabs, sems = refs
    s_local, _, part = hidden.shape
    tokens = s_local * length
    slab = part // 2
    half = tokens // 2
    replica = lax.axis_index("dp")
    arriving = [
        pltpu.make_async_copy(source, target, sems.at[at])
        for at, (source, target) in enumerate(
            ((ids, id_buf), (hidden, buf.at[0]), (cot, buf.at[1]))
        )
    ]
    leaving = [
        pltpu.make_async_copy(out_slabs.at[at], slabs[at], sems.at[3 + at]) for at in range(4)
    ]
    for copy in arriving:
        copy.start()
    arriving[0].wait()
    ids_row = spread_ids(id_buf, (16, tokens), length)
    _, by_group = placements(ids_row[:1], length, capacity, slots)
    for group in range(2):
        mine = by_group[group * half : (group + 1) * half]
        clusters = matmul(ids_row.astype(jnp.float32).astype(jnp.bfloat16), mine, TRANS_RHS)
        turned[group] = jnp.concatenate(
            [clusters.astype(jnp.bfloat16), jnp.zeros((16, 128 - half), jnp.bfloat16)], axis=1
        )
    for which in range(2):
        arriving[1 + which].wait()
        flat = buf[which].reshape(tokens, part)
        ordered[which] = matmul(by_group, flat).astype(jnp.bfloat16)
    for turn in range(4):
        pair = (turn // 2) ^ (replica & 1)
        group = (turn % 2) ^ (replica >> 1)
        cols = pl.ds(pl.multiple_of(pair * slab, slab), slab)
        at = pl.ds(pl.multiple_of(group * half, half), half)
        for which in range(2):
            out_slabs[turn, which * half : (which + 1) * half] = ordered[which, at, cols]
        out_slabs[turn, tokens:] = jnp.zeros((16, slab), jnp.bfloat16)
        out_slabs[turn, tokens:, :128] = turned[group]
        leaving[turn].start()
    for copy in leaving:
        copy.wait()


def repack_kernel(length, capacity, *refs):
    slabs, outs = refs[:4], refs[5:]
    experts, rows = len(outs), outs[0].shape[2]
    half = (slabs[0].shape[0] - 16) // 2
    core, replica = lax.axis_index("segment"), lax.axis_index("dp")
    for turn, slab in enumerate(slabs):
        near = turn // 2 + 2 * ((turn % 2) ^ (replica >> 1) ^ core)
        ids_row = slab[2 * half :, :128].astype(jnp.float32)[:1, :half].astype(jnp.int32)
        rank, _ = ranked(ids_row, length)
        token = lax.rem(lax.broadcasted_iota(jnp.int32, ids_row.shape, 1), length)
        step = ids_row ^ lax.axis_index("expert")
        place = one_hot((step * (capacity // 2) + rank) * length + token, experts * rows)
        for which in range(2):
            moved = matmul(place, slab[which * half : (which + 1) * half]).astype(jnp.bfloat16)
            for e in range(experts):
                outs[e][which, near] = moved[e * rows : (e + 1) * rows]


def unpack(sizes, id_buf, back, out):
    length, capacity, slots = sizes
    groups, rows, width = back.shape
    s_local = out.shape[0]
    ids_row = spread_ids(id_buf, (8, s_local * length), length)[:1]
    place, _ = placements(ids_row, length, capacity, slots)
    moved = matmul(place, back[...].reshape(groups * rows, width), TRANS_LHS)
    out[...] = moved.astype(jnp.bfloat16).reshape(s_local, length, width)


def split_three(value):
    top = value.astype(jnp.bfloat16).astype(jnp.float32)
    mid = (value - top).astype(jnp.bfloat16).astype(jnp.float32)
    low = (value - top - mid).astype(jnp.bfloat16).astype(jnp.float32)
    return [top, mid, low]


def side_by_side(columns, tokens):
    lane = lax.broadcasted_iota(jnp.int32, (tokens, 128), 1)
    block = jnp.zeros((tokens, 128), jnp.float32)
    at = 0
    for column in columns:
        for piece in split_three(column):
            block = jnp.where(lane == at, piece, block)
            at += 1
    return block.astype(jnp.bfloat16)


def lanes(value):
    total = value[:, :128]
    for start in range(128, value.shape[1], 128):
        total = total + value[:, start : start + 128]
    return total


def row_sum(parts):
    return jnp.sum(parts, axis=1, keepdims=True)


def chain_kernel(
    recv_in, own_dn, own_up, own_gain, other_dn, other_up, other_gain,
    out, small,
    recv, dn_buf, up_buf, gain_buf, entering, middle, d_norms, sems,
):
    phase = lax.axis_index("segment")
    experts, phases, _, rows, part = recv.shape
    tokens = experts * rows
    width = phases * part
    rank = dn_buf.shape[2]
    own, other = (own_dn, own_up, own_gain), (other_dn, other_up, other_gain)

    def copies(sources, at):
        return [
            pltpu.make_async_copy(source, buffer.at[at], sems.at[at, which])
            for which, (source, buffer) in enumerate(zip(sources, (dn_buf, up_buf, gain_buf)))
        ]

    def fetch(at):
        for this in range(2):

            @pl.when(phase == this)
            def _():
                for copy in copies(own if at == this else other, at):
                    copy.start()

    arriving = [
        pltpu.make_async_copy(recv_in.at[:, :, at], recv.at[:, :, at], sems.at[2, at])
        for at in range(2)
    ]
    arriving[0].start()
    fetch(0)
    waits = [copies(own, at) for at in range(2)]
    cols = range(0, width, CHUNK)

    def block(which, col):
        half, start = col // part, col % part
        return jnp.concatenate(
            [recv[e, half, which, :, start : start + CHUNK] for e in range(experts)], axis=0
        )

    def inverse_of(ref, mean):
        total = jnp.zeros((tokens, 128), jnp.float32)
        for col in cols:
            center = ref[:, col : col + CHUNK].astype(jnp.float32) - mean
            total = total + lanes(center * center)
        return lax.rsqrt(row_sum(total) / width + EPS)

    def down(ref, mean, inverse, at):
        pre = jnp.zeros((tokens, rank), jnp.float32)
        for col in cols:
            here = slice(col, col + CHUNK)
            normed = (ref[:, here].astype(jnp.float32) - mean) * inverse
            lowered = (normed * gain_buf[at, :, here].astype(jnp.float32)).astype(jnp.bfloat16)
            pre = pre + matmul(lowered, dn_buf[at, here, :])
        return pre

    total = jnp.zeros((tokens, 128), jnp.float32)
    arriving[0].wait()
    for col in cols:
        value = block(0, col)
        entering[:, col : col + CHUNK] = value
        total = total + lanes(value.astype(jnp.float32))
    mean_0 = row_sum(total) / width
    inverse_0 = inverse_of(entering, mean_0)
    waits[0][0].wait()
    waits[0][2].wait()
    arriving[1].start()
    fetch(1)
    pre_0 = down(entering, mean_0, inverse_0, 0)
    act_0 = gelu_value(pre_0).astype(jnp.bfloat16)
    slope_0 = gelu_slope(pre_0)

    waits[0][1].wait()
    total = jnp.zeros((tokens, 128), jnp.float32)
    for col in cols:
        here = slice(col, col + CHUNK)
        value = entering[:, here].astype(jnp.float32) + matmul(act_0, up_buf[0, :, here])
        value = value.astype(jnp.bfloat16)
        middle[:, here] = value
        total = total + lanes(value.astype(jnp.float32))
    mean_1 = row_sum(total) / width
    inverse_1 = inverse_of(middle, mean_1)
    for copy in waits[1] + arriving[1:]:
        copy.wait()
    d_act = jnp.zeros((tokens, rank), jnp.float32)
    for col in cols:
        d_act = d_act + matmul(block(1, col), up_buf[1, :, col : col + CHUNK], TRANS_RHS)
    pre_1 = down(middle, mean_1, inverse_1, 1)
    act_1 = gelu_value(pre_1).astype(jnp.bfloat16)
    d_pre_1 = (d_act * gelu_slope(pre_1)).astype(jnp.bfloat16)

    total = jnp.zeros((tokens, 128), jnp.float32)
    cross = jnp.zeros((tokens, 128), jnp.float32)
    for col in cols:
        here = slice(col, col + CHUNK)
        wide = middle[:, here].astype(jnp.float32)
        d_norm = matmul(d_pre_1, dn_buf[1, here, :], TRANS_RHS)
        d_norm = d_norm * gain_buf[1, :, here].astype(jnp.float32)
        d_norms[:, here] = d_norm
        total = total + lanes(d_norm)
        cross = cross + lanes(d_norm * ((wide - mean_1) * inverse_1))
        leaving = (wide + matmul(act_1, up_buf[1, :, here])).astype(jnp.bfloat16)
        half, start = col // part, col % part
        for e in range(experts):
            out[e, half, :, start : start + CHUNK] = leaving[e * rows : (e + 1) * rows]
    shift = row_sum(total) / width
    along = row_sum(cross) / width
    d_act = jnp.zeros((tokens, rank), jnp.float32)
    for col in cols:
        here = slice(col, col + CHUNK)
        normed = (middle[:, here].astype(jnp.float32) - mean_1) * inverse_1
        grad = block(1, col).astype(jnp.float32) + inverse_1 * (
            d_norms[:, here] - shift - normed * along
        )
        d_act = d_act + matmul(grad.astype(jnp.bfloat16), up_buf[0, :, here], TRANS_RHS)
    d_pre_0 = (d_act * slope_0).astype(jnp.bfloat16)
    for at, value in enumerate((act_0, act_1, d_pre_0, d_pre_1)):
        small[:, at * rank : (at + 1) * rank] = value
    moments = (mean_0, inverse_0, mean_1, inverse_1, shift, along)
    small[:, 4 * rank :] = side_by_side(moments, tokens)


def gradient_kernel(experts, sources, sizes, *refs):
    sides, refs = (refs[:experts], refs[experts : 2 * experts]), refs[2 * experts :]
    smalls, refs = refs[:sources], refs[sources:]
    own, other, refs = refs[:3], refs[3:6], refs[6:]
    (ids, back, out_hidden, grad_dn, grad_upper, id_buf, dn_buf, up_buf, gain_buf, small, moments,
     lows, grads, ups, downs, sems) = refs
    id_copy = pltpu.make_async_copy(ids, id_buf, sems.at[4])
    id_copy.start()
    core = lax.axis_index("segment")
    place = lax.axis_index("dp")
    _, replicas, _, slab = sides[0][0].shape
    rows = smalls[0].shape[0]
    rank = dn_buf.shape[1]
    features = pl.ds(pl.multiple_of(place * slab, slab), slab)

    def copies(up, gain_first, dn, gain_second):
        moves = (
            (up.at[:, features], up_buf),
            (dn.at[features, :], dn_buf),
            (gain_first.at[:, features], gain_buf.at[0]),
            (gain_second.at[:, features], gain_buf.at[1]),
        )
        return [
            pltpu.make_async_copy(source, target, sems.at[at])
            for at, (source, target) in enumerate(moves)
        ]

    @pl.when(core == 0)
    def _():
        for copy in copies(own[1], own[2], other[0], other[2]):
            copy.start()

    @pl.when(core != 0)
    def _():
        for copy in copies(other[1], other[2], own[0], own[2]):
            copy.start()

    per_expert = rows // experts
    for source in range(sources):
        for step in range(experts):
            to = source * rows + step * per_expert
            start = (lax.axis_index("expert") ^ step) * per_expert
            small[to : to + per_expert] = smalls[source][
                pl.ds(pl.multiple_of(start, per_expert), per_expert)
            ]

    def sliced(source, which, here):
        side, near = sides[source // replicas], source % replicas
        return jnp.concatenate([side[e][which, near, :, here] for e in range(experts)], axis=0)

    id_copy.wait()
    unpack(sizes, id_buf, back, out_hidden)
    held = lax.broadcasted_iota(jnp.int32, (128, 6 * 128), 0)
    wanted = lax.broadcasted_iota(jnp.int32, (128, 6 * 128), 1) // 128
    adds = (held // 3 == wanted).astype(jnp.float32).astype(jnp.bfloat16)
    moments[...] = matmul(small[:, 4 * rank :], adds)
    for copy in copies(own[1], own[2], other[0], other[2]):
        copy.wait()

    columns = 256

    def moment(at, index):
        value = moments[at, index * 128 : (index + 1) * 128]
        return jnp.concatenate([value] * (columns // 128), axis=1)

    for col in range(0, slab, columns):
        here = slice(col, col + columns)
        ups[...] = matmul(small[:, :rank], up_buf[:, here])
        scales = [gain_buf[at, :, here].astype(jnp.float32) for at in range(2)]

        @pl.when(core == 0)
        def _():
            downs[...] = matmul(small[:, 3 * rank : 4 * rank], dn_buf[here, :], TRANS_RHS)
            for source in range(sources):
                at = slice(source * rows, (source + 1) * rows)
                wide = sliced(source, 0, here).astype(jnp.float32)
                normed = (wide - moment(at, 0)) * moment(at, 1)
                lows[at, here] = (normed * scales[0]).astype(jnp.bfloat16)
                middle = (wide + ups[at]).astype(jnp.bfloat16).astype(jnp.float32)
                inverse = moment(at, 3)
                normed = (middle - moment(at, 2)) * inverse
                d_norm = downs[at] * scales[1]
                grads[at, here] = (
                    sliced(source, 1, here).astype(jnp.float32)
                    + inverse * (d_norm - moment(at, 4) - normed * moment(at, 5))
                ).astype(jnp.bfloat16)

        @pl.when(core != 0)
        def _():
            for source in range(sources):
                at = slice(source * rows, (source + 1) * rows)
                wide = sliced(source, 0, here).astype(jnp.float32)
                middle = (wide + ups[at]).astype(jnp.bfloat16).astype(jnp.float32)
                normed = (middle - moment(at, 2)) * moment(at, 3)
                lows[at, here] = (normed * scales[1]).astype(jnp.bfloat16)
                grads[at, here] = sliced(source, 1, here)

    def finish(act, d_pre):
        for col in range(0, slab, columns):
            here = slice(col, col + columns)
            turned = matmul(d_pre, lows[:, here], TRANS_LHS).astype(jnp.bfloat16)
            grad_dn[here, :] = turned.T
            grad_upper[:, here] = matmul(act, grads[:, here], TRANS_LHS).astype(jnp.bfloat16)

    @pl.when(core == 0)
    def _():
        finish(small[:, :rank], small[:, 2 * rank : 3 * rank])

    @pl.when(core != 0)
    def _():
        finish(small[:, rank : 2 * rank], small[:, 3 * rank : 4 * rank])


VMEM = pl.BlockSpec(memory_space=pltpu.VMEM)
HBM = pl.BlockSpec(memory_space=pltpu.HBM)


def call(kernel, name, grant, in_specs, outs, scratch=(), outs_in=VMEM, flops=0, moved=MIB):
    return pl.pallas_call(
        kernel,
        out_shape=tuple(jax.ShapeDtypeStruct(*out) for out in outs),
        in_specs=in_specs,
        out_specs=tuple(outs_in for _ in outs),
        scratch_shapes=list(scratch),
        compiler_params=pltpu.CompilerParams(vmem_limit_bytes=grant * MIB),
        cost_estimate=pl.CostEstimate(flops=flops, bytes_accessed=moved, transcendentals=0),
        name=name,
    )


def across(block, axis, distance):
    size = lax.axis_size(axis)
    return lax.ppermute(block, axis, [(i, i ^ distance) for i in range(size)])


def slab_route(replicas, pair, low):
    route = []
    for replica in range(replicas):
        for core in range(2):
            chip = 2 * core + ((replica & 1) ^ pair)
            route.append((2 * replica + core, 2 * chip + ((replica >> 1) ^ low)))
    return route


def on_device_two_phases(hidden_in, cotangent, cluster_ids, w_down, w_up, gain):
    experts = lax.axis_size("expert")
    replicas = lax.axis_size("dp")
    s_local, length, part = hidden_in.shape
    width = 2 * part
    capacity = 2 * s_local // experts
    slots = experts * capacity
    groups = 2 * experts
    rows = slots * length // groups
    tokens = experts * rows
    own = (w_down[0, 0], w_up[0, 0], gain[0])
    rank = own[0].shape[1]
    slab = width // replicas
    bf16, f32 = jnp.bfloat16, jnp.float32
    sizes = (length, capacity, slots)
    sections = ("expert", "segment")

    other = tuple(across(array, "segment", 1) for array in own)
    half = s_local * length // 2
    (send,) = call(
        functools.partial(pack_kernel, *sizes),
        "pack",
        60,
        [HBM] * 3,
        [((groups, 2, rows, part), bf16)],
        [
            pltpu.SMEM(cluster_ids.shape, jnp.int32),
            pltpu.VMEM((2,) + hidden_in.shape, bf16),
            pltpu.VMEM((groups, 2, rows, part), bf16),
            pltpu.SemaphoreType.DMA((5,)),
        ],
        outs_in=HBM,
    )(cluster_ids, hidden_in, cotangent)
    slabs = call(
        functools.partial(slab_kernel, *sizes),
        "slabs",
        60,
        [HBM] * 4,
        [((2 * half + 16, slab), bf16)] * 4,
        [
            pltpu.SMEM(cluster_ids.shape, jnp.int32),
            pltpu.VMEM((2,) + hidden_in.shape, bf16),
            pltpu.VMEM((2, 2 * half, part), bf16),
            pltpu.VMEM((2, 16, 128), bf16),
            pltpu.VMEM((4, 2 * half + 16, slab), bf16),
            pltpu.SemaphoreType.DMA((7,)),
        ],
        outs_in=HBM,
    )(cluster_ids, hidden_in, cotangent, send)
    recv = lax.all_to_all(send, sections, split_axis=0, concat_axis=0, tiled=True)
    recv = recv.reshape(experts, 2, 2, rows, part)
    slabs = [
        lax.ppermute(block, ("dp", "segment"), slab_route(replicas, turn // 2, turn % 2))
        for turn, block in enumerate(slabs)
    ]
    out, small = call(
        chain_kernel,
        "chain",
        60,
        [HBM] * 7,
        [((experts, 2, rows, part), bf16), ((tokens, 4 * rank + 128), bf16)],
        [
            pltpu.VMEM(recv.shape, bf16),
            pltpu.VMEM((2, width, rank), bf16),
            pltpu.VMEM((2, rank, width), bf16),
            pltpu.VMEM((2, 1, width), bf16),
            pltpu.VMEM((tokens, width), bf16),
            pltpu.VMEM((tokens, width), bf16),
            pltpu.VMEM((tokens, width), f32),
            pltpu.SemaphoreType.DMA((3, 3)),
        ],
        flops=7 * 2 * tokens * width * rank,
        moved=10 * MIB,
    )(recv, *own, *other)
    slices = call(
        functools.partial(repack_kernel, length, capacity),
        "repack",
        60,
        [VMEM] * 4 + [HBM],
        [((2, replicas, rows, slab), bf16)] * experts,
    )(*slabs, small)
    mine = [slices[0]] + [across(slices[step], "expert", step) for step in range(1, experts)]
    theirs = [across(block, "segment", 1) for block in mine]
    near = [small] + [across(small, "dp", step) for step in range(1, replicas)]
    smalls = near + [across(piece, "segment", 1) for piece in near]

    back = lax.all_to_all(
        out.reshape(groups, rows, part), sections, split_axis=0, concat_axis=0, tiled=True
    )

    sources = 2 * replicas
    all_tokens = sources * tokens
    out_hidden, grad_dn, grad_upper = call(
        functools.partial(gradient_kernel, experts, sources, sizes),
        "gradients",
        60,
        [VMEM] * (2 * experts + sources) + [HBM] * 7 + [VMEM],
        [(hidden_in.shape, bf16), ((slab, rank), bf16), ((rank, slab), bf16)],
        [
            pltpu.SMEM(cluster_ids.shape, jnp.int32),
            pltpu.VMEM((slab, rank), bf16),
            pltpu.VMEM((rank, slab), bf16),
            pltpu.VMEM((2, 1, slab), bf16),
            pltpu.VMEM((all_tokens, 4 * rank + 128), bf16),
            pltpu.VMEM((all_tokens, 6 * 128), f32),
            pltpu.VMEM((all_tokens, slab), bf16),
            pltpu.VMEM((all_tokens, slab), bf16),
            pltpu.VMEM((all_tokens, 256), f32),
            pltpu.VMEM((all_tokens, 256), f32),
            pltpu.SemaphoreType.DMA((5,)),
        ],
    )(*mine, *theirs, *smalls, *own, *other, cluster_ids, back)
    return (out_hidden, grad_dn[None, None], grad_upper[None, None])


def solution(mesh):
    two = dict(mesh.shape) == {"expert": 4, "dp": 4, "segment": 2}
    on_device = on_device_two_phases if two else on_device_pipelined
    return jax.shard_map(
        on_device,
        mesh=mesh,
        in_specs=(
            P(("expert", "dp"), None, "segment"),
            P(("expert", "dp"), None, "segment"),
            P(("expert", "dp")),
            P("expert", "segment", None, None),
            P("expert", "segment", None, None),
            P("expert", "segment", None),
        ),
        out_specs=(
            P(("expert", "dp"), None, "segment"),
            P("expert", "segment", "dp", None),
            P("expert", "segment", None, "dp"),
        ),
        check_vma=False,
    )
```

```python
import functools

import jax
import jax.numpy as jnp
from jax import lax
from jax.experimental import pallas as pl
from jax.experimental.pallas import tpu as pltpu
from jax.sharding import PartitionSpec as P

MICRO = 4


EPS = 1e-05
C_ZERO = 0.7978845608028654
C_ONE = 0.044715


def shifted(block, axis, distance):
    devices = range(lax.axis_size(axis))
    route = [(i - distance, i) for i in devices if i - distance in devices]
    return lax.ppermute(block, axis, route)


def from_root(block, axis, holder):
    block = jnp.where(lax.axis_index(axis) == holder, block, jnp.zeros_like(block))
    return lax.psum(block, axis)


def gelu_value(z):
    return 0.5 * z * (1.0 + jnp.tanh(C_ZERO * (z + C_ONE * z * z * z)))


def gelu_slope(z):
    tval = jnp.tanh(C_ZERO * (z + C_ONE * z * z * z))
    return 0.5 * (1.0 + tval) + 0.5 * z * (1.0 - tval * tval) * C_ZERO * (1.0 + 3.0 * C_ONE * z * z)


def normalize(hidden):
    wide = hidden.astype(jnp.float32)
    center = wide - jnp.mean(wide, axis=-1, keepdims=True)
    inverse = lax.rsqrt(jnp.mean(center * center, axis=-1, keepdims=True) + EPS)
    return (wide, center * inverse, inverse)


def phase_forward(hidden, w_dn, w_upper, scale):
    wide, normed, inverse = normalize(hidden)
    lowered = (normed * scale).astype(jnp.bfloat16)
    pre = jnp.dot(lowered, w_dn, preferred_element_type=jnp.float32)
    act = gelu_value(pre).astype(jnp.bfloat16)
    leaving = (wide + jnp.dot(act, w_upper, preferred_element_type=jnp.float32)).astype(
        jnp.bfloat16
    )
    return (leaving, pre)


def phase_backward(hidden, grad_in, pre, w_dn, w_upper, scale):
    wide, normed, inverse = normalize(hidden)
    lowered = (normed * scale).astype(jnp.bfloat16)
    act = gelu_value(pre).astype(jnp.bfloat16)
    d_act = jnp.dot(grad_in, w_upper.T, preferred_element_type=jnp.float32)
    d_pre = (d_act * gelu_slope(pre)).astype(jnp.bfloat16)
    d_low = jnp.dot(d_pre, w_dn.T, preferred_element_type=jnp.float32)
    d_norm = d_low * scale
    d_wide = inverse * (
        d_norm
        - jnp.mean(d_norm, axis=-1, keepdims=True)
        - normed * jnp.mean(d_norm * normed, axis=-1, keepdims=True)
    )
    grad_out = (grad_in.astype(jnp.float32) + d_wide).astype(jnp.bfloat16)
    return (grad_out, lowered, act, d_pre)


def put_slot(buffer, value, slot, valid):
    old_value = lax.dynamic_index_in_dim(buffer, slot, 0, keepdims=False)
    return lax.dynamic_update_index_in_dim(buffer, jnp.where(valid, value, old_value), slot, 0)


def on_device_pipelined(hidden_in, cotangent, cluster_ids, w_down, w_up, gain):
    experts = lax.axis_size("expert")
    phases = lax.axis_size("segment")
    phase = lax.axis_index("segment")
    s_local, length, quarter = hidden_in.shape
    capacity = 2 * s_local // experts
    slots = experts * capacity
    same = (cluster_ids[:, None] == cluster_ids[None, :]).astype(jnp.int32)
    earlier = jnp.sum(jnp.tril(same, -1), axis=1)
    target = cluster_ids * capacity + earlier
    place = (jnp.arange(slots, dtype=jnp.int32)[:, None] == target[None, :]).astype(jnp.bfloat16)

    def to_slots(local):
        flat = local.reshape(s_local, -1)
        moved = jnp.dot(place, flat, preferred_element_type=jnp.float32).astype(jnp.bfloat16)
        return moved.reshape((slots,) + local.shape[1:])

    full_in, full_cot = (
        lax.all_gather(hidden_in, "segment", axis=2, tiled=True),
        lax.all_gather(cotangent, "segment", axis=2, tiled=True),
    )
    slot_in, slot_cot = (
        lax.all_to_all(to_slots(full_in), "expert", split_axis=0, concat_axis=0, tiled=True),
        lax.all_to_all(to_slots(full_cot), "expert", split_axis=0, concat_axis=0, tiled=True),
    )
    width = slot_in.shape[2]
    micro_rows = slots * length // MICRO
    inputs = slot_in.reshape(MICRO, micro_rows, width)
    cots = slot_cot.reshape(MICRO, micro_rows, width)
    w_dn = w_down[0, 0]
    w_upper = w_up[0, 0]
    rank = w_dn.shape[1]
    scale = gain[0, 0].astype(jnp.float32)
    ticks = MICRO + phases - 1

    def forward_tick(tick, carry):
        received, saved, pres, results = carry
        which = tick - phase
        valid = (which >= 0) & (which < MICRO)
        slot = jnp.clip(which, 0, MICRO - 1)
        first = lax.dynamic_index_in_dim(inputs, jnp.minimum(tick, MICRO - 1), 0, keepdims=False)
        entering = jnp.where(phase == 0, first, received)
        leaving, pre = phase_forward(entering, w_dn, w_upper, scale)
        saved = put_slot(saved, entering, slot, valid)
        pres = put_slot(pres, pre, slot, valid)
        results = put_slot(results, leaving, slot, valid & (phase == phases - 1))
        received = shifted(leaving, "segment", 1)
        return (received, saved, pres, results)

    start = (
        jnp.zeros((micro_rows, width), jnp.bfloat16),
        jnp.zeros((MICRO, micro_rows, width), jnp.bfloat16),
        jnp.zeros((MICRO, micro_rows, rank), jnp.float32),
        jnp.zeros((MICRO, micro_rows, width), jnp.bfloat16),
    )
    received, saved, pres, results = lax.fori_loop(0, ticks, forward_tick, start)

    def backward_tick(tick, carry):
        received, lows, acts, dpres, grads = carry
        which = tick - (phases - 1 - phase)
        valid = (which >= 0) & (which < MICRO)
        slot = jnp.clip(which, 0, MICRO - 1)
        last = lax.dynamic_index_in_dim(cots, jnp.minimum(tick, MICRO - 1), 0, keepdims=False)
        grad_in = jnp.where(phase == phases - 1, last, received)
        hidden = lax.dynamic_index_in_dim(saved, slot, 0, keepdims=False)
        pre = lax.dynamic_index_in_dim(pres, slot, 0, keepdims=False)
        grad_out, lowered, act, d_pre = phase_backward(hidden, grad_in, pre, w_dn, w_upper, scale)
        lows = put_slot(lows, lowered, slot, valid)
        acts = put_slot(acts, act, slot, valid)
        dpres = put_slot(dpres, d_pre, slot, valid)
        grads = put_slot(grads, grad_in, slot, valid)
        received = shifted(grad_out, "segment", -1)
        return (received, lows, acts, dpres, grads)

    start_back = (
        jnp.zeros((micro_rows, width), jnp.bfloat16),
        jnp.zeros((MICRO, micro_rows, width), jnp.bfloat16),
        jnp.zeros((MICRO, micro_rows, rank), jnp.bfloat16),
        jnp.zeros((MICRO, micro_rows, rank), jnp.bfloat16),
        jnp.zeros((MICRO, micro_rows, width), jnp.bfloat16),
    )
    received, lows, acts, dpres, grads = lax.fori_loop(0, ticks, backward_tick, start_back)
    contract = (((0,), (0,)), ((), ()))
    grad_dn = lax.dot_general(
        lows.reshape(-1, width),
        dpres.reshape(-1, rank),
        contract,
        preferred_element_type=jnp.float32,
    )
    grad_upper = lax.dot_general(
        acts.reshape(-1, rank),
        grads.reshape(-1, width),
        contract,
        preferred_element_type=jnp.float32,
    )
    summed_dn, summed_upper = (
        lax.psum_scatter(
            grad_dn.astype(jnp.bfloat16), "dp", scatter_dimension=0, tiled=True
        ).astype(jnp.float32),
        lax.psum_scatter(
            grad_upper.astype(jnp.bfloat16), "dp", scatter_dimension=1, tiled=True
        ).astype(jnp.float32),
    )
    returned = from_root(results, "segment", phases - 1)
    returned = returned.reshape(slots, length, width)
    own = lax.dynamic_slice_in_dim(returned, phase * quarter, quarter, 2)
    back = lax.all_to_all(own, "expert", split_axis=0, concat_axis=0, tiled=True)
    out_hidden = jnp.dot(place.T, back.reshape(slots, -1), preferred_element_type=jnp.float32)
    out_hidden = out_hidden.astype(jnp.bfloat16).reshape(s_local, length, quarter)
    return (
        out_hidden,
        summed_dn.astype(jnp.bfloat16)[None, None],
        summed_upper.astype(jnp.bfloat16)[None, None],
    )


CHUNK = 512
MIB = 1024 * 1024
TRANS_RHS = (((1,), (1,)), ((), ()))
TRANS_LHS = (((0,), (0,)), ((), ()))


def matmul(left, right, dims=(((1,), (0,)), ((), ()))):
    return lax.dot_general(left, right, dims, preferred_element_type=jnp.float32)


def spread_ids(ids, shape, length):
    lane = lax.broadcasted_iota(jnp.int32, shape, 1)
    spread = jnp.zeros(shape, jnp.int32)
    for n in range(ids.shape[0]):
        spread = jnp.where(lane // length == n, ids[n], spread)
    return spread


def ranked(ids_row, length):
    tokens = ids_row.shape[1]
    kinds = lax.broadcasted_iota(jnp.int32, (8, tokens), 0)
    member = (kinds == ids_row).astype(jnp.float32)
    at_col = lax.broadcasted_iota(jnp.int32, (tokens, tokens), 0)
    at_row = lax.broadcasted_iota(jnp.int32, (tokens, tokens), 1)
    before = (lax.rem(at_col, length) == 0) & (at_col // length < at_row // length)
    counts = matmul(member.astype(jnp.bfloat16), before.astype(jnp.float32).astype(jnp.bfloat16))
    rank = jnp.sum(member * counts, axis=0, keepdims=True)
    total = jnp.sum(member, axis=1, keepdims=True) * (1.0 / length)
    lower = jnp.sum(jnp.where(kinds < ids_row, total, 0.0), axis=0, keepdims=True)
    return rank.astype(jnp.int32), lower.astype(jnp.int32)


def one_hot(target, rows):
    wanted = lax.broadcasted_iota(jnp.int32, (rows, target.shape[1]), 0)
    return (wanted == target).astype(jnp.float32).astype(jnp.bfloat16)


def placements(ids_row, length, capacity, slots):
    rank, lower = ranked(ids_row, length)
    token = lax.rem(lax.broadcasted_iota(jnp.int32, ids_row.shape, 1), length)
    place = rank + lower
    group = lax.rem(place, 2)
    per_core = capacity // 2
    packed = ((ids_row * 2 + group) * per_core + rank // 2) * length + token
    tokens = ids_row.shape[1]
    ordered = group * (tokens // 2) + (place // 2) * length + token
    return one_hot(packed, slots * length), one_hot(ordered, tokens)


def pack_kernel(length, capacity, slots, ids, hidden, cot, send, id_buf, buf, packed, sems):
    groups, _, rows, part = send.shape
    tokens = hidden.shape[0] * length
    arriving = [
        pltpu.make_async_copy(source, target, sems.at[at])
        for at, (source, target) in enumerate(
            ((ids, id_buf), (hidden, buf.at[0]), (cot, buf.at[1]))
        )
    ]
    leaving = [
        pltpu.make_async_copy(packed.at[:, at], send.at[:, at], sems.at[3 + at]) for at in range(2)
    ]
    for copy in arriving:
        copy.start()
    arriving[0].wait()
    ids_row = spread_ids(id_buf, (8, tokens), length)[:1]
    place, _ = placements(ids_row, length, capacity, slots)
    for which in range(2):
        arriving[1 + which].wait()
        moved = matmul(place, buf[which].reshape(tokens, part)).astype(jnp.bfloat16)
        for group in range(groups):
            packed[group, which] = moved[group * rows : (group + 1) * rows]
        leaving[which].start()
    for copy in leaving:
        copy.wait()


def slab_kernel(length, capacity, slots, ids, hidden, cot, _, *refs):
    slabs, refs = refs[:4], refs[4:]
    id_buf, buf, ordered, turned, out_slabs, sems = refs
    s_local, _, part = hidden.shape
    tokens = s_local * length
    slab = part // 2
    half = tokens // 2
    replica = lax.axis_index("dp")
    arriving = [
        pltpu.make_async_copy(source, target, sems.at[at])
        for at, (source, target) in enumerate(
            ((ids, id_buf), (hidden, buf.at[0]), (cot, buf.at[1]))
        )
    ]
    leaving = [
        pltpu.make_async_copy(out_slabs.at[at], slabs[at], sems.at[3 + at]) for at in range(4)
    ]
    for copy in arriving:
        copy.start()
    arriving[0].wait()
    ids_row = spread_ids(id_buf, (16, tokens), length)
    _, by_group = placements(ids_row[:1], length, capacity, slots)
    for group in range(2):
        mine = by_group[group * half : (group + 1) * half]
        clusters = matmul(ids_row.astype(jnp.float32).astype(jnp.bfloat16), mine, TRANS_RHS)
        turned[group] = jnp.concatenate(
            [clusters.astype(jnp.bfloat16), jnp.zeros((16, 128 - half), jnp.bfloat16)], axis=1
        )
    for which in range(2):
        arriving[1 + which].wait()
        flat = buf[which].reshape(tokens, part)
        ordered[which] = matmul(by_group, flat).astype(jnp.bfloat16)
    for turn in range(4):
        pair = (turn // 2) ^ (replica & 1)
        group = (turn % 2) ^ (replica >> 1)
        cols = pl.ds(pl.multiple_of(pair * slab, slab), slab)
        at = pl.ds(pl.multiple_of(group * half, half), half)
        for which in range(2):
            out_slabs[turn, which * half : (which + 1) * half] = ordered[which, at, cols]
        out_slabs[turn, tokens:] = jnp.zeros((16, slab), jnp.bfloat16)
        out_slabs[turn, tokens:, :128] = turned[group]
        leaving[turn].start()
    for copy in leaving:
        copy.wait()


def repack_kernel(length, capacity, *refs):
    slabs, outs = refs[:4], refs[5:]
    experts, rows = len(outs), outs[0].shape[2]
    half = (slabs[0].shape[0] - 16) // 2
    core, replica = lax.axis_index("segment"), lax.axis_index("dp")
    for turn, slab in enumerate(slabs):
        near = turn // 2 + 2 * ((turn % 2) ^ (replica >> 1) ^ core)
        ids_row = slab[2 * half :, :128].astype(jnp.float32)[:1, :half].astype(jnp.int32)
        rank, _ = ranked(ids_row, length)
        token = lax.rem(lax.broadcasted_iota(jnp.int32, ids_row.shape, 1), length)
        step = ids_row ^ lax.axis_index("expert")
        place = one_hot((step * (capacity // 2) + rank) * length + token, experts * rows)
        for which in range(2):
            moved = matmul(place, slab[which * half : (which + 1) * half]).astype(jnp.bfloat16)
            for e in range(experts):
                outs[e][which, near] = moved[e * rows : (e + 1) * rows]


def unpack(sizes, id_buf, back, out):
    length, capacity, slots = sizes
    groups, rows, width = back.shape
    s_local = out.shape[0]
    ids_row = spread_ids(id_buf, (8, s_local * length), length)[:1]
    place, _ = placements(ids_row, length, capacity, slots)
    moved = matmul(place, back[...].reshape(groups * rows, width), TRANS_LHS)
    out[...] = moved.astype(jnp.bfloat16).reshape(s_local, length, width)


def split_three(value):
    top = value.astype(jnp.bfloat16).astype(jnp.float32)
    mid = (value - top).astype(jnp.bfloat16).astype(jnp.float32)
    low = (value - top - mid).astype(jnp.bfloat16).astype(jnp.float32)
    return [top, mid, low]


def side_by_side(columns, tokens):
    lane = lax.broadcasted_iota(jnp.int32, (tokens, 128), 1)
    block = jnp.zeros((tokens, 128), jnp.float32)
    at = 0
    for column in columns:
        for piece in split_three(column):
            block = jnp.where(lane == at, piece, block)
            at += 1
    return block.astype(jnp.bfloat16)


def lanes(value):
    total = value[:, :128]
    for start in range(128, value.shape[1], 128):
        total = total + value[:, start : start + 128]
    return total


def row_sum(parts):
    return jnp.sum(parts, axis=1, keepdims=True)


def chain_kernel(
    recv_in, own_dn, own_up, own_gain, other_dn, other_up, other_gain,
    out, small,
    recv, dn_buf, up_buf, gain_buf, entering, middle, d_norms, sems,
):
    phase = lax.axis_index("segment")
    experts, phases, _, rows, part = recv.shape
    tokens = experts * rows
    width = phases * part
    rank = dn_buf.shape[2]
    own, other = (own_dn, own_up, own_gain), (other_dn, other_up, other_gain)

    def copies(sources, at):
        return [
            pltpu.make_async_copy(source, buffer.at[at], sems.at[at, which])
            for which, (source, buffer) in enumerate(zip(sources, (dn_buf, up_buf, gain_buf)))
        ]

    def fetch(at):
        for this in range(2):

            @pl.when(phase == this)
            def _():
                for copy in copies(own if at == this else other, at):
                    copy.start()

    arriving = [
        pltpu.make_async_copy(recv_in.at[:, :, at], recv.at[:, :, at], sems.at[2, at])
        for at in range(2)
    ]
    arriving[0].start()
    fetch(0)
    waits = [copies(own, at) for at in range(2)]
    cols = range(0, width, CHUNK)

    def block(which, col):
        half, start = col // part, col % part
        return jnp.concatenate(
            [recv[e, half, which, :, start : start + CHUNK] for e in range(experts)], axis=0
        )

    def inverse_of(ref, mean):
        total = jnp.zeros((tokens, 128), jnp.float32)
        for col in cols:
            center = ref[:, col : col + CHUNK].astype(jnp.float32) - mean
            total = total + lanes(center * center)
        return lax.rsqrt(row_sum(total) / width + EPS)

    def down(ref, mean, inverse, at):
        pre = jnp.zeros((tokens, rank), jnp.float32)
        for col in cols:
            here = slice(col, col + CHUNK)
            normed = (ref[:, here].astype(jnp.float32) - mean) * inverse
            lowered = (normed * gain_buf[at, :, here].astype(jnp.float32)).astype(jnp.bfloat16)
            pre = pre + matmul(lowered, dn_buf[at, here, :])
        return pre

    total = jnp.zeros((tokens, 128), jnp.float32)
    arriving[0].wait()
    for col in cols:
        value = block(0, col)
        entering[:, col : col + CHUNK] = value
        total = total + lanes(value.astype(jnp.float32))
    mean_0 = row_sum(total) / width
    inverse_0 = inverse_of(entering, mean_0)
    waits[0][0].wait()
    waits[0][2].wait()
    arriving[1].start()
    fetch(1)
    pre_0 = down(entering, mean_0, inverse_0, 0)
    act_0 = gelu_value(pre_0).astype(jnp.bfloat16)
    slope_0 = gelu_slope(pre_0)

    waits[0][1].wait()
    total = jnp.zeros((tokens, 128), jnp.float32)
    for col in cols:
        here = slice(col, col + CHUNK)
        value = entering[:, here].astype(jnp.float32) + matmul(act_0, up_buf[0, :, here])
        value = value.astype(jnp.bfloat16)
        middle[:, here] = value
        total = total + lanes(value.astype(jnp.float32))
    mean_1 = row_sum(total) / width
    inverse_1 = inverse_of(middle, mean_1)
    for copy in waits[1] + arriving[1:]:
        copy.wait()
    d_act = jnp.zeros((tokens, rank), jnp.float32)
    for col in cols:
        d_act = d_act + matmul(block(1, col), up_buf[1, :, col : col + CHUNK], TRANS_RHS)
    pre_1 = down(middle, mean_1, inverse_1, 1)
    act_1 = gelu_value(pre_1).astype(jnp.bfloat16)
    d_pre_1 = (d_act * gelu_slope(pre_1)).astype(jnp.bfloat16)

    total = jnp.zeros((tokens, 128), jnp.float32)
    cross = jnp.zeros((tokens, 128), jnp.float32)
    for col in cols:
        here = slice(col, col + CHUNK)
        wide = middle[:, here].astype(jnp.float32)
        d_norm = matmul(d_pre_1, dn_buf[1, here, :], TRANS_RHS)
        d_norm = d_norm * gain_buf[1, :, here].astype(jnp.float32)
        d_norms[:, here] = d_norm
        total = total + lanes(d_norm)
        cross = cross + lanes(d_norm * ((wide - mean_1) * inverse_1))
        leaving = (wide + matmul(act_1, up_buf[1, :, here])).astype(jnp.bfloat16)
        half, start = col // part, col % part
        for e in range(experts):
            out[e, half, :, start : start + CHUNK] = leaving[e * rows : (e + 1) * rows]
    shift = row_sum(total) / width
    along = row_sum(cross) / width
    d_act = jnp.zeros((tokens, rank), jnp.float32)
    for col in cols:
        here = slice(col, col + CHUNK)
        normed = (middle[:, here].astype(jnp.float32) - mean_1) * inverse_1
        grad = block(1, col).astype(jnp.float32) + inverse_1 * (
            d_norms[:, here] - shift - normed * along
        )
        d_act = d_act + matmul(grad.astype(jnp.bfloat16), up_buf[0, :, here], TRANS_RHS)
    d_pre_0 = (d_act * slope_0).astype(jnp.bfloat16)
    moments = (mean_0, inverse_0, mean_1, inverse_1, shift, along)
    kept = (act_0, act_1, d_pre_0, d_pre_1, side_by_side(moments, tokens))
    for e in range(experts):
        start = pl.multiple_of((e ^ lax.axis_index("expert")) * rows, rows)
        for at, value in enumerate(kept):
            cols = slice(at * rank, at * rank + value.shape[1])
            small[pl.ds(start, rows), cols] = value[e * rows : (e + 1) * rows]


def gradient_kernel(experts, sources, sizes, *refs):
    sides, refs = refs[: 2 * experts], refs[2 * experts :]
    smalls, refs = refs[:sources], refs[sources:]
    own, other, refs = refs[:3], refs[3:6], refs[6:]
    ids, back_in, out_hidden, grad_dn, grad_upper = refs[:5]
    (id_buf, back, result, dn_buf, up_buf, gain_buf, wide_buf, small, moments, turned, lows, grads,
     dn_out, up_out, small_sems, wide_sems, sems) = refs[5:]
    core = lax.axis_index("segment")
    place = lax.axis_index("dp")
    rows, slab = smalls[0].shape[0], sides[0].shape[3]
    replicas = sources // 2
    rank = dn_buf.shape[1]
    columns = 256
    chunks = range(0, slab, columns)
    features = pl.ds(pl.multiple_of(place * slab, slab), slab)

    def weight_copies(up, gain_first, dn, gain_second):
        moves = (
            (up.at[:, features], up_buf),
            (gain_first.at[:, features], gain_buf.at[0]),
            (gain_second.at[:, features], gain_buf.at[1]),
            (dn.at[features, :], dn_buf),
        )
        return [
            pltpu.make_async_copy(source, target, sems.at[at])
            for at, (source, target) in enumerate(moves)
        ]

    early = [
        pltpu.make_async_copy(ids, id_buf, sems.at[4]),
        pltpu.make_async_copy(back_in, back, sems.at[5]),
    ]
    small_copies = [
        pltpu.make_async_copy(
            source, small.at[at * rows : (at + 1) * rows], small_sems.at[at]
        )
        for at, source in enumerate(smalls)
    ]
    wide_copies = [
        [
            pltpu.make_async_copy(
                side.at[:, :, :, col : col + columns],
                wide_buf.at[at, :, :, :, col : col + columns],
                wide_sems.at[col // columns, at],
            )
            for at, side in enumerate(sides)
        ]
        for col in chunks
    ]
    for copy in early + small_copies:
        copy.start()

    @pl.when(core == 0)
    def _():
        for copy in weight_copies(own[1], own[2], other[0], other[2]):
            copy.start()

    @pl.when(core != 0)
    def _():
        for copy in weight_copies(other[1], other[2], own[0], own[2]):
            copy.start()

    for copies in wide_copies:
        for copy in copies:
            copy.start()
    for copy in early:
        copy.wait()
    unpack(sizes, id_buf, back, result)
    leaving = [pltpu.make_async_copy(result, out_hidden, sems.at[6])]
    leaving[0].start()
    for copy in small_copies + weight_copies(own[1], own[2], other[0], other[2]):
        copy.wait()

    def sliced(source, which, here):
        first, near = (source // replicas) * experts, source % replicas
        return jnp.concatenate(
            [wide_buf[first + step, which, near, :, here] for step in range(experts)], axis=0
        )

    def moment(at, index):
        value = moments[at, index * 128 : (index + 1) * 128]
        return jnp.concatenate([value] * (columns // 128), axis=1)

    def work(first):
        held = lax.broadcasted_iota(jnp.int32, (128, 6 * 128), 0)
        wanted = lax.broadcasted_iota(jnp.int32, (128, 6 * 128), 1) // 128
        adds = (held // 3 == wanted).astype(jnp.float32).astype(jnp.bfloat16)
        moments[...] = matmul(small[:, 4 * rank :], adds)
        act, d_pre = (0, 2) if first else (1, 3)
        turned[0] = small[:, act * rank : (act + 1) * rank].T
        turned[1] = small[:, d_pre * rank : (d_pre + 1) * rank].T
        for index, col in enumerate(chunks):
            here = slice(col, col + columns)
            for copy in wide_copies[index]:
                copy.wait()
            ups = matmul(small[:, :rank], up_buf[:, here])
            scales = [gain_buf[at, :, here].astype(jnp.float32) for at in range(2)]
            if first:
                downs = matmul(small[:, 3 * rank : 4 * rank], dn_buf[here, :], TRANS_RHS)
            for source in range(sources):
                at = slice(source * rows, (source + 1) * rows)
                wide = sliced(source, 0, here).astype(jnp.float32)
                grad_in = sliced(source, 1, here)
                middle = (wide + ups[at]).astype(jnp.bfloat16).astype(jnp.float32)
                inverse = moment(at, 3)
                normed = (middle - moment(at, 2)) * inverse
                if first:
                    entered = (wide - moment(at, 0)) * moment(at, 1)
                    lows[index, at] = (entered * scales[0]).astype(jnp.bfloat16)
                    d_norm = downs[at] * scales[1]
                    grads[index, at] = (
                        grad_in.astype(jnp.float32)
                        + inverse * (d_norm - moment(at, 4) - normed * moment(at, 5))
                    ).astype(jnp.bfloat16)
                else:
                    lows[index, at] = (normed * scales[1]).astype(jnp.bfloat16)
                    grads[index, at] = grad_in
            dn_out[here, :] = matmul(turned[1], lows[index]).astype(jnp.bfloat16).T
            up_out[index] = matmul(turned[0], grads[index]).astype(jnp.bfloat16)
            for copy in out_copies(index, here):
                copy.start()

    def out_copies(index, here):
        return [
            pltpu.make_async_copy(
                dn_out.at[here, :], grad_dn.at[here, :], sems.at[7 + 2 * index]
            ),
            pltpu.make_async_copy(
                up_out.at[index], grad_upper.at[:, here], sems.at[8 + 2 * index]
            ),
        ]

    @pl.when(core == 0)
    def _():
        work(True)

    @pl.when(core != 0)
    def _():
        work(False)

    for index, col in enumerate(chunks):
        leaving += out_copies(index, slice(col, col + columns))
    for copy in leaving:
        copy.wait()


VMEM = pl.BlockSpec(memory_space=pltpu.VMEM)
HBM = pl.BlockSpec(memory_space=pltpu.HBM)


def call(kernel, name, grant, in_specs, outs, scratch=(), outs_in=VMEM, flops=0, moved=MIB):
    return pl.pallas_call(
        kernel,
        out_shape=tuple(jax.ShapeDtypeStruct(*out) for out in outs),
        in_specs=in_specs,
        out_specs=tuple(outs_in for _ in outs),
        scratch_shapes=list(scratch),
        compiler_params=pltpu.CompilerParams(vmem_limit_bytes=grant * MIB),
        cost_estimate=pl.CostEstimate(flops=flops, bytes_accessed=moved, transcendentals=0),
        name=name,
    )


def across(block, axis, distance):
    size = lax.axis_size(axis)
    return lax.ppermute(block, axis, [(i, i ^ distance) for i in range(size)])


def slab_route(replicas, pair, low):
    route = []
    for replica in range(replicas):
        for core in range(2):
            chip = 2 * core + ((replica & 1) ^ pair)
            route.append((2 * replica + core, 2 * chip + ((replica >> 1) ^ low)))
    return route


def on_device_two_phases(hidden_in, cotangent, cluster_ids, w_down, w_up, gain):
    experts = lax.axis_size("expert")
    replicas = lax.axis_size("dp")
    s_local, length, part = hidden_in.shape
    width = 2 * part
    capacity = 2 * s_local // experts
    slots = experts * capacity
    groups = 2 * experts
    rows = slots * length // groups
    tokens = experts * rows
    own = (w_down[0, 0], w_up[0, 0], gain[0])
    rank = own[0].shape[1]
    slab = width // replicas
    bf16, f32 = jnp.bfloat16, jnp.float32
    sizes = (length, capacity, slots)
    sections = ("expert", "segment")

    other = tuple(across(array, "segment", 1) for array in own)
    half = s_local * length // 2
    (send,) = call(
        functools.partial(pack_kernel, *sizes),
        "pack",
        60,
        [HBM] * 3,
        [((groups, 2, rows, part), bf16)],
        [
            pltpu.SMEM(cluster_ids.shape, jnp.int32),
            pltpu.VMEM((2,) + hidden_in.shape, bf16),
            pltpu.VMEM((groups, 2, rows, part), bf16),
            pltpu.SemaphoreType.DMA((5,)),
        ],
        outs_in=HBM,
    )(cluster_ids, hidden_in, cotangent)
    slabs = call(
        functools.partial(slab_kernel, *sizes),
        "slabs",
        60,
        [HBM] * 4,
        [((2 * half + 16, slab), bf16)] * 4,
        [
            pltpu.SMEM(cluster_ids.shape, jnp.int32),
            pltpu.VMEM((2,) + hidden_in.shape, bf16),
            pltpu.VMEM((2, 2 * half, part), bf16),
            pltpu.VMEM((2, 16, 128), bf16),
            pltpu.VMEM((4, 2 * half + 16, slab), bf16),
            pltpu.SemaphoreType.DMA((7,)),
        ],
        outs_in=HBM,
    )(cluster_ids, hidden_in, cotangent, send)
    recv = lax.all_to_all(send, sections, split_axis=0, concat_axis=0, tiled=True)
    recv = recv.reshape(experts, 2, 2, rows, part)
    slabs = [
        lax.ppermute(block, ("dp", "segment"), slab_route(replicas, turn // 2, turn % 2))
        for turn, block in enumerate(slabs)
    ]
    out, small = call(
        chain_kernel,
        "chain",
        50,
        [HBM] * 7,
        [((experts, 2, rows, part), bf16), ((tokens, 4 * rank + 128), bf16)],
        [
            pltpu.VMEM(recv.shape, bf16),
            pltpu.VMEM((2, width, rank), bf16),
            pltpu.VMEM((2, rank, width), bf16),
            pltpu.VMEM((2, 1, width), bf16),
            pltpu.VMEM((tokens, width), bf16),
            pltpu.VMEM((tokens, width), bf16),
            pltpu.VMEM((tokens, width), f32),
            pltpu.SemaphoreType.DMA((3, 3)),
        ],
        flops=7 * 2 * tokens * width * rank,
        moved=10 * MIB,
    )(recv, *own, *other)
    slices = call(
        functools.partial(repack_kernel, length, capacity),
        "repack",
        16,
        [VMEM] * 4 + [HBM],
        [((2, replicas, rows, slab), bf16)] * experts,
    )(*slabs, small)
    mine = [slices[0]] + [across(slices[step], "expert", step) for step in range(1, experts)]
    theirs = [across(block, "segment", 1) for block in mine]
    one_away = across(small, "dp", 1)
    near = [small, one_away, across(small, "dp", 2), across(one_away, "dp", 2)]
    smalls = near + [across(piece, "segment", 1) for piece in near]

    back = lax.all_to_all(
        out.reshape(groups, rows, part), sections, split_axis=0, concat_axis=0, tiled=True
    )

    sources = 2 * replicas
    all_tokens = sources * tokens
    out_hidden, grad_dn, grad_upper = call(
        functools.partial(gradient_kernel, experts, sources, sizes),
        "gradients",
        60,
        [HBM] * (2 * experts + sources + 8),
        [(hidden_in.shape, bf16), ((slab, rank), bf16), ((rank, slab), bf16)],
        [
            pltpu.SMEM(cluster_ids.shape, jnp.int32),
            pltpu.VMEM(back.shape, bf16),
            pltpu.VMEM(hidden_in.shape, bf16),
            pltpu.VMEM((slab, rank), bf16),
            pltpu.VMEM((rank, slab), bf16),
            pltpu.VMEM((2, 1, slab), bf16),
            pltpu.VMEM((2 * experts, 2, replicas, rows, slab), bf16),
            pltpu.VMEM((all_tokens, 4 * rank + 128), bf16),
            pltpu.VMEM((all_tokens, 6 * 128), f32),
            pltpu.VMEM((2, rank, all_tokens), bf16),
            pltpu.VMEM((slab // 256, all_tokens, 256), bf16),
            pltpu.VMEM((slab // 256, all_tokens, 256), bf16),
            pltpu.VMEM((slab, rank), bf16),
            pltpu.VMEM((slab // 256, rank, 256), bf16),
            pltpu.SemaphoreType.DMA((sources,)),
            pltpu.SemaphoreType.DMA((slab // 256, 2 * experts)),
            pltpu.SemaphoreType.DMA((7 + 2 * (slab // 256),)),
        ],
        outs_in=HBM,
    )(*mine, *theirs, *smalls, *own, *other, cluster_ids, back)
    return (out_hidden, grad_dn[None, None], grad_upper[None, None])


def solution(mesh):
    two = dict(mesh.shape) == {"expert": 4, "dp": 4, "segment": 2}
    on_device = on_device_two_phases if two else on_device_pipelined
    return jax.shard_map(
        on_device,
        mesh=mesh,
        in_specs=(
            P(("expert", "dp"), None, "segment"),
            P(("expert", "dp"), None, "segment"),
            P(("expert", "dp")),
            P("expert", "segment", None, None),
            P("expert", "segment", None, None),
            P("expert", "segment", None),
        ),
        out_specs=(
            P(("expert", "dp"), None, "segment"),
            P("expert", "segment", "dp", None),
            P("expert", "segment", None, "dp"),
        ),
        check_vma=False,
    )
```

```python
import functools

import jax
import jax.numpy as jnp
from jax import lax
from jax.experimental import pallas as pl
from jax.experimental.pallas import tpu as pltpu
from jax.sharding import PartitionSpec as P

MICRO = 4


EPS = 1e-05
C_ZERO = 0.7978845608028654
C_ONE = 0.044715


def shifted(block, axis, distance):
    devices = range(lax.axis_size(axis))
    route = [(i - distance, i) for i in devices if i - distance in devices]
    return lax.ppermute(block, axis, route)


def from_root(block, axis, holder):
    block = jnp.where(lax.axis_index(axis) == holder, block, jnp.zeros_like(block))
    return lax.psum(block, axis)


def gelu_value(z):
    return 0.5 * z * (1.0 + jnp.tanh(C_ZERO * (z + C_ONE * z * z * z)))


def gelu_slope(z):
    tval = jnp.tanh(C_ZERO * (z + C_ONE * z * z * z))
    return 0.5 * (1.0 + tval) + 0.5 * z * (1.0 - tval * tval) * C_ZERO * (1.0 + 3.0 * C_ONE * z * z)


def normalize(hidden):
    wide = hidden.astype(jnp.float32)
    center = wide - jnp.mean(wide, axis=-1, keepdims=True)
    inverse = lax.rsqrt(jnp.mean(center * center, axis=-1, keepdims=True) + EPS)
    return (wide, center * inverse, inverse)


def phase_forward(hidden, w_dn, w_upper, scale):
    wide, normed, inverse = normalize(hidden)
    lowered = (normed * scale).astype(jnp.bfloat16)
    pre = jnp.dot(lowered, w_dn, preferred_element_type=jnp.float32)
    act = gelu_value(pre).astype(jnp.bfloat16)
    leaving = (wide + jnp.dot(act, w_upper, preferred_element_type=jnp.float32)).astype(
        jnp.bfloat16
    )
    return (leaving, pre)


def phase_backward(hidden, grad_in, pre, w_dn, w_upper, scale):
    wide, normed, inverse = normalize(hidden)
    lowered = (normed * scale).astype(jnp.bfloat16)
    act = gelu_value(pre).astype(jnp.bfloat16)
    d_act = jnp.dot(grad_in, w_upper.T, preferred_element_type=jnp.float32)
    d_pre = (d_act * gelu_slope(pre)).astype(jnp.bfloat16)
    d_low = jnp.dot(d_pre, w_dn.T, preferred_element_type=jnp.float32)
    d_norm = d_low * scale
    d_wide = inverse * (
        d_norm
        - jnp.mean(d_norm, axis=-1, keepdims=True)
        - normed * jnp.mean(d_norm * normed, axis=-1, keepdims=True)
    )
    grad_out = (grad_in.astype(jnp.float32) + d_wide).astype(jnp.bfloat16)
    return (grad_out, lowered, act, d_pre)


def put_slot(buffer, value, slot, valid):
    old_value = lax.dynamic_index_in_dim(buffer, slot, 0, keepdims=False)
    return lax.dynamic_update_index_in_dim(buffer, jnp.where(valid, value, old_value), slot, 0)


def on_device_pipelined(hidden_in, cotangent, cluster_ids, w_down, w_up, gain):
    experts = lax.axis_size("expert")
    phases = lax.axis_size("segment")
    phase = lax.axis_index("segment")
    s_local, length, quarter = hidden_in.shape
    capacity = 2 * s_local // experts
    slots = experts * capacity
    same = (cluster_ids[:, None] == cluster_ids[None, :]).astype(jnp.int32)
    earlier = jnp.sum(jnp.tril(same, -1), axis=1)
    target = cluster_ids * capacity + earlier
    place = (jnp.arange(slots, dtype=jnp.int32)[:, None] == target[None, :]).astype(jnp.bfloat16)

    def to_slots(local):
        flat = local.reshape(s_local, -1)
        moved = jnp.dot(place, flat, preferred_element_type=jnp.float32).astype(jnp.bfloat16)
        return moved.reshape((slots,) + local.shape[1:])

    full_in, full_cot = (
        lax.all_gather(hidden_in, "segment", axis=2, tiled=True),
        lax.all_gather(cotangent, "segment", axis=2, tiled=True),
    )
    slot_in, slot_cot = (
        lax.all_to_all(to_slots(full_in), "expert", split_axis=0, concat_axis=0, tiled=True),
        lax.all_to_all(to_slots(full_cot), "expert", split_axis=0, concat_axis=0, tiled=True),
    )
    width = slot_in.shape[2]
    micro_rows = slots * length // MICRO
    inputs = slot_in.reshape(MICRO, micro_rows, width)
    cots = slot_cot.reshape(MICRO, micro_rows, width)
    w_dn = w_down[0, 0]
    w_upper = w_up[0, 0]
    rank = w_dn.shape[1]
    scale = gain[0, 0].astype(jnp.float32)
    ticks = MICRO + phases - 1

    def forward_tick(tick, carry):
        received, saved, pres, results = carry
        which = tick - phase
        valid = (which >= 0) & (which < MICRO)
        slot = jnp.clip(which, 0, MICRO - 1)
        first = lax.dynamic_index_in_dim(inputs, jnp.minimum(tick, MICRO - 1), 0, keepdims=False)
        entering = jnp.where(phase == 0, first, received)
        leaving, pre = phase_forward(entering, w_dn, w_upper, scale)
        saved = put_slot(saved, entering, slot, valid)
        pres = put_slot(pres, pre, slot, valid)
        results = put_slot(results, leaving, slot, valid & (phase == phases - 1))
        received = shifted(leaving, "segment", 1)
        return (received, saved, pres, results)

    start = (
        jnp.zeros((micro_rows, width), jnp.bfloat16),
        jnp.zeros((MICRO, micro_rows, width), jnp.bfloat16),
        jnp.zeros((MICRO, micro_rows, rank), jnp.float32),
        jnp.zeros((MICRO, micro_rows, width), jnp.bfloat16),
    )
    received, saved, pres, results = lax.fori_loop(0, ticks, forward_tick, start)

    def backward_tick(tick, carry):
        received, lows, acts, dpres, grads = carry
        which = tick - (phases - 1 - phase)
        valid = (which >= 0) & (which < MICRO)
        slot = jnp.clip(which, 0, MICRO - 1)
        last = lax.dynamic_index_in_dim(cots, jnp.minimum(tick, MICRO - 1), 0, keepdims=False)
        grad_in = jnp.where(phase == phases - 1, last, received)
        hidden = lax.dynamic_index_in_dim(saved, slot, 0, keepdims=False)
        pre = lax.dynamic_index_in_dim(pres, slot, 0, keepdims=False)
        grad_out, lowered, act, d_pre = phase_backward(hidden, grad_in, pre, w_dn, w_upper, scale)
        lows = put_slot(lows, lowered, slot, valid)
        acts = put_slot(acts, act, slot, valid)
        dpres = put_slot(dpres, d_pre, slot, valid)
        grads = put_slot(grads, grad_in, slot, valid)
        received = shifted(grad_out, "segment", -1)
        return (received, lows, acts, dpres, grads)

    start_back = (
        jnp.zeros((micro_rows, width), jnp.bfloat16),
        jnp.zeros((MICRO, micro_rows, width), jnp.bfloat16),
        jnp.zeros((MICRO, micro_rows, rank), jnp.bfloat16),
        jnp.zeros((MICRO, micro_rows, rank), jnp.bfloat16),
        jnp.zeros((MICRO, micro_rows, width), jnp.bfloat16),
    )
    received, lows, acts, dpres, grads = lax.fori_loop(0, ticks, backward_tick, start_back)
    contract = (((0,), (0,)), ((), ()))
    grad_dn = lax.dot_general(
        lows.reshape(-1, width),
        dpres.reshape(-1, rank),
        contract,
        preferred_element_type=jnp.float32,
    )
    grad_upper = lax.dot_general(
        acts.reshape(-1, rank),
        grads.reshape(-1, width),
        contract,
        preferred_element_type=jnp.float32,
    )
    summed_dn, summed_upper = (
        lax.psum_scatter(
            grad_dn.astype(jnp.bfloat16), "dp", scatter_dimension=0, tiled=True
        ).astype(jnp.float32),
        lax.psum_scatter(
            grad_upper.astype(jnp.bfloat16), "dp", scatter_dimension=1, tiled=True
        ).astype(jnp.float32),
    )
    returned = from_root(results, "segment", phases - 1)
    returned = returned.reshape(slots, length, width)
    own = lax.dynamic_slice_in_dim(returned, phase * quarter, quarter, 2)
    back = lax.all_to_all(own, "expert", split_axis=0, concat_axis=0, tiled=True)
    out_hidden = jnp.dot(place.T, back.reshape(slots, -1), preferred_element_type=jnp.float32)
    out_hidden = out_hidden.astype(jnp.bfloat16).reshape(s_local, length, quarter)
    return (
        out_hidden,
        summed_dn.astype(jnp.bfloat16)[None, None],
        summed_upper.astype(jnp.bfloat16)[None, None],
    )


CHUNK = 512
MIB = 1024 * 1024
TRANS_RHS = (((1,), (1,)), ((), ()))
TRANS_LHS = (((0,), (0,)), ((), ()))


def matmul(left, right, dims=(((1,), (0,)), ((), ()))):
    return lax.dot_general(left, right, dims, preferred_element_type=jnp.float32)


def spread_ids(ids, shape, length):
    lane = lax.broadcasted_iota(jnp.int32, shape, 1)
    spread = jnp.zeros(shape, jnp.int32)
    for n in range(ids.shape[0]):
        spread = jnp.where(lane // length == n, ids[n], spread)
    return spread


def ranked(ids_row, length):
    tokens = ids_row.shape[1]
    kinds = lax.broadcasted_iota(jnp.int32, (8, tokens), 0)
    member = (kinds == ids_row).astype(jnp.float32)
    at_col = lax.broadcasted_iota(jnp.int32, (tokens, tokens), 0)
    at_row = lax.broadcasted_iota(jnp.int32, (tokens, tokens), 1)
    before = (lax.rem(at_col, length) == 0) & (at_col // length < at_row // length)
    counts = matmul(member.astype(jnp.bfloat16), before.astype(jnp.float32).astype(jnp.bfloat16))
    rank = jnp.sum(member * counts, axis=0, keepdims=True)
    total = jnp.sum(member, axis=1, keepdims=True) * (1.0 / length)
    lower = jnp.sum(jnp.where(kinds < ids_row, total, 0.0), axis=0, keepdims=True)
    return rank.astype(jnp.int32), lower.astype(jnp.int32)


def one_hot(target, rows):
    wanted = lax.broadcasted_iota(jnp.int32, (rows, target.shape[1]), 0)
    return (wanted == target).astype(jnp.float32).astype(jnp.bfloat16)


def placements(ids_row, length, capacity, slots):
    rank, lower = ranked(ids_row, length)
    token = lax.rem(lax.broadcasted_iota(jnp.int32, ids_row.shape, 1), length)
    place = rank + lower
    group = lax.rem(place, 2)
    per_core = capacity // 2
    packed = ((ids_row * 2 + group) * per_core + rank // 2) * length + token
    tokens = ids_row.shape[1]
    ordered = group * (tokens // 2) + (place // 2) * length + token
    return one_hot(packed, slots * length), one_hot(ordered, tokens)


def pack_kernel(length, capacity, slots, ids, hidden, cot, send, id_buf, buf, packed, sems):
    groups, _, rows, part = send.shape
    tokens = hidden.shape[0] * length
    arriving = [
        pltpu.make_async_copy(source, target, sems.at[at])
        for at, (source, target) in enumerate(
            ((ids, id_buf), (hidden, buf.at[0]), (cot, buf.at[1]))
        )
    ]
    leaving = [
        pltpu.make_async_copy(packed.at[:, at], send.at[:, at], sems.at[3 + at]) for at in range(2)
    ]
    for copy in arriving:
        copy.start()
    arriving[0].wait()
    ids_row = spread_ids(id_buf, (8, tokens), length)[:1]
    place, _ = placements(ids_row, length, capacity, slots)
    for which in range(2):
        arriving[1 + which].wait()
        moved = matmul(place, buf[which].reshape(tokens, part)).astype(jnp.bfloat16)
        for group in range(groups):
            packed[group, which] = moved[group * rows : (group + 1) * rows]
        leaving[which].start()
    for copy in leaving:
        copy.wait()


def slab_kernel(length, capacity, slots, ids, hidden, cot, _, *refs):
    slabs, refs = refs[:4], refs[4:]
    id_buf, buf, ordered, turned, out_slabs, sems = refs
    s_local, _, part = hidden.shape
    tokens = s_local * length
    slab = part // 2
    half = tokens // 2
    replica = lax.axis_index("dp")
    arriving = [
        pltpu.make_async_copy(source, target, sems.at[at])
        for at, (source, target) in enumerate(
            ((ids, id_buf), (hidden, buf.at[0]), (cot, buf.at[1]))
        )
    ]
    leaving = [
        pltpu.make_async_copy(out_slabs.at[at], slabs[at], sems.at[3 + at]) for at in range(4)
    ]
    for copy in arriving:
        copy.start()
    arriving[0].wait()
    ids_row = spread_ids(id_buf, (16, tokens), length)
    _, by_group = placements(ids_row[:1], length, capacity, slots)
    for group in range(2):
        mine = by_group[group * half : (group + 1) * half]
        clusters = matmul(ids_row.astype(jnp.float32).astype(jnp.bfloat16), mine, TRANS_RHS)
        turned[group] = jnp.concatenate(
            [clusters.astype(jnp.bfloat16), jnp.zeros((16, 128 - half), jnp.bfloat16)], axis=1
        )
    for which in range(2):
        arriving[1 + which].wait()
        flat = buf[which].reshape(tokens, part)
        ordered[which] = matmul(by_group, flat).astype(jnp.bfloat16)
    for turn in range(4):
        pair = (turn // 2) ^ (replica & 1)
        group = (turn % 2) ^ (replica >> 1)
        cols = pl.ds(pl.multiple_of(pair * slab, slab), slab)
        at = pl.ds(pl.multiple_of(group * half, half), half)
        for which in range(2):
            out_slabs[turn, which * half : (which + 1) * half] = ordered[which, at, cols]
        out_slabs[turn, tokens:] = jnp.zeros((16, slab), jnp.bfloat16)
        out_slabs[turn, tokens:, :128] = turned[group]
        leaving[turn].start()
    for copy in leaving:
        copy.wait()


def repack_kernel(length, capacity, *refs):
    slabs, outs = refs[:4], refs[5:]
    experts, rows = len(outs), outs[0].shape[2]
    half = (slabs[0].shape[0] - 16) // 2
    core, replica = lax.axis_index("segment"), lax.axis_index("dp")
    for turn, slab in enumerate(slabs):
        near = turn // 2 + 2 * ((turn % 2) ^ (replica >> 1) ^ core)
        ids_row = slab[2 * half :, :128].astype(jnp.float32)[:1, :half].astype(jnp.int32)
        rank, _ = ranked(ids_row, length)
        token = lax.rem(lax.broadcasted_iota(jnp.int32, ids_row.shape, 1), length)
        step = ids_row ^ lax.axis_index("expert")
        place = one_hot((step * (capacity // 2) + rank) * length + token, experts * rows)
        for which in range(2):
            moved = matmul(place, slab[which * half : (which + 1) * half]).astype(jnp.bfloat16)
            for e in range(experts):
                outs[e][which, near] = moved[e * rows : (e + 1) * rows]


def unpack(sizes, id_buf, back, out):
    length, capacity, slots = sizes
    groups, rows, width = back.shape
    s_local = out.shape[0]
    ids_row = spread_ids(id_buf, (8, s_local * length), length)[:1]
    place, _ = placements(ids_row, length, capacity, slots)
    moved = matmul(place, back[...].reshape(groups * rows, width), TRANS_LHS)
    out[...] = moved.astype(jnp.bfloat16).reshape(s_local, length, width)


def split_three(value):
    top = value.astype(jnp.bfloat16).astype(jnp.float32)
    mid = (value - top).astype(jnp.bfloat16).astype(jnp.float32)
    low = (value - top - mid).astype(jnp.bfloat16).astype(jnp.float32)
    return [top, mid, low]


def side_by_side(columns, tokens):
    lane = lax.broadcasted_iota(jnp.int32, (tokens, 128), 1)
    block = jnp.zeros((tokens, 128), jnp.float32)
    at = 0
    for column in columns:
        for piece in split_three(column):
            block = jnp.where(lane == at, piece, block)
            at += 1
    return block.astype(jnp.bfloat16)


def lanes(value):
    total = value[:, :128]
    for start in range(128, value.shape[1], 128):
        total = total + value[:, start : start + 128]
    return total


def row_sum(parts):
    return jnp.sum(parts, axis=1, keepdims=True)


def chain_kernel(
    recv_in, own_dn, own_up, own_gain, other_dn, other_up, other_gain,
    out, small,
    recv, dn_buf, up_buf, gain_buf, entering, middle, d_norms, sems,
):
    phase = lax.axis_index("segment")
    experts, phases, _, rows, part = recv.shape
    tokens = experts * rows
    width = phases * part
    rank = dn_buf.shape[2]
    own, other = (own_dn, own_up, own_gain), (other_dn, other_up, other_gain)

    def copies(sources, at):
        return [
            pltpu.make_async_copy(source, buffer.at[at], sems.at[at, which])
            for which, (source, buffer) in enumerate(zip(sources, (dn_buf, up_buf, gain_buf)))
        ]

    def fetch(at):
        for this in range(2):

            @pl.when(phase == this)
            def _():
                for copy in copies(own if at == this else other, at):
                    copy.start()

    arriving = [
        pltpu.make_async_copy(recv_in.at[:, :, at], recv.at[:, :, at], sems.at[2, at])
        for at in range(2)
    ]
    arriving[0].start()
    fetch(0)
    waits = [copies(own, at) for at in range(2)]
    cols = range(0, width, CHUNK)

    def block(which, col):
        half, start = col // part, col % part
        return jnp.concatenate(
            [recv[e, half, which, :, start : start + CHUNK] for e in range(experts)], axis=0
        )

    def inverse_of(ref, mean):
        total = jnp.zeros((tokens, 128), jnp.float32)
        for col in cols:
            center = ref[:, col : col + CHUNK].astype(jnp.float32) - mean
            total = total + lanes(center * center)
        return lax.rsqrt(row_sum(total) / width + EPS)

    def down(ref, mean, inverse, at):
        pre = jnp.zeros((tokens, rank), jnp.float32)
        for col in cols:
            here = slice(col, col + CHUNK)
            normed = (ref[:, here].astype(jnp.float32) - mean) * inverse
            lowered = (normed * gain_buf[at, :, here].astype(jnp.float32)).astype(jnp.bfloat16)
            pre = pre + matmul(lowered, dn_buf[at, here, :])
        return pre

    total = jnp.zeros((tokens, 128), jnp.float32)
    arriving[0].wait()
    for col in cols:
        value = block(0, col)
        entering[:, col : col + CHUNK] = value
        total = total + lanes(value.astype(jnp.float32))
    mean_0 = row_sum(total) / width
    inverse_0 = inverse_of(entering, mean_0)
    waits[0][0].wait()
    waits[0][2].wait()
    arriving[1].start()
    fetch(1)
    pre_0 = down(entering, mean_0, inverse_0, 0)
    act_0 = gelu_value(pre_0).astype(jnp.bfloat16)
    slope_0 = gelu_slope(pre_0)

    waits[0][1].wait()
    total = jnp.zeros((tokens, 128), jnp.float32)
    for col in cols:
        here = slice(col, col + CHUNK)
        value = entering[:, here].astype(jnp.float32) + matmul(act_0, up_buf[0, :, here])
        value = value.astype(jnp.bfloat16)
        middle[:, here] = value
        total = total + lanes(value.astype(jnp.float32))
    mean_1 = row_sum(total) / width
    inverse_1 = inverse_of(middle, mean_1)
    for copy in waits[1] + arriving[1:]:
        copy.wait()
    d_act = jnp.zeros((tokens, rank), jnp.float32)
    for col in cols:
        d_act = d_act + matmul(block(1, col), up_buf[1, :, col : col + CHUNK], TRANS_RHS)
    pre_1 = down(middle, mean_1, inverse_1, 1)
    act_1 = gelu_value(pre_1).astype(jnp.bfloat16)
    d_pre_1 = (d_act * gelu_slope(pre_1)).astype(jnp.bfloat16)

    total = jnp.zeros((tokens, 128), jnp.float32)
    cross = jnp.zeros((tokens, 128), jnp.float32)
    for col in cols:
        here = slice(col, col + CHUNK)
        wide = middle[:, here].astype(jnp.float32)
        d_norm = matmul(d_pre_1, dn_buf[1, here, :], TRANS_RHS)
        d_norm = d_norm * gain_buf[1, :, here].astype(jnp.float32)
        d_norms[:, here] = d_norm
        total = total + lanes(d_norm)
        cross = cross + lanes(d_norm * ((wide - mean_1) * inverse_1))
        leaving = (wide + matmul(act_1, up_buf[1, :, here])).astype(jnp.bfloat16)
        half, start = col // part, col % part
        for e in range(experts):
            out[e, half, :, start : start + CHUNK] = leaving[e * rows : (e + 1) * rows]
    shift = row_sum(total) / width
    along = row_sum(cross) / width
    d_act = jnp.zeros((tokens, rank), jnp.float32)
    for col in cols:
        here = slice(col, col + CHUNK)
        normed = (middle[:, here].astype(jnp.float32) - mean_1) * inverse_1
        grad = block(1, col).astype(jnp.float32) + inverse_1 * (
            d_norms[:, here] - shift - normed * along
        )
        d_act = d_act + matmul(grad.astype(jnp.bfloat16), up_buf[0, :, here], TRANS_RHS)
    d_pre_0 = (d_act * slope_0).astype(jnp.bfloat16)
    moments = (mean_0, inverse_0, mean_1, inverse_1, shift, along)
    kept = (act_0, act_1, d_pre_0, d_pre_1, side_by_side(moments, tokens))
    for e in range(experts):
        start = pl.multiple_of((e ^ lax.axis_index("expert")) * rows, rows)
        for at, value in enumerate(kept):
            cols = slice(at * rank, at * rank + value.shape[1])
            small[pl.ds(start, rows), cols] = value[e * rows : (e + 1) * rows]


def gradient_kernel(experts, sources, sizes, *refs):
    sides, refs = refs[: 2 * experts], refs[2 * experts :]
    smalls, refs = refs[:sources], refs[sources:]
    own, other, refs = refs[:3], refs[3:6], refs[6:]
    ids, back_in, out_hidden, grad_dn, grad_upper = refs[:5]
    (id_buf, back, result, dn_buf, up_buf, gain_buf, wide_buf, small, moments, turned, lows, grads,
     dn_out, up_out, small_sems, wide_sems, sems) = refs[5:]
    core = lax.axis_index("segment")
    place = lax.axis_index("dp")
    rows, slab = smalls[0].shape[0], sides[0].shape[3]
    replicas = sources // 2
    rank = dn_buf.shape[1]
    columns = 256
    chunks = range(0, slab, columns)
    features = pl.ds(pl.multiple_of(place * slab, slab), slab)

    def weight_copies(up, gain_first, dn, gain_second):
        moves = (
            (up.at[:, features], up_buf),
            (gain_first.at[:, features], gain_buf.at[0]),
            (gain_second.at[:, features], gain_buf.at[1]),
            (dn.at[features, :], dn_buf),
        )
        return [
            pltpu.make_async_copy(source, target, sems.at[at])
            for at, (source, target) in enumerate(moves)
        ]

    early = [
        pltpu.make_async_copy(ids, id_buf, sems.at[4]),
        pltpu.make_async_copy(back_in, back, sems.at[5]),
    ]
    small_copies = [
        pltpu.make_async_copy(
            source, small.at[at * rows : (at + 1) * rows], small_sems.at[at]
        )
        for at, source in enumerate(smalls)
    ]
    wide_copies = [
        [
            pltpu.make_async_copy(
                side.at[:, :, :, col : col + columns],
                wide_buf.at[at, :, :, :, col : col + columns],
                wide_sems.at[col // columns, at],
            )
            for at, side in enumerate(sides)
        ]
        for col in chunks
    ]
    for copy in early + small_copies:
        copy.start()

    @pl.when(core == 0)
    def _():
        for copy in weight_copies(own[1], own[2], other[0], other[2]):
            copy.start()

    @pl.when(core != 0)
    def _():
        for copy in weight_copies(other[1], other[2], own[0], own[2]):
            copy.start()

    for copies in wide_copies:
        for copy in copies:
            copy.start()
    for copy in early:
        copy.wait()
    unpack(sizes, id_buf, back, result)
    leaving = [pltpu.make_async_copy(result, out_hidden, sems.at[6])]
    leaving[0].start()
    for copy in small_copies + weight_copies(own[1], own[2], other[0], other[2]):
        copy.wait()

    def sliced(source, which, here):
        first, near = (source // replicas) * experts, source % replicas
        return jnp.concatenate(
            [wide_buf[first + step, which, near, :, here] for step in range(experts)], axis=0
        )

    def moment(at, index):
        value = moments[at, index * 128 : (index + 1) * 128]
        return jnp.concatenate([value] * (columns // 128), axis=1)

    def work(first):
        held = lax.broadcasted_iota(jnp.int32, (128, 6 * 128), 0)
        wanted = lax.broadcasted_iota(jnp.int32, (128, 6 * 128), 1) // 128
        adds = (held // 3 == wanted).astype(jnp.float32).astype(jnp.bfloat16)
        moments[...] = matmul(small[:, 4 * rank :], adds)
        act, d_pre = (0, 2) if first else (1, 3)
        turned[0] = small[:, act * rank : (act + 1) * rank].T
        turned[1] = small[:, d_pre * rank : (d_pre + 1) * rank].T
        for index, col in enumerate(chunks):
            here = slice(col, col + columns)
            for copy in wide_copies[index]:
                copy.wait()
            ups = matmul(small[:, :rank], up_buf[:, here])
            scales = [gain_buf[at, :, here].astype(jnp.float32) for at in range(2)]
            if first:
                downs = matmul(small[:, 3 * rank : 4 * rank], dn_buf[here, :], TRANS_RHS)
            for source in range(sources):
                at = slice(source * rows, (source + 1) * rows)
                wide = sliced(source, 0, here).astype(jnp.float32)
                grad_in = sliced(source, 1, here)
                middle = (wide + ups[at]).astype(jnp.bfloat16).astype(jnp.float32)
                inverse = moment(at, 3)
                normed = (middle - moment(at, 2)) * inverse
                if first:
                    entered = (wide - moment(at, 0)) * moment(at, 1)
                    lows[index, at] = (entered * scales[0]).astype(jnp.bfloat16)
                    d_norm = downs[at] * scales[1]
                    grads[index, at] = (
                        grad_in.astype(jnp.float32)
                        + inverse * (d_norm - moment(at, 4) - normed * moment(at, 5))
                    ).astype(jnp.bfloat16)
                else:
                    lows[index, at] = (normed * scales[1]).astype(jnp.bfloat16)
                    grads[index, at] = grad_in
            dn_out[here, :] = matmul(turned[1], lows[index]).astype(jnp.bfloat16).T
            up_out[index] = matmul(turned[0], grads[index]).astype(jnp.bfloat16)
            for copy in out_copies(index, here):
                copy.start()

    def out_copies(index, here):
        return [
            pltpu.make_async_copy(
                dn_out.at[here, :], grad_dn.at[here, :], sems.at[7 + 2 * index]
            ),
            pltpu.make_async_copy(
                up_out.at[index], grad_upper.at[:, here], sems.at[8 + 2 * index]
            ),
        ]

    @pl.when(core == 0)
    def _():
        work(True)

    @pl.when(core != 0)
    def _():
        work(False)

    for index, col in enumerate(chunks):
        leaving += out_copies(index, slice(col, col + columns))
    for copy in leaving:
        copy.wait()


VMEM = pl.BlockSpec(memory_space=pltpu.VMEM)
HBM = pl.BlockSpec(memory_space=pltpu.HBM)


def call(kernel, name, grant, in_specs, outs, scratch=(), outs_in=VMEM, flops=0, moved=MIB):
    return pl.pallas_call(
        kernel,
        out_shape=tuple(jax.ShapeDtypeStruct(*out) for out in outs),
        in_specs=in_specs,
        out_specs=tuple(outs_in for _ in outs),
        scratch_shapes=list(scratch),
        compiler_params=pltpu.CompilerParams(vmem_limit_bytes=grant * MIB),
        cost_estimate=pl.CostEstimate(flops=flops, bytes_accessed=moved, transcendentals=0),
        name=name,
    )


def across(block, axis, distance):
    size = lax.axis_size(axis)
    return lax.ppermute(block, axis, [(i, i ^ distance) for i in range(size)])


def slab_route(replicas, pair, low):
    route = []
    for replica in range(replicas):
        for core in range(2):
            chip = 2 * core + ((replica & 1) ^ pair)
            route.append((2 * replica + core, 2 * chip + ((replica >> 1) ^ low)))
    return route


def on_device_two_phases(hidden_in, cotangent, cluster_ids, w_down, w_up, gain):
    experts = lax.axis_size("expert")
    replicas = lax.axis_size("dp")
    s_local, length, part = hidden_in.shape
    width = 2 * part
    capacity = 2 * s_local // experts
    slots = experts * capacity
    groups = 2 * experts
    rows = slots * length // groups
    tokens = experts * rows
    own = (w_down[0, 0], w_up[0, 0], gain[0])
    rank = own[0].shape[1]
    slab = width // replicas
    bf16, f32 = jnp.bfloat16, jnp.float32
    sizes = (length, capacity, slots)
    sections = ("expert", "segment")

    other = tuple(across(array, "segment", 1) for array in own)
    half = s_local * length // 2
    (send,) = call(
        functools.partial(pack_kernel, *sizes),
        "pack",
        60,
        [HBM] * 3,
        [((groups, 2, rows, part), bf16)],
        [
            pltpu.SMEM(cluster_ids.shape, jnp.int32),
            pltpu.VMEM((2,) + hidden_in.shape, bf16),
            pltpu.VMEM((groups, 2, rows, part), bf16),
            pltpu.SemaphoreType.DMA((5,)),
        ],
        outs_in=HBM,
    )(cluster_ids, hidden_in, cotangent)
    slabs = call(
        functools.partial(slab_kernel, *sizes),
        "slabs",
        60,
        [HBM] * 4,
        [((2 * half + 16, slab), bf16)] * 4,
        [
            pltpu.SMEM(cluster_ids.shape, jnp.int32),
            pltpu.VMEM((2,) + hidden_in.shape, bf16),
            pltpu.VMEM((2, 2 * half, part), bf16),
            pltpu.VMEM((2, 16, 128), bf16),
            pltpu.VMEM((4, 2 * half + 16, slab), bf16),
            pltpu.SemaphoreType.DMA((7,)),
        ],
        outs_in=HBM,
    )(cluster_ids, hidden_in, cotangent, send)
    recv = lax.all_to_all(send, sections, split_axis=0, concat_axis=0, tiled=True)
    recv = recv.reshape(experts, 2, 2, rows, part)
    slabs = [
        lax.ppermute(block, ("dp", "segment"), slab_route(replicas, turn // 2, turn % 2))
        for turn, block in enumerate(slabs)
    ]
    out, small = call(
        chain_kernel,
        "chain",
        50,
        [HBM] * 7,
        [((experts, 2, rows, part), bf16), ((tokens, 4 * rank + 128), bf16)],
        [
            pltpu.VMEM(recv.shape, bf16),
            pltpu.VMEM((2, width, rank), bf16),
            pltpu.VMEM((2, rank, width), bf16),
            pltpu.VMEM((2, 1, width), bf16),
            pltpu.VMEM((tokens, width), bf16),
            pltpu.VMEM((tokens, width), bf16),
            pltpu.VMEM((tokens, width), f32),
            pltpu.SemaphoreType.DMA((3, 3)),
        ],
        flops=7 * 2 * tokens * width * rank,
        moved=10 * MIB,
    )(recv, *own, *other)
    slices = call(
        functools.partial(repack_kernel, length, capacity),
        "repack",
        16,
        [VMEM] * 4 + [HBM],
        [((2, replicas, rows, slab), bf16)] * experts,
    )(*slabs, small)
    mine = [slices[0]] + [across(slices[step], "expert", step) for step in range(1, experts)]
    theirs = [across(block, "segment", 1) for block in mine]
    near = [small] + [across(small, "dp", step) for step in range(1, replicas)]
    near[:2] = lax.optimization_barrier(tuple(near[:2]))
    smalls = near + [across(piece, "segment", 1) for piece in near]

    back = lax.all_to_all(
        out.reshape(groups, rows, part), sections, split_axis=0, concat_axis=0, tiled=True
    )

    sources = 2 * replicas
    all_tokens = sources * tokens
    out_hidden, grad_dn, grad_upper = call(
        functools.partial(gradient_kernel, experts, sources, sizes),
        "gradients",
        60,
        [HBM] * (2 * experts + sources + 8),
        [(hidden_in.shape, bf16), ((slab, rank), bf16), ((rank, slab), bf16)],
        [
            pltpu.SMEM(cluster_ids.shape, jnp.int32),
            pltpu.VMEM(back.shape, bf16),
            pltpu.VMEM(hidden_in.shape, bf16),
            pltpu.VMEM((slab, rank), bf16),
            pltpu.VMEM((rank, slab), bf16),
            pltpu.VMEM((2, 1, slab), bf16),
            pltpu.VMEM((2 * experts, 2, replicas, rows, slab), bf16),
            pltpu.VMEM((all_tokens, 4 * rank + 128), bf16),
            pltpu.VMEM((all_tokens, 6 * 128), f32),
            pltpu.VMEM((2, rank, all_tokens), bf16),
            pltpu.VMEM((slab // 256, all_tokens, 256), bf16),
            pltpu.VMEM((slab // 256, all_tokens, 256), bf16),
            pltpu.VMEM((slab, rank), bf16),
            pltpu.VMEM((slab // 256, rank, 256), bf16),
            pltpu.SemaphoreType.DMA((sources,)),
            pltpu.SemaphoreType.DMA((slab // 256, 2 * experts)),
            pltpu.SemaphoreType.DMA((7 + 2 * (slab // 256),)),
        ],
        outs_in=HBM,
    )(*mine, *theirs, *smalls, *own, *other, cluster_ids, back)
    return (out_hidden, grad_dn[None, None], grad_upper[None, None])


def solution(mesh):
    two = dict(mesh.shape) == {"expert": 4, "dp": 4, "segment": 2}
    on_device = on_device_two_phases if two else on_device_pipelined
    return jax.shard_map(
        on_device,
        mesh=mesh,
        in_specs=(
            P(("expert", "dp"), None, "segment"),
            P(("expert", "dp"), None, "segment"),
            P(("expert", "dp")),
            P("expert", "segment", None, None),
            P("expert", "segment", None, None),
            P("expert", "segment", None),
        ),
        out_specs=(
            P(("expert", "dp"), None, "segment"),
            P("expert", "segment", "dp", None),
            P("expert", "segment", None, "dp"),
        ),
        check_vma=False,
    )
```

```python
import functools

import jax
import jax.numpy as jnp
from jax import lax
from jax.experimental import pallas as pl
from jax.experimental.pallas import tpu as pltpu
from jax.sharding import PartitionSpec as P

MICRO = 4


EPS = 1e-05
C_ZERO = 0.7978845608028654
C_ONE = 0.044715


def shifted(block, axis, distance):
    devices = range(lax.axis_size(axis))
    route = [(i - distance, i) for i in devices if i - distance in devices]
    return lax.ppermute(block, axis, route)


def from_root(block, axis, holder):
    block = jnp.where(lax.axis_index(axis) == holder, block, jnp.zeros_like(block))
    return lax.psum(block, axis)


def gelu_value(z):
    return 0.5 * z * (1.0 + jnp.tanh(C_ZERO * (z + C_ONE * z * z * z)))


def gelu_slope(z):
    tval = jnp.tanh(C_ZERO * (z + C_ONE * z * z * z))
    return 0.5 * (1.0 + tval) + 0.5 * z * (1.0 - tval * tval) * C_ZERO * (1.0 + 3.0 * C_ONE * z * z)


def normalize(hidden):
    wide = hidden.astype(jnp.float32)
    center = wide - jnp.mean(wide, axis=-1, keepdims=True)
    inverse = lax.rsqrt(jnp.mean(center * center, axis=-1, keepdims=True) + EPS)
    return (wide, center * inverse, inverse)


def phase_forward(hidden, w_dn, w_upper, scale):
    wide, normed, inverse = normalize(hidden)
    lowered = (normed * scale).astype(jnp.bfloat16)
    pre = jnp.dot(lowered, w_dn, preferred_element_type=jnp.float32)
    act = gelu_value(pre).astype(jnp.bfloat16)
    leaving = (wide + jnp.dot(act, w_upper, preferred_element_type=jnp.float32)).astype(
        jnp.bfloat16
    )
    return (leaving, pre)


def phase_backward(hidden, grad_in, pre, w_dn, w_upper, scale):
    wide, normed, inverse = normalize(hidden)
    lowered = (normed * scale).astype(jnp.bfloat16)
    act = gelu_value(pre).astype(jnp.bfloat16)
    d_act = jnp.dot(grad_in, w_upper.T, preferred_element_type=jnp.float32)
    d_pre = (d_act * gelu_slope(pre)).astype(jnp.bfloat16)
    d_low = jnp.dot(d_pre, w_dn.T, preferred_element_type=jnp.float32)
    d_norm = d_low * scale
    d_wide = inverse * (
        d_norm
        - jnp.mean(d_norm, axis=-1, keepdims=True)
        - normed * jnp.mean(d_norm * normed, axis=-1, keepdims=True)
    )
    grad_out = (grad_in.astype(jnp.float32) + d_wide).astype(jnp.bfloat16)
    return (grad_out, lowered, act, d_pre)


def put_slot(buffer, value, slot, valid):
    old_value = lax.dynamic_index_in_dim(buffer, slot, 0, keepdims=False)
    return lax.dynamic_update_index_in_dim(buffer, jnp.where(valid, value, old_value), slot, 0)


def on_device_pipelined(hidden_in, cotangent, cluster_ids, w_down, w_up, gain):
    experts = lax.axis_size("expert")
    phases = lax.axis_size("segment")
    phase = lax.axis_index("segment")
    s_local, length, quarter = hidden_in.shape
    capacity = 2 * s_local // experts
    slots = experts * capacity
    same = (cluster_ids[:, None] == cluster_ids[None, :]).astype(jnp.int32)
    earlier = jnp.sum(jnp.tril(same, -1), axis=1)
    target = cluster_ids * capacity + earlier
    place = (jnp.arange(slots, dtype=jnp.int32)[:, None] == target[None, :]).astype(jnp.bfloat16)

    def to_slots(local):
        flat = local.reshape(s_local, -1)
        moved = jnp.dot(place, flat, preferred_element_type=jnp.float32).astype(jnp.bfloat16)
        return moved.reshape((slots,) + local.shape[1:])

    full_in, full_cot = (
        lax.all_gather(hidden_in, "segment", axis=2, tiled=True),
        lax.all_gather(cotangent, "segment", axis=2, tiled=True),
    )
    slot_in, slot_cot = (
        lax.all_to_all(to_slots(full_in), "expert", split_axis=0, concat_axis=0, tiled=True),
        lax.all_to_all(to_slots(full_cot), "expert", split_axis=0, concat_axis=0, tiled=True),
    )
    width = slot_in.shape[2]
    micro_rows = slots * length // MICRO
    inputs = slot_in.reshape(MICRO, micro_rows, width)
    cots = slot_cot.reshape(MICRO, micro_rows, width)
    w_dn = w_down[0, 0]
    w_upper = w_up[0, 0]
    rank = w_dn.shape[1]
    scale = gain[0, 0].astype(jnp.float32)
    ticks = MICRO + phases - 1

    def forward_tick(tick, carry):
        received, saved, pres, results = carry
        which = tick - phase
        valid = (which >= 0) & (which < MICRO)
        slot = jnp.clip(which, 0, MICRO - 1)
        first = lax.dynamic_index_in_dim(inputs, jnp.minimum(tick, MICRO - 1), 0, keepdims=False)
        entering = jnp.where(phase == 0, first, received)
        leaving, pre = phase_forward(entering, w_dn, w_upper, scale)
        saved = put_slot(saved, entering, slot, valid)
        pres = put_slot(pres, pre, slot, valid)
        results = put_slot(results, leaving, slot, valid & (phase == phases - 1))
        received = shifted(leaving, "segment", 1)
        return (received, saved, pres, results)

    start = (
        jnp.zeros((micro_rows, width), jnp.bfloat16),
        jnp.zeros((MICRO, micro_rows, width), jnp.bfloat16),
        jnp.zeros((MICRO, micro_rows, rank), jnp.float32),
        jnp.zeros((MICRO, micro_rows, width), jnp.bfloat16),
    )
    received, saved, pres, results = lax.fori_loop(0, ticks, forward_tick, start)

    def backward_tick(tick, carry):
        received, lows, acts, dpres, grads = carry
        which = tick - (phases - 1 - phase)
        valid = (which >= 0) & (which < MICRO)
        slot = jnp.clip(which, 0, MICRO - 1)
        last = lax.dynamic_index_in_dim(cots, jnp.minimum(tick, MICRO - 1), 0, keepdims=False)
        grad_in = jnp.where(phase == phases - 1, last, received)
        hidden = lax.dynamic_index_in_dim(saved, slot, 0, keepdims=False)
        pre = lax.dynamic_index_in_dim(pres, slot, 0, keepdims=False)
        grad_out, lowered, act, d_pre = phase_backward(hidden, grad_in, pre, w_dn, w_upper, scale)
        lows = put_slot(lows, lowered, slot, valid)
        acts = put_slot(acts, act, slot, valid)
        dpres = put_slot(dpres, d_pre, slot, valid)
        grads = put_slot(grads, grad_in, slot, valid)
        received = shifted(grad_out, "segment", -1)
        return (received, lows, acts, dpres, grads)

    start_back = (
        jnp.zeros((micro_rows, width), jnp.bfloat16),
        jnp.zeros((MICRO, micro_rows, width), jnp.bfloat16),
        jnp.zeros((MICRO, micro_rows, rank), jnp.bfloat16),
        jnp.zeros((MICRO, micro_rows, rank), jnp.bfloat16),
        jnp.zeros((MICRO, micro_rows, width), jnp.bfloat16),
    )
    received, lows, acts, dpres, grads = lax.fori_loop(0, ticks, backward_tick, start_back)
    contract = (((0,), (0,)), ((), ()))
    grad_dn = lax.dot_general(
        lows.reshape(-1, width),
        dpres.reshape(-1, rank),
        contract,
        preferred_element_type=jnp.float32,
    )
    grad_upper = lax.dot_general(
        acts.reshape(-1, rank),
        grads.reshape(-1, width),
        contract,
        preferred_element_type=jnp.float32,
    )
    summed_dn, summed_upper = (
        lax.psum_scatter(
            grad_dn.astype(jnp.bfloat16), "dp", scatter_dimension=0, tiled=True
        ).astype(jnp.float32),
        lax.psum_scatter(
            grad_upper.astype(jnp.bfloat16), "dp", scatter_dimension=1, tiled=True
        ).astype(jnp.float32),
    )
    returned = from_root(results, "segment", phases - 1)
    returned = returned.reshape(slots, length, width)
    own = lax.dynamic_slice_in_dim(returned, phase * quarter, quarter, 2)
    back = lax.all_to_all(own, "expert", split_axis=0, concat_axis=0, tiled=True)
    out_hidden = jnp.dot(place.T, back.reshape(slots, -1), preferred_element_type=jnp.float32)
    out_hidden = out_hidden.astype(jnp.bfloat16).reshape(s_local, length, quarter)
    return (
        out_hidden,
        summed_dn.astype(jnp.bfloat16)[None, None],
        summed_upper.astype(jnp.bfloat16)[None, None],
    )


CHUNK = 512
MIB = 1024 * 1024
TRANS_RHS = (((1,), (1,)), ((), ()))
TRANS_LHS = (((0,), (0,)), ((), ()))


def matmul(left, right, dims=(((1,), (0,)), ((), ()))):
    return lax.dot_general(left, right, dims, preferred_element_type=jnp.float32)


def spread_ids(ids, shape, length):
    lane = lax.broadcasted_iota(jnp.int32, shape, 1)
    spread = jnp.zeros(shape, jnp.int32)
    for n in range(ids.shape[0]):
        spread = jnp.where(lane // length == n, ids[n], spread)
    return spread


def ranked(ids_row, length):
    tokens = ids_row.shape[1]
    kinds = lax.broadcasted_iota(jnp.int32, (8, tokens), 0)
    member = (kinds == ids_row).astype(jnp.float32)
    at_col = lax.broadcasted_iota(jnp.int32, (tokens, tokens), 0)
    at_row = lax.broadcasted_iota(jnp.int32, (tokens, tokens), 1)
    before = (lax.rem(at_col, length) == 0) & (at_col // length < at_row // length)
    counts = matmul(member.astype(jnp.bfloat16), before.astype(jnp.float32).astype(jnp.bfloat16))
    rank = jnp.sum(member * counts, axis=0, keepdims=True)
    total = jnp.sum(member, axis=1, keepdims=True) * (1.0 / length)
    lower = jnp.sum(jnp.where(kinds < ids_row, total, 0.0), axis=0, keepdims=True)
    return rank.astype(jnp.int32), lower.astype(jnp.int32)


def one_hot(target, rows):
    wanted = lax.broadcasted_iota(jnp.int32, (rows, target.shape[1]), 0)
    return (wanted == target).astype(jnp.float32).astype(jnp.bfloat16)


def placements(ids_row, length, capacity, slots):
    rank, lower = ranked(ids_row, length)
    token = lax.rem(lax.broadcasted_iota(jnp.int32, ids_row.shape, 1), length)
    place = rank + lower
    group = lax.rem(place, 2)
    per_core = capacity // 2
    packed = ((ids_row * 2 + group) * per_core + rank // 2) * length + token
    tokens = ids_row.shape[1]
    ordered = group * (tokens // 2) + (place // 2) * length + token
    return one_hot(packed, slots * length), one_hot(ordered, tokens)


def pack_kernel(length, capacity, slots, ids, hidden, cot, send, id_buf, buf, packed, sems):
    groups, _, rows, part = send.shape
    tokens = hidden.shape[0] * length
    arriving = [
        pltpu.make_async_copy(source, target, sems.at[at])
        for at, (source, target) in enumerate(
            ((ids, id_buf), (hidden, buf.at[0]), (cot, buf.at[1]))
        )
    ]
    leaving = [
        pltpu.make_async_copy(packed.at[:, at], send.at[:, at], sems.at[3 + at]) for at in range(2)
    ]
    for copy in arriving:
        copy.start()
    arriving[0].wait()
    ids_row = spread_ids(id_buf, (8, tokens), length)[:1]
    place, _ = placements(ids_row, length, capacity, slots)
    for which in range(2):
        arriving[1 + which].wait()
        moved = matmul(place, buf[which].reshape(tokens, part)).astype(jnp.bfloat16)
        for group in range(groups):
            packed[group, which] = moved[group * rows : (group + 1) * rows]
        leaving[which].start()
    for copy in leaving:
        copy.wait()


def slab_kernel(length, capacity, slots, ids, hidden, cot, _, *refs):
    slabs, refs = refs[:4], refs[4:]
    id_buf, buf, ordered, turned, out_slabs, sems = refs
    s_local, _, part = hidden.shape
    tokens = s_local * length
    slab = part // 2
    half = tokens // 2
    replica = lax.axis_index("dp")
    arriving = [
        pltpu.make_async_copy(source, target, sems.at[at])
        for at, (source, target) in enumerate(
            ((ids, id_buf), (hidden, buf.at[0]), (cot, buf.at[1]))
        )
    ]
    leaving = [
        pltpu.make_async_copy(out_slabs.at[at], slabs[at], sems.at[3 + at]) for at in range(4)
    ]
    for copy in arriving:
        copy.start()
    arriving[0].wait()
    ids_row = spread_ids(id_buf, (16, tokens), length)
    _, by_group = placements(ids_row[:1], length, capacity, slots)
    for group in range(2):
        mine = by_group[group * half : (group + 1) * half]
        clusters = matmul(ids_row.astype(jnp.float32).astype(jnp.bfloat16), mine, TRANS_RHS)
        turned[group] = jnp.concatenate(
            [clusters.astype(jnp.bfloat16), jnp.zeros((16, 128 - half), jnp.bfloat16)], axis=1
        )
    for which in range(2):
        arriving[1 + which].wait()
        flat = buf[which].reshape(tokens, part)
        ordered[which] = matmul(by_group, flat).astype(jnp.bfloat16)
    for turn in range(4):
        pair = (turn // 2) ^ (replica & 1)
        group = (turn % 2) ^ (replica >> 1)
        cols = pl.ds(pl.multiple_of(pair * slab, slab), slab)
        at = pl.ds(pl.multiple_of(group * half, half), half)
        for which in range(2):
            out_slabs[turn, which * half : (which + 1) * half] = ordered[which, at, cols]
        out_slabs[turn, tokens:] = jnp.zeros((16, slab), jnp.bfloat16)
        out_slabs[turn, tokens:, :128] = turned[group]
        leaving[turn].start()
    for copy in leaving:
        copy.wait()


def repack_kernel(length, capacity, *refs):
    slabs, outs = refs[:4], refs[5:]
    experts, rows = len(outs), outs[0].shape[2]
    half = (slabs[0].shape[0] - 16) // 2
    core, replica = lax.axis_index("segment"), lax.axis_index("dp")
    for turn, slab in enumerate(slabs):
        near = turn // 2 + 2 * ((turn % 2) ^ (replica >> 1) ^ core)
        ids_row = slab[2 * half :, :128].astype(jnp.float32)[:1, :half].astype(jnp.int32)
        rank, _ = ranked(ids_row, length)
        token = lax.rem(lax.broadcasted_iota(jnp.int32, ids_row.shape, 1), length)
        step = ids_row ^ lax.axis_index("expert")
        place = one_hot((step * (capacity // 2) + rank) * length + token, experts * rows)
        for which in range(2):
            moved = matmul(place, slab[which * half : (which + 1) * half]).astype(jnp.bfloat16)
            for e in range(experts):
                outs[e][which, near] = moved[e * rows : (e + 1) * rows]


def unpack(sizes, id_buf, back, out):
    length, capacity, slots = sizes
    groups, rows, width = back.shape
    s_local = out.shape[0]
    ids_row = spread_ids(id_buf, (8, s_local * length), length)[:1]
    place, _ = placements(ids_row, length, capacity, slots)
    moved = matmul(place, back[...].reshape(groups * rows, width), TRANS_LHS)
    out[...] = moved.astype(jnp.bfloat16).reshape(s_local, length, width)


def split_three(value):
    top = value.astype(jnp.bfloat16).astype(jnp.float32)
    mid = (value - top).astype(jnp.bfloat16).astype(jnp.float32)
    low = (value - top - mid).astype(jnp.bfloat16).astype(jnp.float32)
    return [top, mid, low]


def side_by_side(columns, tokens):
    lane = lax.broadcasted_iota(jnp.int32, (tokens, 128), 1)
    block = jnp.zeros((tokens, 128), jnp.float32)
    at = 0
    for column in columns:
        for piece in split_three(column):
            block = jnp.where(lane == at, piece, block)
            at += 1
    return block.astype(jnp.bfloat16)


def lanes(value):
    total = value[:, :128]
    for start in range(128, value.shape[1], 128):
        total = total + value[:, start : start + 128]
    return total


def row_sum(parts):
    return jnp.sum(parts, axis=1, keepdims=True)


def chain_kernel(
    recv_in, own_dn, own_up, own_gain, other_dn, other_up, other_gain,
    out, small,
    recv, dn_buf, up_buf, gain_buf, entering, middle, d_norms, sems,
):
    phase = lax.axis_index("segment")
    experts, phases, _, rows, part = recv.shape
    tokens = experts * rows
    width = phases * part
    rank = dn_buf.shape[2]
    own, other = (own_dn, own_up, own_gain), (other_dn, other_up, other_gain)

    def copies(sources, at):
        return [
            pltpu.make_async_copy(source, buffer.at[at], sems.at[at, which])
            for which, (source, buffer) in enumerate(zip(sources, (dn_buf, up_buf, gain_buf)))
        ]

    def fetch(at):
        for this in range(2):

            @pl.when(phase == this)
            def _():
                for copy in copies(own if at == this else other, at):
                    copy.start()

    arriving = [
        pltpu.make_async_copy(recv_in.at[:, :, at], recv.at[:, :, at], sems.at[2, at])
        for at in range(2)
    ]
    arriving[0].start()
    fetch(0)
    waits = [copies(own, at) for at in range(2)]
    cols = range(0, width, CHUNK)

    def block(which, col):
        half, start = col // part, col % part
        return jnp.concatenate(
            [recv[e, half, which, :, start : start + CHUNK] for e in range(experts)], axis=0
        )

    def inverse_of(ref, mean):
        total = jnp.zeros((tokens, 128), jnp.float32)
        for col in cols:
            center = ref[:, col : col + CHUNK].astype(jnp.float32) - mean
            total = total + lanes(center * center)
        return lax.rsqrt(row_sum(total) / width + EPS)

    def down(ref, mean, inverse, at):
        pre = jnp.zeros((tokens, rank), jnp.float32)
        for col in cols:
            here = slice(col, col + CHUNK)
            normed = (ref[:, here].astype(jnp.float32) - mean) * inverse
            lowered = (normed * gain_buf[at, :, here].astype(jnp.float32)).astype(jnp.bfloat16)
            pre = pre + matmul(lowered, dn_buf[at, here, :])
        return pre

    total = jnp.zeros((tokens, 128), jnp.float32)
    arriving[0].wait()
    for col in cols:
        value = block(0, col)
        entering[:, col : col + CHUNK] = value
        total = total + lanes(value.astype(jnp.float32))
    mean_0 = row_sum(total) / width
    inverse_0 = inverse_of(entering, mean_0)
    waits[0][0].wait()
    waits[0][2].wait()
    arriving[1].start()
    fetch(1)
    pre_0 = down(entering, mean_0, inverse_0, 0)
    act_0 = gelu_value(pre_0).astype(jnp.bfloat16)
    slope_0 = gelu_slope(pre_0)

    waits[0][1].wait()
    total = jnp.zeros((tokens, 128), jnp.float32)
    for col in cols:
        here = slice(col, col + CHUNK)
        value = entering[:, here].astype(jnp.float32) + matmul(act_0, up_buf[0, :, here])
        value = value.astype(jnp.bfloat16)
        middle[:, here] = value
        total = total + lanes(value.astype(jnp.float32))
    mean_1 = row_sum(total) / width
    inverse_1 = inverse_of(middle, mean_1)
    for copy in waits[1] + arriving[1:]:
        copy.wait()
    d_act = jnp.zeros((tokens, rank), jnp.float32)
    for col in cols:
        d_act = d_act + matmul(block(1, col), up_buf[1, :, col : col + CHUNK], TRANS_RHS)
    pre_1 = down(middle, mean_1, inverse_1, 1)
    act_1 = gelu_value(pre_1).astype(jnp.bfloat16)
    d_pre_1 = (d_act * gelu_slope(pre_1)).astype(jnp.bfloat16)

    total = jnp.zeros((tokens, 128), jnp.float32)
    cross = jnp.zeros((tokens, 128), jnp.float32)
    for col in cols:
        here = slice(col, col + CHUNK)
        wide = middle[:, here].astype(jnp.float32)
        d_norm = matmul(d_pre_1, dn_buf[1, here, :], TRANS_RHS)
        d_norm = d_norm * gain_buf[1, :, here].astype(jnp.float32)
        d_norms[:, here] = d_norm
        total = total + lanes(d_norm)
        cross = cross + lanes(d_norm * ((wide - mean_1) * inverse_1))
        leaving = (wide + matmul(act_1, up_buf[1, :, here])).astype(jnp.bfloat16)
        half, start = col // part, col % part
        for e in range(experts):
            out[e, half, :, start : start + CHUNK] = leaving[e * rows : (e + 1) * rows]
    shift = row_sum(total) / width
    along = row_sum(cross) / width
    d_act = jnp.zeros((tokens, rank), jnp.float32)
    for col in cols:
        here = slice(col, col + CHUNK)
        normed = (middle[:, here].astype(jnp.float32) - mean_1) * inverse_1
        grad = block(1, col).astype(jnp.float32) + inverse_1 * (
            d_norms[:, here] - shift - normed * along
        )
        d_act = d_act + matmul(grad.astype(jnp.bfloat16), up_buf[0, :, here], TRANS_RHS)
    d_pre_0 = (d_act * slope_0).astype(jnp.bfloat16)
    moments = (mean_0, inverse_0, mean_1, inverse_1, shift, along)
    kept = (act_0, act_1, d_pre_0, d_pre_1, side_by_side(moments, tokens))
    for e in range(experts):
        start = pl.multiple_of((e ^ lax.axis_index("expert")) * rows, rows)
        for at, value in enumerate(kept):
            cols = slice(at * rank, at * rank + value.shape[1])
            small[pl.ds(start, rows), cols] = value[e * rows : (e + 1) * rows]


def gradient_kernel(experts, sources, sizes, *refs):
    sides, refs = refs[: 2 * experts], refs[2 * experts :]
    smalls, refs = refs[:sources], refs[sources:]
    own, other, refs = refs[:3], refs[3:6], refs[6:]
    ids, back_in, out_hidden, grad_dn, grad_upper = refs[:5]
    (id_buf, back, result, dn_buf, up_buf, gain_buf, wide_buf, small, moments, turned, lows, grads,
     dn_out, up_out, small_sems, wide_sems, sems) = refs[5:]
    core = lax.axis_index("segment")
    place = lax.axis_index("dp")
    rows, slab = smalls[0].shape[0], sides[0].shape[3]
    replicas = sources // 2
    rank = dn_buf.shape[1]
    columns = 256
    chunks = range(0, slab, columns)
    features = pl.ds(pl.multiple_of(place * slab, slab), slab)

    def weight_copies(up, gain_first, dn, gain_second):
        moves = (
            (up.at[:, features], up_buf),
            (gain_first.at[:, features], gain_buf.at[0]),
            (gain_second.at[:, features], gain_buf.at[1]),
            (dn.at[features, :], dn_buf),
        )
        return [
            pltpu.make_async_copy(source, target, sems.at[at])
            for at, (source, target) in enumerate(moves)
        ]

    early = [
        pltpu.make_async_copy(ids, id_buf, sems.at[4]),
        pltpu.make_async_copy(back_in, back, sems.at[5]),
    ]
    small_copies = [
        pltpu.make_async_copy(
            source, small.at[at * rows : (at + 1) * rows], small_sems.at[at]
        )
        for at, source in enumerate(smalls)
    ]
    wide_copies = [
        [
            pltpu.make_async_copy(
                side.at[:, :, :, col : col + columns],
                wide_buf.at[at, :, :, :, col : col + columns],
                wide_sems.at[col // columns, at],
            )
            for at, side in enumerate(sides)
        ]
        for col in chunks
    ]
    for copy in early + small_copies:
        copy.start()

    @pl.when(core == 0)
    def _():
        for copy in weight_copies(own[1], own[2], other[0], other[2]):
            copy.start()

    @pl.when(core != 0)
    def _():
        for copy in weight_copies(other[1], other[2], own[0], own[2]):
            copy.start()

    for copies in wide_copies:
        for copy in copies:
            copy.start()
    for copy in early:
        copy.wait()
    unpack(sizes, id_buf, back, result)
    leaving = [pltpu.make_async_copy(result, out_hidden, sems.at[6])]
    leaving[0].start()
    for copy in small_copies + weight_copies(own[1], own[2], other[0], other[2]):
        copy.wait()

    def sliced(source, which, here):
        first, near = (source // replicas) * experts, source % replicas
        return jnp.concatenate(
            [wide_buf[first + step, which, near, :, here] for step in range(experts)], axis=0
        )

    def moment(at, index):
        value = moments[at, index * 128 : (index + 1) * 128]
        return jnp.concatenate([value] * (columns // 128), axis=1)

    def work(first):
        held = lax.broadcasted_iota(jnp.int32, (128, 6 * 128), 0)
        wanted = lax.broadcasted_iota(jnp.int32, (128, 6 * 128), 1) // 128
        adds = (held // 3 == wanted).astype(jnp.float32).astype(jnp.bfloat16)
        moments[...] = matmul(small[:, 4 * rank :], adds)
        act, d_pre = (0, 2) if first else (1, 3)
        turned[0] = small[:, act * rank : (act + 1) * rank].T
        turned[1] = small[:, d_pre * rank : (d_pre + 1) * rank].T
        for index, col in enumerate(chunks):
            here = slice(col, col + columns)
            for copy in wide_copies[index]:
                copy.wait()
            ups = matmul(small[:, :rank], up_buf[:, here])
            scales = [gain_buf[at, :, here].astype(jnp.float32) for at in range(2)]
            if first:
                downs = matmul(small[:, 3 * rank : 4 * rank], dn_buf[here, :], TRANS_RHS)
            for source in range(sources):
                at = slice(source * rows, (source + 1) * rows)
                wide = sliced(source, 0, here).astype(jnp.float32)
                grad_in = sliced(source, 1, here)
                middle = (wide + ups[at]).astype(jnp.bfloat16).astype(jnp.float32)
                inverse = moment(at, 3)
                normed = (middle - moment(at, 2)) * inverse
                if first:
                    entered = (wide - moment(at, 0)) * moment(at, 1)
                    lows[index, at] = (entered * scales[0]).astype(jnp.bfloat16)
                    d_norm = downs[at] * scales[1]
                    grads[index, at] = (
                        grad_in.astype(jnp.float32)
                        + inverse * (d_norm - moment(at, 4) - normed * moment(at, 5))
                    ).astype(jnp.bfloat16)
                else:
                    lows[index, at] = (normed * scales[1]).astype(jnp.bfloat16)
                    grads[index, at] = grad_in
            dn_out[here, :] = matmul(turned[1], lows[index]).astype(jnp.bfloat16).T
            up_out[index] = matmul(turned[0], grads[index]).astype(jnp.bfloat16)
            for copy in out_copies(index, here):
                copy.start()

    def out_copies(index, here):
        return [
            pltpu.make_async_copy(
                dn_out.at[here, :], grad_dn.at[here, :], sems.at[7 + 2 * index]
            ),
            pltpu.make_async_copy(
                up_out.at[index], grad_upper.at[:, here], sems.at[8 + 2 * index]
            ),
        ]

    @pl.when(core == 0)
    def _():
        work(True)

    @pl.when(core != 0)
    def _():
        work(False)

    for index, col in enumerate(chunks):
        leaving += out_copies(index, slice(col, col + columns))
    for copy in leaving:
        copy.wait()


VMEM = pl.BlockSpec(memory_space=pltpu.VMEM)
HBM = pl.BlockSpec(memory_space=pltpu.HBM)


def call(kernel, name, grant, in_specs, outs, scratch=(), outs_in=VMEM, flops=0, moved=MIB):
    return pl.pallas_call(
        kernel,
        out_shape=tuple(jax.ShapeDtypeStruct(*out) for out in outs),
        in_specs=in_specs,
        out_specs=tuple(outs_in for _ in outs),
        scratch_shapes=list(scratch),
        compiler_params=pltpu.CompilerParams(vmem_limit_bytes=grant * MIB),
        cost_estimate=pl.CostEstimate(flops=flops, bytes_accessed=moved, transcendentals=0),
        name=name,
    )


def across(block, axis, distance):
    size = lax.axis_size(axis)
    return lax.ppermute(block, axis, [(i, i ^ distance) for i in range(size)])


def slab_route(replicas, pair, low):
    route = []
    for replica in range(replicas):
        for core in range(2):
            chip = 2 * core + ((replica & 1) ^ pair)
            route.append((2 * replica + core, 2 * chip + ((replica >> 1) ^ low)))
    return route


def on_device_two_phases(hidden_in, cotangent, cluster_ids, w_down, w_up, gain):
    experts = lax.axis_size("expert")
    replicas = lax.axis_size("dp")
    s_local, length, part = hidden_in.shape
    width = 2 * part
    capacity = 2 * s_local // experts
    slots = experts * capacity
    groups = 2 * experts
    rows = slots * length // groups
    tokens = experts * rows
    own = (w_down[0, 0], w_up[0, 0], gain[0])
    rank = own[0].shape[1]
    slab = width // replicas
    bf16, f32 = jnp.bfloat16, jnp.float32
    sizes = (length, capacity, slots)
    sections = ("expert", "segment")

    other = tuple(across(array, "segment", 1) for array in own)
    half = s_local * length // 2
    (send,) = call(
        functools.partial(pack_kernel, *sizes),
        "pack",
        60,
        [HBM] * 3,
        [((groups, 2, rows, part), bf16)],
        [
            pltpu.SMEM(cluster_ids.shape, jnp.int32),
            pltpu.VMEM((2,) + hidden_in.shape, bf16),
            pltpu.VMEM((groups, 2, rows, part), bf16),
            pltpu.SemaphoreType.DMA((5,)),
        ],
        outs_in=HBM,
    )(cluster_ids, hidden_in, cotangent)
    slabs = call(
        functools.partial(slab_kernel, *sizes),
        "slabs",
        60,
        [HBM] * 4,
        [((2 * half + 16, slab), bf16)] * 4,
        [
            pltpu.SMEM(cluster_ids.shape, jnp.int32),
            pltpu.VMEM((2,) + hidden_in.shape, bf16),
            pltpu.VMEM((2, 2 * half, part), bf16),
            pltpu.VMEM((2, 16, 128), bf16),
            pltpu.VMEM((4, 2 * half + 16, slab), bf16),
            pltpu.SemaphoreType.DMA((7,)),
        ],
        outs_in=HBM,
    )(cluster_ids, hidden_in, cotangent, send)
    recv = lax.all_to_all(send, sections, split_axis=0, concat_axis=0, tiled=True)
    recv = recv.reshape(experts, 2, 2, rows, part)
    slabs = [
        lax.ppermute(block, ("dp", "segment"), slab_route(replicas, turn // 2, turn % 2))
        for turn, block in enumerate(slabs)
    ]
    out, small = call(
        chain_kernel,
        "chain",
        50,
        [HBM] * 7,
        [((experts, 2, rows, part), bf16), ((tokens, 4 * rank + 128), bf16)],
        [
            pltpu.VMEM(recv.shape, bf16),
            pltpu.VMEM((2, width, rank), bf16),
            pltpu.VMEM((2, rank, width), bf16),
            pltpu.VMEM((2, 1, width), bf16),
            pltpu.VMEM((tokens, width), bf16),
            pltpu.VMEM((tokens, width), bf16),
            pltpu.VMEM((tokens, width), f32),
            pltpu.SemaphoreType.DMA((3, 3)),
        ],
        flops=7 * 2 * tokens * width * rank,
        moved=10 * MIB,
    )(recv, *own, *other)
    slices = call(
        functools.partial(repack_kernel, length, capacity),
        "repack",
        16,
        [VMEM] * 4 + [HBM],
        [((2, replicas, rows, slab), bf16)] * experts,
    )(*slabs, small)
    mine = [slices[0]] + [across(slices[step], "expert", step) for step in range(1, experts)]
    mine[:2] = lax.optimization_barrier(tuple(mine[:2]))
    theirs = [across(block, "segment", 1) for block in mine]
    near = [small] + [across(small, "dp", step) for step in range(1, replicas)]
    near[:2] = lax.optimization_barrier(tuple(near[:2]))
    smalls = near + [across(piece, "segment", 1) for piece in near]

    back = lax.all_to_all(
        out.reshape(groups, rows, part), sections, split_axis=0, concat_axis=0, tiled=True
    )

    sources = 2 * replicas
    all_tokens = sources * tokens
    out_hidden, grad_dn, grad_upper = call(
        functools.partial(gradient_kernel, experts, sources, sizes),
        "gradients",
        60,
        [HBM] * (2 * experts + sources + 8),
        [(hidden_in.shape, bf16), ((slab, rank), bf16), ((rank, slab), bf16)],
        [
            pltpu.SMEM(cluster_ids.shape, jnp.int32),
            pltpu.VMEM(back.shape, bf16),
            pltpu.VMEM(hidden_in.shape, bf16),
            pltpu.VMEM((slab, rank), bf16),
            pltpu.VMEM((rank, slab), bf16),
            pltpu.VMEM((2, 1, slab), bf16),
            pltpu.VMEM((2 * experts, 2, replicas, rows, slab), bf16),
            pltpu.VMEM((all_tokens, 4 * rank + 128), bf16),
            pltpu.VMEM((all_tokens, 6 * 128), f32),
            pltpu.VMEM((2, rank, all_tokens), bf16),
            pltpu.VMEM((slab // 256, all_tokens, 256), bf16),
            pltpu.VMEM((slab // 256, all_tokens, 256), bf16),
            pltpu.VMEM((slab, rank), bf16),
            pltpu.VMEM((slab // 256, rank, 256), bf16),
            pltpu.SemaphoreType.DMA((sources,)),
            pltpu.SemaphoreType.DMA((slab // 256, 2 * experts)),
            pltpu.SemaphoreType.DMA((7 + 2 * (slab // 256),)),
        ],
        outs_in=HBM,
    )(*mine, *theirs, *smalls, *own, *other, cluster_ids, back)
    return (out_hidden, grad_dn[None, None], grad_upper[None, None])


def solution(mesh):
    two = dict(mesh.shape) == {"expert": 4, "dp": 4, "segment": 2}
    on_device = on_device_two_phases if two else on_device_pipelined
    return jax.shard_map(
        on_device,
        mesh=mesh,
        in_specs=(
            P(("expert", "dp"), None, "segment"),
            P(("expert", "dp"), None, "segment"),
            P(("expert", "dp")),
            P("expert", "segment", None, None),
            P("expert", "segment", None, None),
            P("expert", "segment", None),
        ),
        out_specs=(
            P(("expert", "dp"), None, "segment"),
            P("expert", "segment", "dp", None),
            P("expert", "segment", None, "dp"),
        ),
        check_vma=False,
    )
```

```python
import functools

import jax
import jax.numpy as jnp
from jax import lax
from jax.experimental import pallas as pl
from jax.experimental.pallas import tpu as pltpu
from jax.sharding import PartitionSpec as P

MICRO = 4


EPS = 1e-05
C_ZERO = 0.7978845608028654
C_ONE = 0.044715


def shifted(block, axis, distance):
    devices = range(lax.axis_size(axis))
    route = [(i - distance, i) for i in devices if i - distance in devices]
    return lax.ppermute(block, axis, route)


def from_root(block, axis, holder):
    block = jnp.where(lax.axis_index(axis) == holder, block, jnp.zeros_like(block))
    return lax.psum(block, axis)


def gelu_value(z):
    return 0.5 * z * (1.0 + jnp.tanh(C_ZERO * (z + C_ONE * z * z * z)))


def gelu_slope(z):
    tval = jnp.tanh(C_ZERO * (z + C_ONE * z * z * z))
    return 0.5 * (1.0 + tval) + 0.5 * z * (1.0 - tval * tval) * C_ZERO * (1.0 + 3.0 * C_ONE * z * z)


def normalize(hidden):
    wide = hidden.astype(jnp.float32)
    center = wide - jnp.mean(wide, axis=-1, keepdims=True)
    inverse = lax.rsqrt(jnp.mean(center * center, axis=-1, keepdims=True) + EPS)
    return (wide, center * inverse, inverse)


def phase_forward(hidden, w_dn, w_upper, scale):
    wide, normed, inverse = normalize(hidden)
    lowered = (normed * scale).astype(jnp.bfloat16)
    pre = jnp.dot(lowered, w_dn, preferred_element_type=jnp.float32)
    act = gelu_value(pre).astype(jnp.bfloat16)
    leaving = (wide + jnp.dot(act, w_upper, preferred_element_type=jnp.float32)).astype(
        jnp.bfloat16
    )
    return (leaving, pre)


def phase_backward(hidden, grad_in, pre, w_dn, w_upper, scale):
    wide, normed, inverse = normalize(hidden)
    lowered = (normed * scale).astype(jnp.bfloat16)
    act = gelu_value(pre).astype(jnp.bfloat16)
    d_act = jnp.dot(grad_in, w_upper.T, preferred_element_type=jnp.float32)
    d_pre = (d_act * gelu_slope(pre)).astype(jnp.bfloat16)
    d_low = jnp.dot(d_pre, w_dn.T, preferred_element_type=jnp.float32)
    d_norm = d_low * scale
    d_wide = inverse * (
        d_norm
        - jnp.mean(d_norm, axis=-1, keepdims=True)
        - normed * jnp.mean(d_norm * normed, axis=-1, keepdims=True)
    )
    grad_out = (grad_in.astype(jnp.float32) + d_wide).astype(jnp.bfloat16)
    return (grad_out, lowered, act, d_pre)


def put_slot(buffer, value, slot, valid):
    old_value = lax.dynamic_index_in_dim(buffer, slot, 0, keepdims=False)
    return lax.dynamic_update_index_in_dim(buffer, jnp.where(valid, value, old_value), slot, 0)


def on_device_pipelined(hidden_in, cotangent, cluster_ids, w_down, w_up, gain):
    experts = lax.axis_size("expert")
    phases = lax.axis_size("segment")
    phase = lax.axis_index("segment")
    s_local, length, quarter = hidden_in.shape
    capacity = 2 * s_local // experts
    slots = experts * capacity
    same = (cluster_ids[:, None] == cluster_ids[None, :]).astype(jnp.int32)
    earlier = jnp.sum(jnp.tril(same, -1), axis=1)
    target = cluster_ids * capacity + earlier
    place = (jnp.arange(slots, dtype=jnp.int32)[:, None] == target[None, :]).astype(jnp.bfloat16)

    def to_slots(local):
        flat = local.reshape(s_local, -1)
        moved = jnp.dot(place, flat, preferred_element_type=jnp.float32).astype(jnp.bfloat16)
        return moved.reshape((slots,) + local.shape[1:])

    full_in, full_cot = (
        lax.all_gather(hidden_in, "segment", axis=2, tiled=True),
        lax.all_gather(cotangent, "segment", axis=2, tiled=True),
    )
    slot_in, slot_cot = (
        lax.all_to_all(to_slots(full_in), "expert", split_axis=0, concat_axis=0, tiled=True),
        lax.all_to_all(to_slots(full_cot), "expert", split_axis=0, concat_axis=0, tiled=True),
    )
    width = slot_in.shape[2]
    micro_rows = slots * length // MICRO
    inputs = slot_in.reshape(MICRO, micro_rows, width)
    cots = slot_cot.reshape(MICRO, micro_rows, width)
    w_dn = w_down[0, 0]
    w_upper = w_up[0, 0]
    rank = w_dn.shape[1]
    scale = gain[0, 0].astype(jnp.float32)
    ticks = MICRO + phases - 1

    def forward_tick(tick, carry):
        received, saved, pres, results = carry
        which = tick - phase
        valid = (which >= 0) & (which < MICRO)
        slot = jnp.clip(which, 0, MICRO - 1)
        first = lax.dynamic_index_in_dim(inputs, jnp.minimum(tick, MICRO - 1), 0, keepdims=False)
        entering = jnp.where(phase == 0, first, received)
        leaving, pre = phase_forward(entering, w_dn, w_upper, scale)
        saved = put_slot(saved, entering, slot, valid)
        pres = put_slot(pres, pre, slot, valid)
        results = put_slot(results, leaving, slot, valid & (phase == phases - 1))
        received = shifted(leaving, "segment", 1)
        return (received, saved, pres, results)

    start = (
        jnp.zeros((micro_rows, width), jnp.bfloat16),
        jnp.zeros((MICRO, micro_rows, width), jnp.bfloat16),
        jnp.zeros((MICRO, micro_rows, rank), jnp.float32),
        jnp.zeros((MICRO, micro_rows, width), jnp.bfloat16),
    )
    received, saved, pres, results = lax.fori_loop(0, ticks, forward_tick, start)

    def backward_tick(tick, carry):
        received, lows, acts, dpres, grads = carry
        which = tick - (phases - 1 - phase)
        valid = (which >= 0) & (which < MICRO)
        slot = jnp.clip(which, 0, MICRO - 1)
        last = lax.dynamic_index_in_dim(cots, jnp.minimum(tick, MICRO - 1), 0, keepdims=False)
        grad_in = jnp.where(phase == phases - 1, last, received)
        hidden = lax.dynamic_index_in_dim(saved, slot, 0, keepdims=False)
        pre = lax.dynamic_index_in_dim(pres, slot, 0, keepdims=False)
        grad_out, lowered, act, d_pre = phase_backward(hidden, grad_in, pre, w_dn, w_upper, scale)
        lows = put_slot(lows, lowered, slot, valid)
        acts = put_slot(acts, act, slot, valid)
        dpres = put_slot(dpres, d_pre, slot, valid)
        grads = put_slot(grads, grad_in, slot, valid)
        received = shifted(grad_out, "segment", -1)
        return (received, lows, acts, dpres, grads)

    start_back = (
        jnp.zeros((micro_rows, width), jnp.bfloat16),
        jnp.zeros((MICRO, micro_rows, width), jnp.bfloat16),
        jnp.zeros((MICRO, micro_rows, rank), jnp.bfloat16),
        jnp.zeros((MICRO, micro_rows, rank), jnp.bfloat16),
        jnp.zeros((MICRO, micro_rows, width), jnp.bfloat16),
    )
    received, lows, acts, dpres, grads = lax.fori_loop(0, ticks, backward_tick, start_back)
    contract = (((0,), (0,)), ((), ()))
    grad_dn = lax.dot_general(
        lows.reshape(-1, width),
        dpres.reshape(-1, rank),
        contract,
        preferred_element_type=jnp.float32,
    )
    grad_upper = lax.dot_general(
        acts.reshape(-1, rank),
        grads.reshape(-1, width),
        contract,
        preferred_element_type=jnp.float32,
    )
    summed_dn, summed_upper = (
        lax.psum_scatter(
            grad_dn.astype(jnp.bfloat16), "dp", scatter_dimension=0, tiled=True
        ).astype(jnp.float32),
        lax.psum_scatter(
            grad_upper.astype(jnp.bfloat16), "dp", scatter_dimension=1, tiled=True
        ).astype(jnp.float32),
    )
    returned = from_root(results, "segment", phases - 1)
    returned = returned.reshape(slots, length, width)
    own = lax.dynamic_slice_in_dim(returned, phase * quarter, quarter, 2)
    back = lax.all_to_all(own, "expert", split_axis=0, concat_axis=0, tiled=True)
    out_hidden = jnp.dot(place.T, back.reshape(slots, -1), preferred_element_type=jnp.float32)
    out_hidden = out_hidden.astype(jnp.bfloat16).reshape(s_local, length, quarter)
    return (
        out_hidden,
        summed_dn.astype(jnp.bfloat16)[None, None],
        summed_upper.astype(jnp.bfloat16)[None, None],
    )


CHUNK = 512
MIB = 1024 * 1024
TRANS_RHS = (((1,), (1,)), ((), ()))
TRANS_LHS = (((0,), (0,)), ((), ()))


def matmul(left, right, dims=(((1,), (0,)), ((), ()))):
    return lax.dot_general(left, right, dims, preferred_element_type=jnp.float32)


def spread_ids(ids, shape, length):
    lane = lax.broadcasted_iota(jnp.int32, shape, 1)
    spread = jnp.zeros(shape, jnp.int32)
    for n in range(ids.shape[0]):
        spread = jnp.where(lane // length == n, ids[n], spread)
    return spread


def ranked(ids_row, length):
    tokens = ids_row.shape[1]
    kinds = lax.broadcasted_iota(jnp.int32, (8, tokens), 0)
    member = (kinds == ids_row).astype(jnp.float32)
    at_col = lax.broadcasted_iota(jnp.int32, (tokens, tokens), 0)
    at_row = lax.broadcasted_iota(jnp.int32, (tokens, tokens), 1)
    before = (lax.rem(at_col, length) == 0) & (at_col // length < at_row // length)
    counts = matmul(member.astype(jnp.bfloat16), before.astype(jnp.float32).astype(jnp.bfloat16))
    rank = jnp.sum(member * counts, axis=0, keepdims=True)
    total = jnp.sum(member, axis=1, keepdims=True) * (1.0 / length)
    lower = jnp.sum(jnp.where(kinds < ids_row, total, 0.0), axis=0, keepdims=True)
    return rank.astype(jnp.int32), lower.astype(jnp.int32)


def one_hot(target, rows):
    wanted = lax.broadcasted_iota(jnp.int32, (rows, target.shape[1]), 0)
    return (wanted == target).astype(jnp.float32).astype(jnp.bfloat16)


def placements(ids_row, length, capacity, slots):
    rank, lower = ranked(ids_row, length)
    token = lax.rem(lax.broadcasted_iota(jnp.int32, ids_row.shape, 1), length)
    place = rank + lower
    group = lax.rem(place, 2)
    per_core = capacity // 2
    packed = ((ids_row * 2 + group) * per_core + rank // 2) * length + token
    tokens = ids_row.shape[1]
    ordered = group * (tokens // 2) + (place // 2) * length + token
    return one_hot(packed, slots * length), one_hot(ordered, tokens)


def pack_kernel(length, capacity, slots, ids, hidden, cot, send, id_buf, buf, packed, sems):
    groups, _, rows, part = send.shape
    tokens = hidden.shape[0] * length
    arriving = [
        pltpu.make_async_copy(source, target, sems.at[at])
        for at, (source, target) in enumerate(
            ((ids, id_buf), (hidden, buf.at[0]), (cot, buf.at[1]))
        )
    ]
    leaving = [
        pltpu.make_async_copy(packed.at[:, at], send.at[:, at], sems.at[3 + at]) for at in range(2)
    ]
    for copy in arriving:
        copy.start()
    arriving[0].wait()
    ids_row = spread_ids(id_buf, (8, tokens), length)[:1]
    place, _ = placements(ids_row, length, capacity, slots)
    for which in range(2):
        arriving[1 + which].wait()
        moved = matmul(place, buf[which].reshape(tokens, part)).astype(jnp.bfloat16)
        for group in range(groups):
            packed[group, which] = moved[group * rows : (group + 1) * rows]
        leaving[which].start()
    for copy in leaving:
        copy.wait()


def slab_kernel(length, capacity, slots, ids, hidden, cot, _, *refs):
    slabs, refs = refs[:4], refs[4:]
    id_buf, buf, ordered, turned, out_slabs, sems = refs
    s_local, _, part = hidden.shape
    tokens = s_local * length
    slab = part // 2
    half = tokens // 2
    replica = lax.axis_index("dp")
    arriving = [
        pltpu.make_async_copy(source, target, sems.at[at])
        for at, (source, target) in enumerate(
            ((ids, id_buf), (hidden, buf.at[0]), (cot, buf.at[1]))
        )
    ]
    leaving = [
        pltpu.make_async_copy(out_slabs.at[at], slabs[at], sems.at[3 + at]) for at in range(4)
    ]
    for copy in arriving:
        copy.start()
    arriving[0].wait()
    ids_row = spread_ids(id_buf, (16, tokens), length)
    _, by_group = placements(ids_row[:1], length, capacity, slots)
    for group in range(2):
        mine = by_group[group * half : (group + 1) * half]
        clusters = matmul(ids_row.astype(jnp.float32).astype(jnp.bfloat16), mine, TRANS_RHS)
        turned[group] = jnp.concatenate(
            [clusters.astype(jnp.bfloat16), jnp.zeros((16, 128 - half), jnp.bfloat16)], axis=1
        )
    for which in range(2):
        arriving[1 + which].wait()
        flat = buf[which].reshape(tokens, part)
        ordered[which] = matmul(by_group, flat).astype(jnp.bfloat16)
    for turn in range(4):
        pair = (turn // 2) ^ (replica & 1)
        group = (turn % 2) ^ (replica >> 1)
        cols = pl.ds(pl.multiple_of(pair * slab, slab), slab)
        at = pl.ds(pl.multiple_of(group * half, half), half)
        for which in range(2):
            out_slabs[turn, which * half : (which + 1) * half] = ordered[which, at, cols]
        out_slabs[turn, tokens:] = jnp.zeros((16, slab), jnp.bfloat16)
        out_slabs[turn, tokens:, :128] = turned[group]
        leaving[turn].start()
    for copy in leaving:
        copy.wait()


def repack_kernel(length, capacity, *refs):
    slabs, recv, outs, sems = refs[:4], refs[4], refs[6:-1], refs[-1]
    kept, sent = outs[0], outs[1:]
    _, _, rows, slab = kept.shape
    experts = len(outs)
    half = (slabs[0].shape[0] - 16) // 2
    core, replica = lax.axis_index("segment"), lax.axis_index("dp")
    expert = lax.axis_index("expert")
    per_part = recv.shape[4] // slab
    part = replica // per_part
    cols = pl.ds(pl.multiple_of((replica - part * per_part) * slab, slab), slab)
    cuts = [
        pltpu.make_async_copy(
            recv.at[e, part, :, :, cols], kept.at[:, 3 + (e ^ expert)], sems.at[e]
        )
        for e in range(experts)
    ]
    for cut in cuts:
        cut.start()
    far_low = (replica >> 1) ^ core ^ 1

    def place_rows(held, near):
        ids_row = held[2 * half :, :128].astype(jnp.float32)[:1, :half].astype(jnp.int32)
        rank, _ = ranked(ids_row, length)
        token = lax.rem(lax.broadcasted_iota(jnp.int32, ids_row.shape, 1), length)
        step = ids_row ^ expert
        place = one_hot((step * (capacity // 2) + rank) * length + token, experts * rows)
        for which in range(2):
            moved = matmul(place, held[which * half : (which + 1) * half]).astype(jnp.bfloat16)
            kept[which, near - 1] = moved[:rows]
            for step_at, out in enumerate(sent):
                out[which, near - 1] = moved[(step_at + 1) * rows : (step_at + 2) * rows]

    place_rows(jnp.where(far_low == 1, slabs[1][...], slabs[0][...]), 2)
    for low in range(2):
        place_rows(slabs[2 + low][...], 1 + 2 * (low ^ (replica >> 1) ^ core))
    for cut in cuts:
        cut.wait()


def unpack(sizes, id_buf, back, out):
    length, capacity, slots = sizes
    groups, rows, width = back.shape
    s_local = out.shape[0]
    ids_row = spread_ids(id_buf, (8, s_local * length), length)[:1]
    place, _ = placements(ids_row, length, capacity, slots)
    moved = matmul(place, back[...].reshape(groups * rows, width), TRANS_LHS)
    out[...] = moved.astype(jnp.bfloat16).reshape(s_local, length, width)


def split_three(value):
    top = value.astype(jnp.bfloat16).astype(jnp.float32)
    mid = (value - top).astype(jnp.bfloat16).astype(jnp.float32)
    low = (value - top - mid).astype(jnp.bfloat16).astype(jnp.float32)
    return [top, mid, low]


def side_by_side(columns, tokens):
    lane = lax.broadcasted_iota(jnp.int32, (tokens, 128), 1)
    block = jnp.zeros((tokens, 128), jnp.float32)
    at = 0
    for column in columns:
        for piece in split_three(column):
            block = jnp.where(lane == at, piece, block)
            at += 1
    return block.astype(jnp.bfloat16)


def lanes(value):
    total = value[:, :128]
    for start in range(128, value.shape[1], 128):
        total = total + value[:, start : start + 128]
    return total


def row_sum(parts):
    return jnp.sum(parts, axis=1, keepdims=True)


def chain_kernel(
    recv_in, own_dn, own_up, own_gain, other_dn, other_up, other_gain,
    out, small,
    recv, dn_buf, up_buf, gain_buf, entering, middle, d_norms, sems,
):
    phase = lax.axis_index("segment")
    experts, phases, _, rows, part = recv.shape
    tokens = experts * rows
    width = phases * part
    rank = dn_buf.shape[2]
    own, other = (own_dn, own_up, own_gain), (other_dn, other_up, other_gain)

    def copies(sources, at):
        return [
            pltpu.make_async_copy(source, buffer.at[at], sems.at[at, which])
            for which, (source, buffer) in enumerate(zip(sources, (dn_buf, up_buf, gain_buf)))
        ]

    def fetch(at):
        for this in range(2):

            @pl.when(phase == this)
            def _():
                for copy in copies(own if at == this else other, at):
                    copy.start()

    arriving = [
        pltpu.make_async_copy(recv_in.at[:, :, at], recv.at[:, :, at], sems.at[2, at])
        for at in range(2)
    ]
    arriving[0].start()
    fetch(0)
    waits = [copies(own, at) for at in range(2)]
    cols = range(0, width, CHUNK)

    def block(which, col):
        half, start = col // part, col % part
        return jnp.concatenate(
            [recv[e, half, which, :, start : start + CHUNK] for e in range(experts)], axis=0
        )

    def inverse_of(ref, mean):
        total = jnp.zeros((tokens, 128), jnp.float32)
        for col in cols:
            center = ref[:, col : col + CHUNK].astype(jnp.float32) - mean
            total = total + lanes(center * center)
        return lax.rsqrt(row_sum(total) / width + EPS)

    def down(ref, mean, inverse, at):
        pre = jnp.zeros((tokens, rank), jnp.float32)
        for col in cols:
            here = slice(col, col + CHUNK)
            normed = (ref[:, here].astype(jnp.float32) - mean) * inverse
            lowered = (normed * gain_buf[at, :, here].astype(jnp.float32)).astype(jnp.bfloat16)
            pre = pre + matmul(lowered, dn_buf[at, here, :])
        return pre

    total = jnp.zeros((tokens, 128), jnp.float32)
    arriving[0].wait()
    for col in cols:
        value = block(0, col)
        entering[:, col : col + CHUNK] = value
        total = total + lanes(value.astype(jnp.float32))
    mean_0 = row_sum(total) / width
    inverse_0 = inverse_of(entering, mean_0)
    waits[0][0].wait()
    waits[0][2].wait()
    arriving[1].start()
    fetch(1)
    pre_0 = down(entering, mean_0, inverse_0, 0)
    act_0 = gelu_value(pre_0).astype(jnp.bfloat16)
    slope_0 = gelu_slope(pre_0)

    waits[0][1].wait()
    total = jnp.zeros((tokens, 128), jnp.float32)
    for col in cols:
        here = slice(col, col + CHUNK)
        value = entering[:, here].astype(jnp.float32) + matmul(act_0, up_buf[0, :, here])
        value = value.astype(jnp.bfloat16)
        middle[:, here] = value
        total = total + lanes(value.astype(jnp.float32))
    mean_1 = row_sum(total) / width
    inverse_1 = inverse_of(middle, mean_1)
    for copy in waits[1] + arriving[1:]:
        copy.wait()
    d_act = jnp.zeros((tokens, rank), jnp.float32)
    for col in cols:
        d_act = d_act + matmul(block(1, col), up_buf[1, :, col : col + CHUNK], TRANS_RHS)
    pre_1 = down(middle, mean_1, inverse_1, 1)
    act_1 = gelu_value(pre_1).astype(jnp.bfloat16)
    d_pre_1 = (d_act * gelu_slope(pre_1)).astype(jnp.bfloat16)

    total = jnp.zeros((tokens, 128), jnp.float32)
    cross = jnp.zeros((tokens, 128), jnp.float32)
    for col in cols:
        here = slice(col, col + CHUNK)
        wide = middle[:, here].astype(jnp.float32)
        d_norm = matmul(d_pre_1, dn_buf[1, here, :], TRANS_RHS)
        d_norm = d_norm * gain_buf[1, :, here].astype(jnp.float32)
        d_norms[:, here] = d_norm
        total = total + lanes(d_norm)
        cross = cross + lanes(d_norm * ((wide - mean_1) * inverse_1))
        leaving = (wide + matmul(act_1, up_buf[1, :, here])).astype(jnp.bfloat16)
        half, start = col // part, col % part
        for e in range(experts):
            out[e, half, :, start : start + CHUNK] = leaving[e * rows : (e + 1) * rows]
    shift = row_sum(total) / width
    along = row_sum(cross) / width
    d_act = jnp.zeros((tokens, rank), jnp.float32)
    for col in cols:
        here = slice(col, col + CHUNK)
        normed = (middle[:, here].astype(jnp.float32) - mean_1) * inverse_1
        grad = block(1, col).astype(jnp.float32) + inverse_1 * (
            d_norms[:, here] - shift - normed * along
        )
        d_act = d_act + matmul(grad.astype(jnp.bfloat16), up_buf[0, :, here], TRANS_RHS)
    d_pre_0 = (d_act * slope_0).astype(jnp.bfloat16)
    moments = (mean_0, inverse_0, mean_1, inverse_1, shift, along)
    kept = (act_0, act_1, d_pre_0, d_pre_1, side_by_side(moments, tokens))
    for e in range(experts):
        start = pl.multiple_of((e ^ lax.axis_index("expert")) * rows, rows)
        for at, value in enumerate(kept):
            cols = slice(at * rank, at * rank + value.shape[1])
            small[pl.ds(start, rows), cols] = value[e * rows : (e + 1) * rows]


def gradient_kernel(experts, sources, sizes, *refs):
    sides, refs = refs[: 2 * experts], refs[2 * experts :]
    smalls, refs = refs[:sources], refs[sources:]
    own, other, refs = refs[:3], refs[3:6], refs[6:]
    ids, back_in, out_hidden, grad_dn, grad_upper = refs[:5]
    (id_buf, back, result, dn_buf, up_buf, gain_buf, wide_buf, small, moments, turned, lows, grads,
     dn_out, up_out, small_sems, wide_sems, sems) = refs[5:]
    core = lax.axis_index("segment")
    place = lax.axis_index("dp")
    rows, slab = smalls[0].shape[0], sides[0].shape[3]
    replicas = sources // 2
    blocks = [side.shape[1] for side in sides[:experts]]
    starts = [sum(blocks[:step]) for step in range(experts)]
    rank = dn_buf.shape[1]
    columns = 256
    chunks = range(0, slab, columns)
    features = pl.ds(pl.multiple_of(place * slab, slab), slab)

    def weight_copies(up, gain_first, dn, gain_second):
        moves = (
            (up.at[:, features], up_buf),
            (gain_first.at[:, features], gain_buf.at[0]),
            (gain_second.at[:, features], gain_buf.at[1]),
            (dn.at[features, :], dn_buf),
        )
        return [
            pltpu.make_async_copy(source, target, sems.at[at])
            for at, (source, target) in enumerate(moves)
        ]

    early = [
        pltpu.make_async_copy(ids, id_buf, sems.at[4]),
        pltpu.make_async_copy(back_in, back, sems.at[5]),
    ]
    small_copies = [
        pltpu.make_async_copy(
            source, small.at[at * rows : (at + 1) * rows], small_sems.at[at]
        )
        for at, source in enumerate(smalls)
    ]
    wide_copies = [
        [
            pltpu.make_async_copy(
                side.at[:, :, :, col : col + columns],
                wide_buf.at[
                    at // experts,
                    :,
                    starts[at % experts] : starts[at % experts] + blocks[at % experts],
                    :,
                    col : col + columns,
                ],
                wide_sems.at[col // columns, at],
            )
            for at, side in enumerate(sides)
        ]
        for col in chunks
    ]
    for copy in early + small_copies:
        copy.start()

    @pl.when(core == 0)
    def _():
        for copy in weight_copies(own[1], own[2], other[0], other[2]):
            copy.start()

    @pl.when(core != 0)
    def _():
        for copy in weight_copies(other[1], other[2], own[0], own[2]):
            copy.start()

    for copies in wide_copies:
        for copy in copies:
            copy.start()
    for copy in early:
        copy.wait()
    unpack(sizes, id_buf, back, result)
    leaving = [pltpu.make_async_copy(result, out_hidden, sems.at[6])]
    leaving[0].start()
    for copy in small_copies + weight_copies(own[1], own[2], other[0], other[2]):
        copy.wait()

    def sliced(source, which, here):
        side, near = source // replicas, source % replicas
        at = [
            replicas - 1 + step if near == 0 else starts[step] + near - 1
            for step in range(experts)
        ]
        return jnp.concatenate([wide_buf[side, which, one, :, here] for one in at], axis=0)

    def moment(at, index):
        value = moments[at, index * 128 : (index + 1) * 128]
        return jnp.concatenate([value] * (columns // 128), axis=1)

    def work(first):
        held = lax.broadcasted_iota(jnp.int32, (128, 6 * 128), 0)
        wanted = lax.broadcasted_iota(jnp.int32, (128, 6 * 128), 1) // 128
        adds = (held // 3 == wanted).astype(jnp.float32).astype(jnp.bfloat16)
        moments[...] = matmul(small[:, 4 * rank :], adds)
        act, d_pre = (0, 2) if first else (1, 3)
        turned[0] = small[:, act * rank : (act + 1) * rank].T
        turned[1] = small[:, d_pre * rank : (d_pre + 1) * rank].T
        for index, col in enumerate(chunks):
            here = slice(col, col + columns)
            for copy in wide_copies[index]:
                copy.wait()
            ups = matmul(small[:, :rank], up_buf[:, here])
            scales = [gain_buf[at, :, here].astype(jnp.float32) for at in range(2)]
            if first:
                downs = matmul(small[:, 3 * rank : 4 * rank], dn_buf[here, :], TRANS_RHS)
            for source in range(sources):
                at = slice(source * rows, (source + 1) * rows)
                wide = sliced(source, 0, here).astype(jnp.float32)
                grad_in = sliced(source, 1, here)
                middle = (wide + ups[at]).astype(jnp.bfloat16).astype(jnp.float32)
                inverse = moment(at, 3)
                normed = (middle - moment(at, 2)) * inverse
                if first:
                    entered = (wide - moment(at, 0)) * moment(at, 1)
                    lows[index, at] = (entered * scales[0]).astype(jnp.bfloat16)
                    d_norm = downs[at] * scales[1]
                    grads[index, at] = (
                        grad_in.astype(jnp.float32)
                        + inverse * (d_norm - moment(at, 4) - normed * moment(at, 5))
                    ).astype(jnp.bfloat16)
                else:
                    lows[index, at] = (normed * scales[1]).astype(jnp.bfloat16)
                    grads[index, at] = grad_in
            dn_out[here, :] = matmul(turned[1], lows[index]).astype(jnp.bfloat16).T
            up_out[index] = matmul(turned[0], grads[index]).astype(jnp.bfloat16)
            for copy in out_copies(index, here):
                copy.start()

    def out_copies(index, here):
        return [
            pltpu.make_async_copy(
                dn_out.at[here, :], grad_dn.at[here, :], sems.at[7 + 2 * index]
            ),
            pltpu.make_async_copy(
                up_out.at[index], grad_upper.at[:, here], sems.at[8 + 2 * index]
            ),
        ]

    @pl.when(core == 0)
    def _():
        work(True)

    @pl.when(core != 0)
    def _():
        work(False)

    for index, col in enumerate(chunks):
        leaving += out_copies(index, slice(col, col + columns))
    for copy in leaving:
        copy.wait()


VMEM = pl.BlockSpec(memory_space=pltpu.VMEM)
HBM = pl.BlockSpec(memory_space=pltpu.HBM)


def call(kernel, name, grant, in_specs, outs, scratch=(), outs_in=VMEM, flops=0, moved=MIB):
    return pl.pallas_call(
        kernel,
        out_shape=tuple(jax.ShapeDtypeStruct(*out) for out in outs),
        in_specs=in_specs,
        out_specs=tuple(outs_in for _ in outs),
        scratch_shapes=list(scratch),
        compiler_params=pltpu.CompilerParams(vmem_limit_bytes=grant * MIB),
        cost_estimate=pl.CostEstimate(flops=flops, bytes_accessed=moved, transcendentals=0),
        name=name,
    )


def across(block, axis, distance):
    size = lax.axis_size(axis)
    return lax.ppermute(block, axis, [(i, i ^ distance) for i in range(size)])


def slab_route(replicas, pair, low):
    route = []
    for replica in range(replicas):
        for core in range(2):
            chip = 2 * core + ((replica & 1) ^ pair)
            route.append((2 * replica + core, 2 * chip + ((replica >> 1) ^ low)))
    return route


def on_device_two_phases(hidden_in, cotangent, cluster_ids, w_down, w_up, gain):
    experts = lax.axis_size("expert")
    replicas = lax.axis_size("dp")
    s_local, length, part = hidden_in.shape
    width = 2 * part
    capacity = 2 * s_local // experts
    slots = experts * capacity
    groups = 2 * experts
    rows = slots * length // groups
    tokens = experts * rows
    own = (w_down[0, 0], w_up[0, 0], gain[0])
    rank = own[0].shape[1]
    slab = width // replicas
    bf16, f32 = jnp.bfloat16, jnp.float32
    sizes = (length, capacity, slots)
    sections = ("expert", "segment")

    other = tuple(across(array, "segment", 1) for array in own)
    half = s_local * length // 2
    (send,) = call(
        functools.partial(pack_kernel, *sizes),
        "pack",
        60,
        [HBM] * 3,
        [((groups, 2, rows, part), bf16)],
        [
            pltpu.SMEM(cluster_ids.shape, jnp.int32),
            pltpu.VMEM((2,) + hidden_in.shape, bf16),
            pltpu.VMEM((groups, 2, rows, part), bf16),
            pltpu.SemaphoreType.DMA((5,)),
        ],
        outs_in=HBM,
    )(cluster_ids, hidden_in, cotangent)
    slabs = call(
        functools.partial(slab_kernel, *sizes),
        "slabs",
        60,
        [HBM] * 4,
        [((2 * half + 16, slab), bf16)] * 4,
        [
            pltpu.SMEM(cluster_ids.shape, jnp.int32),
            pltpu.VMEM((2,) + hidden_in.shape, bf16),
            pltpu.VMEM((2, 2 * half, part), bf16),
            pltpu.VMEM((2, 16, 128), bf16),
            pltpu.VMEM((4, 2 * half + 16, slab), bf16),
            pltpu.SemaphoreType.DMA((7,)),
        ],
        outs_in=HBM,
    )(cluster_ids, hidden_in, cotangent, send)
    recv = lax.all_to_all(send, sections, split_axis=0, concat_axis=0, tiled=True)
    recv = recv.reshape(experts, 2, 2, rows, part)
    slabs = [
        lax.ppermute(block, ("dp", "segment"), slab_route(replicas, turn // 2, turn % 2))
        for turn, block in enumerate(slabs)
    ]
    out, small = call(
        chain_kernel,
        "chain",
        50,
        [HBM] * 7,
        [((experts, 2, rows, part), bf16), ((tokens, 4 * rank + 128), bf16)],
        [
            pltpu.VMEM(recv.shape, bf16),
            pltpu.VMEM((2, width, rank), bf16),
            pltpu.VMEM((2, rank, width), bf16),
            pltpu.VMEM((2, 1, width), bf16),
            pltpu.VMEM((tokens, width), bf16),
            pltpu.VMEM((tokens, width), bf16),
            pltpu.VMEM((tokens, width), f32),
            pltpu.SemaphoreType.DMA((3, 3)),
        ],
        flops=7 * 2 * tokens * width * rank,
        moved=10 * MIB,
    )(recv, *own, *other)
    slices = call(
        functools.partial(repack_kernel, length, capacity),
        "repack",
        16,
        [VMEM] * 4 + [HBM] * 2,
        [((2, replicas - 1 + experts, rows, slab), bf16)]
        + [((2, replicas - 1, rows, slab), bf16)] * (experts - 1),
        [pltpu.SemaphoreType.DMA((experts,))],
    )(*slabs, recv, small)
    small, *slices = lax.optimization_barrier((small, *slices))
    mine = [slices[0]] + [across(slices[step], "expert", step) for step in range(1, experts)]
    mine[:2] = lax.optimization_barrier(tuple(mine[:2]))
    theirs = [across(block, "segment", 1) for block in mine]
    near = [small] + [across(small, "dp", step) for step in range(1, replicas - 1)]
    near[:2] = lax.optimization_barrier(tuple(near[:2]))
    near.append(across(near[0], "dp", replicas - 1))
    smalls = near + [across(piece, "segment", 1) for piece in near]

    back = lax.all_to_all(
        out.reshape(groups, rows, part), sections, split_axis=0, concat_axis=0, tiled=True
    )

    sources = 2 * replicas
    all_tokens = sources * tokens
    out_hidden, grad_dn, grad_upper = call(
        functools.partial(gradient_kernel, experts, sources, sizes),
        "gradients",
        60,
        [HBM] * (2 * experts + sources + 8),
        [(hidden_in.shape, bf16), ((slab, rank), bf16), ((rank, slab), bf16)],
        [
            pltpu.SMEM(cluster_ids.shape, jnp.int32),
            pltpu.VMEM(back.shape, bf16),
            pltpu.VMEM(hidden_in.shape, bf16),
            pltpu.VMEM((slab, rank), bf16),
            pltpu.VMEM((rank, slab), bf16),
            pltpu.VMEM((2, 1, slab), bf16),
            pltpu.VMEM((2, 2, replicas * experts, rows, slab), bf16),
            pltpu.VMEM((all_tokens, 4 * rank + 128), bf16),
            pltpu.VMEM((all_tokens, 6 * 128), f32),
            pltpu.VMEM((2, rank, all_tokens), bf16),
            pltpu.VMEM((slab // 256, all_tokens, 256), bf16),
            pltpu.VMEM((slab // 256, all_tokens, 256), bf16),
            pltpu.VMEM((slab, rank), bf16),
            pltpu.VMEM((slab // 256, rank, 256), bf16),
            pltpu.SemaphoreType.DMA((sources,)),
            pltpu.SemaphoreType.DMA((slab // 256, 2 * experts)),
            pltpu.SemaphoreType.DMA((7 + 2 * (slab // 256),)),
        ],
        outs_in=HBM,
    )(*mine, *theirs, *smalls, *own, *other, cluster_ids, back)
    return (out_hidden, grad_dn[None, None], grad_upper[None, None])


def solution(mesh):
    two = dict(mesh.shape) == {"expert": 4, "dp": 4, "segment": 2}
    on_device = on_device_two_phases if two else on_device_pipelined
    return jax.shard_map(
        on_device,
        mesh=mesh,
        in_specs=(
            P(("expert", "dp"), None, "segment"),
            P(("expert", "dp"), None, "segment"),
            P(("expert", "dp")),
            P("expert", "segment", None, None),
            P("expert", "segment", None, None),
            P("expert", "segment", None),
        ),
        out_specs=(
            P(("expert", "dp"), None, "segment"),
            P("expert", "segment", "dp", None),
            P("expert", "segment", None, "dp"),
        ),
        check_vma=False,
    )
```

```python
import functools

import jax
import jax.numpy as jnp
from jax import lax
from jax.experimental import pallas as pl
from jax.experimental.pallas import tpu as pltpu
from jax.sharding import PartitionSpec as P

MICRO = 4


EPS = 1e-05
C_ZERO = 0.7978845608028654
C_ONE = 0.044715


def shifted(block, axis, distance):
    devices = range(lax.axis_size(axis))
    route = [(i - distance, i) for i in devices if i - distance in devices]
    return lax.ppermute(block, axis, route)


def from_root(block, axis, holder):
    block = jnp.where(lax.axis_index(axis) == holder, block, jnp.zeros_like(block))
    return lax.psum(block, axis)


def gelu_value(z):
    return 0.5 * z * (1.0 + jnp.tanh(C_ZERO * (z + C_ONE * z * z * z)))


def gelu_slope(z):
    tval = jnp.tanh(C_ZERO * (z + C_ONE * z * z * z))
    return 0.5 * (1.0 + tval) + 0.5 * z * (1.0 - tval * tval) * C_ZERO * (1.0 + 3.0 * C_ONE * z * z)


def normalize(hidden):
    wide = hidden.astype(jnp.float32)
    center = wide - jnp.mean(wide, axis=-1, keepdims=True)
    inverse = lax.rsqrt(jnp.mean(center * center, axis=-1, keepdims=True) + EPS)
    return (wide, center * inverse, inverse)


def phase_forward(hidden, w_dn, w_upper, scale):
    wide, normed, inverse = normalize(hidden)
    lowered = (normed * scale).astype(jnp.bfloat16)
    pre = jnp.dot(lowered, w_dn, preferred_element_type=jnp.float32)
    act = gelu_value(pre).astype(jnp.bfloat16)
    leaving = (wide + jnp.dot(act, w_upper, preferred_element_type=jnp.float32)).astype(
        jnp.bfloat16
    )
    return (leaving, pre)


def phase_backward(hidden, grad_in, pre, w_dn, w_upper, scale):
    wide, normed, inverse = normalize(hidden)
    lowered = (normed * scale).astype(jnp.bfloat16)
    act = gelu_value(pre).astype(jnp.bfloat16)
    d_act = jnp.dot(grad_in, w_upper.T, preferred_element_type=jnp.float32)
    d_pre = (d_act * gelu_slope(pre)).astype(jnp.bfloat16)
    d_low = jnp.dot(d_pre, w_dn.T, preferred_element_type=jnp.float32)
    d_norm = d_low * scale
    d_wide = inverse * (
        d_norm
        - jnp.mean(d_norm, axis=-1, keepdims=True)
        - normed * jnp.mean(d_norm * normed, axis=-1, keepdims=True)
    )
    grad_out = (grad_in.astype(jnp.float32) + d_wide).astype(jnp.bfloat16)
    return (grad_out, lowered, act, d_pre)


def put_slot(buffer, value, slot, valid):
    old_value = lax.dynamic_index_in_dim(buffer, slot, 0, keepdims=False)
    return lax.dynamic_update_index_in_dim(buffer, jnp.where(valid, value, old_value), slot, 0)


def on_device_pipelined(hidden_in, cotangent, cluster_ids, w_down, w_up, gain):
    experts = lax.axis_size("expert")
    phases = lax.axis_size("segment")
    phase = lax.axis_index("segment")
    s_local, length, quarter = hidden_in.shape
    capacity = 2 * s_local // experts
    slots = experts * capacity
    same = (cluster_ids[:, None] == cluster_ids[None, :]).astype(jnp.int32)
    earlier = jnp.sum(jnp.tril(same, -1), axis=1)
    target = cluster_ids * capacity + earlier
    place = (jnp.arange(slots, dtype=jnp.int32)[:, None] == target[None, :]).astype(jnp.bfloat16)

    def to_slots(local):
        flat = local.reshape(s_local, -1)
        moved = jnp.dot(place, flat, preferred_element_type=jnp.float32).astype(jnp.bfloat16)
        return moved.reshape((slots,) + local.shape[1:])

    full_in, full_cot = (
        lax.all_gather(hidden_in, "segment", axis=2, tiled=True),
        lax.all_gather(cotangent, "segment", axis=2, tiled=True),
    )
    slot_in, slot_cot = (
        lax.all_to_all(to_slots(full_in), "expert", split_axis=0, concat_axis=0, tiled=True),
        lax.all_to_all(to_slots(full_cot), "expert", split_axis=0, concat_axis=0, tiled=True),
    )
    width = slot_in.shape[2]
    micro_rows = slots * length // MICRO
    inputs = slot_in.reshape(MICRO, micro_rows, width)
    cots = slot_cot.reshape(MICRO, micro_rows, width)
    w_dn = w_down[0, 0]
    w_upper = w_up[0, 0]
    rank = w_dn.shape[1]
    scale = gain[0, 0].astype(jnp.float32)
    ticks = MICRO + phases - 1

    def forward_tick(tick, carry):
        received, saved, pres, results = carry
        which = tick - phase
        valid = (which >= 0) & (which < MICRO)
        slot = jnp.clip(which, 0, MICRO - 1)
        first = lax.dynamic_index_in_dim(inputs, jnp.minimum(tick, MICRO - 1), 0, keepdims=False)
        entering = jnp.where(phase == 0, first, received)
        leaving, pre = phase_forward(entering, w_dn, w_upper, scale)
        saved = put_slot(saved, entering, slot, valid)
        pres = put_slot(pres, pre, slot, valid)
        results = put_slot(results, leaving, slot, valid & (phase == phases - 1))
        received = shifted(leaving, "segment", 1)
        return (received, saved, pres, results)

    start = (
        jnp.zeros((micro_rows, width), jnp.bfloat16),
        jnp.zeros((MICRO, micro_rows, width), jnp.bfloat16),
        jnp.zeros((MICRO, micro_rows, rank), jnp.float32),
        jnp.zeros((MICRO, micro_rows, width), jnp.bfloat16),
    )
    received, saved, pres, results = lax.fori_loop(0, ticks, forward_tick, start)

    def backward_tick(tick, carry):
        received, lows, acts, dpres, grads = carry
        which = tick - (phases - 1 - phase)
        valid = (which >= 0) & (which < MICRO)
        slot = jnp.clip(which, 0, MICRO - 1)
        last = lax.dynamic_index_in_dim(cots, jnp.minimum(tick, MICRO - 1), 0, keepdims=False)
        grad_in = jnp.where(phase == phases - 1, last, received)
        hidden = lax.dynamic_index_in_dim(saved, slot, 0, keepdims=False)
        pre = lax.dynamic_index_in_dim(pres, slot, 0, keepdims=False)
        grad_out, lowered, act, d_pre = phase_backward(hidden, grad_in, pre, w_dn, w_upper, scale)
        lows = put_slot(lows, lowered, slot, valid)
        acts = put_slot(acts, act, slot, valid)
        dpres = put_slot(dpres, d_pre, slot, valid)
        grads = put_slot(grads, grad_in, slot, valid)
        received = shifted(grad_out, "segment", -1)
        return (received, lows, acts, dpres, grads)

    start_back = (
        jnp.zeros((micro_rows, width), jnp.bfloat16),
        jnp.zeros((MICRO, micro_rows, width), jnp.bfloat16),
        jnp.zeros((MICRO, micro_rows, rank), jnp.bfloat16),
        jnp.zeros((MICRO, micro_rows, rank), jnp.bfloat16),
        jnp.zeros((MICRO, micro_rows, width), jnp.bfloat16),
    )
    received, lows, acts, dpres, grads = lax.fori_loop(0, ticks, backward_tick, start_back)
    contract = (((0,), (0,)), ((), ()))
    grad_dn = lax.dot_general(
        lows.reshape(-1, width),
        dpres.reshape(-1, rank),
        contract,
        preferred_element_type=jnp.float32,
    )
    grad_upper = lax.dot_general(
        acts.reshape(-1, rank),
        grads.reshape(-1, width),
        contract,
        preferred_element_type=jnp.float32,
    )
    summed_dn, summed_upper = (
        lax.psum_scatter(
            grad_dn.astype(jnp.bfloat16), "dp", scatter_dimension=0, tiled=True
        ).astype(jnp.float32),
        lax.psum_scatter(
            grad_upper.astype(jnp.bfloat16), "dp", scatter_dimension=1, tiled=True
        ).astype(jnp.float32),
    )
    returned = from_root(results, "segment", phases - 1)
    returned = returned.reshape(slots, length, width)
    own = lax.dynamic_slice_in_dim(returned, phase * quarter, quarter, 2)
    back = lax.all_to_all(own, "expert", split_axis=0, concat_axis=0, tiled=True)
    out_hidden = jnp.dot(place.T, back.reshape(slots, -1), preferred_element_type=jnp.float32)
    out_hidden = out_hidden.astype(jnp.bfloat16).reshape(s_local, length, quarter)
    return (
        out_hidden,
        summed_dn.astype(jnp.bfloat16)[None, None],
        summed_upper.astype(jnp.bfloat16)[None, None],
    )


CHUNK = 512
MIB = 1024 * 1024
TRANS_RHS = (((1,), (1,)), ((), ()))
TRANS_LHS = (((0,), (0,)), ((), ()))


def matmul(left, right, dims=(((1,), (0,)), ((), ()))):
    return lax.dot_general(left, right, dims, preferred_element_type=jnp.float32)


def spread_ids(ids, shape, length):
    lane = lax.broadcasted_iota(jnp.int32, shape, 1)
    spread = jnp.zeros(shape, jnp.int32)
    for n in range(ids.shape[0]):
        spread = jnp.where(lane // length == n, ids[n], spread)
    return spread


def ranked(ids_row, length):
    tokens = ids_row.shape[1]
    kinds = lax.broadcasted_iota(jnp.int32, (8, tokens), 0)
    member = (kinds == ids_row).astype(jnp.float32)
    at_col = lax.broadcasted_iota(jnp.int32, (tokens, tokens), 0)
    at_row = lax.broadcasted_iota(jnp.int32, (tokens, tokens), 1)
    before = (lax.rem(at_col, length) == 0) & (at_col // length < at_row // length)
    counts = matmul(member.astype(jnp.bfloat16), before.astype(jnp.float32).astype(jnp.bfloat16))
    rank = jnp.sum(member * counts, axis=0, keepdims=True)
    total = jnp.sum(member, axis=1, keepdims=True) * (1.0 / length)
    lower = jnp.sum(jnp.where(kinds < ids_row, total, 0.0), axis=0, keepdims=True)
    return rank.astype(jnp.int32), lower.astype(jnp.int32)


def one_hot(target, rows):
    wanted = lax.broadcasted_iota(jnp.int32, (rows, target.shape[1]), 0)
    return (wanted == target).astype(jnp.float32).astype(jnp.bfloat16)


def placements(ids_row, length, capacity, slots):
    rank, lower = ranked(ids_row, length)
    token = lax.rem(lax.broadcasted_iota(jnp.int32, ids_row.shape, 1), length)
    place = rank + lower
    group = lax.rem(place, 2)
    per_core = capacity // 2
    packed = ((ids_row * 2 + group) * per_core + rank // 2) * length + token
    tokens = ids_row.shape[1]
    ordered = group * (tokens // 2) + (place // 2) * length + token
    return one_hot(packed, slots * length), one_hot(ordered, tokens)


def pack_kernel(length, capacity, slots, ids, hidden, cot, send, id_buf, buf, packed, sems):
    groups, _, rows, part = send.shape
    tokens = hidden.shape[0] * length
    arriving = [
        pltpu.make_async_copy(source, target, sems.at[at])
        for at, (source, target) in enumerate(
            ((ids, id_buf), (hidden, buf.at[0]), (cot, buf.at[1]))
        )
    ]
    leaving = [
        pltpu.make_async_copy(packed.at[:, at], send.at[:, at], sems.at[3 + at]) for at in range(2)
    ]
    for copy in arriving:
        copy.start()
    arriving[0].wait()
    ids_row = spread_ids(id_buf, (8, tokens), length)[:1]
    place, _ = placements(ids_row, length, capacity, slots)
    for which in range(2):
        arriving[1 + which].wait()
        moved = matmul(place, buf[which].reshape(tokens, part)).astype(jnp.bfloat16)
        for group in range(groups):
            packed[group, which] = moved[group * rows : (group + 1) * rows]
        leaving[which].start()
    for copy in leaving:
        copy.wait()


def slab_kernel(length, capacity, slots, ids, hidden, cot, _, *refs):
    slabs, refs = refs[:4], refs[4:]
    id_buf, buf, ordered, turned, out_slabs, sems = refs
    s_local, _, part = hidden.shape
    tokens = s_local * length
    slab = part // 2
    half = tokens // 2
    replica = lax.axis_index("dp")
    arriving = [
        pltpu.make_async_copy(source, target, sems.at[at])
        for at, (source, target) in enumerate(
            ((ids, id_buf), (hidden, buf.at[0]), (cot, buf.at[1]))
        )
    ]
    leaving = [
        pltpu.make_async_copy(out_slabs.at[at], slabs[at], sems.at[3 + at]) for at in range(4)
    ]
    for copy in arriving:
        copy.start()
    arriving[0].wait()
    ids_row = spread_ids(id_buf, (16, tokens), length)
    _, by_group = placements(ids_row[:1], length, capacity, slots)
    for group in range(2):
        mine = by_group[group * half : (group + 1) * half]
        clusters = matmul(ids_row.astype(jnp.float32).astype(jnp.bfloat16), mine, TRANS_RHS)
        turned[group] = jnp.concatenate(
            [clusters.astype(jnp.bfloat16), jnp.zeros((16, 128 - half), jnp.bfloat16)], axis=1
        )
    for which in range(2):
        arriving[1 + which].wait()
        flat = buf[which].reshape(tokens, part)
        ordered[which] = matmul(by_group, flat).astype(jnp.bfloat16)
    for turn in range(4):
        pair = (turn // 2) ^ (replica & 1)
        group = (turn % 2) ^ (replica >> 1)
        cols = pl.ds(pl.multiple_of(pair * slab, slab), slab)
        at = pl.ds(pl.multiple_of(group * half, half), half)
        for which in range(2):
            out_slabs[turn, which * half : (which + 1) * half] = ordered[which, at, cols]
        out_slabs[turn, tokens:] = jnp.zeros((16, slab), jnp.bfloat16)
        out_slabs[turn, tokens:, :128] = turned[group]
        leaving[turn].start()
    for copy in leaving:
        copy.wait()


def repack_kernel(length, capacity, *refs):
    slabs, recv, outs, sems = refs[:4], refs[4], refs[6:-1], refs[-1]
    kept, sent = outs[0], outs[1:]
    _, _, rows, slab = kept.shape
    experts = len(outs)
    half = (slabs[0].shape[0] - 16) // 2
    core, replica = lax.axis_index("segment"), lax.axis_index("dp")
    expert = lax.axis_index("expert")
    per_part = recv.shape[4] // slab
    part = replica // per_part
    cols = pl.ds(pl.multiple_of((replica - part * per_part) * slab, slab), slab)
    cuts = [
        pltpu.make_async_copy(
            recv.at[e, part, :, :, cols], kept.at[:, 3 + (e ^ expert)], sems.at[e]
        )
        for e in range(experts)
    ]
    for cut in cuts:
        cut.start()
    far_low = (replica >> 1) ^ core ^ 1

    def place_rows(held, near):
        ids_row = held[2 * half :, :128].astype(jnp.float32)[:1, :half].astype(jnp.int32)
        rank, _ = ranked(ids_row, length)
        token = lax.rem(lax.broadcasted_iota(jnp.int32, ids_row.shape, 1), length)
        step = ids_row ^ expert
        place = one_hot((step * (capacity // 2) + rank) * length + token, experts * rows)
        for which in range(2):
            moved = matmul(place, held[which * half : (which + 1) * half]).astype(jnp.bfloat16)
            kept[which, near - 1] = moved[:rows]
            for step_at, out in enumerate(sent):
                out[which, near - 1] = moved[(step_at + 1) * rows : (step_at + 2) * rows]

    place_rows(jnp.where(far_low == 1, slabs[1][...], slabs[0][...]), 2)
    for low in range(2):
        place_rows(slabs[2 + low][...], 1 + 2 * (low ^ (replica >> 1) ^ core))
    for cut in cuts:
        cut.wait()


def unpack(sizes, id_buf, back, out):
    length, capacity, slots = sizes
    groups, rows, width = back.shape
    s_local = out.shape[0]
    ids_row = spread_ids(id_buf, (8, s_local * length), length)[:1]
    place, _ = placements(ids_row, length, capacity, slots)
    moved = matmul(place, back[...].reshape(groups * rows, width), TRANS_LHS)
    out[...] = moved.astype(jnp.bfloat16).reshape(s_local, length, width)


def split_three(value):
    top = value.astype(jnp.bfloat16).astype(jnp.float32)
    mid = (value - top).astype(jnp.bfloat16).astype(jnp.float32)
    low = (value - top - mid).astype(jnp.bfloat16).astype(jnp.float32)
    return [top, mid, low]


def side_by_side(columns, tokens):
    lane = lax.broadcasted_iota(jnp.int32, (tokens, 128), 1)
    block = jnp.zeros((tokens, 128), jnp.float32)
    at = 0
    for column in columns:
        for piece in split_three(column):
            block = jnp.where(lane == at, piece, block)
            at += 1
    return block.astype(jnp.bfloat16)


def lanes(value):
    total = value[:, :128]
    for start in range(128, value.shape[1], 128):
        total = total + value[:, start : start + 128]
    return total


def row_sum(parts):
    return jnp.sum(parts, axis=1, keepdims=True)


def chain_kernel(
    recv_in, own_dn, own_up, own_gain, other_dn, other_up, other_gain,
    out, small,
    recv, dn_buf, up_buf, gain_buf, entering, middle, d_norms, sems,
):
    phase = lax.axis_index("segment")
    experts, phases, _, rows, part = recv.shape
    tokens = experts * rows
    width = phases * part
    rank = dn_buf.shape[2]
    own, other = (own_dn, own_up, own_gain), (other_dn, other_up, other_gain)

    def copies(sources, at):
        return [
            pltpu.make_async_copy(source, buffer.at[at], sems.at[at, which])
            for which, (source, buffer) in enumerate(zip(sources, (dn_buf, up_buf, gain_buf)))
        ]

    def fetch(at):
        for this in range(2):

            @pl.when(phase == this)
            def _():
                for copy in copies(own if at == this else other, at):
                    copy.start()

    arriving = [
        pltpu.make_async_copy(recv_in.at[:, :, at], recv.at[:, :, at], sems.at[2, at])
        for at in range(2)
    ]
    arriving[0].start()
    fetch(0)
    waits = [copies(own, at) for at in range(2)]
    cols = range(0, width, CHUNK)

    def block(which, col):
        half, start = col // part, col % part
        return jnp.concatenate(
            [recv[e, half, which, :, start : start + CHUNK] for e in range(experts)], axis=0
        )

    def inverse_of(ref, mean):
        total = jnp.zeros((tokens, 128), jnp.float32)
        for col in cols:
            center = ref[:, col : col + CHUNK].astype(jnp.float32) - mean
            total = total + lanes(center * center)
        return lax.rsqrt(row_sum(total) / width + EPS)

    def down(ref, mean, inverse, at):
        pre = jnp.zeros((tokens, rank), jnp.float32)
        for col in cols:
            here = slice(col, col + CHUNK)
            normed = (ref[:, here].astype(jnp.float32) - mean) * inverse
            lowered = (normed * gain_buf[at, :, here].astype(jnp.float32)).astype(jnp.bfloat16)
            pre = pre + matmul(lowered, dn_buf[at, here, :])
        return pre

    total = jnp.zeros((tokens, 128), jnp.float32)
    arriving[0].wait()
    for col in cols:
        value = block(0, col)
        entering[:, col : col + CHUNK] = value
        total = total + lanes(value.astype(jnp.float32))
    mean_0 = row_sum(total) / width
    inverse_0 = inverse_of(entering, mean_0)
    waits[0][0].wait()
    waits[0][2].wait()
    arriving[1].start()
    fetch(1)
    pre_0 = down(entering, mean_0, inverse_0, 0)
    act_0 = gelu_value(pre_0).astype(jnp.bfloat16)
    slope_0 = gelu_slope(pre_0)

    waits[0][1].wait()
    total = jnp.zeros((tokens, 128), jnp.float32)
    for col in cols:
        here = slice(col, col + CHUNK)
        value = entering[:, here].astype(jnp.float32) + matmul(act_0, up_buf[0, :, here])
        value = value.astype(jnp.bfloat16)
        middle[:, here] = value
        total = total + lanes(value.astype(jnp.float32))
    mean_1 = row_sum(total) / width
    inverse_1 = inverse_of(middle, mean_1)
    for copy in waits[1] + arriving[1:]:
        copy.wait()
    d_act = jnp.zeros((tokens, rank), jnp.float32)
    for col in cols:
        d_act = d_act + matmul(block(1, col), up_buf[1, :, col : col + CHUNK], TRANS_RHS)
    pre_1 = down(middle, mean_1, inverse_1, 1)
    act_1 = gelu_value(pre_1).astype(jnp.bfloat16)
    d_pre_1 = (d_act * gelu_slope(pre_1)).astype(jnp.bfloat16)

    total = jnp.zeros((tokens, 128), jnp.float32)
    cross = jnp.zeros((tokens, 128), jnp.float32)
    for col in cols:
        here = slice(col, col + CHUNK)
        wide = middle[:, here].astype(jnp.float32)
        d_norm = matmul(d_pre_1, dn_buf[1, here, :], TRANS_RHS)
        d_norm = d_norm * gain_buf[1, :, here].astype(jnp.float32)
        d_norms[:, here] = d_norm
        total = total + lanes(d_norm)
        cross = cross + lanes(d_norm * ((wide - mean_1) * inverse_1))
        leaving = (wide + matmul(act_1, up_buf[1, :, here])).astype(jnp.bfloat16)
        half, start = col // part, col % part
        for e in range(experts):
            out[e, half, :, start : start + CHUNK] = leaving[e * rows : (e + 1) * rows]
    shift = row_sum(total) / width
    along = row_sum(cross) / width
    d_act = jnp.zeros((tokens, rank), jnp.float32)
    for col in cols:
        here = slice(col, col + CHUNK)
        normed = (middle[:, here].astype(jnp.float32) - mean_1) * inverse_1
        grad = block(1, col).astype(jnp.float32) + inverse_1 * (
            d_norms[:, here] - shift - normed * along
        )
        d_act = d_act + matmul(grad.astype(jnp.bfloat16), up_buf[0, :, here], TRANS_RHS)
    d_pre_0 = (d_act * slope_0).astype(jnp.bfloat16)
    moments = (mean_0, inverse_0, mean_1, inverse_1, shift, along)
    kept = (act_0, act_1, d_pre_0, d_pre_1, side_by_side(moments, tokens))
    for e in range(experts):
        start = pl.multiple_of((e ^ lax.axis_index("expert")) * rows, rows)
        for at, value in enumerate(kept):
            cols = slice(at * rank, at * rank + value.shape[1])
            small[pl.ds(start, rows), cols] = value[e * rows : (e + 1) * rows]


def gradient_kernel(experts, sources, sizes, *refs):
    sides, refs = refs[: 2 * experts], refs[2 * experts :]
    smalls, refs = refs[:sources], refs[sources:]
    own, other, refs = refs[:3], refs[3:6], refs[6:]
    ids, back_in, out_hidden, grad_dn, grad_upper = refs[:5]
    (id_buf, back, result, dn_buf, up_buf, gain_buf, wide_buf, small, moments, turned, lows, grads,
     dn_out, up_out, small_sems, wide_sems, sems) = refs[5:]
    core = lax.axis_index("segment")
    place = lax.axis_index("dp")
    rows, slab = smalls[0].shape[0], sides[0].shape[3]
    replicas = sources // 2
    blocks = [side.shape[1] for side in sides[:experts]]
    starts = [sum(blocks[:step]) for step in range(experts)]
    rank = dn_buf.shape[1]
    columns = 256
    chunks = range(0, slab, columns)
    features = pl.ds(pl.multiple_of(place * slab, slab), slab)

    def weight_copies(up, gain_first, dn, gain_second):
        moves = (
            (up.at[:, features], up_buf),
            (gain_first.at[:, features], gain_buf.at[0]),
            (gain_second.at[:, features], gain_buf.at[1]),
            (dn.at[features, :], dn_buf),
        )
        return [
            pltpu.make_async_copy(source, target, sems.at[at])
            for at, (source, target) in enumerate(moves)
        ]

    early = [
        pltpu.make_async_copy(ids, id_buf, sems.at[4]),
        pltpu.make_async_copy(back_in, back, sems.at[5]),
    ]
    small_copies = [
        pltpu.make_async_copy(
            source, small.at[at * rows : (at + 1) * rows], small_sems.at[at]
        )
        for at, source in enumerate(smalls)
    ]
    wide_copies = [
        [
            pltpu.make_async_copy(
                side.at[:, :, :, col : col + columns],
                wide_buf.at[
                    at // experts,
                    :,
                    starts[at % experts] : starts[at % experts] + blocks[at % experts],
                    :,
                    col : col + columns,
                ],
                wide_sems.at[col // columns, at],
            )
            for at, side in enumerate(sides)
        ]
        for col in chunks
    ]
    for copy in early + small_copies:
        copy.start()

    @pl.when(core == 0)
    def _():
        for copy in weight_copies(own[1], own[2], other[0], other[2]):
            copy.start()

    @pl.when(core != 0)
    def _():
        for copy in weight_copies(other[1], other[2], own[0], own[2]):
            copy.start()

    for copies in wide_copies:
        for copy in copies:
            copy.start()
    for copy in early:
        copy.wait()
    unpack(sizes, id_buf, back, result)
    leaving = [pltpu.make_async_copy(result, out_hidden, sems.at[6])]
    leaving[0].start()
    for copy in small_copies + weight_copies(own[1], own[2], other[0], other[2]):
        copy.wait()

    def sliced(source, which, here):
        side, near = source // replicas, source % replicas
        at = [
            replicas - 1 + step if near == 0 else starts[step] + near - 1
            for step in range(experts)
        ]
        return jnp.concatenate([wide_buf[side, which, one, :, here] for one in at], axis=0)

    def moment(at, index):
        value = moments[at, index * 128 : (index + 1) * 128]
        return jnp.concatenate([value] * (columns // 128), axis=1)

    def work(first):
        held = lax.broadcasted_iota(jnp.int32, (128, 6 * 128), 0)
        wanted = lax.broadcasted_iota(jnp.int32, (128, 6 * 128), 1) // 128
        adds = (held // 3 == wanted).astype(jnp.float32).astype(jnp.bfloat16)
        moments[...] = matmul(small[:, 4 * rank :], adds)
        act, d_pre = (0, 2) if first else (1, 3)
        turned[0] = small[:, act * rank : (act + 1) * rank].T
        turned[1] = small[:, d_pre * rank : (d_pre + 1) * rank].T
        for index, col in enumerate(chunks):
            here = slice(col, col + columns)
            for copy in wide_copies[index]:
                copy.wait()
            ups = matmul(small[:, :rank], up_buf[:, here])
            scales = [gain_buf[at, :, here].astype(jnp.float32) for at in range(2)]
            if first:
                downs = matmul(small[:, 3 * rank : 4 * rank], dn_buf[here, :], TRANS_RHS)
            for source in range(sources):
                at = slice(source * rows, (source + 1) * rows)
                wide = sliced(source, 0, here).astype(jnp.float32)
                grad_in = sliced(source, 1, here)
                middle = (wide + ups[at]).astype(jnp.bfloat16).astype(jnp.float32)
                inverse = moment(at, 3)
                normed = (middle - moment(at, 2)) * inverse
                if first:
                    entered = (wide - moment(at, 0)) * moment(at, 1)
                    lows[index, at] = (entered * scales[0]).astype(jnp.bfloat16)
                    d_norm = downs[at] * scales[1]
                    grads[index, at] = (
                        grad_in.astype(jnp.float32)
                        + inverse * (d_norm - moment(at, 4) - normed * moment(at, 5))
                    ).astype(jnp.bfloat16)
                else:
                    lows[index, at] = (normed * scales[1]).astype(jnp.bfloat16)
                    grads[index, at] = grad_in
            dn_out[here, :] = matmul(turned[1], lows[index]).astype(jnp.bfloat16).T
            up_out[index] = matmul(turned[0], grads[index]).astype(jnp.bfloat16)
            for copy in out_copies(index, here):
                copy.start()

    def out_copies(index, here):
        return [
            pltpu.make_async_copy(
                dn_out.at[here, :], grad_dn.at[here, :], sems.at[7 + 2 * index]
            ),
            pltpu.make_async_copy(
                up_out.at[index], grad_upper.at[:, here], sems.at[8 + 2 * index]
            ),
        ]

    @pl.when(core == 0)
    def _():
        work(True)

    @pl.when(core != 0)
    def _():
        work(False)

    for index, col in enumerate(chunks):
        leaving += out_copies(index, slice(col, col + columns))
    for copy in leaving:
        copy.wait()


VMEM = pl.BlockSpec(memory_space=pltpu.VMEM)
HBM = pl.BlockSpec(memory_space=pltpu.HBM)


def call(kernel, name, grant, in_specs, outs, scratch=(), outs_in=VMEM, flops=0, moved=MIB):
    return pl.pallas_call(
        kernel,
        out_shape=tuple(jax.ShapeDtypeStruct(*out) for out in outs),
        in_specs=in_specs,
        out_specs=tuple(outs_in for _ in outs),
        scratch_shapes=list(scratch),
        compiler_params=pltpu.CompilerParams(vmem_limit_bytes=grant * MIB),
        cost_estimate=pl.CostEstimate(flops=flops, bytes_accessed=moved, transcendentals=0),
        name=name,
    )


def across(block, axis, distance):
    size = lax.axis_size(axis)
    return lax.ppermute(block, axis, [(i, i ^ distance) for i in range(size)])


def slab_route(replicas, pair, low):
    route = []
    for replica in range(replicas):
        for core in range(2):
            chip = 2 * core + ((replica & 1) ^ pair)
            route.append((2 * replica + core, 2 * chip + ((replica >> 1) ^ low)))
    return route


def on_device_two_phases(hidden_in, cotangent, cluster_ids, w_down, w_up, gain):
    experts = lax.axis_size("expert")
    replicas = lax.axis_size("dp")
    s_local, length, part = hidden_in.shape
    width = 2 * part
    capacity = 2 * s_local // experts
    slots = experts * capacity
    groups = 2 * experts
    rows = slots * length // groups
    tokens = experts * rows
    own = (w_down[0, 0], w_up[0, 0], gain[0])
    rank = own[0].shape[1]
    slab = width // replicas
    bf16, f32 = jnp.bfloat16, jnp.float32
    sizes = (length, capacity, slots)
    sections = ("expert", "segment")

    other = tuple(across(array, "segment", 1) for array in own)
    half = s_local * length // 2
    (send,) = call(
        functools.partial(pack_kernel, *sizes),
        "pack",
        60,
        [HBM] * 3,
        [((groups, 2, rows, part), bf16)],
        [
            pltpu.SMEM(cluster_ids.shape, jnp.int32),
            pltpu.VMEM((2,) + hidden_in.shape, bf16),
            pltpu.VMEM((groups, 2, rows, part), bf16),
            pltpu.SemaphoreType.DMA((5,)),
        ],
        outs_in=HBM,
    )(cluster_ids, hidden_in, cotangent)
    slabs = call(
        functools.partial(slab_kernel, *sizes),
        "slabs",
        60,
        [HBM] * 4,
        [((2 * half + 16, slab), bf16)] * 4,
        [
            pltpu.SMEM(cluster_ids.shape, jnp.int32),
            pltpu.VMEM((2,) + hidden_in.shape, bf16),
            pltpu.VMEM((2, 2 * half, part), bf16),
            pltpu.VMEM((2, 16, 128), bf16),
            pltpu.VMEM((4, 2 * half + 16, slab), bf16),
            pltpu.SemaphoreType.DMA((7,)),
        ],
        outs_in=HBM,
    )(cluster_ids, hidden_in, cotangent, send)
    recv = lax.all_to_all(send, sections, split_axis=0, concat_axis=0, tiled=True)
    recv = recv.reshape(experts, 2, 2, rows, part)
    slabs = [
        lax.ppermute(block, ("dp", "segment"), slab_route(replicas, turn // 2, turn % 2))
        for turn, block in enumerate(slabs)
    ]
    out, small = call(
        chain_kernel,
        "chain",
        50,
        [HBM] * 7,
        [((experts, 2, rows, part), bf16), ((tokens, 4 * rank + 128), bf16)],
        [
            pltpu.VMEM(recv.shape, bf16),
            pltpu.VMEM((2, width, rank), bf16),
            pltpu.VMEM((2, rank, width), bf16),
            pltpu.VMEM((2, 1, width), bf16),
            pltpu.VMEM((tokens, width), bf16),
            pltpu.VMEM((tokens, width), bf16),
            pltpu.VMEM((tokens, width), f32),
            pltpu.SemaphoreType.DMA((3, 3)),
        ],
        flops=7 * 2 * tokens * width * rank,
        moved=10 * MIB,
    )(recv, *own, *other)
    slices = call(
        functools.partial(repack_kernel, length, capacity),
        "repack",
        16,
        [VMEM] * 4 + [HBM] * 2,
        [((2, replicas - 1 + experts, rows, slab), bf16)]
        + [((2, replicas - 1, rows, slab), bf16)] * (experts - 1),
        [pltpu.SemaphoreType.DMA((experts,))],
    )(*slabs, recv, small)
    small, *slices = lax.optimization_barrier((small, *slices))
    mine = [slices[0]] + [across(slices[step], "expert", step) for step in range(1, experts)]
    mine[:2] = lax.optimization_barrier(tuple(mine[:2]))
    theirs = [across(block, "segment", 1) for block in mine]
    near = [small] + [across(small, "dp", step) for step in range(1, replicas)]
    near[:2] = lax.optimization_barrier(tuple(near[:2]))
    smalls = near + [across(piece, "segment", 1) for piece in near]

    back = lax.all_to_all(
        out.reshape(groups, rows, part), sections, split_axis=0, concat_axis=0, tiled=True
    )

    sources = 2 * replicas
    all_tokens = sources * tokens
    out_hidden, grad_dn, grad_upper = call(
        functools.partial(gradient_kernel, experts, sources, sizes),
        "gradients",
        60,
        [HBM] * (2 * experts + sources + 8),
        [(hidden_in.shape, bf16), ((slab, rank), bf16), ((rank, slab), bf16)],
        [
            pltpu.SMEM(cluster_ids.shape, jnp.int32),
            pltpu.VMEM(back.shape, bf16),
            pltpu.VMEM(hidden_in.shape, bf16),
            pltpu.VMEM((slab, rank), bf16),
            pltpu.VMEM((rank, slab), bf16),
            pltpu.VMEM((2, 1, slab), bf16),
            pltpu.VMEM((2, 2, replicas * experts, rows, slab), bf16),
            pltpu.VMEM((all_tokens, 4 * rank + 128), bf16),
            pltpu.VMEM((all_tokens, 6 * 128), f32),
            pltpu.VMEM((2, rank, all_tokens), bf16),
            pltpu.VMEM((slab // 256, all_tokens, 256), bf16),
            pltpu.VMEM((slab // 256, all_tokens, 256), bf16),
            pltpu.VMEM((slab, rank), bf16),
            pltpu.VMEM((slab // 256, rank, 256), bf16),
            pltpu.SemaphoreType.DMA((sources,)),
            pltpu.SemaphoreType.DMA((slab // 256, 2 * experts)),
            pltpu.SemaphoreType.DMA((7 + 2 * (slab // 256),)),
        ],
        outs_in=HBM,
    )(*mine, *theirs, *smalls, *own, *other, cluster_ids, back)
    return (out_hidden, grad_dn[None, None], grad_upper[None, None])


def solution(mesh):
    two = dict(mesh.shape) == {"expert": 4, "dp": 4, "segment": 2}
    on_device = on_device_two_phases if two else on_device_pipelined
    return jax.shard_map(
        on_device,
        mesh=mesh,
        in_specs=(
            P(("expert", "dp"), None, "segment"),
            P(("expert", "dp"), None, "segment"),
            P(("expert", "dp")),
            P("expert", "segment", None, None),
            P("expert", "segment", None, None),
            P("expert", "segment", None),
        ),
        out_specs=(
            P(("expert", "dp"), None, "segment"),
            P("expert", "segment", "dp", None),
            P("expert", "segment", None, "dp"),
        ),
        check_vma=False,
    )
```

```python
import functools

import jax
import jax.numpy as jnp
from jax import lax
from jax.experimental import pallas as pl
from jax.experimental.pallas import tpu as pltpu
from jax.sharding import PartitionSpec as P

MICRO = 4


EPS = 1e-05
C_ZERO = 0.7978845608028654
C_ONE = 0.044715


def shifted(block, axis, distance):
    devices = range(lax.axis_size(axis))
    route = [(i - distance, i) for i in devices if i - distance in devices]
    return lax.ppermute(block, axis, route)


def from_root(block, axis, holder):
    block = jnp.where(lax.axis_index(axis) == holder, block, jnp.zeros_like(block))
    return lax.psum(block, axis)


def gelu_value(z):
    return 0.5 * z * (1.0 + jnp.tanh(C_ZERO * (z + C_ONE * z * z * z)))


def gelu_slope(z):
    tval = jnp.tanh(C_ZERO * (z + C_ONE * z * z * z))
    return 0.5 * (1.0 + tval) + 0.5 * z * (1.0 - tval * tval) * C_ZERO * (1.0 + 3.0 * C_ONE * z * z)


def normalize(hidden):
    wide = hidden.astype(jnp.float32)
    center = wide - jnp.mean(wide, axis=-1, keepdims=True)
    inverse = lax.rsqrt(jnp.mean(center * center, axis=-1, keepdims=True) + EPS)
    return (wide, center * inverse, inverse)


def phase_forward(hidden, w_dn, w_upper, scale):
    wide, normed, inverse = normalize(hidden)
    lowered = (normed * scale).astype(jnp.bfloat16)
    pre = jnp.dot(lowered, w_dn, preferred_element_type=jnp.float32)
    act = gelu_value(pre).astype(jnp.bfloat16)
    leaving = (wide + jnp.dot(act, w_upper, preferred_element_type=jnp.float32)).astype(
        jnp.bfloat16
    )
    return (leaving, pre)


def phase_backward(hidden, grad_in, pre, w_dn, w_upper, scale):
    wide, normed, inverse = normalize(hidden)
    lowered = (normed * scale).astype(jnp.bfloat16)
    act = gelu_value(pre).astype(jnp.bfloat16)
    d_act = jnp.dot(grad_in, w_upper.T, preferred_element_type=jnp.float32)
    d_pre = (d_act * gelu_slope(pre)).astype(jnp.bfloat16)
    d_low = jnp.dot(d_pre, w_dn.T, preferred_element_type=jnp.float32)
    d_norm = d_low * scale
    d_wide = inverse * (
        d_norm
        - jnp.mean(d_norm, axis=-1, keepdims=True)
        - normed * jnp.mean(d_norm * normed, axis=-1, keepdims=True)
    )
    grad_out = (grad_in.astype(jnp.float32) + d_wide).astype(jnp.bfloat16)
    return (grad_out, lowered, act, d_pre)


def put_slot(buffer, value, slot, valid):
    old_value = lax.dynamic_index_in_dim(buffer, slot, 0, keepdims=False)
    return lax.dynamic_update_index_in_dim(buffer, jnp.where(valid, value, old_value), slot, 0)


def on_device_pipelined(hidden_in, cotangent, cluster_ids, w_down, w_up, gain):
    experts = lax.axis_size("expert")
    phases = lax.axis_size("segment")
    phase = lax.axis_index("segment")
    s_local, length, quarter = hidden_in.shape
    capacity = 2 * s_local // experts
    slots = experts * capacity
    same = (cluster_ids[:, None] == cluster_ids[None, :]).astype(jnp.int32)
    earlier = jnp.sum(jnp.tril(same, -1), axis=1)
    target = cluster_ids * capacity + earlier
    place = (jnp.arange(slots, dtype=jnp.int32)[:, None] == target[None, :]).astype(jnp.bfloat16)

    def to_slots(local):
        flat = local.reshape(s_local, -1)
        moved = jnp.dot(place, flat, preferred_element_type=jnp.float32).astype(jnp.bfloat16)
        return moved.reshape((slots,) + local.shape[1:])

    full_in, full_cot = (
        lax.all_gather(hidden_in, "segment", axis=2, tiled=True),
        lax.all_gather(cotangent, "segment", axis=2, tiled=True),
    )
    slot_in, slot_cot = (
        lax.all_to_all(to_slots(full_in), "expert", split_axis=0, concat_axis=0, tiled=True),
        lax.all_to_all(to_slots(full_cot), "expert", split_axis=0, concat_axis=0, tiled=True),
    )
    width = slot_in.shape[2]
    micro_rows = slots * length // MICRO
    inputs = slot_in.reshape(MICRO, micro_rows, width)
    cots = slot_cot.reshape(MICRO, micro_rows, width)
    w_dn = w_down[0, 0]
    w_upper = w_up[0, 0]
    rank = w_dn.shape[1]
    scale = gain[0, 0].astype(jnp.float32)
    ticks = MICRO + phases - 1

    def forward_tick(tick, carry):
        received, saved, pres, results = carry
        which = tick - phase
        valid = (which >= 0) & (which < MICRO)
        slot = jnp.clip(which, 0, MICRO - 1)
        first = lax.dynamic_index_in_dim(inputs, jnp.minimum(tick, MICRO - 1), 0, keepdims=False)
        entering = jnp.where(phase == 0, first, received)
        leaving, pre = phase_forward(entering, w_dn, w_upper, scale)
        saved = put_slot(saved, entering, slot, valid)
        pres = put_slot(pres, pre, slot, valid)
        results = put_slot(results, leaving, slot, valid & (phase == phases - 1))
        received = shifted(leaving, "segment", 1)
        return (received, saved, pres, results)

    start = (
        jnp.zeros((micro_rows, width), jnp.bfloat16),
        jnp.zeros((MICRO, micro_rows, width), jnp.bfloat16),
        jnp.zeros((MICRO, micro_rows, rank), jnp.float32),
        jnp.zeros((MICRO, micro_rows, width), jnp.bfloat16),
    )
    received, saved, pres, results = lax.fori_loop(0, ticks, forward_tick, start)

    def backward_tick(tick, carry):
        received, lows, acts, dpres, grads = carry
        which = tick - (phases - 1 - phase)
        valid = (which >= 0) & (which < MICRO)
        slot = jnp.clip(which, 0, MICRO - 1)
        last = lax.dynamic_index_in_dim(cots, jnp.minimum(tick, MICRO - 1), 0, keepdims=False)
        grad_in = jnp.where(phase == phases - 1, last, received)
        hidden = lax.dynamic_index_in_dim(saved, slot, 0, keepdims=False)
        pre = lax.dynamic_index_in_dim(pres, slot, 0, keepdims=False)
        grad_out, lowered, act, d_pre = phase_backward(hidden, grad_in, pre, w_dn, w_upper, scale)
        lows = put_slot(lows, lowered, slot, valid)
        acts = put_slot(acts, act, slot, valid)
        dpres = put_slot(dpres, d_pre, slot, valid)
        grads = put_slot(grads, grad_in, slot, valid)
        received = shifted(grad_out, "segment", -1)
        return (received, lows, acts, dpres, grads)

    start_back = (
        jnp.zeros((micro_rows, width), jnp.bfloat16),
        jnp.zeros((MICRO, micro_rows, width), jnp.bfloat16),
        jnp.zeros((MICRO, micro_rows, rank), jnp.bfloat16),
        jnp.zeros((MICRO, micro_rows, rank), jnp.bfloat16),
        jnp.zeros((MICRO, micro_rows, width), jnp.bfloat16),
    )
    received, lows, acts, dpres, grads = lax.fori_loop(0, ticks, backward_tick, start_back)
    contract = (((0,), (0,)), ((), ()))
    grad_dn = lax.dot_general(
        lows.reshape(-1, width),
        dpres.reshape(-1, rank),
        contract,
        preferred_element_type=jnp.float32,
    )
    grad_upper = lax.dot_general(
        acts.reshape(-1, rank),
        grads.reshape(-1, width),
        contract,
        preferred_element_type=jnp.float32,
    )
    summed_dn, summed_upper = (
        lax.psum_scatter(
            grad_dn.astype(jnp.bfloat16), "dp", scatter_dimension=0, tiled=True
        ).astype(jnp.float32),
        lax.psum_scatter(
            grad_upper.astype(jnp.bfloat16), "dp", scatter_dimension=1, tiled=True
        ).astype(jnp.float32),
    )
    returned = from_root(results, "segment", phases - 1)
    returned = returned.reshape(slots, length, width)
    own = lax.dynamic_slice_in_dim(returned, phase * quarter, quarter, 2)
    back = lax.all_to_all(own, "expert", split_axis=0, concat_axis=0, tiled=True)
    out_hidden = jnp.dot(place.T, back.reshape(slots, -1), preferred_element_type=jnp.float32)
    out_hidden = out_hidden.astype(jnp.bfloat16).reshape(s_local, length, quarter)
    return (
        out_hidden,
        summed_dn.astype(jnp.bfloat16)[None, None],
        summed_upper.astype(jnp.bfloat16)[None, None],
    )


CHUNK = 512
MIB = 1024 * 1024
TRANS_RHS = (((1,), (1,)), ((), ()))
TRANS_LHS = (((0,), (0,)), ((), ()))


def matmul(left, right, dims=(((1,), (0,)), ((), ()))):
    return lax.dot_general(left, right, dims, preferred_element_type=jnp.float32)


def spread_ids(ids, shape, length):
    lane = lax.broadcasted_iota(jnp.int32, shape, 1)
    spread = jnp.zeros(shape, jnp.int32)
    for n in range(ids.shape[0]):
        spread = jnp.where(lane // length == n, ids[n], spread)
    return spread


def ranked(ids_row, length):
    tokens = ids_row.shape[1]
    kinds = lax.broadcasted_iota(jnp.int32, (8, tokens), 0)
    member = (kinds == ids_row).astype(jnp.float32)
    at_col = lax.broadcasted_iota(jnp.int32, (tokens, tokens), 0)
    at_row = lax.broadcasted_iota(jnp.int32, (tokens, tokens), 1)
    before = (lax.rem(at_col, length) == 0) & (at_col // length < at_row // length)
    counts = matmul(member.astype(jnp.bfloat16), before.astype(jnp.float32).astype(jnp.bfloat16))
    rank = jnp.sum(member * counts, axis=0, keepdims=True)
    total = jnp.sum(member, axis=1, keepdims=True) * (1.0 / length)
    lower = jnp.sum(jnp.where(kinds < ids_row, total, 0.0), axis=0, keepdims=True)
    return rank.astype(jnp.int32), lower.astype(jnp.int32)


def one_hot(target, rows):
    wanted = lax.broadcasted_iota(jnp.int32, (rows, target.shape[1]), 0)
    return (wanted == target).astype(jnp.float32).astype(jnp.bfloat16)


def placements(ids_row, length, capacity, slots):
    rank, lower = ranked(ids_row, length)
    token = lax.rem(lax.broadcasted_iota(jnp.int32, ids_row.shape, 1), length)
    place = rank + lower
    group = lax.rem(place, 2)
    per_core = capacity // 2
    packed = ((ids_row * 2 + group) * per_core + rank // 2) * length + token
    tokens = ids_row.shape[1]
    ordered = group * (tokens // 2) + (place // 2) * length + token
    return one_hot(packed, slots * length), one_hot(ordered, tokens)


def pack_kernel(length, capacity, slots, ids, hidden, cot, send, id_buf, buf, packed, sems):
    groups, _, rows, part = send.shape
    tokens = hidden.shape[0] * length
    arriving = [
        pltpu.make_async_copy(source, target, sems.at[at])
        for at, (source, target) in enumerate(
            ((ids, id_buf), (hidden, buf.at[0]), (cot, buf.at[1]))
        )
    ]
    leaving = [
        pltpu.make_async_copy(packed.at[:, at], send.at[:, at], sems.at[3 + at]) for at in range(2)
    ]
    for copy in arriving:
        copy.start()
    arriving[0].wait()
    ids_row = spread_ids(id_buf, (8, tokens), length)[:1]
    place, _ = placements(ids_row, length, capacity, slots)
    for which in range(2):
        arriving[1 + which].wait()
        moved = matmul(place, buf[which].reshape(tokens, part)).astype(jnp.bfloat16)
        for group in range(groups):
            packed[group, which] = moved[group * rows : (group + 1) * rows]
        leaving[which].start()
    for copy in leaving:
        copy.wait()


def slab_kernel(length, capacity, slots, ids, hidden, cot, _, *refs):
    slabs, refs = refs[:4], refs[4:]
    id_buf, buf, ordered, turned, out_slabs, sems = refs
    s_local, _, part = hidden.shape
    tokens = s_local * length
    slab = part // 2
    half = tokens // 2
    replica = lax.axis_index("dp")
    arriving = [
        pltpu.make_async_copy(source, target, sems.at[at])
        for at, (source, target) in enumerate(
            ((ids, id_buf), (hidden, buf.at[0]), (cot, buf.at[1]))
        )
    ]
    leaving = [
        pltpu.make_async_copy(out_slabs.at[at], slabs[at], sems.at[3 + at]) for at in range(4)
    ]
    for copy in arriving:
        copy.start()
    arriving[0].wait()
    ids_row = spread_ids(id_buf, (16, tokens), length)
    _, by_group = placements(ids_row[:1], length, capacity, slots)
    for group in range(2):
        mine = by_group[group * half : (group + 1) * half]
        clusters = matmul(ids_row.astype(jnp.float32).astype(jnp.bfloat16), mine, TRANS_RHS)
        turned[group] = jnp.concatenate(
            [clusters.astype(jnp.bfloat16), jnp.zeros((16, 128 - half), jnp.bfloat16)], axis=1
        )
    for which in range(2):
        arriving[1 + which].wait()
        flat = buf[which].reshape(tokens, part)
        ordered[which] = matmul(by_group, flat).astype(jnp.bfloat16)
    for turn in range(4):
        pair = (turn // 2) ^ (replica & 1)
        group = (turn % 2) ^ (replica >> 1)
        cols = pl.ds(pl.multiple_of(pair * slab, slab), slab)
        at = pl.ds(pl.multiple_of(group * half, half), half)
        for which in range(2):
            out_slabs[turn, which * half : (which + 1) * half] = ordered[which, at, cols]
        out_slabs[turn, tokens:] = jnp.zeros((16, slab), jnp.bfloat16)
        out_slabs[turn, tokens:, :128] = turned[group]
        leaving[turn].start()
    for copy in leaving:
        copy.wait()


def repack_kernel(length, capacity, *refs):
    slabs, recv, outs, sems = refs[:4], refs[4], refs[6:-1], refs[-1]
    kept, sent = outs[0], outs[1:]
    _, _, rows, slab = kept.shape
    experts = len(outs)
    half = (slabs[0].shape[0] - 16) // 2
    core, replica = lax.axis_index("segment"), lax.axis_index("dp")
    expert = lax.axis_index("expert")
    per_part = recv.shape[4] // slab
    part = replica // per_part
    cols = pl.ds(pl.multiple_of((replica - part * per_part) * slab, slab), slab)
    cuts = [
        pltpu.make_async_copy(
            recv.at[e, part, :, :, cols], kept.at[:, 3 + (e ^ expert)], sems.at[e]
        )
        for e in range(experts)
    ]
    for cut in cuts:
        cut.start()
    far_low = (replica >> 1) ^ core ^ 1

    def place_rows(held, near):
        ids_row = held[2 * half :, :128].astype(jnp.float32)[:1, :half].astype(jnp.int32)
        rank, _ = ranked(ids_row, length)
        token = lax.rem(lax.broadcasted_iota(jnp.int32, ids_row.shape, 1), length)
        step = ids_row ^ expert
        place = one_hot((step * (capacity // 2) + rank) * length + token, experts * rows)
        for which in range(2):
            moved = matmul(place, held[which * half : (which + 1) * half]).astype(jnp.bfloat16)
            kept[which, near - 1] = moved[:rows]
            for step_at, out in enumerate(sent):
                out[which, near - 1] = moved[(step_at + 1) * rows : (step_at + 2) * rows]

    place_rows(jnp.where(far_low == 1, slabs[1][...], slabs[0][...]), 2)
    for low in range(2):
        place_rows(slabs[2 + low][...], 1 + 2 * (low ^ (replica >> 1) ^ core))
    for cut in cuts:
        cut.wait()


def unpack(sizes, id_buf, back, out):
    length, capacity, slots = sizes
    groups, rows, width = back.shape
    s_local = out.shape[0]
    ids_row = spread_ids(id_buf, (8, s_local * length), length)[:1]
    place, _ = placements(ids_row, length, capacity, slots)
    moved = matmul(place, back[...].reshape(groups * rows, width), TRANS_LHS)
    out[...] = moved.astype(jnp.bfloat16).reshape(s_local, length, width)


def split_three(value):
    top = value.astype(jnp.bfloat16).astype(jnp.float32)
    mid = (value - top).astype(jnp.bfloat16).astype(jnp.float32)
    low = (value - top - mid).astype(jnp.bfloat16).astype(jnp.float32)
    return [top, mid, low]


def side_by_side(columns, tokens):
    lane = lax.broadcasted_iota(jnp.int32, (tokens, 128), 1)
    block = jnp.zeros((tokens, 128), jnp.float32)
    at = 0
    for column in columns:
        for piece in split_three(column):
            block = jnp.where(lane == at, piece, block)
            at += 1
    return block.astype(jnp.bfloat16)


def lanes(value):
    total = value[:, :128]
    for start in range(128, value.shape[1], 128):
        total = total + value[:, start : start + 128]
    return total


def row_sum(parts):
    return jnp.sum(parts, axis=1, keepdims=True)


def chain_kernel(
    recv_in, own_dn, own_up, own_gain, other_dn, other_up, other_gain,
    out, small,
    recv, dn_buf, up_buf, gain_buf, entering, middle, d_norms, sems,
):
    phase = lax.axis_index("segment")
    experts, phases, _, rows, part = recv.shape
    tokens = experts * rows
    width = phases * part
    rank = dn_buf.shape[2]
    own, other = (own_dn, own_up, own_gain), (other_dn, other_up, other_gain)

    def copies(sources, at):
        return [
            pltpu.make_async_copy(source, buffer.at[at], sems.at[at, which])
            for which, (source, buffer) in enumerate(zip(sources, (dn_buf, up_buf, gain_buf)))
        ]

    def fetch(at):
        for this in range(2):

            @pl.when(phase == this)
            def _():
                for copy in copies(own if at == this else other, at):
                    copy.start()

    arriving = [
        pltpu.make_async_copy(recv_in.at[:, :, at], recv.at[:, :, at], sems.at[2, at])
        for at in range(2)
    ]
    arriving[0].start()
    fetch(0)
    waits = [copies(own, at) for at in range(2)]
    cols = range(0, width, CHUNK)

    def block(which, col):
        half, start = col // part, col % part
        return jnp.concatenate(
            [recv[e, half, which, :, start : start + CHUNK] for e in range(experts)], axis=0
        )

    def inverse_of(ref, mean):
        total = jnp.zeros((tokens, 128), jnp.float32)
        for col in cols:
            center = ref[:, col : col + CHUNK].astype(jnp.float32) - mean
            total = total + lanes(center * center)
        return lax.rsqrt(row_sum(total) / width + EPS)

    def down(ref, mean, inverse, at):
        pre = jnp.zeros((tokens, rank), jnp.float32)
        for col in cols:
            here = slice(col, col + CHUNK)
            normed = (ref[:, here].astype(jnp.float32) - mean) * inverse
            lowered = (normed * gain_buf[at, :, here].astype(jnp.float32)).astype(jnp.bfloat16)
            pre = pre + matmul(lowered, dn_buf[at, here, :])
        return pre

    total = jnp.zeros((tokens, 128), jnp.float32)
    arriving[0].wait()
    for col in cols:
        value = block(0, col)
        entering[:, col : col + CHUNK] = value
        total = total + lanes(value.astype(jnp.float32))
    mean_0 = row_sum(total) / width
    inverse_0 = inverse_of(entering, mean_0)
    waits[0][0].wait()
    waits[0][2].wait()
    arriving[1].start()
    fetch(1)
    pre_0 = down(entering, mean_0, inverse_0, 0)
    act_0 = gelu_value(pre_0).astype(jnp.bfloat16)
    slope_0 = gelu_slope(pre_0)

    waits[0][1].wait()
    total = jnp.zeros((tokens, 128), jnp.float32)
    for col in cols:
        here = slice(col, col + CHUNK)
        value = entering[:, here].astype(jnp.float32) + matmul(act_0, up_buf[0, :, here])
        value = value.astype(jnp.bfloat16)
        middle[:, here] = value
        total = total + lanes(value.astype(jnp.float32))
    mean_1 = row_sum(total) / width
    inverse_1 = inverse_of(middle, mean_1)
    for copy in waits[1] + arriving[1:]:
        copy.wait()
    d_act = jnp.zeros((tokens, rank), jnp.float32)
    for col in cols:
        d_act = d_act + matmul(block(1, col), up_buf[1, :, col : col + CHUNK], TRANS_RHS)
    pre_1 = down(middle, mean_1, inverse_1, 1)
    act_1 = gelu_value(pre_1).astype(jnp.bfloat16)
    d_pre_1 = (d_act * gelu_slope(pre_1)).astype(jnp.bfloat16)

    total = jnp.zeros((tokens, 128), jnp.float32)
    cross = jnp.zeros((tokens, 128), jnp.float32)
    for col in cols:
        here = slice(col, col + CHUNK)
        wide = middle[:, here].astype(jnp.float32)
        d_norm = matmul(d_pre_1, dn_buf[1, here, :], TRANS_RHS)
        d_norm = d_norm * gain_buf[1, :, here].astype(jnp.float32)
        d_norms[:, here] = d_norm
        total = total + lanes(d_norm)
        cross = cross + lanes(d_norm * ((wide - mean_1) * inverse_1))
        leaving = (wide + matmul(act_1, up_buf[1, :, here])).astype(jnp.bfloat16)
        half, start = col // part, col % part
        for e in range(experts):
            out[e, half, :, start : start + CHUNK] = leaving[e * rows : (e + 1) * rows]
    shift = row_sum(total) / width
    along = row_sum(cross) / width
    d_act = jnp.zeros((tokens, rank), jnp.float32)
    for col in cols:
        here = slice(col, col + CHUNK)
        normed = (middle[:, here].astype(jnp.float32) - mean_1) * inverse_1
        grad = block(1, col).astype(jnp.float32) + inverse_1 * (
            d_norms[:, here] - shift - normed * along
        )
        d_act = d_act + matmul(grad.astype(jnp.bfloat16), up_buf[0, :, here], TRANS_RHS)
    d_pre_0 = (d_act * slope_0).astype(jnp.bfloat16)
    moments = (mean_0, inverse_0, mean_1, inverse_1, shift, along)
    kept = (act_0, act_1, d_pre_0, d_pre_1, side_by_side(moments, tokens))
    for e in range(experts):
        start = pl.multiple_of((e ^ lax.axis_index("expert")) * rows, rows)
        for at, value in enumerate(kept):
            cols = slice(at * rank, at * rank + value.shape[1])
            small[pl.ds(start, rows), cols] = value[e * rows : (e + 1) * rows]


def gradient_kernel(experts, sources, sizes, *refs):
    sides, refs = refs[: 2 * experts], refs[2 * experts :]
    smalls, refs = refs[:sources], refs[sources:]
    own, other, refs = refs[:3], refs[3:6], refs[6:]
    ids, back_in, out_hidden, grad_dn, grad_upper = refs[:5]
    (id_buf, back, result, dn_buf, up_buf, gain_buf, wide_buf, small, moments, turned, lows, grads,
     dn_out, up_out, small_sems, wide_sems, sems) = refs[5:]
    core = lax.axis_index("segment")
    place = lax.axis_index("dp")
    rows, slab = smalls[0].shape[0], sides[0].shape[3]
    replicas = sources // 2
    blocks = [side.shape[1] for side in sides[:experts]]
    starts = [sum(blocks[:step]) for step in range(experts)]
    rank = dn_buf.shape[1]
    columns = 256
    chunks = range(0, slab, columns)
    features = pl.ds(pl.multiple_of(place * slab, slab), slab)

    def weight_copies(up, gain_first, dn, gain_second):
        moves = (
            (up.at[:, features], up_buf),
            (gain_first.at[:, features], gain_buf.at[0]),
            (gain_second.at[:, features], gain_buf.at[1]),
            (dn.at[features, :], dn_buf),
        )
        return [
            pltpu.make_async_copy(source, target, sems.at[at])
            for at, (source, target) in enumerate(moves)
        ]

    early = [
        pltpu.make_async_copy(ids, id_buf, sems.at[4]),
        pltpu.make_async_copy(back_in, back, sems.at[5]),
    ]
    small_copies = [
        pltpu.make_async_copy(
            source, small.at[at * rows : (at + 1) * rows], small_sems.at[at]
        )
        for at, source in enumerate(smalls)
    ]
    wide_copies = [
        [
            pltpu.make_async_copy(
                side.at[:, :, :, col : col + columns],
                wide_buf.at[
                    at // experts,
                    :,
                    starts[at % experts] : starts[at % experts] + blocks[at % experts],
                    :,
                    col : col + columns,
                ],
                wide_sems.at[col // columns, at],
            )
            for at, side in enumerate(sides)
        ]
        for col in chunks
    ]
    for copy in early + small_copies:
        copy.start()

    @pl.when(core == 0)
    def _():
        for copy in weight_copies(own[1], own[2], other[0], other[2]):
            copy.start()

    @pl.when(core != 0)
    def _():
        for copy in weight_copies(other[1], other[2], own[0], own[2]):
            copy.start()

    for copies in wide_copies:
        for copy in copies:
            copy.start()
    for copy in early:
        copy.wait()
    unpack(sizes, id_buf, back, result)
    leaving = [pltpu.make_async_copy(result, out_hidden, sems.at[6])]
    leaving[0].start()
    for copy in small_copies + weight_copies(own[1], own[2], other[0], other[2]):
        copy.wait()

    def sliced(source, which, here):
        side, near = source // replicas, source % replicas
        at = [
            replicas - 1 + step if near == 0 else starts[step] + near - 1
            for step in range(experts)
        ]
        return jnp.concatenate([wide_buf[side, which, one, :, here] for one in at], axis=0)

    def moment(at, index):
        value = moments[at, index * 128 : (index + 1) * 128]
        return jnp.concatenate([value] * (columns // 128), axis=1)

    def work(first):
        held = lax.broadcasted_iota(jnp.int32, (128, 6 * 128), 0)
        wanted = lax.broadcasted_iota(jnp.int32, (128, 6 * 128), 1) // 128
        adds = (held // 3 == wanted).astype(jnp.float32).astype(jnp.bfloat16)
        moments[...] = matmul(small[:, 4 * rank :], adds)
        act, d_pre = (0, 2) if first else (1, 3)
        turned[0] = small[:, act * rank : (act + 1) * rank].T
        turned[1] = small[:, d_pre * rank : (d_pre + 1) * rank].T
        for index, col in enumerate(chunks):
            here = slice(col, col + columns)
            for copy in wide_copies[index]:
                copy.wait()
            ups = matmul(small[:, :rank], up_buf[:, here])
            scales = [gain_buf[at, :, here].astype(jnp.float32) for at in range(2)]
            if first:
                downs = matmul(small[:, 3 * rank : 4 * rank], dn_buf[here, :], TRANS_RHS)
            for source in range(sources):
                at = slice(source * rows, (source + 1) * rows)
                wide = sliced(source, 0, here).astype(jnp.float32)
                grad_in = sliced(source, 1, here)
                middle = (wide + ups[at]).astype(jnp.bfloat16).astype(jnp.float32)
                inverse = moment(at, 3)
                normed = (middle - moment(at, 2)) * inverse
                if first:
                    entered = (wide - moment(at, 0)) * moment(at, 1)
                    lows[index, at] = (entered * scales[0]).astype(jnp.bfloat16)
                    d_norm = downs[at] * scales[1]
                    grads[index, at] = (
                        grad_in.astype(jnp.float32)
                        + inverse * (d_norm - moment(at, 4) - normed * moment(at, 5))
                    ).astype(jnp.bfloat16)
                else:
                    lows[index, at] = (normed * scales[1]).astype(jnp.bfloat16)
                    grads[index, at] = grad_in
            dn_out[here, :] = matmul(turned[1], lows[index]).astype(jnp.bfloat16).T
            up_out[index] = matmul(turned[0], grads[index]).astype(jnp.bfloat16)
            for copy in out_copies(index, here):
                copy.start()

    def out_copies(index, here):
        return [
            pltpu.make_async_copy(
                dn_out.at[here, :], grad_dn.at[here, :], sems.at[7 + 2 * index]
            ),
            pltpu.make_async_copy(
                up_out.at[index], grad_upper.at[:, here], sems.at[8 + 2 * index]
            ),
        ]

    @pl.when(core == 0)
    def _():
        work(True)

    @pl.when(core != 0)
    def _():
        work(False)

    for index, col in enumerate(chunks):
        leaving += out_copies(index, slice(col, col + columns))
    for copy in leaving:
        copy.wait()


VMEM = pl.BlockSpec(memory_space=pltpu.VMEM)
HBM = pl.BlockSpec(memory_space=pltpu.HBM)


def call(kernel, name, grant, in_specs, outs, scratch=(), outs_in=VMEM, flops=0, moved=MIB):
    return pl.pallas_call(
        kernel,
        out_shape=tuple(jax.ShapeDtypeStruct(*out) for out in outs),
        in_specs=in_specs,
        out_specs=tuple(outs_in for _ in outs),
        scratch_shapes=list(scratch),
        compiler_params=pltpu.CompilerParams(vmem_limit_bytes=grant * MIB),
        cost_estimate=pl.CostEstimate(flops=flops, bytes_accessed=moved, transcendentals=0),
        name=name,
    )


def across(block, axis, distance):
    size = lax.axis_size(axis)
    return lax.ppermute(block, axis, [(i, i ^ distance) for i in range(size)])


def slab_route(replicas, pair, low):
    route = []
    for replica in range(replicas):
        for core in range(2):
            chip = 2 * core + ((replica & 1) ^ pair)
            route.append((2 * replica + core, 2 * chip + ((replica >> 1) ^ low)))
    return route


def on_device_two_phases(hidden_in, cotangent, cluster_ids, w_down, w_up, gain):
    experts = lax.axis_size("expert")
    replicas = lax.axis_size("dp")
    s_local, length, part = hidden_in.shape
    width = 2 * part
    capacity = 2 * s_local // experts
    slots = experts * capacity
    groups = 2 * experts
    rows = slots * length // groups
    tokens = experts * rows
    own = (w_down[0, 0], w_up[0, 0], gain[0])
    rank = own[0].shape[1]
    slab = width // replicas
    bf16, f32 = jnp.bfloat16, jnp.float32
    sizes = (length, capacity, slots)
    sections = ("expert", "segment")

    other = tuple(across(array, "segment", 1) for array in own)
    half = s_local * length // 2
    (send,) = call(
        functools.partial(pack_kernel, *sizes),
        "pack",
        60,
        [HBM] * 3,
        [((groups, 2, rows, part), bf16)],
        [
            pltpu.SMEM(cluster_ids.shape, jnp.int32),
            pltpu.VMEM((2,) + hidden_in.shape, bf16),
            pltpu.VMEM((groups, 2, rows, part), bf16),
            pltpu.SemaphoreType.DMA((5,)),
        ],
        outs_in=HBM,
    )(cluster_ids, hidden_in, cotangent)
    slabs = call(
        functools.partial(slab_kernel, *sizes),
        "slabs",
        60,
        [HBM] * 4,
        [((2 * half + 16, slab), bf16)] * 4,
        [
            pltpu.SMEM(cluster_ids.shape, jnp.int32),
            pltpu.VMEM((2,) + hidden_in.shape, bf16),
            pltpu.VMEM((2, 2 * half, part), bf16),
            pltpu.VMEM((2, 16, 128), bf16),
            pltpu.VMEM((4, 2 * half + 16, slab), bf16),
            pltpu.SemaphoreType.DMA((7,)),
        ],
        outs_in=HBM,
    )(cluster_ids, hidden_in, cotangent, send)
    recv = lax.all_to_all(send, sections, split_axis=0, concat_axis=0, tiled=True)
    recv = recv.reshape(experts, 2, 2, rows, part)
    slabs = [
        lax.ppermute(block, ("dp", "segment"), slab_route(replicas, turn // 2, turn % 2))
        for turn, block in enumerate(slabs)
    ]
    out, small = call(
        chain_kernel,
        "chain",
        50,
        [HBM] * 7,
        [((experts, 2, rows, part), bf16), ((tokens, 4 * rank + 128), bf16)],
        [
            pltpu.VMEM(recv.shape, bf16),
            pltpu.VMEM((2, width, rank), bf16),
            pltpu.VMEM((2, rank, width), bf16),
            pltpu.VMEM((2, 1, width), bf16),
            pltpu.VMEM((tokens, width), bf16),
            pltpu.VMEM((tokens, width), bf16),
            pltpu.VMEM((tokens, width), f32),
            pltpu.SemaphoreType.DMA((3, 3)),
        ],
        flops=7 * 2 * tokens * width * rank,
        moved=10 * MIB,
    )(recv, *own, *other)
    slices = call(
        functools.partial(repack_kernel, length, capacity),
        "repack",
        16,
        [VMEM] * 4 + [HBM] * 2,
        [((2, replicas - 1 + experts, rows, slab), bf16)]
        + [((2, replicas - 1, rows, slab), bf16)] * (experts - 1),
        [pltpu.SemaphoreType.DMA((experts,))],
    )(*slabs, recv, small)
    small, *slices = lax.optimization_barrier((small, *slices))
    mine = [slices[0]] + [across(slices[step], "expert", step) for step in range(1, experts)]
    mine[:2] = lax.optimization_barrier(tuple(mine[:2]))
    near = [small] + [across(small, "dp", step) for step in range(1, replicas - 1)]
    near[:2] = lax.optimization_barrier(tuple(near[:2]))
    last = across(near[0], "dp", replicas - 1)
    *near, mine[-1] = lax.optimization_barrier((*near, mine[-1]))
    near.append(last)
    theirs = [across(block, "segment", 1) for block in mine]
    smalls = near + [across(piece, "segment", 1) for piece in near]

    back = lax.all_to_all(
        out.reshape(groups, rows, part), sections, split_axis=0, concat_axis=0, tiled=True
    )

    sources = 2 * replicas
    all_tokens = sources * tokens
    out_hidden, grad_dn, grad_upper = call(
        functools.partial(gradient_kernel, experts, sources, sizes),
        "gradients",
        60,
        [HBM] * (2 * experts + sources + 8),
        [(hidden_in.shape, bf16), ((slab, rank), bf16), ((rank, slab), bf16)],
        [
            pltpu.SMEM(cluster_ids.shape, jnp.int32),
            pltpu.VMEM(back.shape, bf16),
            pltpu.VMEM(hidden_in.shape, bf16),
            pltpu.VMEM((slab, rank), bf16),
            pltpu.VMEM((rank, slab), bf16),
            pltpu.VMEM((2, 1, slab), bf16),
            pltpu.VMEM((2, 2, replicas * experts, rows, slab), bf16),
            pltpu.VMEM((all_tokens, 4 * rank + 128), bf16),
            pltpu.VMEM((all_tokens, 6 * 128), f32),
            pltpu.VMEM((2, rank, all_tokens), bf16),
            pltpu.VMEM((slab // 256, all_tokens, 256), bf16),
            pltpu.VMEM((slab // 256, all_tokens, 256), bf16),
            pltpu.VMEM((slab, rank), bf16),
            pltpu.VMEM((slab // 256, rank, 256), bf16),
            pltpu.SemaphoreType.DMA((sources,)),
            pltpu.SemaphoreType.DMA((slab // 256, 2 * experts)),
            pltpu.SemaphoreType.DMA((7 + 2 * (slab // 256),)),
        ],
        outs_in=HBM,
    )(*mine, *theirs, *smalls, *own, *other, cluster_ids, back)
    return (out_hidden, grad_dn[None, None], grad_upper[None, None])


def solution(mesh):
    two = dict(mesh.shape) == {"expert": 4, "dp": 4, "segment": 2}
    on_device = on_device_two_phases if two else on_device_pipelined
    return jax.shard_map(
        on_device,
        mesh=mesh,
        in_specs=(
            P(("expert", "dp"), None, "segment"),
            P(("expert", "dp"), None, "segment"),
            P(("expert", "dp")),
            P("expert", "segment", None, None),
            P("expert", "segment", None, None),
            P("expert", "segment", None),
        ),
        out_specs=(
            P(("expert", "dp"), None, "segment"),
            P("expert", "segment", "dp", None),
            P("expert", "segment", None, "dp"),
        ),
        check_vma=False,
    )
```

```python
import functools

import jax
import jax.numpy as jnp
from jax import lax
from jax.experimental import pallas as pl
from jax.experimental.pallas import tpu as pltpu
from jax.sharding import PartitionSpec as P

MICRO = 4


EPS = 1e-05
C_ZERO = 0.7978845608028654
C_ONE = 0.044715


def shifted(block, axis, distance):
    devices = range(lax.axis_size(axis))
    route = [(i - distance, i) for i in devices if i - distance in devices]
    return lax.ppermute(block, axis, route)


def from_root(block, axis, holder):
    block = jnp.where(lax.axis_index(axis) == holder, block, jnp.zeros_like(block))
    return lax.psum(block, axis)


def gelu_value(z):
    return 0.5 * z * (1.0 + jnp.tanh(C_ZERO * (z + C_ONE * z * z * z)))


def gelu_slope(z):
    tval = jnp.tanh(C_ZERO * (z + C_ONE * z * z * z))
    return 0.5 * (1.0 + tval) + 0.5 * z * (1.0 - tval * tval) * C_ZERO * (1.0 + 3.0 * C_ONE * z * z)


def normalize(hidden):
    wide = hidden.astype(jnp.float32)
    center = wide - jnp.mean(wide, axis=-1, keepdims=True)
    inverse = lax.rsqrt(jnp.mean(center * center, axis=-1, keepdims=True) + EPS)
    return (wide, center * inverse, inverse)


def phase_forward(hidden, w_dn, w_upper, scale):
    wide, normed, inverse = normalize(hidden)
    lowered = (normed * scale).astype(jnp.bfloat16)
    pre = jnp.dot(lowered, w_dn, preferred_element_type=jnp.float32)
    act = gelu_value(pre).astype(jnp.bfloat16)
    leaving = (wide + jnp.dot(act, w_upper, preferred_element_type=jnp.float32)).astype(
        jnp.bfloat16
    )
    return (leaving, pre)


def phase_backward(hidden, grad_in, pre, w_dn, w_upper, scale):
    wide, normed, inverse = normalize(hidden)
    lowered = (normed * scale).astype(jnp.bfloat16)
    act = gelu_value(pre).astype(jnp.bfloat16)
    d_act = jnp.dot(grad_in, w_upper.T, preferred_element_type=jnp.float32)
    d_pre = (d_act * gelu_slope(pre)).astype(jnp.bfloat16)
    d_low = jnp.dot(d_pre, w_dn.T, preferred_element_type=jnp.float32)
    d_norm = d_low * scale
    d_wide = inverse * (
        d_norm
        - jnp.mean(d_norm, axis=-1, keepdims=True)
        - normed * jnp.mean(d_norm * normed, axis=-1, keepdims=True)
    )
    grad_out = (grad_in.astype(jnp.float32) + d_wide).astype(jnp.bfloat16)
    return (grad_out, lowered, act, d_pre)


def put_slot(buffer, value, slot, valid):
    old_value = lax.dynamic_index_in_dim(buffer, slot, 0, keepdims=False)
    return lax.dynamic_update_index_in_dim(buffer, jnp.where(valid, value, old_value), slot, 0)


def on_device_pipelined(hidden_in, cotangent, cluster_ids, w_down, w_up, gain):
    experts = lax.axis_size("expert")
    phases = lax.axis_size("segment")
    phase = lax.axis_index("segment")
    s_local, length, quarter = hidden_in.shape
    capacity = 2 * s_local // experts
    slots = experts * capacity
    same = (cluster_ids[:, None] == cluster_ids[None, :]).astype(jnp.int32)
    earlier = jnp.sum(jnp.tril(same, -1), axis=1)
    target = cluster_ids * capacity + earlier
    place = (jnp.arange(slots, dtype=jnp.int32)[:, None] == target[None, :]).astype(jnp.bfloat16)

    def to_slots(local):
        flat = local.reshape(s_local, -1)
        moved = jnp.dot(place, flat, preferred_element_type=jnp.float32).astype(jnp.bfloat16)
        return moved.reshape((slots,) + local.shape[1:])

    full_in, full_cot = (
        lax.all_gather(hidden_in, "segment", axis=2, tiled=True),
        lax.all_gather(cotangent, "segment", axis=2, tiled=True),
    )
    slot_in, slot_cot = (
        lax.all_to_all(to_slots(full_in), "expert", split_axis=0, concat_axis=0, tiled=True),
        lax.all_to_all(to_slots(full_cot), "expert", split_axis=0, concat_axis=0, tiled=True),
    )
    width = slot_in.shape[2]
    micro_rows = slots * length // MICRO
    inputs = slot_in.reshape(MICRO, micro_rows, width)
    cots = slot_cot.reshape(MICRO, micro_rows, width)
    w_dn = w_down[0, 0]
    w_upper = w_up[0, 0]
    rank = w_dn.shape[1]
    scale = gain[0, 0].astype(jnp.float32)
    ticks = MICRO + phases - 1

    def forward_tick(tick, carry):
        received, saved, pres, results = carry
        which = tick - phase
        valid = (which >= 0) & (which < MICRO)
        slot = jnp.clip(which, 0, MICRO - 1)
        first = lax.dynamic_index_in_dim(inputs, jnp.minimum(tick, MICRO - 1), 0, keepdims=False)
        entering = jnp.where(phase == 0, first, received)
        leaving, pre = phase_forward(entering, w_dn, w_upper, scale)
        saved = put_slot(saved, entering, slot, valid)
        pres = put_slot(pres, pre, slot, valid)
        results = put_slot(results, leaving, slot, valid & (phase == phases - 1))
        received = shifted(leaving, "segment", 1)
        return (received, saved, pres, results)

    start = (
        jnp.zeros((micro_rows, width), jnp.bfloat16),
        jnp.zeros((MICRO, micro_rows, width), jnp.bfloat16),
        jnp.zeros((MICRO, micro_rows, rank), jnp.float32),
        jnp.zeros((MICRO, micro_rows, width), jnp.bfloat16),
    )
    received, saved, pres, results = lax.fori_loop(0, ticks, forward_tick, start)

    def backward_tick(tick, carry):
        received, lows, acts, dpres, grads = carry
        which = tick - (phases - 1 - phase)
        valid = (which >= 0) & (which < MICRO)
        slot = jnp.clip(which, 0, MICRO - 1)
        last = lax.dynamic_index_in_dim(cots, jnp.minimum(tick, MICRO - 1), 0, keepdims=False)
        grad_in = jnp.where(phase == phases - 1, last, received)
        hidden = lax.dynamic_index_in_dim(saved, slot, 0, keepdims=False)
        pre = lax.dynamic_index_in_dim(pres, slot, 0, keepdims=False)
        grad_out, lowered, act, d_pre = phase_backward(hidden, grad_in, pre, w_dn, w_upper, scale)
        lows = put_slot(lows, lowered, slot, valid)
        acts = put_slot(acts, act, slot, valid)
        dpres = put_slot(dpres, d_pre, slot, valid)
        grads = put_slot(grads, grad_in, slot, valid)
        received = shifted(grad_out, "segment", -1)
        return (received, lows, acts, dpres, grads)

    start_back = (
        jnp.zeros((micro_rows, width), jnp.bfloat16),
        jnp.zeros((MICRO, micro_rows, width), jnp.bfloat16),
        jnp.zeros((MICRO, micro_rows, rank), jnp.bfloat16),
        jnp.zeros((MICRO, micro_rows, rank), jnp.bfloat16),
        jnp.zeros((MICRO, micro_rows, width), jnp.bfloat16),
    )
    received, lows, acts, dpres, grads = lax.fori_loop(0, ticks, backward_tick, start_back)
    contract = (((0,), (0,)), ((), ()))
    grad_dn = lax.dot_general(
        lows.reshape(-1, width),
        dpres.reshape(-1, rank),
        contract,
        preferred_element_type=jnp.float32,
    )
    grad_upper = lax.dot_general(
        acts.reshape(-1, rank),
        grads.reshape(-1, width),
        contract,
        preferred_element_type=jnp.float32,
    )
    summed_dn, summed_upper = (
        lax.psum_scatter(
            grad_dn.astype(jnp.bfloat16), "dp", scatter_dimension=0, tiled=True
        ).astype(jnp.float32),
        lax.psum_scatter(
            grad_upper.astype(jnp.bfloat16), "dp", scatter_dimension=1, tiled=True
        ).astype(jnp.float32),
    )
    returned = from_root(results, "segment", phases - 1)
    returned = returned.reshape(slots, length, width)
    own = lax.dynamic_slice_in_dim(returned, phase * quarter, quarter, 2)
    back = lax.all_to_all(own, "expert", split_axis=0, concat_axis=0, tiled=True)
    out_hidden = jnp.dot(place.T, back.reshape(slots, -1), preferred_element_type=jnp.float32)
    out_hidden = out_hidden.astype(jnp.bfloat16).reshape(s_local, length, quarter)
    return (
        out_hidden,
        summed_dn.astype(jnp.bfloat16)[None, None],
        summed_upper.astype(jnp.bfloat16)[None, None],
    )


CHUNK = 512
MIB = 1024 * 1024
TRANS_RHS = (((1,), (1,)), ((), ()))
TRANS_LHS = (((0,), (0,)), ((), ()))


def matmul(left, right, dims=(((1,), (0,)), ((), ()))):
    return lax.dot_general(left, right, dims, preferred_element_type=jnp.float32)


def spread_ids(ids, shape, length):
    lane = lax.broadcasted_iota(jnp.int32, shape, 1)
    spread = jnp.zeros(shape, jnp.int32)
    for n in range(ids.shape[0]):
        spread = jnp.where(lane // length == n, ids[n], spread)
    return spread


def ranked(ids_row, length):
    tokens = ids_row.shape[1]
    kinds = lax.broadcasted_iota(jnp.int32, (8, tokens), 0)
    member = (kinds == ids_row).astype(jnp.float32)
    at_col = lax.broadcasted_iota(jnp.int32, (tokens, tokens), 0)
    at_row = lax.broadcasted_iota(jnp.int32, (tokens, tokens), 1)
    before = (lax.rem(at_col, length) == 0) & (at_col // length < at_row // length)
    counts = matmul(member.astype(jnp.bfloat16), before.astype(jnp.float32).astype(jnp.bfloat16))
    rank = jnp.sum(member * counts, axis=0, keepdims=True)
    total = jnp.sum(member, axis=1, keepdims=True) * (1.0 / length)
    lower = jnp.sum(jnp.where(kinds < ids_row, total, 0.0), axis=0, keepdims=True)
    return rank.astype(jnp.int32), lower.astype(jnp.int32)


def one_hot(target, rows):
    wanted = lax.broadcasted_iota(jnp.int32, (rows, target.shape[1]), 0)
    return (wanted == target).astype(jnp.float32).astype(jnp.bfloat16)


def placements(ids_row, length, capacity, slots):
    rank, lower = ranked(ids_row, length)
    token = lax.rem(lax.broadcasted_iota(jnp.int32, ids_row.shape, 1), length)
    place = rank + lower
    group = lax.rem(place, 2)
    per_core = capacity // 2
    packed = ((ids_row * 2 + group) * per_core + rank // 2) * length + token
    tokens = ids_row.shape[1]
    ordered = group * (tokens // 2) + (place // 2) * length + token
    return one_hot(packed, slots * length), one_hot(ordered, tokens)


def pack_kernel(length, capacity, slots, ids, hidden, cot, send, id_buf, buf, packed, sems):
    groups, _, rows, part = send.shape
    tokens = hidden.shape[0] * length
    arriving = [
        pltpu.make_async_copy(source, target, sems.at[at])
        for at, (source, target) in enumerate(
            ((ids, id_buf), (hidden, buf.at[0]), (cot, buf.at[1]))
        )
    ]
    leaving = [
        pltpu.make_async_copy(packed.at[:, at], send.at[:, at], sems.at[3 + at]) for at in range(2)
    ]
    for copy in arriving:
        copy.start()
    arriving[0].wait()
    ids_row = spread_ids(id_buf, (8, tokens), length)[:1]
    place, _ = placements(ids_row, length, capacity, slots)
    for which in range(2):
        arriving[1 + which].wait()
        moved = matmul(place, buf[which].reshape(tokens, part)).astype(jnp.bfloat16)
        for group in range(groups):
            packed[group, which] = moved[group * rows : (group + 1) * rows]
        leaving[which].start()
    for copy in leaving:
        copy.wait()


def slab_kernel(length, capacity, slots, ids, hidden, cot, _, *refs):
    slabs, refs = refs[:4], refs[4:]
    id_buf, buf, ordered, turned, out_slabs, sems = refs
    s_local, _, part = hidden.shape
    tokens = s_local * length
    slab = part // 2
    half = tokens // 2
    replica = lax.axis_index("dp")
    arriving = [
        pltpu.make_async_copy(source, target, sems.at[at])
        for at, (source, target) in enumerate(
            ((ids, id_buf), (hidden, buf.at[0]), (cot, buf.at[1]))
        )
    ]
    leaving = [
        pltpu.make_async_copy(out_slabs.at[at], slabs[at], sems.at[3 + at]) for at in range(4)
    ]
    for copy in arriving:
        copy.start()
    arriving[0].wait()
    ids_row = spread_ids(id_buf, (16, tokens), length)
    _, by_group = placements(ids_row[:1], length, capacity, slots)
    for group in range(2):
        mine = by_group[group * half : (group + 1) * half]
        clusters = matmul(ids_row.astype(jnp.float32).astype(jnp.bfloat16), mine, TRANS_RHS)
        turned[group] = jnp.concatenate(
            [clusters.astype(jnp.bfloat16), jnp.zeros((16, 128 - half), jnp.bfloat16)], axis=1
        )
    for which in range(2):
        arriving[1 + which].wait()
        flat = buf[which].reshape(tokens, part)
        ordered[which] = matmul(by_group, flat).astype(jnp.bfloat16)
    for turn in range(4):
        pair = (turn // 2) ^ (replica & 1)
        group = (turn % 2) ^ (replica >> 1)
        cols = pl.ds(pl.multiple_of(pair * slab, slab), slab)
        at = pl.ds(pl.multiple_of(group * half, half), half)
        for which in range(2):
            out_slabs[turn, which * half : (which + 1) * half] = ordered[which, at, cols]
        out_slabs[turn, tokens:] = jnp.zeros((16, slab), jnp.bfloat16)
        out_slabs[turn, tokens:, :128] = turned[group]
        leaving[turn].start()
    for copy in leaving:
        copy.wait()


def repack_kernel(length, capacity, *refs):
    slabs, recv, outs, sems = refs[:4], refs[4], refs[6:-1], refs[-1]
    kept, sent = outs[0], outs[1:]
    _, _, rows, slab = kept.shape
    experts = len(outs)
    half = (slabs[0].shape[0] - 16) // 2
    core, replica = lax.axis_index("segment"), lax.axis_index("dp")
    expert = lax.axis_index("expert")
    per_part = recv.shape[4] // slab
    part = replica // per_part
    cols = pl.ds(pl.multiple_of((replica - part * per_part) * slab, slab), slab)
    cuts = [
        pltpu.make_async_copy(
            recv.at[e, part, :, :, cols], kept.at[:, 3 + (e ^ expert)], sems.at[e]
        )
        for e in range(experts)
    ]
    for cut in cuts:
        cut.start()
    far_low = (replica >> 1) ^ core ^ 1

    def place_rows(held, near):
        ids_row = held[2 * half :, :128].astype(jnp.float32)[:1, :half].astype(jnp.int32)
        rank, _ = ranked(ids_row, length)
        token = lax.rem(lax.broadcasted_iota(jnp.int32, ids_row.shape, 1), length)
        step = ids_row ^ expert
        place = one_hot((step * (capacity // 2) + rank) * length + token, experts * rows)
        for which in range(2):
            moved = matmul(place, held[which * half : (which + 1) * half]).astype(jnp.bfloat16)
            kept[which, near - 1] = moved[:rows]
            for step_at, out in enumerate(sent):
                out[which, near - 1] = moved[(step_at + 1) * rows : (step_at + 2) * rows]

    place_rows(jnp.where(far_low == 1, slabs[1][...], slabs[0][...]), 2)
    for low in range(2):
        place_rows(slabs[2 + low][...], 1 + 2 * (low ^ (replica >> 1) ^ core))
    for cut in cuts:
        cut.wait()


def unpack(sizes, id_buf, back, out):
    length, capacity, slots = sizes
    groups, rows, width = back.shape
    s_local = out.shape[0]
    ids_row = spread_ids(id_buf, (8, s_local * length), length)[:1]
    place, _ = placements(ids_row, length, capacity, slots)
    moved = matmul(place, back[...].reshape(groups * rows, width), TRANS_LHS)
    out[...] = moved.astype(jnp.bfloat16).reshape(s_local, length, width)


def split_three(value):
    top = value.astype(jnp.bfloat16).astype(jnp.float32)
    mid = (value - top).astype(jnp.bfloat16).astype(jnp.float32)
    low = (value - top - mid).astype(jnp.bfloat16).astype(jnp.float32)
    return [top, mid, low]


def side_by_side(columns, tokens):
    lane = lax.broadcasted_iota(jnp.int32, (tokens, 128), 1)
    block = jnp.zeros((tokens, 128), jnp.float32)
    at = 0
    for column in columns:
        for piece in split_three(column):
            block = jnp.where(lane == at, piece, block)
            at += 1
    return block.astype(jnp.bfloat16)


def lanes(value):
    total = value[:, :128]
    for start in range(128, value.shape[1], 128):
        total = total + value[:, start : start + 128]
    return total


def row_sum(parts):
    return jnp.sum(parts, axis=1, keepdims=True)


def chain_kernel(
    recv_in, own_dn, own_up, own_gain, other_dn, other_up, other_gain,
    out, small,
    recv, dn_buf, up_buf, gain_buf, entering, middle, d_norms, sems,
):
    phase = lax.axis_index("segment")
    experts, phases, _, rows, part = recv.shape
    tokens = experts * rows
    width = phases * part
    rank = dn_buf.shape[2]
    own, other = (own_dn, own_up, own_gain), (other_dn, other_up, other_gain)

    def copies(sources, at):
        return [
            pltpu.make_async_copy(source, buffer.at[at], sems.at[at, which])
            for which, (source, buffer) in enumerate(zip(sources, (dn_buf, up_buf, gain_buf)))
        ]

    def fetch(at):
        for this in range(2):

            @pl.when(phase == this)
            def _():
                for copy in copies(own if at == this else other, at):
                    copy.start()

    arriving = [
        pltpu.make_async_copy(recv_in.at[:, :, at], recv.at[:, :, at], sems.at[2, at])
        for at in range(2)
    ]
    arriving[0].start()
    fetch(0)
    waits = [copies(own, at) for at in range(2)]
    cols = range(0, width, CHUNK)

    def block(which, col):
        half, start = col // part, col % part
        return jnp.concatenate(
            [recv[e, half, which, :, start : start + CHUNK] for e in range(experts)], axis=0
        )

    def inverse_of(ref, mean):
        total = jnp.zeros((tokens, 128), jnp.float32)
        for col in cols:
            center = ref[:, col : col + CHUNK].astype(jnp.float32) - mean
            total = total + lanes(center * center)
        return lax.rsqrt(row_sum(total) / width + EPS)

    def down(ref, mean, inverse, at):
        pre = jnp.zeros((tokens, rank), jnp.float32)
        for col in cols:
            here = slice(col, col + CHUNK)
            normed = (ref[:, here].astype(jnp.float32) - mean) * inverse
            lowered = (normed * gain_buf[at, :, here].astype(jnp.float32)).astype(jnp.bfloat16)
            pre = pre + matmul(lowered, dn_buf[at, here, :])
        return pre

    total = jnp.zeros((tokens, 128), jnp.float32)
    arriving[0].wait()
    for col in cols:
        value = block(0, col)
        entering[:, col : col + CHUNK] = value
        total = total + lanes(value.astype(jnp.float32))
    mean_0 = row_sum(total) / width
    inverse_0 = inverse_of(entering, mean_0)
    waits[0][0].wait()
    waits[0][2].wait()
    arriving[1].start()
    fetch(1)
    pre_0 = down(entering, mean_0, inverse_0, 0)
    act_0 = gelu_value(pre_0).astype(jnp.bfloat16)
    slope_0 = gelu_slope(pre_0)

    waits[0][1].wait()
    total = jnp.zeros((tokens, 128), jnp.float32)
    for col in cols:
        here = slice(col, col + CHUNK)
        value = entering[:, here].astype(jnp.float32) + matmul(act_0, up_buf[0, :, here])
        value = value.astype(jnp.bfloat16)
        middle[:, here] = value
        total = total + lanes(value.astype(jnp.float32))
    mean_1 = row_sum(total) / width
    inverse_1 = inverse_of(middle, mean_1)
    for copy in waits[1] + arriving[1:]:
        copy.wait()
    d_act = jnp.zeros((tokens, rank), jnp.float32)
    for col in cols:
        d_act = d_act + matmul(block(1, col), up_buf[1, :, col : col + CHUNK], TRANS_RHS)
    pre_1 = down(middle, mean_1, inverse_1, 1)
    act_1 = gelu_value(pre_1).astype(jnp.bfloat16)
    d_pre_1 = (d_act * gelu_slope(pre_1)).astype(jnp.bfloat16)

    total = jnp.zeros((tokens, 128), jnp.float32)
    cross = jnp.zeros((tokens, 128), jnp.float32)
    for col in cols:
        here = slice(col, col + CHUNK)
        wide = middle[:, here].astype(jnp.float32)
        d_norm = matmul(d_pre_1, dn_buf[1, here, :], TRANS_RHS)
        d_norm = d_norm * gain_buf[1, :, here].astype(jnp.float32)
        d_norms[:, here] = d_norm
        total = total + lanes(d_norm)
        cross = cross + lanes(d_norm * ((wide - mean_1) * inverse_1))
        leaving = (wide + matmul(act_1, up_buf[1, :, here])).astype(jnp.bfloat16)
        half, start = col // part, col % part
        for e in range(experts):
            out[e, half, :, start : start + CHUNK] = leaving[e * rows : (e + 1) * rows]
    shift = row_sum(total) / width
    along = row_sum(cross) / width
    d_act = jnp.zeros((tokens, rank), jnp.float32)
    for col in cols:
        here = slice(col, col + CHUNK)
        normed = (middle[:, here].astype(jnp.float32) - mean_1) * inverse_1
        grad = block(1, col).astype(jnp.float32) + inverse_1 * (
            d_norms[:, here] - shift - normed * along
        )
        d_act = d_act + matmul(grad.astype(jnp.bfloat16), up_buf[0, :, here], TRANS_RHS)
    d_pre_0 = (d_act * slope_0).astype(jnp.bfloat16)
    moments = (mean_0, inverse_0, mean_1, inverse_1, shift, along)
    kept = (act_0, act_1, d_pre_0, d_pre_1, side_by_side(moments, tokens))
    for e in range(experts):
        start = pl.multiple_of((e ^ lax.axis_index("expert")) * rows, rows)
        for at, value in enumerate(kept):
            cols = slice(at * rank, at * rank + value.shape[1])
            small[pl.ds(start, rows), cols] = value[e * rows : (e + 1) * rows]


def gradient_kernel(experts, sources, sizes, *refs):
    sides, refs = refs[: 2 * experts], refs[2 * experts :]
    smalls, refs = refs[:sources], refs[sources:]
    own, other, refs = refs[:3], refs[3:6], refs[6:]
    ids, back_in, out_hidden, grad_dn, grad_upper = refs[:5]
    (id_buf, back, result, dn_buf, up_buf, gain_buf, wide_buf, small, moments, turned, lows, grads,
     dn_out, up_out, small_sems, wide_sems, sems) = refs[5:]
    core = lax.axis_index("segment")
    place = lax.axis_index("dp")
    rows, slab = smalls[0].shape[0], sides[0].shape[3]
    replicas = sources // 2
    blocks = [side.shape[1] for side in sides[:experts]]
    starts = [sum(blocks[:step]) for step in range(experts)]
    rank = dn_buf.shape[1]
    columns = 256
    chunks = range(0, slab, columns)
    features = pl.ds(pl.multiple_of(place * slab, slab), slab)

    def weight_copies(up, gain_first, dn, gain_second):
        moves = (
            (up.at[:, features], up_buf),
            (gain_first.at[:, features], gain_buf.at[0]),
            (gain_second.at[:, features], gain_buf.at[1]),
            (dn.at[features, :], dn_buf),
        )
        return [
            pltpu.make_async_copy(source, target, sems.at[at])
            for at, (source, target) in enumerate(moves)
        ]

    early = [
        pltpu.make_async_copy(ids, id_buf, sems.at[4]),
        pltpu.make_async_copy(back_in, back, sems.at[5]),
    ]
    small_copies = [
        pltpu.make_async_copy(
            source, small.at[at * rows : (at + 1) * rows], small_sems.at[at]
        )
        for at, source in enumerate(smalls)
    ]
    wide_copies = [
        [
            pltpu.make_async_copy(
                side.at[:, :, :, col : col + columns],
                wide_buf.at[
                    at // experts,
                    :,
                    starts[at % experts] : starts[at % experts] + blocks[at % experts],
                    :,
                    col : col + columns,
                ],
                wide_sems.at[col // columns, at],
            )
            for at, side in enumerate(sides)
        ]
        for col in chunks
    ]
    for copy in early + small_copies:
        copy.start()

    @pl.when(core == 0)
    def _():
        for copy in weight_copies(own[1], own[2], other[0], other[2]):
            copy.start()

    @pl.when(core != 0)
    def _():
        for copy in weight_copies(other[1], other[2], own[0], own[2]):
            copy.start()

    for copies in wide_copies:
        for copy in copies:
            copy.start()
    for copy in early:
        copy.wait()
    unpack(sizes, id_buf, back, result)
    leaving = [pltpu.make_async_copy(result, out_hidden, sems.at[6])]
    leaving[0].start()
    for copy in small_copies + weight_copies(own[1], own[2], other[0], other[2]):
        copy.wait()

    def sliced(source, which, here):
        side, near = source // replicas, source % replicas
        at = [
            replicas - 1 + step if near == 0 else starts[step] + near - 1
            for step in range(experts)
        ]
        return jnp.concatenate([wide_buf[side, which, one, :, here] for one in at], axis=0)

    def moment(at, index):
        value = moments[at, index * 128 : (index + 1) * 128]
        return jnp.concatenate([value] * (columns // 128), axis=1)

    def work(first):
        held = lax.broadcasted_iota(jnp.int32, (128, 6 * 128), 0)
        wanted = lax.broadcasted_iota(jnp.int32, (128, 6 * 128), 1) // 128
        adds = (held // 3 == wanted).astype(jnp.float32).astype(jnp.bfloat16)
        moments[...] = matmul(small[:, 4 * rank :], adds)
        act, d_pre = (0, 2) if first else (1, 3)
        turned[0] = small[:, act * rank : (act + 1) * rank].T
        turned[1] = small[:, d_pre * rank : (d_pre + 1) * rank].T
        for index, col in enumerate(chunks):
            here = slice(col, col + columns)
            for copy in wide_copies[index]:
                copy.wait()
            ups = matmul(small[:, :rank], up_buf[:, here])
            scales = [gain_buf[at, :, here].astype(jnp.float32) for at in range(2)]
            if first:
                downs = matmul(small[:, 3 * rank : 4 * rank], dn_buf[here, :], TRANS_RHS)
            for source in range(sources):
                at = slice(source * rows, (source + 1) * rows)
                wide = sliced(source, 0, here).astype(jnp.float32)
                grad_in = sliced(source, 1, here)
                middle = (wide + ups[at]).astype(jnp.bfloat16).astype(jnp.float32)
                inverse = moment(at, 3)
                normed = (middle - moment(at, 2)) * inverse
                if first:
                    entered = (wide - moment(at, 0)) * moment(at, 1)
                    lows[index, at] = (entered * scales[0]).astype(jnp.bfloat16)
                    d_norm = downs[at] * scales[1]
                    grads[index, at] = (
                        grad_in.astype(jnp.float32)
                        + inverse * (d_norm - moment(at, 4) - normed * moment(at, 5))
                    ).astype(jnp.bfloat16)
                else:
                    lows[index, at] = (normed * scales[1]).astype(jnp.bfloat16)
                    grads[index, at] = grad_in
            dn_out[here, :] = matmul(turned[1], lows[index]).astype(jnp.bfloat16).T
            up_out[index] = matmul(turned[0], grads[index]).astype(jnp.bfloat16)
            for copy in out_copies(index, here):
                copy.start()

    def out_copies(index, here):
        return [
            pltpu.make_async_copy(
                dn_out.at[here, :], grad_dn.at[here, :], sems.at[7 + 2 * index]
            ),
            pltpu.make_async_copy(
                up_out.at[index], grad_upper.at[:, here], sems.at[8 + 2 * index]
            ),
        ]

    @pl.when(core == 0)
    def _():
        work(True)

    @pl.when(core != 0)
    def _():
        work(False)

    for index, col in enumerate(chunks):
        leaving += out_copies(index, slice(col, col + columns))
    for copy in leaving:
        copy.wait()


VMEM = pl.BlockSpec(memory_space=pltpu.VMEM)
HBM = pl.BlockSpec(memory_space=pltpu.HBM)


def call(kernel, name, grant, in_specs, outs, scratch=(), outs_in=VMEM, flops=0, moved=MIB):
    return pl.pallas_call(
        kernel,
        out_shape=tuple(jax.ShapeDtypeStruct(*out) for out in outs),
        in_specs=in_specs,
        out_specs=tuple(outs_in for _ in outs),
        scratch_shapes=list(scratch),
        compiler_params=pltpu.CompilerParams(vmem_limit_bytes=grant * MIB),
        cost_estimate=pl.CostEstimate(flops=flops, bytes_accessed=moved, transcendentals=0),
        name=name,
    )


def across(block, axis, distance):
    size = lax.axis_size(axis)
    return lax.ppermute(block, axis, [(i, i ^ distance) for i in range(size)])


def slab_route(replicas, pair, low):
    route = []
    for replica in range(replicas):
        for core in range(2):
            chip = 2 * core + ((replica & 1) ^ pair)
            route.append((2 * replica + core, 2 * chip + ((replica >> 1) ^ low)))
    return route


def on_device_two_phases(hidden_in, cotangent, cluster_ids, w_down, w_up, gain):
    experts = lax.axis_size("expert")
    replicas = lax.axis_size("dp")
    s_local, length, part = hidden_in.shape
    width = 2 * part
    capacity = 2 * s_local // experts
    slots = experts * capacity
    groups = 2 * experts
    rows = slots * length // groups
    tokens = experts * rows
    own = (w_down[0, 0], w_up[0, 0], gain[0])
    rank = own[0].shape[1]
    slab = width // replicas
    bf16, f32 = jnp.bfloat16, jnp.float32
    sizes = (length, capacity, slots)
    sections = ("expert", "segment")

    other = tuple(across(array, "segment", 1) for array in own)
    half = s_local * length // 2
    (send,) = call(
        functools.partial(pack_kernel, *sizes),
        "pack",
        60,
        [HBM] * 3,
        [((groups, 2, rows, part), bf16)],
        [
            pltpu.SMEM(cluster_ids.shape, jnp.int32),
            pltpu.VMEM((2,) + hidden_in.shape, bf16),
            pltpu.VMEM((groups, 2, rows, part), bf16),
            pltpu.SemaphoreType.DMA((5,)),
        ],
        outs_in=HBM,
    )(cluster_ids, hidden_in, cotangent)
    slabs = call(
        functools.partial(slab_kernel, *sizes),
        "slabs",
        60,
        [HBM] * 4,
        [((2 * half + 16, slab), bf16)] * 4,
        [
            pltpu.SMEM(cluster_ids.shape, jnp.int32),
            pltpu.VMEM((2,) + hidden_in.shape, bf16),
            pltpu.VMEM((2, 2 * half, part), bf16),
            pltpu.VMEM((2, 16, 128), bf16),
            pltpu.VMEM((4, 2 * half + 16, slab), bf16),
            pltpu.SemaphoreType.DMA((7,)),
        ],
        outs_in=HBM,
    )(cluster_ids, hidden_in, cotangent, send)
    recv = lax.all_to_all(send, sections, split_axis=0, concat_axis=0, tiled=True)
    recv = recv.reshape(experts, 2, 2, rows, part)
    slabs = [
        lax.ppermute(block, ("dp", "segment"), slab_route(replicas, turn // 2, turn % 2))
        for turn, block in enumerate(slabs)
    ]
    out, small = call(
        chain_kernel,
        "chain",
        50,
        [HBM] * 7,
        [((experts, 2, rows, part), bf16), ((tokens, 4 * rank + 128), bf16)],
        [
            pltpu.VMEM(recv.shape, bf16),
            pltpu.VMEM((2, width, rank), bf16),
            pltpu.VMEM((2, rank, width), bf16),
            pltpu.VMEM((2, 1, width), bf16),
            pltpu.VMEM((tokens, width), bf16),
            pltpu.VMEM((tokens, width), bf16),
            pltpu.VMEM((tokens, width), f32),
            pltpu.SemaphoreType.DMA((3, 3)),
        ],
        flops=7 * 2 * tokens * width * rank,
        moved=10 * MIB,
    )(recv, *own, *other)
    slices = call(
        functools.partial(repack_kernel, length, capacity),
        "repack",
        16,
        [VMEM] * 4 + [HBM] * 2,
        [((2, replicas - 1 + experts, rows, slab), bf16)]
        + [((2, replicas - 1, rows, slab), bf16)] * (experts - 1),
        [pltpu.SemaphoreType.DMA((experts,))],
    )(*slabs, recv, small)
    small, *slices = lax.optimization_barrier((small, *slices))
    mine = [slices[0]] + [across(slices[step], "expert", step) for step in range(1, experts)]
    mine[:2] = lax.optimization_barrier(tuple(mine[:2]))
    far = [across(small, "dp", step) for step in range(2, replicas)]
    small, out, mine[1] = lax.optimization_barrier((small, out, mine[1]))
    beside = across(small, "dp", 1)
    theirs = [across(block, "segment", 1) for block in mine]
    small, *far, theirs[-1] = lax.optimization_barrier((small, *far, theirs[-1]))
    near = [small, beside, *far]
    smalls = near + [across(piece, "segment", 1) for piece in near]

    back = lax.all_to_all(
        out.reshape(groups, rows, part), sections, split_axis=0, concat_axis=0, tiled=True
    )

    sources = 2 * replicas
    all_tokens = sources * tokens
    out_hidden, grad_dn, grad_upper = call(
        functools.partial(gradient_kernel, experts, sources, sizes),
        "gradients",
        60,
        [HBM] * (2 * experts + sources + 8),
        [(hidden_in.shape, bf16), ((slab, rank), bf16), ((rank, slab), bf16)],
        [
            pltpu.SMEM(cluster_ids.shape, jnp.int32),
            pltpu.VMEM(back.shape, bf16),
            pltpu.VMEM(hidden_in.shape, bf16),
            pltpu.VMEM((slab, rank), bf16),
            pltpu.VMEM((rank, slab), bf16),
            pltpu.VMEM((2, 1, slab), bf16),
            pltpu.VMEM((2, 2, replicas * experts, rows, slab), bf16),
            pltpu.VMEM((all_tokens, 4 * rank + 128), bf16),
            pltpu.VMEM((all_tokens, 6 * 128), f32),
            pltpu.VMEM((2, rank, all_tokens), bf16),
            pltpu.VMEM((slab // 256, all_tokens, 256), bf16),
            pltpu.VMEM((slab // 256, all_tokens, 256), bf16),
            pltpu.VMEM((slab, rank), bf16),
            pltpu.VMEM((slab // 256, rank, 256), bf16),
            pltpu.SemaphoreType.DMA((sources,)),
            pltpu.SemaphoreType.DMA((slab // 256, 2 * experts)),
            pltpu.SemaphoreType.DMA((7 + 2 * (slab // 256),)),
        ],
        outs_in=HBM,
    )(*mine, *theirs, *smalls, *own, *other, cluster_ids, back)
    return (out_hidden, grad_dn[None, None], grad_upper[None, None])


def solution(mesh):
    two = dict(mesh.shape) == {"expert": 4, "dp": 4, "segment": 2}
    on_device = on_device_two_phases if two else on_device_pipelined
    return jax.shard_map(
        on_device,
        mesh=mesh,
        in_specs=(
            P(("expert", "dp"), None, "segment"),
            P(("expert", "dp"), None, "segment"),
            P(("expert", "dp")),
            P("expert", "segment", None, None),
            P("expert", "segment", None, None),
            P("expert", "segment", None),
        ),
        out_specs=(
            P(("expert", "dp"), None, "segment"),
            P("expert", "segment", "dp", None),
            P("expert", "segment", None, "dp"),
        ),
        check_vma=False,
    )
```

```python
import functools

import jax
import jax.numpy as jnp
from jax import lax
from jax.experimental import pallas as pl
from jax.experimental.pallas import tpu as pltpu
from jax.sharding import PartitionSpec as P

MICRO = 4


EPS = 1e-05
C_ZERO = 0.7978845608028654
C_ONE = 0.044715


def shifted(block, axis, distance):
    devices = range(lax.axis_size(axis))
    route = [(i - distance, i) for i in devices if i - distance in devices]
    return lax.ppermute(block, axis, route)


def from_root(block, axis, holder):
    block = jnp.where(lax.axis_index(axis) == holder, block, jnp.zeros_like(block))
    return lax.psum(block, axis)


def gelu_value(z):
    return 0.5 * z * (1.0 + jnp.tanh(C_ZERO * (z + C_ONE * z * z * z)))


def gelu_slope(z):
    tval = jnp.tanh(C_ZERO * (z + C_ONE * z * z * z))
    return 0.5 * (1.0 + tval) + 0.5 * z * (1.0 - tval * tval) * C_ZERO * (1.0 + 3.0 * C_ONE * z * z)


def normalize(hidden):
    wide = hidden.astype(jnp.float32)
    center = wide - jnp.mean(wide, axis=-1, keepdims=True)
    inverse = lax.rsqrt(jnp.mean(center * center, axis=-1, keepdims=True) + EPS)
    return (wide, center * inverse, inverse)


def phase_forward(hidden, w_dn, w_upper, scale):
    wide, normed, inverse = normalize(hidden)
    lowered = (normed * scale).astype(jnp.bfloat16)
    pre = jnp.dot(lowered, w_dn, preferred_element_type=jnp.float32)
    act = gelu_value(pre).astype(jnp.bfloat16)
    leaving = (wide + jnp.dot(act, w_upper, preferred_element_type=jnp.float32)).astype(
        jnp.bfloat16
    )
    return (leaving, pre)


def phase_backward(hidden, grad_in, pre, w_dn, w_upper, scale):
    wide, normed, inverse = normalize(hidden)
    lowered = (normed * scale).astype(jnp.bfloat16)
    act = gelu_value(pre).astype(jnp.bfloat16)
    d_act = jnp.dot(grad_in, w_upper.T, preferred_element_type=jnp.float32)
    d_pre = (d_act * gelu_slope(pre)).astype(jnp.bfloat16)
    d_low = jnp.dot(d_pre, w_dn.T, preferred_element_type=jnp.float32)
    d_norm = d_low * scale
    d_wide = inverse * (
        d_norm
        - jnp.mean(d_norm, axis=-1, keepdims=True)
        - normed * jnp.mean(d_norm * normed, axis=-1, keepdims=True)
    )
    grad_out = (grad_in.astype(jnp.float32) + d_wide).astype(jnp.bfloat16)
    return (grad_out, lowered, act, d_pre)


def put_slot(buffer, value, slot, valid):
    old_value = lax.dynamic_index_in_dim(buffer, slot, 0, keepdims=False)
    return lax.dynamic_update_index_in_dim(buffer, jnp.where(valid, value, old_value), slot, 0)


def on_device_pipelined(hidden_in, cotangent, cluster_ids, w_down, w_up, gain):
    experts = lax.axis_size("expert")
    phases = lax.axis_size("segment")
    phase = lax.axis_index("segment")
    s_local, length, quarter = hidden_in.shape
    capacity = 2 * s_local // experts
    slots = experts * capacity
    same = (cluster_ids[:, None] == cluster_ids[None, :]).astype(jnp.int32)
    earlier = jnp.sum(jnp.tril(same, -1), axis=1)
    target = cluster_ids * capacity + earlier
    place = (jnp.arange(slots, dtype=jnp.int32)[:, None] == target[None, :]).astype(jnp.bfloat16)

    def to_slots(local):
        flat = local.reshape(s_local, -1)
        moved = jnp.dot(place, flat, preferred_element_type=jnp.float32).astype(jnp.bfloat16)
        return moved.reshape((slots,) + local.shape[1:])

    full_in, full_cot = (
        lax.all_gather(hidden_in, "segment", axis=2, tiled=True),
        lax.all_gather(cotangent, "segment", axis=2, tiled=True),
    )
    slot_in, slot_cot = (
        lax.all_to_all(to_slots(full_in), "expert", split_axis=0, concat_axis=0, tiled=True),
        lax.all_to_all(to_slots(full_cot), "expert", split_axis=0, concat_axis=0, tiled=True),
    )
    width = slot_in.shape[2]
    micro_rows = slots * length // MICRO
    inputs = slot_in.reshape(MICRO, micro_rows, width)
    cots = slot_cot.reshape(MICRO, micro_rows, width)
    w_dn = w_down[0, 0]
    w_upper = w_up[0, 0]
    rank = w_dn.shape[1]
    scale = gain[0, 0].astype(jnp.float32)
    ticks = MICRO + phases - 1

    def forward_tick(tick, carry):
        received, saved, pres, results = carry
        which = tick - phase
        valid = (which >= 0) & (which < MICRO)
        slot = jnp.clip(which, 0, MICRO - 1)
        first = lax.dynamic_index_in_dim(inputs, jnp.minimum(tick, MICRO - 1), 0, keepdims=False)
        entering = jnp.where(phase == 0, first, received)
        leaving, pre = phase_forward(entering, w_dn, w_upper, scale)
        saved = put_slot(saved, entering, slot, valid)
        pres = put_slot(pres, pre, slot, valid)
        results = put_slot(results, leaving, slot, valid & (phase == phases - 1))
        received = shifted(leaving, "segment", 1)
        return (received, saved, pres, results)

    start = (
        jnp.zeros((micro_rows, width), jnp.bfloat16),
        jnp.zeros((MICRO, micro_rows, width), jnp.bfloat16),
        jnp.zeros((MICRO, micro_rows, rank), jnp.float32),
        jnp.zeros((MICRO, micro_rows, width), jnp.bfloat16),
    )
    received, saved, pres, results = lax.fori_loop(0, ticks, forward_tick, start)

    def backward_tick(tick, carry):
        received, lows, acts, dpres, grads = carry
        which = tick - (phases - 1 - phase)
        valid = (which >= 0) & (which < MICRO)
        slot = jnp.clip(which, 0, MICRO - 1)
        last = lax.dynamic_index_in_dim(cots, jnp.minimum(tick, MICRO - 1), 0, keepdims=False)
        grad_in = jnp.where(phase == phases - 1, last, received)
        hidden = lax.dynamic_index_in_dim(saved, slot, 0, keepdims=False)
        pre = lax.dynamic_index_in_dim(pres, slot, 0, keepdims=False)
        grad_out, lowered, act, d_pre = phase_backward(hidden, grad_in, pre, w_dn, w_upper, scale)
        lows = put_slot(lows, lowered, slot, valid)
        acts = put_slot(acts, act, slot, valid)
        dpres = put_slot(dpres, d_pre, slot, valid)
        grads = put_slot(grads, grad_in, slot, valid)
        received = shifted(grad_out, "segment", -1)
        return (received, lows, acts, dpres, grads)

    start_back = (
        jnp.zeros((micro_rows, width), jnp.bfloat16),
        jnp.zeros((MICRO, micro_rows, width), jnp.bfloat16),
        jnp.zeros((MICRO, micro_rows, rank), jnp.bfloat16),
        jnp.zeros((MICRO, micro_rows, rank), jnp.bfloat16),
        jnp.zeros((MICRO, micro_rows, width), jnp.bfloat16),
    )
    received, lows, acts, dpres, grads = lax.fori_loop(0, ticks, backward_tick, start_back)
    contract = (((0,), (0,)), ((), ()))
    grad_dn = lax.dot_general(
        lows.reshape(-1, width),
        dpres.reshape(-1, rank),
        contract,
        preferred_element_type=jnp.float32,
    )
    grad_upper = lax.dot_general(
        acts.reshape(-1, rank),
        grads.reshape(-1, width),
        contract,
        preferred_element_type=jnp.float32,
    )
    summed_dn, summed_upper = (
        lax.psum_scatter(
            grad_dn.astype(jnp.bfloat16), "dp", scatter_dimension=0, tiled=True
        ).astype(jnp.float32),
        lax.psum_scatter(
            grad_upper.astype(jnp.bfloat16), "dp", scatter_dimension=1, tiled=True
        ).astype(jnp.float32),
    )
    returned = from_root(results, "segment", phases - 1)
    returned = returned.reshape(slots, length, width)
    own = lax.dynamic_slice_in_dim(returned, phase * quarter, quarter, 2)
    back = lax.all_to_all(own, "expert", split_axis=0, concat_axis=0, tiled=True)
    out_hidden = jnp.dot(place.T, back.reshape(slots, -1), preferred_element_type=jnp.float32)
    out_hidden = out_hidden.astype(jnp.bfloat16).reshape(s_local, length, quarter)
    return (
        out_hidden,
        summed_dn.astype(jnp.bfloat16)[None, None],
        summed_upper.astype(jnp.bfloat16)[None, None],
    )


CHUNK = 512
MIB = 1024 * 1024
TRANS_RHS = (((1,), (1,)), ((), ()))
TRANS_LHS = (((0,), (0,)), ((), ()))


def matmul(left, right, dims=(((1,), (0,)), ((), ()))):
    return lax.dot_general(left, right, dims, preferred_element_type=jnp.float32)


def spread_ids(ids, shape, length):
    lane = lax.broadcasted_iota(jnp.int32, shape, 1)
    spread = jnp.zeros(shape, jnp.int32)
    for n in range(ids.shape[0]):
        spread = jnp.where(lane // length == n, ids[n], spread)
    return spread


def ranked(ids_row, length):
    tokens = ids_row.shape[1]
    kinds = lax.broadcasted_iota(jnp.int32, (8, tokens), 0)
    member = (kinds == ids_row).astype(jnp.float32)
    at_col = lax.broadcasted_iota(jnp.int32, (tokens, tokens), 0)
    at_row = lax.broadcasted_iota(jnp.int32, (tokens, tokens), 1)
    before = (lax.rem(at_col, length) == 0) & (at_col // length < at_row // length)
    counts = matmul(member.astype(jnp.bfloat16), before.astype(jnp.float32).astype(jnp.bfloat16))
    rank = jnp.sum(member * counts, axis=0, keepdims=True)
    total = jnp.sum(member, axis=1, keepdims=True) * (1.0 / length)
    lower = jnp.sum(jnp.where(kinds < ids_row, total, 0.0), axis=0, keepdims=True)
    return rank.astype(jnp.int32), lower.astype(jnp.int32)


def one_hot(target, rows):
    wanted = lax.broadcasted_iota(jnp.int32, (rows, target.shape[1]), 0)
    return (wanted == target).astype(jnp.float32).astype(jnp.bfloat16)


def placements(ids_row, length, capacity, slots):
    rank, lower = ranked(ids_row, length)
    token = lax.rem(lax.broadcasted_iota(jnp.int32, ids_row.shape, 1), length)
    place = rank + lower
    group = lax.rem(place, 2)
    per_core = capacity // 2
    packed = ((ids_row * 2 + group) * per_core + rank // 2) * length + token
    tokens = ids_row.shape[1]
    ordered = group * (tokens // 2) + (place // 2) * length + token
    return one_hot(packed, slots * length), one_hot(ordered, tokens)


def pack_kernel(length, capacity, slots, ids, hidden, cot, send, id_buf, buf, packed, sems):
    groups, _, rows, part = send.shape
    tokens = hidden.shape[0] * length
    arriving = [
        pltpu.make_async_copy(source, target, sems.at[at])
        for at, (source, target) in enumerate(
            ((ids, id_buf), (hidden, buf.at[0]), (cot, buf.at[1]))
        )
    ]
    leaving = [
        pltpu.make_async_copy(packed.at[:, at], send.at[:, at], sems.at[3 + at]) for at in range(2)
    ]
    for copy in arriving:
        copy.start()
    arriving[0].wait()
    ids_row = spread_ids(id_buf, (8, tokens), length)[:1]
    place, _ = placements(ids_row, length, capacity, slots)
    for which in range(2):
        arriving[1 + which].wait()
        moved = matmul(place, buf[which].reshape(tokens, part)).astype(jnp.bfloat16)
        for group in range(groups):
            packed[group, which] = moved[group * rows : (group + 1) * rows]
        leaving[which].start()
    for copy in leaving:
        copy.wait()


def slab_kernel(length, capacity, slots, ids, hidden, cot, _, *refs):
    slabs, refs = refs[:4], refs[4:]
    id_buf, buf, ordered, turned, out_slabs, sems = refs
    s_local, _, part = hidden.shape
    tokens = s_local * length
    slab = part // 2
    half = tokens // 2
    replica = lax.axis_index("dp")
    arriving = [
        pltpu.make_async_copy(source, target, sems.at[at])
        for at, (source, target) in enumerate(
            ((ids, id_buf), (hidden, buf.at[0]), (cot, buf.at[1]))
        )
    ]
    leaving = [
        pltpu.make_async_copy(out_slabs.at[at], slabs[at], sems.at[3 + at]) for at in range(4)
    ]
    for copy in arriving:
        copy.start()
    arriving[0].wait()
    ids_row = spread_ids(id_buf, (16, tokens), length)
    _, by_group = placements(ids_row[:1], length, capacity, slots)
    for group in range(2):
        mine = by_group[group * half : (group + 1) * half]
        clusters = matmul(ids_row.astype(jnp.float32).astype(jnp.bfloat16), mine, TRANS_RHS)
        turned[group] = jnp.concatenate(
            [clusters.astype(jnp.bfloat16), jnp.zeros((16, 128 - half), jnp.bfloat16)], axis=1
        )
    for which in range(2):
        arriving[1 + which].wait()
        flat = buf[which].reshape(tokens, part)
        ordered[which] = matmul(by_group, flat).astype(jnp.bfloat16)
    for turn in range(4):
        pair = (turn // 2) ^ (replica & 1)
        group = (turn % 2) ^ (replica >> 1)
        cols = pl.ds(pl.multiple_of(pair * slab, slab), slab)
        at = pl.ds(pl.multiple_of(group * half, half), half)
        for which in range(2):
            out_slabs[turn, which * half : (which + 1) * half] = ordered[which, at, cols]
        out_slabs[turn, tokens:] = jnp.zeros((16, slab), jnp.bfloat16)
        out_slabs[turn, tokens:, :128] = turned[group]
        leaving[turn].start()
    for copy in leaving:
        copy.wait()


def repack_kernel(length, capacity, *refs):
    slabs, recv, outs, sems = refs[:4], refs[4], refs[6:-1], refs[-1]
    kept, sent = outs[0], outs[1:]
    _, _, rows, slab = kept.shape
    experts = len(outs)
    half = (slabs[0].shape[0] - 16) // 2
    core, replica = lax.axis_index("segment"), lax.axis_index("dp")
    expert = lax.axis_index("expert")
    per_part = recv.shape[4] // slab
    part = replica // per_part
    cols = pl.ds(pl.multiple_of((replica - part * per_part) * slab, slab), slab)
    cuts = [
        pltpu.make_async_copy(
            recv.at[e, part, :, :, cols], kept.at[:, 3 + (e ^ expert)], sems.at[e]
        )
        for e in range(experts)
    ]
    for cut in cuts:
        cut.start()
    far_low = (replica >> 1) ^ core ^ 1

    def place_rows(held, near):
        ids_row = held[2 * half :, :128].astype(jnp.float32)[:1, :half].astype(jnp.int32)
        rank, _ = ranked(ids_row, length)
        token = lax.rem(lax.broadcasted_iota(jnp.int32, ids_row.shape, 1), length)
        step = ids_row ^ expert
        place = one_hot((step * (capacity // 2) + rank) * length + token, experts * rows)
        for which in range(2):
            moved = matmul(place, held[which * half : (which + 1) * half]).astype(jnp.bfloat16)
            kept[which, near - 1] = moved[:rows]
            for step_at, out in enumerate(sent):
                out[which, near - 1] = moved[(step_at + 1) * rows : (step_at + 2) * rows]

    place_rows(jnp.where(far_low == 1, slabs[1][...], slabs[0][...]), 2)
    for low in range(2):
        place_rows(slabs[2 + low][...], 1 + 2 * (low ^ (replica >> 1) ^ core))
    for cut in cuts:
        cut.wait()


def unpack(sizes, id_buf, back, out):
    length, capacity, slots = sizes
    groups, rows, width = back.shape
    s_local = out.shape[0]
    ids_row = spread_ids(id_buf, (8, s_local * length), length)[:1]
    place, _ = placements(ids_row, length, capacity, slots)
    moved = matmul(place, back[...].reshape(groups * rows, width), TRANS_LHS)
    out[...] = moved.astype(jnp.bfloat16).reshape(s_local, length, width)


def split_three(value):
    top = value.astype(jnp.bfloat16).astype(jnp.float32)
    mid = (value - top).astype(jnp.bfloat16).astype(jnp.float32)
    low = (value - top - mid).astype(jnp.bfloat16).astype(jnp.float32)
    return [top, mid, low]


def side_by_side(columns, tokens):
    lane = lax.broadcasted_iota(jnp.int32, (tokens, 128), 1)
    block = jnp.zeros((tokens, 128), jnp.float32)
    at = 0
    for column in columns:
        for piece in split_three(column):
            block = jnp.where(lane == at, piece, block)
            at += 1
    return block.astype(jnp.bfloat16)


def lanes(value):
    total = value[:, :128]
    for start in range(128, value.shape[1], 128):
        total = total + value[:, start : start + 128]
    return total


def row_sum(parts):
    return jnp.sum(parts, axis=1, keepdims=True)


def chain_kernel(
    recv_in, own_dn, own_up, own_gain, other_dn, other_up, other_gain,
    out, small,
    recv, dn_buf, up_buf, gain_buf, entering, middle, d_norms, sems,
):
    phase = lax.axis_index("segment")
    experts, phases, _, rows, part = recv.shape
    tokens = experts * rows
    width = phases * part
    rank = dn_buf.shape[2]
    own, other = (own_dn, own_up, own_gain), (other_dn, other_up, other_gain)

    def copies(sources, at):
        return [
            pltpu.make_async_copy(source, buffer.at[at], sems.at[at, which])
            for which, (source, buffer) in enumerate(zip(sources, (dn_buf, up_buf, gain_buf)))
        ]

    def fetch(at):
        for this in range(2):

            @pl.when(phase == this)
            def _():
                for copy in copies(own if at == this else other, at):
                    copy.start()

    arriving = [
        pltpu.make_async_copy(recv_in.at[:, :, at], recv.at[:, :, at], sems.at[2, at])
        for at in range(2)
    ]
    arriving[0].start()
    fetch(0)
    waits = [copies(own, at) for at in range(2)]
    cols = range(0, width, CHUNK)

    def block(which, col):
        half, start = col // part, col % part
        return jnp.concatenate(
            [recv[e, half, which, :, start : start + CHUNK] for e in range(experts)], axis=0
        )

    def inverse_of(ref, mean):
        total = jnp.zeros((tokens, 128), jnp.float32)
        for col in cols:
            center = ref[:, col : col + CHUNK].astype(jnp.float32) - mean
            total = total + lanes(center * center)
        return lax.rsqrt(row_sum(total) / width + EPS)

    def down(ref, mean, inverse, at):
        pre = jnp.zeros((tokens, rank), jnp.float32)
        for col in cols:
            here = slice(col, col + CHUNK)
            normed = (ref[:, here].astype(jnp.float32) - mean) * inverse
            lowered = (normed * gain_buf[at, :, here].astype(jnp.float32)).astype(jnp.bfloat16)
            pre = pre + matmul(lowered, dn_buf[at, here, :])
        return pre

    total = jnp.zeros((tokens, 128), jnp.float32)
    arriving[0].wait()
    for col in cols:
        value = block(0, col)
        entering[:, col : col + CHUNK] = value
        total = total + lanes(value.astype(jnp.float32))
    mean_0 = row_sum(total) / width
    inverse_0 = inverse_of(entering, mean_0)
    waits[0][0].wait()
    waits[0][2].wait()
    arriving[1].start()
    fetch(1)
    pre_0 = down(entering, mean_0, inverse_0, 0)
    act_0 = gelu_value(pre_0).astype(jnp.bfloat16)
    slope_0 = gelu_slope(pre_0)

    waits[0][1].wait()
    total = jnp.zeros((tokens, 128), jnp.float32)
    for col in cols:
        here = slice(col, col + CHUNK)
        value = entering[:, here].astype(jnp.float32) + matmul(act_0, up_buf[0, :, here])
        value = value.astype(jnp.bfloat16)
        middle[:, here] = value
        total = total + lanes(value.astype(jnp.float32))
    mean_1 = row_sum(total) / width
    inverse_1 = inverse_of(middle, mean_1)
    for copy in waits[1] + arriving[1:]:
        copy.wait()
    d_act = jnp.zeros((tokens, rank), jnp.float32)
    for col in cols:
        d_act = d_act + matmul(block(1, col), up_buf[1, :, col : col + CHUNK], TRANS_RHS)
    pre_1 = down(middle, mean_1, inverse_1, 1)
    act_1 = gelu_value(pre_1).astype(jnp.bfloat16)
    d_pre_1 = (d_act * gelu_slope(pre_1)).astype(jnp.bfloat16)

    total = jnp.zeros((tokens, 128), jnp.float32)
    cross = jnp.zeros((tokens, 128), jnp.float32)
    for col in cols:
        here = slice(col, col + CHUNK)
        wide = middle[:, here].astype(jnp.float32)
        d_norm = matmul(d_pre_1, dn_buf[1, here, :], TRANS_RHS)
        d_norm = d_norm * gain_buf[1, :, here].astype(jnp.float32)
        d_norms[:, here] = d_norm
        total = total + lanes(d_norm)
        cross = cross + lanes(d_norm * ((wide - mean_1) * inverse_1))
        leaving = (wide + matmul(act_1, up_buf[1, :, here])).astype(jnp.bfloat16)
        half, start = col // part, col % part
        for e in range(experts):
            out[e, half, :, start : start + CHUNK] = leaving[e * rows : (e + 1) * rows]
    shift = row_sum(total) / width
    along = row_sum(cross) / width
    d_act = jnp.zeros((tokens, rank), jnp.float32)
    for col in cols:
        here = slice(col, col + CHUNK)
        normed = (middle[:, here].astype(jnp.float32) - mean_1) * inverse_1
        grad = block(1, col).astype(jnp.float32) + inverse_1 * (
            d_norms[:, here] - shift - normed * along
        )
        d_act = d_act + matmul(grad.astype(jnp.bfloat16), up_buf[0, :, here], TRANS_RHS)
    d_pre_0 = (d_act * slope_0).astype(jnp.bfloat16)
    moments = (mean_0, inverse_0, mean_1, inverse_1, shift, along)
    kept = (act_0, act_1, d_pre_0, d_pre_1, side_by_side(moments, tokens))
    for e in range(experts):
        start = pl.multiple_of((e ^ lax.axis_index("expert")) * rows, rows)
        for at, value in enumerate(kept):
            cols = slice(at * rank, at * rank + value.shape[1])
            small[pl.ds(start, rows), cols] = value[e * rows : (e + 1) * rows]


def gradient_kernel(experts, sources, sizes, *refs):
    sides, refs = refs[: 2 * experts], refs[2 * experts :]
    smalls, refs = refs[:sources], refs[sources:]
    own, other, refs = refs[:3], refs[3:6], refs[6:]
    ids, back_in, out_hidden, grad_dn, grad_upper = refs[:5]
    (id_buf, back, result, dn_buf, up_buf, gain_buf, wide_buf, small, moments, turned, lows, grads,
     dn_out, up_out, small_sems, wide_sems, sems) = refs[5:]
    core = lax.axis_index("segment")
    place = lax.axis_index("dp")
    rows, slab = smalls[0].shape[0], sides[0].shape[3]
    replicas = sources // 2
    blocks = [side.shape[1] for side in sides[:experts]]
    starts = [sum(blocks[:step]) for step in range(experts)]
    rank = dn_buf.shape[1]
    columns = 256
    chunks = range(0, slab, columns)
    features = pl.ds(pl.multiple_of(place * slab, slab), slab)

    def weight_copies(up, gain_first, dn, gain_second):
        moves = (
            (up.at[:, features], up_buf),
            (gain_first.at[:, features], gain_buf.at[0]),
            (gain_second.at[:, features], gain_buf.at[1]),
            (dn.at[features, :], dn_buf),
        )
        return [
            pltpu.make_async_copy(source, target, sems.at[at])
            for at, (source, target) in enumerate(moves)
        ]

    early = [
        pltpu.make_async_copy(ids, id_buf, sems.at[4]),
        pltpu.make_async_copy(back_in, back, sems.at[5]),
    ]
    small_copies = [
        pltpu.make_async_copy(
            source, small.at[at * rows : (at + 1) * rows], small_sems.at[at]
        )
        for at, source in enumerate(smalls)
    ]
    wide_copies = [
        [
            pltpu.make_async_copy(
                side.at[:, :, :, col : col + columns],
                wide_buf.at[
                    at // experts,
                    :,
                    starts[at % experts] : starts[at % experts] + blocks[at % experts],
                    :,
                    col : col + columns,
                ],
                wide_sems.at[col // columns, at],
            )
            for at, side in enumerate(sides)
        ]
        for col in chunks
    ]
    for copy in early + small_copies:
        copy.start()

    @pl.when(core == 0)
    def _():
        for copy in weight_copies(own[1], own[2], other[0], other[2]):
            copy.start()

    @pl.when(core != 0)
    def _():
        for copy in weight_copies(other[1], other[2], own[0], own[2]):
            copy.start()

    for copies in wide_copies:
        for copy in copies:
            copy.start()
    for copy in early:
        copy.wait()
    unpack(sizes, id_buf, back, result)
    leaving = [pltpu.make_async_copy(result, out_hidden, sems.at[6])]
    leaving[0].start()
    for copy in small_copies + weight_copies(own[1], own[2], other[0], other[2]):
        copy.wait()

    def sliced(source, which, here):
        side, near = source // replicas, source % replicas
        at = [
            replicas - 1 + step if near == 0 else starts[step] + near - 1
            for step in range(experts)
        ]
        return jnp.concatenate([wide_buf[side, which, one, :, here] for one in at], axis=0)

    def moment(at, index):
        value = moments[at, index * 128 : (index + 1) * 128]
        return jnp.concatenate([value] * (columns // 128), axis=1)

    def work(first):
        held = lax.broadcasted_iota(jnp.int32, (128, 6 * 128), 0)
        wanted = lax.broadcasted_iota(jnp.int32, (128, 6 * 128), 1) // 128
        adds = (held // 3 == wanted).astype(jnp.float32).astype(jnp.bfloat16)
        moments[...] = matmul(small[:, 4 * rank :], adds)
        act, d_pre = (0, 2) if first else (1, 3)
        turned[0] = small[:, act * rank : (act + 1) * rank].T
        turned[1] = small[:, d_pre * rank : (d_pre + 1) * rank].T
        for index, col in enumerate(chunks):
            here = slice(col, col + columns)
            for copy in wide_copies[index]:
                copy.wait()
            ups = matmul(small[:, :rank], up_buf[:, here])
            scales = [gain_buf[at, :, here].astype(jnp.float32) for at in range(2)]
            if first:
                downs = matmul(small[:, 3 * rank : 4 * rank], dn_buf[here, :], TRANS_RHS)
            for source in range(sources):
                at = slice(source * rows, (source + 1) * rows)
                wide = sliced(source, 0, here).astype(jnp.float32)
                grad_in = sliced(source, 1, here)
                middle = (wide + ups[at]).astype(jnp.bfloat16).astype(jnp.float32)
                inverse = moment(at, 3)
                normed = (middle - moment(at, 2)) * inverse
                if first:
                    entered = (wide - moment(at, 0)) * moment(at, 1)
                    lows[index, at] = (entered * scales[0]).astype(jnp.bfloat16)
                    d_norm = downs[at] * scales[1]
                    grads[index, at] = (
                        grad_in.astype(jnp.float32)
                        + inverse * (d_norm - moment(at, 4) - normed * moment(at, 5))
                    ).astype(jnp.bfloat16)
                else:
                    lows[index, at] = (normed * scales[1]).astype(jnp.bfloat16)
                    grads[index, at] = grad_in
            dn_out[here, :] = matmul(turned[1], lows[index]).astype(jnp.bfloat16).T
            up_out[index] = matmul(turned[0], grads[index]).astype(jnp.bfloat16)
            for copy in out_copies(index, here):
                copy.start()

    def out_copies(index, here):
        return [
            pltpu.make_async_copy(
                dn_out.at[here, :], grad_dn.at[here, :], sems.at[7 + 2 * index]
            ),
            pltpu.make_async_copy(
                up_out.at[index], grad_upper.at[:, here], sems.at[8 + 2 * index]
            ),
        ]

    @pl.when(core == 0)
    def _():
        work(True)

    @pl.when(core != 0)
    def _():
        work(False)

    for index, col in enumerate(chunks):
        leaving += out_copies(index, slice(col, col + columns))
    for copy in leaving:
        copy.wait()


VMEM = pl.BlockSpec(memory_space=pltpu.VMEM)
HBM = pl.BlockSpec(memory_space=pltpu.HBM)


def call(kernel, name, grant, in_specs, outs, scratch=(), outs_in=VMEM, flops=0, moved=MIB):
    return pl.pallas_call(
        kernel,
        out_shape=tuple(jax.ShapeDtypeStruct(*out) for out in outs),
        in_specs=in_specs,
        out_specs=tuple(outs_in for _ in outs),
        scratch_shapes=list(scratch),
        compiler_params=pltpu.CompilerParams(vmem_limit_bytes=grant * MIB),
        cost_estimate=pl.CostEstimate(flops=flops, bytes_accessed=moved, transcendentals=0),
        name=name,
    )


def across(block, axis, distance):
    size = lax.axis_size(axis)
    return lax.ppermute(block, axis, [(i, i ^ distance) for i in range(size)])


def slab_route(replicas, pair, low):
    route = []
    for replica in range(replicas):
        for core in range(2):
            chip = 2 * core + ((replica & 1) ^ pair)
            route.append((2 * replica + core, 2 * chip + ((replica >> 1) ^ low)))
    return route


def on_device_two_phases(hidden_in, cotangent, cluster_ids, w_down, w_up, gain):
    experts = lax.axis_size("expert")
    replicas = lax.axis_size("dp")
    s_local, length, part = hidden_in.shape
    width = 2 * part
    capacity = 2 * s_local // experts
    slots = experts * capacity
    groups = 2 * experts
    rows = slots * length // groups
    tokens = experts * rows
    own = (w_down[0, 0], w_up[0, 0], gain[0])
    rank = own[0].shape[1]
    slab = width // replicas
    bf16, f32 = jnp.bfloat16, jnp.float32
    sizes = (length, capacity, slots)
    sections = ("expert", "segment")

    other = tuple(across(array, "segment", 1) for array in own)
    half = s_local * length // 2
    (send,) = call(
        functools.partial(pack_kernel, *sizes),
        "pack",
        60,
        [HBM] * 3,
        [((groups, 2, rows, part), bf16)],
        [
            pltpu.SMEM(cluster_ids.shape, jnp.int32),
            pltpu.VMEM((2,) + hidden_in.shape, bf16),
            pltpu.VMEM((groups, 2, rows, part), bf16),
            pltpu.SemaphoreType.DMA((5,)),
        ],
        outs_in=HBM,
    )(cluster_ids, hidden_in, cotangent)
    slabs = call(
        functools.partial(slab_kernel, *sizes),
        "slabs",
        60,
        [HBM] * 4,
        [((2 * half + 16, slab), bf16)] * 4,
        [
            pltpu.SMEM(cluster_ids.shape, jnp.int32),
            pltpu.VMEM((2,) + hidden_in.shape, bf16),
            pltpu.VMEM((2, 2 * half, part), bf16),
            pltpu.VMEM((2, 16, 128), bf16),
            pltpu.VMEM((4, 2 * half + 16, slab), bf16),
            pltpu.SemaphoreType.DMA((7,)),
        ],
        outs_in=HBM,
    )(cluster_ids, hidden_in, cotangent, send)
    recv = lax.all_to_all(send, sections, split_axis=0, concat_axis=0, tiled=True)
    recv = recv.reshape(experts, 2, 2, rows, part)
    slabs = [
        lax.ppermute(block, ("dp", "segment"), slab_route(replicas, turn // 2, turn % 2))
        for turn, block in enumerate(slabs)
    ]
    out, small = call(
        chain_kernel,
        "chain",
        50,
        [HBM] * 7,
        [((experts, 2, rows, part), bf16), ((tokens, 4 * rank + 128), bf16)],
        [
            pltpu.VMEM(recv.shape, bf16),
            pltpu.VMEM((2, width, rank), bf16),
            pltpu.VMEM((2, rank, width), bf16),
            pltpu.VMEM((2, 1, width), bf16),
            pltpu.VMEM((tokens, width), bf16),
            pltpu.VMEM((tokens, width), bf16),
            pltpu.VMEM((tokens, width), f32),
            pltpu.SemaphoreType.DMA((3, 3)),
        ],
        flops=7 * 2 * tokens * width * rank,
        moved=10 * MIB,
    )(recv, *own, *other)
    slices = call(
        functools.partial(repack_kernel, length, capacity),
        "repack",
        16,
        [VMEM] * 4 + [HBM] * 2,
        [((2, replicas - 1 + experts, rows, slab), bf16)]
        + [((2, replicas - 1, rows, slab), bf16)] * (experts - 1),
        [pltpu.SemaphoreType.DMA((experts,))],
    )(*slabs, recv, small)
    small, *slices = lax.optimization_barrier((small, *slices))
    mine = [slices[0]] + [across(slices[step], "expert", step) for step in range(1, experts)]
    mine[:2] = lax.optimization_barrier(tuple(mine[:2]))
    near = [small] + [across(small, "dp", step) for step in range(1, replicas - 1)]
    *near[:2], out = lax.optimization_barrier((*near[:2], out))
    last = across(near[0], "dp", replicas - 1)
    *near, mine[-1] = lax.optimization_barrier((*near, mine[-1]))
    near.append(last)
    theirs = [across(block, "segment", 1) for block in mine]
    smalls = near + [across(piece, "segment", 1) for piece in near]

    back = lax.all_to_all(
        out.reshape(groups, rows, part), sections, split_axis=0, concat_axis=0, tiled=True
    )

    sources = 2 * replicas
    all_tokens = sources * tokens
    out_hidden, grad_dn, grad_upper = call(
        functools.partial(gradient_kernel, experts, sources, sizes),
        "gradients",
        60,
        [HBM] * (2 * experts + sources + 8),
        [(hidden_in.shape, bf16), ((slab, rank), bf16), ((rank, slab), bf16)],
        [
            pltpu.SMEM(cluster_ids.shape, jnp.int32),
            pltpu.VMEM(back.shape, bf16),
            pltpu.VMEM(hidden_in.shape, bf16),
            pltpu.VMEM((slab, rank), bf16),
            pltpu.VMEM((rank, slab), bf16),
            pltpu.VMEM((2, 1, slab), bf16),
            pltpu.VMEM((2, 2, replicas * experts, rows, slab), bf16),
            pltpu.VMEM((all_tokens, 4 * rank + 128), bf16),
            pltpu.VMEM((all_tokens, 6 * 128), f32),
            pltpu.VMEM((2, rank, all_tokens), bf16),
            pltpu.VMEM((slab // 256, all_tokens, 256), bf16),
            pltpu.VMEM((slab // 256, all_tokens, 256), bf16),
            pltpu.VMEM((slab, rank), bf16),
            pltpu.VMEM((slab // 256, rank, 256), bf16),
            pltpu.SemaphoreType.DMA((sources,)),
            pltpu.SemaphoreType.DMA((slab // 256, 2 * experts)),
            pltpu.SemaphoreType.DMA((7 + 2 * (slab // 256),)),
        ],
        outs_in=HBM,
    )(*mine, *theirs, *smalls, *own, *other, cluster_ids, back)
    return (out_hidden, grad_dn[None, None], grad_upper[None, None])


def solution(mesh):
    two = dict(mesh.shape) == {"expert": 4, "dp": 4, "segment": 2}
    on_device = on_device_two_phases if two else on_device_pipelined
    return jax.shard_map(
        on_device,
        mesh=mesh,
        in_specs=(
            P(("expert", "dp"), None, "segment"),
            P(("expert", "dp"), None, "segment"),
            P(("expert", "dp")),
            P("expert", "segment", None, None),
            P("expert", "segment", None, None),
            P("expert", "segment", None),
        ),
        out_specs=(
            P(("expert", "dp"), None, "segment"),
            P("expert", "segment", "dp", None),
            P("expert", "segment", None, "dp"),
        ),
        check_vma=False,
    )
```

```python
import functools

import jax
import jax.numpy as jnp
from jax import lax
from jax.experimental import pallas as pl
from jax.experimental.pallas import tpu as pltpu
from jax.sharding import PartitionSpec as P

MICRO = 4


EPS = 1e-05
C_ZERO = 0.7978845608028654
C_ONE = 0.044715


def shifted(block, axis, distance):
    devices = range(lax.axis_size(axis))
    route = [(i - distance, i) for i in devices if i - distance in devices]
    return lax.ppermute(block, axis, route)


def from_root(block, axis, holder):
    block = jnp.where(lax.axis_index(axis) == holder, block, jnp.zeros_like(block))
    return lax.psum(block, axis)


def gelu_value(z):
    return 0.5 * z * (1.0 + jnp.tanh(C_ZERO * (z + C_ONE * z * z * z)))


def gelu_slope(z):
    tval = jnp.tanh(C_ZERO * (z + C_ONE * z * z * z))
    return 0.5 * (1.0 + tval) + 0.5 * z * (1.0 - tval * tval) * C_ZERO * (1.0 + 3.0 * C_ONE * z * z)


def normalize(hidden):
    wide = hidden.astype(jnp.float32)
    center = wide - jnp.mean(wide, axis=-1, keepdims=True)
    inverse = lax.rsqrt(jnp.mean(center * center, axis=-1, keepdims=True) + EPS)
    return (wide, center * inverse, inverse)


def phase_forward(hidden, w_dn, w_upper, scale):
    wide, normed, inverse = normalize(hidden)
    lowered = (normed * scale).astype(jnp.bfloat16)
    pre = jnp.dot(lowered, w_dn, preferred_element_type=jnp.float32)
    act = gelu_value(pre).astype(jnp.bfloat16)
    leaving = (wide + jnp.dot(act, w_upper, preferred_element_type=jnp.float32)).astype(
        jnp.bfloat16
    )
    return (leaving, pre)


def phase_backward(hidden, grad_in, pre, w_dn, w_upper, scale):
    wide, normed, inverse = normalize(hidden)
    lowered = (normed * scale).astype(jnp.bfloat16)
    act = gelu_value(pre).astype(jnp.bfloat16)
    d_act = jnp.dot(grad_in, w_upper.T, preferred_element_type=jnp.float32)
    d_pre = (d_act * gelu_slope(pre)).astype(jnp.bfloat16)
    d_low = jnp.dot(d_pre, w_dn.T, preferred_element_type=jnp.float32)
    d_norm = d_low * scale
    d_wide = inverse * (
        d_norm
        - jnp.mean(d_norm, axis=-1, keepdims=True)
        - normed * jnp.mean(d_norm * normed, axis=-1, keepdims=True)
    )
    grad_out = (grad_in.astype(jnp.float32) + d_wide).astype(jnp.bfloat16)
    return (grad_out, lowered, act, d_pre)


def put_slot(buffer, value, slot, valid):
    old_value = lax.dynamic_index_in_dim(buffer, slot, 0, keepdims=False)
    return lax.dynamic_update_index_in_dim(buffer, jnp.where(valid, value, old_value), slot, 0)


def on_device_pipelined(hidden_in, cotangent, cluster_ids, w_down, w_up, gain):
    experts = lax.axis_size("expert")
    phases = lax.axis_size("segment")
    phase = lax.axis_index("segment")
    s_local, length, quarter = hidden_in.shape
    capacity = 2 * s_local // experts
    slots = experts * capacity
    same = (cluster_ids[:, None] == cluster_ids[None, :]).astype(jnp.int32)
    earlier = jnp.sum(jnp.tril(same, -1), axis=1)
    target = cluster_ids * capacity + earlier
    place = (jnp.arange(slots, dtype=jnp.int32)[:, None] == target[None, :]).astype(jnp.bfloat16)

    def to_slots(local):
        flat = local.reshape(s_local, -1)
        moved = jnp.dot(place, flat, preferred_element_type=jnp.float32).astype(jnp.bfloat16)
        return moved.reshape((slots,) + local.shape[1:])

    full_in, full_cot = (
        lax.all_gather(hidden_in, "segment", axis=2, tiled=True),
        lax.all_gather(cotangent, "segment", axis=2, tiled=True),
    )
    slot_in, slot_cot = (
        lax.all_to_all(to_slots(full_in), "expert", split_axis=0, concat_axis=0, tiled=True),
        lax.all_to_all(to_slots(full_cot), "expert", split_axis=0, concat_axis=0, tiled=True),
    )
    width = slot_in.shape[2]
    micro_rows = slots * length // MICRO
    inputs = slot_in.reshape(MICRO, micro_rows, width)
    cots = slot_cot.reshape(MICRO, micro_rows, width)
    w_dn = w_down[0, 0]
    w_upper = w_up[0, 0]
    rank = w_dn.shape[1]
    scale = gain[0, 0].astype(jnp.float32)
    ticks = MICRO + phases - 1

    def forward_tick(tick, carry):
        received, saved, pres, results = carry
        which = tick - phase
        valid = (which >= 0) & (which < MICRO)
        slot = jnp.clip(which, 0, MICRO - 1)
        first = lax.dynamic_index_in_dim(inputs, jnp.minimum(tick, MICRO - 1), 0, keepdims=False)
        entering = jnp.where(phase == 0, first, received)
        leaving, pre = phase_forward(entering, w_dn, w_upper, scale)
        saved = put_slot(saved, entering, slot, valid)
        pres = put_slot(pres, pre, slot, valid)
        results = put_slot(results, leaving, slot, valid & (phase == phases - 1))
        received = shifted(leaving, "segment", 1)
        return (received, saved, pres, results)

    start = (
        jnp.zeros((micro_rows, width), jnp.bfloat16),
        jnp.zeros((MICRO, micro_rows, width), jnp.bfloat16),
        jnp.zeros((MICRO, micro_rows, rank), jnp.float32),
        jnp.zeros((MICRO, micro_rows, width), jnp.bfloat16),
    )
    received, saved, pres, results = lax.fori_loop(0, ticks, forward_tick, start)

    def backward_tick(tick, carry):
        received, lows, acts, dpres, grads = carry
        which = tick - (phases - 1 - phase)
        valid = (which >= 0) & (which < MICRO)
        slot = jnp.clip(which, 0, MICRO - 1)
        last = lax.dynamic_index_in_dim(cots, jnp.minimum(tick, MICRO - 1), 0, keepdims=False)
        grad_in = jnp.where(phase == phases - 1, last, received)
        hidden = lax.dynamic_index_in_dim(saved, slot, 0, keepdims=False)
        pre = lax.dynamic_index_in_dim(pres, slot, 0, keepdims=False)
        grad_out, lowered, act, d_pre = phase_backward(hidden, grad_in, pre, w_dn, w_upper, scale)
        lows = put_slot(lows, lowered, slot, valid)
        acts = put_slot(acts, act, slot, valid)
        dpres = put_slot(dpres, d_pre, slot, valid)
        grads = put_slot(grads, grad_in, slot, valid)
        received = shifted(grad_out, "segment", -1)
        return (received, lows, acts, dpres, grads)

    start_back = (
        jnp.zeros((micro_rows, width), jnp.bfloat16),
        jnp.zeros((MICRO, micro_rows, width), jnp.bfloat16),
        jnp.zeros((MICRO, micro_rows, rank), jnp.bfloat16),
        jnp.zeros((MICRO, micro_rows, rank), jnp.bfloat16),
        jnp.zeros((MICRO, micro_rows, width), jnp.bfloat16),
    )
    received, lows, acts, dpres, grads = lax.fori_loop(0, ticks, backward_tick, start_back)
    contract = (((0,), (0,)), ((), ()))
    grad_dn = lax.dot_general(
        lows.reshape(-1, width),
        dpres.reshape(-1, rank),
        contract,
        preferred_element_type=jnp.float32,
    )
    grad_upper = lax.dot_general(
        acts.reshape(-1, rank),
        grads.reshape(-1, width),
        contract,
        preferred_element_type=jnp.float32,
    )
    summed_dn, summed_upper = (
        lax.psum_scatter(
            grad_dn.astype(jnp.bfloat16), "dp", scatter_dimension=0, tiled=True
        ).astype(jnp.float32),
        lax.psum_scatter(
            grad_upper.astype(jnp.bfloat16), "dp", scatter_dimension=1, tiled=True
        ).astype(jnp.float32),
    )
    returned = from_root(results, "segment", phases - 1)
    returned = returned.reshape(slots, length, width)
    own = lax.dynamic_slice_in_dim(returned, phase * quarter, quarter, 2)
    back = lax.all_to_all(own, "expert", split_axis=0, concat_axis=0, tiled=True)
    out_hidden = jnp.dot(place.T, back.reshape(slots, -1), preferred_element_type=jnp.float32)
    out_hidden = out_hidden.astype(jnp.bfloat16).reshape(s_local, length, quarter)
    return (
        out_hidden,
        summed_dn.astype(jnp.bfloat16)[None, None],
        summed_upper.astype(jnp.bfloat16)[None, None],
    )


CHUNK = 512
MIB = 1024 * 1024
TRANS_RHS = (((1,), (1,)), ((), ()))
TRANS_LHS = (((0,), (0,)), ((), ()))


def matmul(left, right, dims=(((1,), (0,)), ((), ()))):
    return lax.dot_general(left, right, dims, preferred_element_type=jnp.float32)


def spread_ids(ids, shape, length):
    lane = lax.broadcasted_iota(jnp.int32, shape, 1)
    spread = jnp.zeros(shape, jnp.int32)
    for n in range(ids.shape[0]):
        spread = jnp.where(lane // length == n, ids[n], spread)
    return spread


def ranked(ids_row, length):
    tokens = ids_row.shape[1]
    kinds = lax.broadcasted_iota(jnp.int32, (8, tokens), 0)
    member = (kinds == ids_row).astype(jnp.float32)
    at_col = lax.broadcasted_iota(jnp.int32, (tokens, tokens), 0)
    at_row = lax.broadcasted_iota(jnp.int32, (tokens, tokens), 1)
    before = (lax.rem(at_col, length) == 0) & (at_col // length < at_row // length)
    counts = matmul(member.astype(jnp.bfloat16), before.astype(jnp.float32).astype(jnp.bfloat16))
    rank = jnp.sum(member * counts, axis=0, keepdims=True)
    total = jnp.sum(member, axis=1, keepdims=True) * (1.0 / length)
    lower = jnp.sum(jnp.where(kinds < ids_row, total, 0.0), axis=0, keepdims=True)
    return rank.astype(jnp.int32), lower.astype(jnp.int32)


def one_hot(target, rows):
    wanted = lax.broadcasted_iota(jnp.int32, (rows, target.shape[1]), 0)
    return (wanted == target).astype(jnp.float32).astype(jnp.bfloat16)


def placements(ids_row, length, capacity, slots):
    rank, lower = ranked(ids_row, length)
    token = lax.rem(lax.broadcasted_iota(jnp.int32, ids_row.shape, 1), length)
    place = rank + lower
    group = lax.rem(place, 2)
    per_core = capacity // 2
    packed = ((ids_row * 2 + group) * per_core + rank // 2) * length + token
    tokens = ids_row.shape[1]
    ordered = group * (tokens // 2) + (place // 2) * length + token
    return one_hot(packed, slots * length), one_hot(ordered, tokens)


def pack_kernel(length, capacity, slots, ids, hidden, cot, send, id_buf, buf, packed, sems):
    groups, _, rows, part = send.shape
    tokens = hidden.shape[0] * length
    arriving = [
        pltpu.make_async_copy(source, target, sems.at[at])
        for at, (source, target) in enumerate(
            ((ids, id_buf), (hidden, buf.at[0]), (cot, buf.at[1]))
        )
    ]
    leaving = [
        pltpu.make_async_copy(packed.at[:, at], send.at[:, at], sems.at[3 + at]) for at in range(2)
    ]
    for copy in arriving:
        copy.start()
    arriving[0].wait()
    ids_row = spread_ids(id_buf, (8, tokens), length)[:1]
    place, _ = placements(ids_row, length, capacity, slots)
    for which in range(2):
        arriving[1 + which].wait()
        moved = matmul(place, buf[which].reshape(tokens, part)).astype(jnp.bfloat16)
        for group in range(groups):
            packed[group, which] = moved[group * rows : (group + 1) * rows]
        leaving[which].start()
    for copy in leaving:
        copy.wait()


def slab_kernel(length, capacity, slots, ids, hidden, cot, _, *refs):
    slabs, refs = refs[:4], refs[4:]
    id_buf, buf, ordered, turned, out_slabs, sems = refs
    s_local, _, part = hidden.shape
    tokens = s_local * length
    slab = part // 2
    half = tokens // 2
    replica = lax.axis_index("dp")
    arriving = [
        pltpu.make_async_copy(source, target, sems.at[at])
        for at, (source, target) in enumerate(
            ((ids, id_buf), (hidden, buf.at[0]), (cot, buf.at[1]))
        )
    ]
    leaving = [
        pltpu.make_async_copy(out_slabs.at[at], slabs[at], sems.at[3 + at]) for at in range(4)
    ]
    for copy in arriving:
        copy.start()
    arriving[0].wait()
    ids_row = spread_ids(id_buf, (16, tokens), length)
    _, by_group = placements(ids_row[:1], length, capacity, slots)
    for group in range(2):
        mine = by_group[group * half : (group + 1) * half]
        clusters = matmul(ids_row.astype(jnp.float32).astype(jnp.bfloat16), mine, TRANS_RHS)
        turned[group] = jnp.concatenate(
            [clusters.astype(jnp.bfloat16), jnp.zeros((16, 128 - half), jnp.bfloat16)], axis=1
        )
    for which in range(2):
        arriving[1 + which].wait()
        flat = buf[which].reshape(tokens, part)
        ordered[which] = matmul(by_group, flat).astype(jnp.bfloat16)
    for turn in range(4):
        pair = (turn // 2) ^ (replica & 1)
        group = (turn % 2) ^ (replica >> 1)
        cols = pl.ds(pl.multiple_of(pair * slab, slab), slab)
        at = pl.ds(pl.multiple_of(group * half, half), half)
        for which in range(2):
            out_slabs[turn, which * half : (which + 1) * half] = ordered[which, at, cols]
        out_slabs[turn, tokens:] = jnp.zeros((16, slab), jnp.bfloat16)
        out_slabs[turn, tokens:, :128] = turned[group]
        leaving[turn].start()
    for copy in leaving:
        copy.wait()


def repack_kernel(length, capacity, *refs):
    slabs, recv, outs, sems = refs[:4], refs[4], refs[6:-1], refs[-1]
    kept, sent = outs[0], outs[1:]
    _, _, rows, slab = kept.shape
    experts = len(outs)
    half = (slabs[0].shape[0] - 16) // 2
    core, replica = lax.axis_index("segment"), lax.axis_index("dp")
    expert = lax.axis_index("expert")
    per_part = recv.shape[4] // slab
    part = replica // per_part
    cols = pl.ds(pl.multiple_of((replica - part * per_part) * slab, slab), slab)
    cuts = [
        pltpu.make_async_copy(
            recv.at[e, part, :, :, cols], kept.at[:, 3 + (e ^ expert)], sems.at[e]
        )
        for e in range(experts)
    ]
    for cut in cuts:
        cut.start()
    far_low = (replica >> 1) ^ core ^ 1

    def place_rows(held, near):
        ids_row = held[2 * half :, :128].astype(jnp.float32)[:1, :half].astype(jnp.int32)
        rank, _ = ranked(ids_row, length)
        token = lax.rem(lax.broadcasted_iota(jnp.int32, ids_row.shape, 1), length)
        step = ids_row ^ expert
        place = one_hot((step * (capacity // 2) + rank) * length + token, experts * rows)
        for which in range(2):
            moved = matmul(place, held[which * half : (which + 1) * half]).astype(jnp.bfloat16)
            kept[which, near - 1] = moved[:rows]
            for step_at, out in enumerate(sent):
                out[which, near - 1] = moved[(step_at + 1) * rows : (step_at + 2) * rows]

    place_rows(jnp.where(far_low == 1, slabs[1][...], slabs[0][...]), 2)
    for low in range(2):
        place_rows(slabs[2 + low][...], 1 + 2 * (low ^ (replica >> 1) ^ core))
    for cut in cuts:
        cut.wait()


def unpack(sizes, id_buf, back, out):
    length, capacity, slots = sizes
    groups, rows, width = back.shape
    s_local = out.shape[0]
    ids_row = spread_ids(id_buf, (8, s_local * length), length)[:1]
    place, _ = placements(ids_row, length, capacity, slots)
    moved = matmul(place, back[...].reshape(groups * rows, width), TRANS_LHS)
    out[...] = moved.astype(jnp.bfloat16).reshape(s_local, length, width)


def split_three(value):
    top = value.astype(jnp.bfloat16).astype(jnp.float32)
    mid = (value - top).astype(jnp.bfloat16).astype(jnp.float32)
    low = (value - top - mid).astype(jnp.bfloat16).astype(jnp.float32)
    return [top, mid, low]


def side_by_side(columns, tokens):
    lane = lax.broadcasted_iota(jnp.int32, (tokens, 128), 1)
    block = jnp.zeros((tokens, 128), jnp.float32)
    at = 0
    for column in columns:
        for piece in split_three(column):
            block = jnp.where(lane == at, piece, block)
            at += 1
    return block.astype(jnp.bfloat16)


def lanes(value):
    total = value[:, :128]
    for start in range(128, value.shape[1], 128):
        total = total + value[:, start : start + 128]
    return total


def row_sum(parts):
    return jnp.sum(parts, axis=1, keepdims=True)


def chain_kernel(
    recv_in, own_dn, own_up, own_gain, other_dn, other_up, other_gain,
    out, small,
    recv, dn_buf, up_buf, gain_buf, entering, middle, d_norms, sems,
):
    phase = lax.axis_index("segment")
    experts, phases, _, rows, part = recv.shape
    tokens = experts * rows
    width = phases * part
    rank = dn_buf.shape[2]
    own, other = (own_dn, own_up, own_gain), (other_dn, other_up, other_gain)

    def copies(sources, at):
        return [
            pltpu.make_async_copy(source, buffer.at[at], sems.at[at, which])
            for which, (source, buffer) in enumerate(zip(sources, (dn_buf, up_buf, gain_buf)))
        ]

    def fetch(at):
        for this in range(2):

            @pl.when(phase == this)
            def _():
                for copy in copies(own if at == this else other, at):
                    copy.start()

    arriving = [
        pltpu.make_async_copy(recv_in.at[:, :, at], recv.at[:, :, at], sems.at[2, at])
        for at in range(2)
    ]
    arriving[0].start()
    fetch(0)
    waits = [copies(own, at) for at in range(2)]
    cols = range(0, width, CHUNK)

    def block(which, col):
        half, start = col // part, col % part
        return jnp.concatenate(
            [recv[e, half, which, :, start : start + CHUNK] for e in range(experts)], axis=0
        )

    def inverse_of(ref, mean):
        total = jnp.zeros((tokens, 128), jnp.float32)
        for col in cols:
            center = ref[:, col : col + CHUNK].astype(jnp.float32) - mean
            total = total + lanes(center * center)
        return lax.rsqrt(row_sum(total) / width + EPS)

    def down(ref, mean, inverse, at):
        pre = jnp.zeros((tokens, rank), jnp.float32)
        for col in cols:
            here = slice(col, col + CHUNK)
            normed = (ref[:, here].astype(jnp.float32) - mean) * inverse
            lowered = (normed * gain_buf[at, :, here].astype(jnp.float32)).astype(jnp.bfloat16)
            pre = pre + matmul(lowered, dn_buf[at, here, :])
        return pre

    total = jnp.zeros((tokens, 128), jnp.float32)
    arriving[0].wait()
    for col in cols:
        value = block(0, col)
        entering[:, col : col + CHUNK] = value
        total = total + lanes(value.astype(jnp.float32))
    mean_0 = row_sum(total) / width
    inverse_0 = inverse_of(entering, mean_0)
    waits[0][0].wait()
    waits[0][2].wait()
    arriving[1].start()
    fetch(1)
    pre_0 = down(entering, mean_0, inverse_0, 0)
    act_0 = gelu_value(pre_0).astype(jnp.bfloat16)
    slope_0 = gelu_slope(pre_0)

    waits[0][1].wait()
    total = jnp.zeros((tokens, 128), jnp.float32)
    for col in cols:
        here = slice(col, col + CHUNK)
        value = entering[:, here].astype(jnp.float32) + matmul(act_0, up_buf[0, :, here])
        value = value.astype(jnp.bfloat16)
        middle[:, here] = value
        total = total + lanes(value.astype(jnp.float32))
    mean_1 = row_sum(total) / width
    inverse_1 = inverse_of(middle, mean_1)
    for copy in waits[1] + arriving[1:]:
        copy.wait()
    d_act = jnp.zeros((tokens, rank), jnp.float32)
    for col in cols:
        d_act = d_act + matmul(block(1, col), up_buf[1, :, col : col + CHUNK], TRANS_RHS)
    pre_1 = down(middle, mean_1, inverse_1, 1)
    act_1 = gelu_value(pre_1).astype(jnp.bfloat16)
    d_pre_1 = (d_act * gelu_slope(pre_1)).astype(jnp.bfloat16)

    total = jnp.zeros((tokens, 128), jnp.float32)
    cross = jnp.zeros((tokens, 128), jnp.float32)
    for col in cols:
        here = slice(col, col + CHUNK)
        wide = middle[:, here].astype(jnp.float32)
        d_norm = matmul(d_pre_1, dn_buf[1, here, :], TRANS_RHS)
        d_norm = d_norm * gain_buf[1, :, here].astype(jnp.float32)
        d_norms[:, here] = d_norm
        total = total + lanes(d_norm)
        cross = cross + lanes(d_norm * ((wide - mean_1) * inverse_1))
        leaving = (wide + matmul(act_1, up_buf[1, :, here])).astype(jnp.bfloat16)
        half, start = col // part, col % part
        for e in range(experts):
            out[e, half, :, start : start + CHUNK] = leaving[e * rows : (e + 1) * rows]
    shift = row_sum(total) / width
    along = row_sum(cross) / width
    d_act = jnp.zeros((tokens, rank), jnp.float32)
    for col in cols:
        here = slice(col, col + CHUNK)
        normed = (middle[:, here].astype(jnp.float32) - mean_1) * inverse_1
        grad = block(1, col).astype(jnp.float32) + inverse_1 * (
            d_norms[:, here] - shift - normed * along
        )
        d_act = d_act + matmul(grad.astype(jnp.bfloat16), up_buf[0, :, here], TRANS_RHS)
    d_pre_0 = (d_act * slope_0).astype(jnp.bfloat16)
    moments = (mean_0, inverse_0, mean_1, inverse_1, shift, along)
    kept = (act_0, act_1, d_pre_0, d_pre_1, side_by_side(moments, tokens))
    for e in range(experts):
        start = pl.multiple_of((e ^ lax.axis_index("expert")) * rows, rows)
        for at, value in enumerate(kept):
            cols = slice(at * rank, at * rank + value.shape[1])
            small[pl.ds(start, rows), cols] = value[e * rows : (e + 1) * rows]


def gradient_kernel(experts, sources, sizes, *refs):
    sides, refs = refs[: 2 * experts], refs[2 * experts :]
    smalls, refs = refs[:sources], refs[sources:]
    own, other, refs = refs[:3], refs[3:6], refs[6:]
    ids, back_in, out_hidden, grad_dn, grad_upper = refs[:5]
    (id_buf, back, result, dn_buf, up_buf, gain_buf, wide_buf, small, moments, turned, lows, grads,
     dn_out, up_out, small_sems, wide_sems, sems) = refs[5:]
    core = lax.axis_index("segment")
    place = lax.axis_index("dp")
    rows, slab = smalls[0].shape[0], sides[0].shape[3]
    replicas = sources // 2
    blocks = [side.shape[1] for side in sides[:experts]]
    starts = [sum(blocks[:step]) for step in range(experts)]
    rank = dn_buf.shape[1]
    columns = 256
    chunks = range(0, slab, columns)
    features = pl.ds(pl.multiple_of(place * slab, slab), slab)

    def weight_copies(up, gain_first, dn, gain_second):
        moves = (
            (up.at[:, features], up_buf),
            (gain_first.at[:, features], gain_buf.at[0]),
            (gain_second.at[:, features], gain_buf.at[1]),
            (dn.at[features, :], dn_buf),
        )
        return [
            pltpu.make_async_copy(source, target, sems.at[at])
            for at, (source, target) in enumerate(moves)
        ]

    early = [
        pltpu.make_async_copy(ids, id_buf, sems.at[4]),
        pltpu.make_async_copy(back_in, back, sems.at[5]),
    ]
    small_copies = [
        pltpu.make_async_copy(
            source, small.at[at * rows : (at + 1) * rows], small_sems.at[at]
        )
        for at, source in enumerate(smalls)
    ]
    wide_copies = [
        [
            pltpu.make_async_copy(
                side.at[:, :, :, col : col + columns],
                wide_buf.at[
                    at // experts,
                    :,
                    starts[at % experts] : starts[at % experts] + blocks[at % experts],
                    :,
                    col : col + columns,
                ],
                wide_sems.at[col // columns, at],
            )
            for at, side in enumerate(sides)
        ]
        for col in chunks
    ]
    for copy in early + small_copies:
        copy.start()

    @pl.when(core == 0)
    def _():
        for copy in weight_copies(own[1], own[2], other[0], other[2]):
            copy.start()

    @pl.when(core != 0)
    def _():
        for copy in weight_copies(other[1], other[2], own[0], own[2]):
            copy.start()

    for copies in wide_copies:
        for copy in copies:
            copy.start()
    for copy in early:
        copy.wait()
    unpack(sizes, id_buf, back, result)
    leaving = [pltpu.make_async_copy(result, out_hidden, sems.at[6])]
    leaving[0].start()
    for copy in small_copies + weight_copies(own[1], own[2], other[0], other[2]):
        copy.wait()

    def sliced(source, which, here):
        side, near = source // replicas, source % replicas
        at = [
            replicas - 1 + step if near == 0 else starts[step] + near - 1
            for step in range(experts)
        ]
        return jnp.concatenate([wide_buf[side, which, one, :, here] for one in at], axis=0)

    def moment(at, index):
        value = moments[at, index * 128 : (index + 1) * 128]
        return jnp.concatenate([value] * (columns // 128), axis=1)

    def work(first):
        held = lax.broadcasted_iota(jnp.int32, (128, 6 * 128), 0)
        wanted = lax.broadcasted_iota(jnp.int32, (128, 6 * 128), 1) // 128
        adds = (held // 3 == wanted).astype(jnp.float32).astype(jnp.bfloat16)
        moments[...] = matmul(small[:, 4 * rank :], adds)
        act, d_pre = (0, 2) if first else (1, 3)
        turned[0] = small[:, act * rank : (act + 1) * rank].T
        turned[1] = small[:, d_pre * rank : (d_pre + 1) * rank].T
        for index, col in enumerate(chunks):
            here = slice(col, col + columns)
            for copy in wide_copies[index]:
                copy.wait()
            ups = matmul(small[:, :rank], up_buf[:, here])
            scales = [gain_buf[at, :, here].astype(jnp.float32) for at in range(2)]
            if first:
                downs = matmul(small[:, 3 * rank : 4 * rank], dn_buf[here, :], TRANS_RHS)
            for source in range(sources):
                at = slice(source * rows, (source + 1) * rows)
                wide = sliced(source, 0, here).astype(jnp.float32)
                grad_in = sliced(source, 1, here)
                middle = (wide + ups[at]).astype(jnp.bfloat16).astype(jnp.float32)
                inverse = moment(at, 3)
                normed = (middle - moment(at, 2)) * inverse
                if first:
                    entered = (wide - moment(at, 0)) * moment(at, 1)
                    lows[index, at] = (entered * scales[0]).astype(jnp.bfloat16)
                    d_norm = downs[at] * scales[1]
                    grads[index, at] = (
                        grad_in.astype(jnp.float32)
                        + inverse * (d_norm - moment(at, 4) - normed * moment(at, 5))
                    ).astype(jnp.bfloat16)
                else:
                    lows[index, at] = (normed * scales[1]).astype(jnp.bfloat16)
                    grads[index, at] = grad_in
            dn_out[here, :] = matmul(turned[1], lows[index]).astype(jnp.bfloat16).T
            up_out[index] = matmul(turned[0], grads[index]).astype(jnp.bfloat16)
            for copy in out_copies(index, here):
                copy.start()

    def out_copies(index, here):
        return [
            pltpu.make_async_copy(
                dn_out.at[here, :], grad_dn.at[here, :], sems.at[7 + 2 * index]
            ),
            pltpu.make_async_copy(
                up_out.at[index], grad_upper.at[:, here], sems.at[8 + 2 * index]
            ),
        ]

    @pl.when(core == 0)
    def _():
        work(True)

    @pl.when(core != 0)
    def _():
        work(False)

    for index, col in enumerate(chunks):
        leaving += out_copies(index, slice(col, col + columns))
    for copy in leaving:
        copy.wait()


VMEM = pl.BlockSpec(memory_space=pltpu.VMEM)
HBM = pl.BlockSpec(memory_space=pltpu.HBM)


def call(kernel, name, grant, in_specs, outs, scratch=(), outs_in=VMEM, flops=0, moved=MIB):
    return pl.pallas_call(
        kernel,
        out_shape=tuple(jax.ShapeDtypeStruct(*out) for out in outs),
        in_specs=in_specs,
        out_specs=tuple(outs_in for _ in outs),
        scratch_shapes=list(scratch),
        compiler_params=pltpu.CompilerParams(vmem_limit_bytes=grant * MIB),
        cost_estimate=pl.CostEstimate(flops=flops, bytes_accessed=moved, transcendentals=0),
        name=name,
    )


def across(block, axis, distance):
    size = lax.axis_size(axis)
    return lax.ppermute(block, axis, [(i, i ^ distance) for i in range(size)])


def slab_route(replicas, pair, low):
    route = []
    for replica in range(replicas):
        for core in range(2):
            chip = 2 * core + ((replica & 1) ^ pair)
            route.append((2 * replica + core, 2 * chip + ((replica >> 1) ^ low)))
    return route


def on_device_two_phases(hidden_in, cotangent, cluster_ids, w_down, w_up, gain):
    experts = lax.axis_size("expert")
    replicas = lax.axis_size("dp")
    s_local, length, part = hidden_in.shape
    width = 2 * part
    capacity = 2 * s_local // experts
    slots = experts * capacity
    groups = 2 * experts
    rows = slots * length // groups
    tokens = experts * rows
    own = (w_down[0, 0], w_up[0, 0], gain[0])
    rank = own[0].shape[1]
    slab = width // replicas
    bf16, f32 = jnp.bfloat16, jnp.float32
    sizes = (length, capacity, slots)
    sections = ("expert", "segment")

    other = tuple(across(array, "segment", 1) for array in own)
    half = s_local * length // 2
    (send,) = call(
        functools.partial(pack_kernel, *sizes),
        "pack",
        60,
        [HBM] * 3,
        [((groups, 2, rows, part), bf16)],
        [
            pltpu.SMEM(cluster_ids.shape, jnp.int32),
            pltpu.VMEM((2,) + hidden_in.shape, bf16),
            pltpu.VMEM((groups, 2, rows, part), bf16),
            pltpu.SemaphoreType.DMA((5,)),
        ],
        outs_in=HBM,
    )(cluster_ids, hidden_in, cotangent)
    slabs = call(
        functools.partial(slab_kernel, *sizes),
        "slabs",
        60,
        [HBM] * 4,
        [((2 * half + 16, slab), bf16)] * 4,
        [
            pltpu.SMEM(cluster_ids.shape, jnp.int32),
            pltpu.VMEM((2,) + hidden_in.shape, bf16),
            pltpu.VMEM((2, 2 * half, part), bf16),
            pltpu.VMEM((2, 16, 128), bf16),
            pltpu.VMEM((4, 2 * half + 16, slab), bf16),
            pltpu.SemaphoreType.DMA((7,)),
        ],
        outs_in=HBM,
    )(cluster_ids, hidden_in, cotangent, send)
    recv = lax.all_to_all(send, sections, split_axis=0, concat_axis=0, tiled=True)
    recv = recv.reshape(experts, 2, 2, rows, part)
    slabs = [
        lax.ppermute(block, ("dp", "segment"), slab_route(replicas, turn // 2, turn % 2))
        for turn, block in enumerate(slabs)
    ]
    out, small = call(
        chain_kernel,
        "chain",
        50,
        [HBM] * 7,
        [((experts, 2, rows, part), bf16), ((tokens, 4 * rank + 128), bf16)],
        [
            pltpu.VMEM(recv.shape, bf16),
            pltpu.VMEM((2, width, rank), bf16),
            pltpu.VMEM((2, rank, width), bf16),
            pltpu.VMEM((2, 1, width), bf16),
            pltpu.VMEM((tokens, width), bf16),
            pltpu.VMEM((tokens, width), bf16),
            pltpu.VMEM((tokens, width), f32),
            pltpu.SemaphoreType.DMA((3, 3)),
        ],
        flops=7 * 2 * tokens * width * rank,
        moved=10 * MIB,
    )(recv, *own, *other)
    slices = call(
        functools.partial(repack_kernel, length, capacity),
        "repack",
        16,
        [VMEM] * 4 + [HBM] * 2,
        [((2, replicas - 1 + experts, rows, slab), bf16)]
        + [((2, replicas - 1, rows, slab), bf16)] * (experts - 1),
        [pltpu.SemaphoreType.DMA((experts,))],
    )(*slabs, recv, small)
    small, *slices = lax.optimization_barrier((small, *slices))
    mine = [slices[0]] + [across(slices[step], "expert", step) for step in range(1, experts)]
    mine[:2] = lax.optimization_barrier(tuple(mine[:2]))
    near = [small] + [across(small, "dp", step) for step in range(2, replicas)]
    near[:2] = lax.optimization_barrier(tuple(near[:2]))
    beside = across(near[0], "dp", 1)
    *near, mine[-1] = lax.optimization_barrier((*near, mine[-1]))
    near.insert(1, beside)
    theirs = [across(block, "segment", 1) for block in mine]
    smalls = near + [across(piece, "segment", 1) for piece in near]

    back = lax.all_to_all(
        out.reshape(groups, rows, part), sections, split_axis=0, concat_axis=0, tiled=True
    )

    sources = 2 * replicas
    all_tokens = sources * tokens
    out_hidden, grad_dn, grad_upper = call(
        functools.partial(gradient_kernel, experts, sources, sizes),
        "gradients",
        60,
        [HBM] * (2 * experts + sources + 8),
        [(hidden_in.shape, bf16), ((slab, rank), bf16), ((rank, slab), bf16)],
        [
            pltpu.SMEM(cluster_ids.shape, jnp.int32),
            pltpu.VMEM(back.shape, bf16),
            pltpu.VMEM(hidden_in.shape, bf16),
            pltpu.VMEM((slab, rank), bf16),
            pltpu.VMEM((rank, slab), bf16),
            pltpu.VMEM((2, 1, slab), bf16),
            pltpu.VMEM((2, 2, replicas * experts, rows, slab), bf16),
            pltpu.VMEM((all_tokens, 4 * rank + 128), bf16),
            pltpu.VMEM((all_tokens, 6 * 128), f32),
            pltpu.VMEM((2, rank, all_tokens), bf16),
            pltpu.VMEM((slab // 256, all_tokens, 256), bf16),
            pltpu.VMEM((slab // 256, all_tokens, 256), bf16),
            pltpu.VMEM((slab, rank), bf16),
            pltpu.VMEM((slab // 256, rank, 256), bf16),
            pltpu.SemaphoreType.DMA((sources,)),
            pltpu.SemaphoreType.DMA((slab // 256, 2 * experts)),
            pltpu.SemaphoreType.DMA((7 + 2 * (slab // 256),)),
        ],
        outs_in=HBM,
    )(*mine, *theirs, *smalls, *own, *other, cluster_ids, back)
    return (out_hidden, grad_dn[None, None], grad_upper[None, None])


def solution(mesh):
    two = dict(mesh.shape) == {"expert": 4, "dp": 4, "segment": 2}
    on_device = on_device_two_phases if two else on_device_pipelined
    return jax.shard_map(
        on_device,
        mesh=mesh,
        in_specs=(
            P(("expert", "dp"), None, "segment"),
            P(("expert", "dp"), None, "segment"),
            P(("expert", "dp")),
            P("expert", "segment", None, None),
            P("expert", "segment", None, None),
            P("expert", "segment", None),
        ),
        out_specs=(
            P(("expert", "dp"), None, "segment"),
            P("expert", "segment", "dp", None),
            P("expert", "segment", None, "dp"),
        ),
        check_vma=False,
    )
```

```python
import functools

import jax
import jax.numpy as jnp
from jax import lax
from jax.experimental import pallas as pl
from jax.experimental.pallas import tpu as pltpu
from jax.sharding import PartitionSpec as P

MICRO = 4


EPS = 1e-05
C_ZERO = 0.7978845608028654
C_ONE = 0.044715


def shifted(block, axis, distance):
    devices = range(lax.axis_size(axis))
    route = [(i - distance, i) for i in devices if i - distance in devices]
    return lax.ppermute(block, axis, route)


def from_root(block, axis, holder):
    block = jnp.where(lax.axis_index(axis) == holder, block, jnp.zeros_like(block))
    return lax.psum(block, axis)


def gelu_value(z):
    return 0.5 * z * (1.0 + jnp.tanh(C_ZERO * (z + C_ONE * z * z * z)))


def gelu_slope(z):
    tval = jnp.tanh(C_ZERO * (z + C_ONE * z * z * z))
    return 0.5 * (1.0 + tval) + 0.5 * z * (1.0 - tval * tval) * C_ZERO * (1.0 + 3.0 * C_ONE * z * z)


def normalize(hidden):
    wide = hidden.astype(jnp.float32)
    center = wide - jnp.mean(wide, axis=-1, keepdims=True)
    inverse = lax.rsqrt(jnp.mean(center * center, axis=-1, keepdims=True) + EPS)
    return (wide, center * inverse, inverse)


def phase_forward(hidden, w_dn, w_upper, scale):
    wide, normed, inverse = normalize(hidden)
    lowered = (normed * scale).astype(jnp.bfloat16)
    pre = jnp.dot(lowered, w_dn, preferred_element_type=jnp.float32)
    act = gelu_value(pre).astype(jnp.bfloat16)
    leaving = (wide + jnp.dot(act, w_upper, preferred_element_type=jnp.float32)).astype(
        jnp.bfloat16
    )
    return (leaving, pre)


def phase_backward(hidden, grad_in, pre, w_dn, w_upper, scale):
    wide, normed, inverse = normalize(hidden)
    lowered = (normed * scale).astype(jnp.bfloat16)
    act = gelu_value(pre).astype(jnp.bfloat16)
    d_act = jnp.dot(grad_in, w_upper.T, preferred_element_type=jnp.float32)
    d_pre = (d_act * gelu_slope(pre)).astype(jnp.bfloat16)
    d_low = jnp.dot(d_pre, w_dn.T, preferred_element_type=jnp.float32)
    d_norm = d_low * scale
    d_wide = inverse * (
        d_norm
        - jnp.mean(d_norm, axis=-1, keepdims=True)
        - normed * jnp.mean(d_norm * normed, axis=-1, keepdims=True)
    )
    grad_out = (grad_in.astype(jnp.float32) + d_wide).astype(jnp.bfloat16)
    return (grad_out, lowered, act, d_pre)


def put_slot(buffer, value, slot, valid):
    old_value = lax.dynamic_index_in_dim(buffer, slot, 0, keepdims=False)
    return lax.dynamic_update_index_in_dim(buffer, jnp.where(valid, value, old_value), slot, 0)


def on_device_pipelined(hidden_in, cotangent, cluster_ids, w_down, w_up, gain):
    experts = lax.axis_size("expert")
    phases = lax.axis_size("segment")
    phase = lax.axis_index("segment")
    s_local, length, quarter = hidden_in.shape
    capacity = 2 * s_local // experts
    slots = experts * capacity
    same = (cluster_ids[:, None] == cluster_ids[None, :]).astype(jnp.int32)
    earlier = jnp.sum(jnp.tril(same, -1), axis=1)
    target = cluster_ids * capacity + earlier
    place = (jnp.arange(slots, dtype=jnp.int32)[:, None] == target[None, :]).astype(jnp.bfloat16)

    def to_slots(local):
        flat = local.reshape(s_local, -1)
        moved = jnp.dot(place, flat, preferred_element_type=jnp.float32).astype(jnp.bfloat16)
        return moved.reshape((slots,) + local.shape[1:])

    full_in, full_cot = (
        lax.all_gather(hidden_in, "segment", axis=2, tiled=True),
        lax.all_gather(cotangent, "segment", axis=2, tiled=True),
    )
    slot_in, slot_cot = (
        lax.all_to_all(to_slots(full_in), "expert", split_axis=0, concat_axis=0, tiled=True),
        lax.all_to_all(to_slots(full_cot), "expert", split_axis=0, concat_axis=0, tiled=True),
    )
    width = slot_in.shape[2]
    micro_rows = slots * length // MICRO
    inputs = slot_in.reshape(MICRO, micro_rows, width)
    cots = slot_cot.reshape(MICRO, micro_rows, width)
    w_dn = w_down[0, 0]
    w_upper = w_up[0, 0]
    rank = w_dn.shape[1]
    scale = gain[0, 0].astype(jnp.float32)
    ticks = MICRO + phases - 1

    def forward_tick(tick, carry):
        received, saved, pres, results = carry
        which = tick - phase
        valid = (which >= 0) & (which < MICRO)
        slot = jnp.clip(which, 0, MICRO - 1)
        first = lax.dynamic_index_in_dim(inputs, jnp.minimum(tick, MICRO - 1), 0, keepdims=False)
        entering = jnp.where(phase == 0, first, received)
        leaving, pre = phase_forward(entering, w_dn, w_upper, scale)
        saved = put_slot(saved, entering, slot, valid)
        pres = put_slot(pres, pre, slot, valid)
        results = put_slot(results, leaving, slot, valid & (phase == phases - 1))
        received = shifted(leaving, "segment", 1)
        return (received, saved, pres, results)

    start = (
        jnp.zeros((micro_rows, width), jnp.bfloat16),
        jnp.zeros((MICRO, micro_rows, width), jnp.bfloat16),
        jnp.zeros((MICRO, micro_rows, rank), jnp.float32),
        jnp.zeros((MICRO, micro_rows, width), jnp.bfloat16),
    )
    received, saved, pres, results = lax.fori_loop(0, ticks, forward_tick, start)

    def backward_tick(tick, carry):
        received, lows, acts, dpres, grads = carry
        which = tick - (phases - 1 - phase)
        valid = (which >= 0) & (which < MICRO)
        slot = jnp.clip(which, 0, MICRO - 1)
        last = lax.dynamic_index_in_dim(cots, jnp.minimum(tick, MICRO - 1), 0, keepdims=False)
        grad_in = jnp.where(phase == phases - 1, last, received)
        hidden = lax.dynamic_index_in_dim(saved, slot, 0, keepdims=False)
        pre = lax.dynamic_index_in_dim(pres, slot, 0, keepdims=False)
        grad_out, lowered, act, d_pre = phase_backward(hidden, grad_in, pre, w_dn, w_upper, scale)
        lows = put_slot(lows, lowered, slot, valid)
        acts = put_slot(acts, act, slot, valid)
        dpres = put_slot(dpres, d_pre, slot, valid)
        grads = put_slot(grads, grad_in, slot, valid)
        received = shifted(grad_out, "segment", -1)
        return (received, lows, acts, dpres, grads)

    start_back = (
        jnp.zeros((micro_rows, width), jnp.bfloat16),
        jnp.zeros((MICRO, micro_rows, width), jnp.bfloat16),
        jnp.zeros((MICRO, micro_rows, rank), jnp.bfloat16),
        jnp.zeros((MICRO, micro_rows, rank), jnp.bfloat16),
        jnp.zeros((MICRO, micro_rows, width), jnp.bfloat16),
    )
    received, lows, acts, dpres, grads = lax.fori_loop(0, ticks, backward_tick, start_back)
    contract = (((0,), (0,)), ((), ()))
    grad_dn = lax.dot_general(
        lows.reshape(-1, width),
        dpres.reshape(-1, rank),
        contract,
        preferred_element_type=jnp.float32,
    )
    grad_upper = lax.dot_general(
        acts.reshape(-1, rank),
        grads.reshape(-1, width),
        contract,
        preferred_element_type=jnp.float32,
    )
    summed_dn, summed_upper = (
        lax.psum_scatter(
            grad_dn.astype(jnp.bfloat16), "dp", scatter_dimension=0, tiled=True
        ).astype(jnp.float32),
        lax.psum_scatter(
            grad_upper.astype(jnp.bfloat16), "dp", scatter_dimension=1, tiled=True
        ).astype(jnp.float32),
    )
    returned = from_root(results, "segment", phases - 1)
    returned = returned.reshape(slots, length, width)
    own = lax.dynamic_slice_in_dim(returned, phase * quarter, quarter, 2)
    back = lax.all_to_all(own, "expert", split_axis=0, concat_axis=0, tiled=True)
    out_hidden = jnp.dot(place.T, back.reshape(slots, -1), preferred_element_type=jnp.float32)
    out_hidden = out_hidden.astype(jnp.bfloat16).reshape(s_local, length, quarter)
    return (
        out_hidden,
        summed_dn.astype(jnp.bfloat16)[None, None],
        summed_upper.astype(jnp.bfloat16)[None, None],
    )


CHUNK = 512
MIB = 1024 * 1024
TRANS_RHS = (((1,), (1,)), ((), ()))
TRANS_LHS = (((0,), (0,)), ((), ()))


def matmul(left, right, dims=(((1,), (0,)), ((), ()))):
    return lax.dot_general(left, right, dims, preferred_element_type=jnp.float32)


def spread_ids(ids, shape, length):
    lane = lax.broadcasted_iota(jnp.int32, shape, 1)
    spread = jnp.zeros(shape, jnp.int32)
    for n in range(ids.shape[0]):
        spread = jnp.where(lane // length == n, ids[n], spread)
    return spread


def ranked(ids_row, length):
    tokens = ids_row.shape[1]
    kinds = lax.broadcasted_iota(jnp.int32, (8, tokens), 0)
    member = (kinds == ids_row).astype(jnp.float32)
    at_col = lax.broadcasted_iota(jnp.int32, (tokens, tokens), 0)
    at_row = lax.broadcasted_iota(jnp.int32, (tokens, tokens), 1)
    before = (lax.rem(at_col, length) == 0) & (at_col // length < at_row // length)
    counts = matmul(member.astype(jnp.bfloat16), before.astype(jnp.float32).astype(jnp.bfloat16))
    rank = jnp.sum(member * counts, axis=0, keepdims=True)
    total = jnp.sum(member, axis=1, keepdims=True) * (1.0 / length)
    lower = jnp.sum(jnp.where(kinds < ids_row, total, 0.0), axis=0, keepdims=True)
    return rank.astype(jnp.int32), lower.astype(jnp.int32)


def one_hot(target, rows):
    wanted = lax.broadcasted_iota(jnp.int32, (rows, target.shape[1]), 0)
    return (wanted == target).astype(jnp.float32).astype(jnp.bfloat16)


def placements(ids_row, length, capacity, slots):
    rank, lower = ranked(ids_row, length)
    token = lax.rem(lax.broadcasted_iota(jnp.int32, ids_row.shape, 1), length)
    place = rank + lower
    group = lax.rem(place, 2)
    per_core = capacity // 2
    packed = ((ids_row * 2 + group) * per_core + rank // 2) * length + token
    tokens = ids_row.shape[1]
    ordered = group * (tokens // 2) + (place // 2) * length + token
    return one_hot(packed, slots * length), one_hot(ordered, tokens)


def pack_kernel(length, capacity, slots, ids, hidden, cot, send, id_buf, buf, packed, sems):
    groups, _, rows, part = send.shape
    tokens = hidden.shape[0] * length
    arriving = [
        pltpu.make_async_copy(source, target, sems.at[at])
        for at, (source, target) in enumerate(
            ((ids, id_buf), (hidden, buf.at[0]), (cot, buf.at[1]))
        )
    ]
    leaving = [
        pltpu.make_async_copy(packed.at[:, at], send.at[:, at], sems.at[3 + at]) for at in range(2)
    ]
    for copy in arriving:
        copy.start()
    arriving[0].wait()
    ids_row = spread_ids(id_buf, (8, tokens), length)[:1]
    place, _ = placements(ids_row, length, capacity, slots)
    for which in range(2):
        arriving[1 + which].wait()
        moved = matmul(place, buf[which].reshape(tokens, part)).astype(jnp.bfloat16)
        for group in range(groups):
            packed[group, which] = moved[group * rows : (group + 1) * rows]
        leaving[which].start()
    for copy in leaving:
        copy.wait()


def slab_kernel(length, capacity, slots, ids, hidden, cot, _, *refs):
    slabs, refs = refs[:4], refs[4:]
    id_buf, buf, ordered, turned, out_slabs, sems = refs
    s_local, _, part = hidden.shape
    tokens = s_local * length
    slab = part // 2
    half = tokens // 2
    replica = lax.axis_index("dp")
    arriving = [
        pltpu.make_async_copy(source, target, sems.at[at])
        for at, (source, target) in enumerate(
            ((ids, id_buf), (hidden, buf.at[0]), (cot, buf.at[1]))
        )
    ]
    leaving = [
        pltpu.make_async_copy(out_slabs.at[at], slabs[at], sems.at[3 + at]) for at in range(4)
    ]
    for copy in arriving:
        copy.start()
    arriving[0].wait()
    ids_row = spread_ids(id_buf, (16, tokens), length)
    _, by_group = placements(ids_row[:1], length, capacity, slots)
    for group in range(2):
        mine = by_group[group * half : (group + 1) * half]
        clusters = matmul(ids_row.astype(jnp.float32).astype(jnp.bfloat16), mine, TRANS_RHS)
        turned[group] = jnp.concatenate(
            [clusters.astype(jnp.bfloat16), jnp.zeros((16, 128 - half), jnp.bfloat16)], axis=1
        )
    for which in range(2):
        arriving[1 + which].wait()
        flat = buf[which].reshape(tokens, part)
        ordered[which] = matmul(by_group, flat).astype(jnp.bfloat16)
    for turn in range(4):
        pair = (turn // 2) ^ (replica & 1)
        group = (turn % 2) ^ (replica >> 1)
        cols = pl.ds(pl.multiple_of(pair * slab, slab), slab)
        at = pl.ds(pl.multiple_of(group * half, half), half)
        for which in range(2):
            out_slabs[turn, which * half : (which + 1) * half] = ordered[which, at, cols]
        out_slabs[turn, tokens:] = jnp.zeros((16, slab), jnp.bfloat16)
        out_slabs[turn, tokens:, :128] = turned[group]
        leaving[turn].start()
    for copy in leaving:
        copy.wait()


def repack_kernel(length, capacity, *refs):
    slabs, recv, outs, sems = refs[:4], refs[4], refs[6:-1], refs[-1]
    kept, sent = outs[0], outs[1:]
    _, _, rows, slab = kept.shape
    experts = len(outs)
    half = (slabs[0].shape[0] - 16) // 2
    core, replica = lax.axis_index("segment"), lax.axis_index("dp")
    expert = lax.axis_index("expert")
    per_part = recv.shape[4] // slab
    part = replica // per_part
    cols = pl.ds(pl.multiple_of((replica - part * per_part) * slab, slab), slab)
    cuts = [
        pltpu.make_async_copy(
            recv.at[e, part, :, :, cols], kept.at[:, 3 + (e ^ expert)], sems.at[e]
        )
        for e in range(experts)
    ]
    for cut in cuts:
        cut.start()
    far_low = (replica >> 1) ^ core ^ 1

    def place_rows(held, near):
        ids_row = held[2 * half :, :128].astype(jnp.float32)[:1, :half].astype(jnp.int32)
        rank, _ = ranked(ids_row, length)
        token = lax.rem(lax.broadcasted_iota(jnp.int32, ids_row.shape, 1), length)
        step = ids_row ^ expert
        place = one_hot((step * (capacity // 2) + rank) * length + token, experts * rows)
        for which in range(2):
            moved = matmul(place, held[which * half : (which + 1) * half]).astype(jnp.bfloat16)
            kept[which, near - 1] = moved[:rows]
            for step_at, out in enumerate(sent):
                out[which, near - 1] = moved[(step_at + 1) * rows : (step_at + 2) * rows]

    place_rows(jnp.where(far_low == 1, slabs[1][...], slabs[0][...]), 2)
    for low in range(2):
        place_rows(slabs[2 + low][...], 1 + 2 * (low ^ (replica >> 1) ^ core))
    for cut in cuts:
        cut.wait()


def unpack(sizes, id_buf, back, out):
    length, capacity, slots = sizes
    groups, rows, width = back.shape
    s_local = out.shape[0]
    ids_row = spread_ids(id_buf, (8, s_local * length), length)[:1]
    place, _ = placements(ids_row, length, capacity, slots)
    moved = matmul(place, back[...].reshape(groups * rows, width), TRANS_LHS)
    out[...] = moved.astype(jnp.bfloat16).reshape(s_local, length, width)


def split_three(value):
    top = value.astype(jnp.bfloat16).astype(jnp.float32)
    mid = (value - top).astype(jnp.bfloat16).astype(jnp.float32)
    low = (value - top - mid).astype(jnp.bfloat16).astype(jnp.float32)
    return [top, mid, low]


def side_by_side(columns, tokens):
    lane = lax.broadcasted_iota(jnp.int32, (tokens, 128), 1)
    block = jnp.zeros((tokens, 128), jnp.float32)
    at = 0
    for column in columns:
        for piece in split_three(column):
            block = jnp.where(lane == at, piece, block)
            at += 1
    return block.astype(jnp.bfloat16)


def lanes(value):
    total = value[:, :128]
    for start in range(128, value.shape[1], 128):
        total = total + value[:, start : start + 128]
    return total


def row_sum(parts):
    return jnp.sum(parts, axis=1, keepdims=True)


def chain_kernel(
    recv_in, own_dn, own_up, own_gain, other_dn, other_up, other_gain,
    out, small,
    recv, dn_buf, up_buf, gain_buf, entering, middle, d_norms, sems,
):
    phase = lax.axis_index("segment")
    experts, phases, _, rows, part = recv.shape
    tokens = experts * rows
    width = phases * part
    rank = dn_buf.shape[2]
    own, other = (own_dn, own_up, own_gain), (other_dn, other_up, other_gain)

    def copies(sources, at):
        return [
            pltpu.make_async_copy(source, buffer.at[at], sems.at[at, which])
            for which, (source, buffer) in enumerate(zip(sources, (dn_buf, up_buf, gain_buf)))
        ]

    def fetch(at):
        for this in range(2):

            @pl.when(phase == this)
            def _():
                for copy in copies(own if at == this else other, at):
                    copy.start()

    arriving = [
        pltpu.make_async_copy(recv_in.at[:, :, at], recv.at[:, :, at], sems.at[2, at])
        for at in range(2)
    ]
    arriving[0].start()
    fetch(0)
    waits = [copies(own, at) for at in range(2)]
    cols = range(0, width, CHUNK)

    def block(which, col):
        half, start = col // part, col % part
        return jnp.concatenate(
            [recv[e, half, which, :, start : start + CHUNK] for e in range(experts)], axis=0
        )

    def inverse_of(ref, mean):
        total = jnp.zeros((tokens, 128), jnp.float32)
        for col in cols:
            center = ref[:, col : col + CHUNK].astype(jnp.float32) - mean
            total = total + lanes(center * center)
        return lax.rsqrt(row_sum(total) / width + EPS)

    def down(ref, mean, inverse, at):
        pre = jnp.zeros((tokens, rank), jnp.float32)
        for col in cols:
            here = slice(col, col + CHUNK)
            normed = (ref[:, here].astype(jnp.float32) - mean) * inverse
            lowered = (normed * gain_buf[at, :, here].astype(jnp.float32)).astype(jnp.bfloat16)
            pre = pre + matmul(lowered, dn_buf[at, here, :])
        return pre

    total = jnp.zeros((tokens, 128), jnp.float32)
    arriving[0].wait()
    for col in cols:
        value = block(0, col)
        entering[:, col : col + CHUNK] = value
        total = total + lanes(value.astype(jnp.float32))
    mean_0 = row_sum(total) / width
    inverse_0 = inverse_of(entering, mean_0)
    waits[0][0].wait()
    waits[0][2].wait()
    arriving[1].start()
    fetch(1)
    pre_0 = down(entering, mean_0, inverse_0, 0)
    act_0 = gelu_value(pre_0).astype(jnp.bfloat16)
    slope_0 = gelu_slope(pre_0)

    waits[0][1].wait()
    total = jnp.zeros((tokens, 128), jnp.float32)
    for col in cols:
        here = slice(col, col + CHUNK)
        value = entering[:, here].astype(jnp.float32) + matmul(act_0, up_buf[0, :, here])
        value = value.astype(jnp.bfloat16)
        middle[:, here] = value
        total = total + lanes(value.astype(jnp.float32))
    mean_1 = row_sum(total) / width
    inverse_1 = inverse_of(middle, mean_1)
    for copy in waits[1] + arriving[1:]:
        copy.wait()
    d_act = jnp.zeros((tokens, rank), jnp.float32)
    for col in cols:
        d_act = d_act + matmul(block(1, col), up_buf[1, :, col : col + CHUNK], TRANS_RHS)
    pre_1 = down(middle, mean_1, inverse_1, 1)
    act_1 = gelu_value(pre_1).astype(jnp.bfloat16)
    d_pre_1 = (d_act * gelu_slope(pre_1)).astype(jnp.bfloat16)

    total = jnp.zeros((tokens, 128), jnp.float32)
    cross = jnp.zeros((tokens, 128), jnp.float32)
    for col in cols:
        here = slice(col, col + CHUNK)
        wide = middle[:, here].astype(jnp.float32)
        d_norm = matmul(d_pre_1, dn_buf[1, here, :], TRANS_RHS)
        d_norm = d_norm * gain_buf[1, :, here].astype(jnp.float32)
        d_norms[:, here] = d_norm
        total = total + lanes(d_norm)
        cross = cross + lanes(d_norm * ((wide - mean_1) * inverse_1))
        leaving = (wide + matmul(act_1, up_buf[1, :, here])).astype(jnp.bfloat16)
        half, start = col // part, col % part
        for e in range(experts):
            out[e, half, :, start : start + CHUNK] = leaving[e * rows : (e + 1) * rows]
    shift = row_sum(total) / width
    along = row_sum(cross) / width
    d_act = jnp.zeros((tokens, rank), jnp.float32)
    for col in cols:
        here = slice(col, col + CHUNK)
        normed = (middle[:, here].astype(jnp.float32) - mean_1) * inverse_1
        grad = block(1, col).astype(jnp.float32) + inverse_1 * (
            d_norms[:, here] - shift - normed * along
        )
        d_act = d_act + matmul(grad.astype(jnp.bfloat16), up_buf[0, :, here], TRANS_RHS)
    d_pre_0 = (d_act * slope_0).astype(jnp.bfloat16)
    moments = (mean_0, inverse_0, mean_1, inverse_1, shift, along)
    kept = (act_0, act_1, d_pre_0, d_pre_1, side_by_side(moments, tokens))
    for e in range(experts):
        start = pl.multiple_of((e ^ lax.axis_index("expert")) * rows, rows)
        for at, value in enumerate(kept):
            cols = slice(at * rank, at * rank + value.shape[1])
            small[pl.ds(start, rows), cols] = value[e * rows : (e + 1) * rows]


def gradient_kernel(experts, sources, sizes, *refs):
    sides, refs = refs[: 2 * experts], refs[2 * experts :]
    smalls, refs = refs[:sources], refs[sources:]
    own, other, refs = refs[:3], refs[3:6], refs[6:]
    ids, back_in, out_hidden, grad_dn, grad_upper = refs[:5]
    (id_buf, back, result, dn_buf, up_buf, gain_buf, wide_buf, small, moments, turned, lows, grads,
     dn_out, up_out, small_sems, wide_sems, sems) = refs[5:]
    core = lax.axis_index("segment")
    place = lax.axis_index("dp")
    rows, slab = smalls[0].shape[0], sides[0].shape[3]
    replicas = sources // 2
    blocks = [side.shape[1] for side in sides[:experts]]
    starts = [sum(blocks[:step]) for step in range(experts)]
    rank = dn_buf.shape[1]
    columns = 256
    chunks = range(0, slab, columns)
    features = pl.ds(pl.multiple_of(place * slab, slab), slab)

    def weight_copies(up, gain_first, dn, gain_second):
        moves = (
            (up.at[:, features], up_buf),
            (gain_first.at[:, features], gain_buf.at[0]),
            (gain_second.at[:, features], gain_buf.at[1]),
            (dn.at[features, :], dn_buf),
        )
        return [
            pltpu.make_async_copy(source, target, sems.at[at])
            for at, (source, target) in enumerate(moves)
        ]

    early = [
        pltpu.make_async_copy(ids, id_buf, sems.at[4]),
        pltpu.make_async_copy(back_in, back, sems.at[5]),
    ]
    small_copies = [
        pltpu.make_async_copy(
            source, small.at[at * rows : (at + 1) * rows], small_sems.at[at]
        )
        for at, source in enumerate(smalls)
    ]
    wide_copies = [
        [
            pltpu.make_async_copy(
                side.at[:, :, :, col : col + columns],
                wide_buf.at[
                    at // experts,
                    :,
                    starts[at % experts] : starts[at % experts] + blocks[at % experts],
                    :,
                    col : col + columns,
                ],
                wide_sems.at[col // columns, at],
            )
            for at, side in enumerate(sides)
        ]
        for col in chunks
    ]
    for copy in early + small_copies:
        copy.start()

    @pl.when(core == 0)
    def _():
        for copy in weight_copies(own[1], own[2], other[0], other[2]):
            copy.start()

    @pl.when(core != 0)
    def _():
        for copy in weight_copies(other[1], other[2], own[0], own[2]):
            copy.start()

    for copies in wide_copies:
        for copy in copies:
            copy.start()
    for copy in early:
        copy.wait()
    unpack(sizes, id_buf, back, result)
    leaving = [pltpu.make_async_copy(result, out_hidden, sems.at[6])]
    leaving[0].start()
    for copy in small_copies + weight_copies(own[1], own[2], other[0], other[2]):
        copy.wait()

    def sliced(source, which, here):
        side, near = source // replicas, source % replicas
        at = [
            replicas - 1 + step if near == 0 else starts[step] + near - 1
            for step in range(experts)
        ]
        return jnp.concatenate([wide_buf[side, which, one, :, here] for one in at], axis=0)

    def moment(at, index):
        value = moments[at, index * 128 : (index + 1) * 128]
        return jnp.concatenate([value] * (columns // 128), axis=1)

    def work(first):
        held = lax.broadcasted_iota(jnp.int32, (128, 6 * 128), 0)
        wanted = lax.broadcasted_iota(jnp.int32, (128, 6 * 128), 1) // 128
        adds = (held // 3 == wanted).astype(jnp.float32).astype(jnp.bfloat16)
        moments[...] = matmul(small[:, 4 * rank :], adds)
        act, d_pre = (0, 2) if first else (1, 3)
        turned[0] = small[:, act * rank : (act + 1) * rank].T
        turned[1] = small[:, d_pre * rank : (d_pre + 1) * rank].T
        for index, col in enumerate(chunks):
            here = slice(col, col + columns)
            for copy in wide_copies[index]:
                copy.wait()
            ups = matmul(small[:, :rank], up_buf[:, here])
            scales = [gain_buf[at, :, here].astype(jnp.float32) for at in range(2)]
            if first:
                downs = matmul(small[:, 3 * rank : 4 * rank], dn_buf[here, :], TRANS_RHS)
            for source in range(sources):
                at = slice(source * rows, (source + 1) * rows)
                wide = sliced(source, 0, here).astype(jnp.float32)
                grad_in = sliced(source, 1, here)
                middle = (wide + ups[at]).astype(jnp.bfloat16).astype(jnp.float32)
                inverse = moment(at, 3)
                normed = (middle - moment(at, 2)) * inverse
                if first:
                    entered = (wide - moment(at, 0)) * moment(at, 1)
                    lows[index, at] = (entered * scales[0]).astype(jnp.bfloat16)
                    d_norm = downs[at] * scales[1]
                    grads[index, at] = (
                        grad_in.astype(jnp.float32)
                        + inverse * (d_norm - moment(at, 4) - normed * moment(at, 5))
                    ).astype(jnp.bfloat16)
                else:
                    lows[index, at] = (normed * scales[1]).astype(jnp.bfloat16)
                    grads[index, at] = grad_in
            dn_out[here, :] = matmul(turned[1], lows[index]).astype(jnp.bfloat16).T
            up_out[index] = matmul(turned[0], grads[index]).astype(jnp.bfloat16)
            for copy in out_copies(index, here):
                copy.start()

    def out_copies(index, here):
        return [
            pltpu.make_async_copy(
                dn_out.at[here, :], grad_dn.at[here, :], sems.at[7 + 2 * index]
            ),
            pltpu.make_async_copy(
                up_out.at[index], grad_upper.at[:, here], sems.at[8 + 2 * index]
            ),
        ]

    @pl.when(core == 0)
    def _():
        work(True)

    @pl.when(core != 0)
    def _():
        work(False)

    for index, col in enumerate(chunks):
        leaving += out_copies(index, slice(col, col + columns))
    for copy in leaving:
        copy.wait()


VMEM = pl.BlockSpec(memory_space=pltpu.VMEM)
HBM = pl.BlockSpec(memory_space=pltpu.HBM)


def call(kernel, name, grant, in_specs, outs, scratch=(), outs_in=VMEM, flops=0, moved=MIB):
    return pl.pallas_call(
        kernel,
        out_shape=tuple(jax.ShapeDtypeStruct(*out) for out in outs),
        in_specs=in_specs,
        out_specs=tuple(outs_in for _ in outs),
        scratch_shapes=list(scratch),
        compiler_params=pltpu.CompilerParams(vmem_limit_bytes=grant * MIB),
        cost_estimate=pl.CostEstimate(flops=flops, bytes_accessed=moved, transcendentals=0),
        name=name,
    )


def across(block, axis, distance):
    size = lax.axis_size(axis)
    return lax.ppermute(block, axis, [(i, i ^ distance) for i in range(size)])


def slab_route(replicas, pair, low):
    route = []
    for replica in range(replicas):
        for core in range(2):
            chip = 2 * core + ((replica & 1) ^ pair)
            route.append((2 * replica + core, 2 * chip + ((replica >> 1) ^ low)))
    return route


def on_device_two_phases(hidden_in, cotangent, cluster_ids, w_down, w_up, gain):
    experts = lax.axis_size("expert")
    replicas = lax.axis_size("dp")
    s_local, length, part = hidden_in.shape
    width = 2 * part
    capacity = 2 * s_local // experts
    slots = experts * capacity
    groups = 2 * experts
    rows = slots * length // groups
    tokens = experts * rows
    own = (w_down[0, 0], w_up[0, 0], gain[0])
    rank = own[0].shape[1]
    slab = width // replicas
    bf16, f32 = jnp.bfloat16, jnp.float32
    sizes = (length, capacity, slots)
    sections = ("expert", "segment")

    other = tuple(across(array, "segment", 1) for array in own)
    half = s_local * length // 2
    (send,) = call(
        functools.partial(pack_kernel, *sizes),
        "pack",
        60,
        [HBM] * 3,
        [((groups, 2, rows, part), bf16)],
        [
            pltpu.SMEM(cluster_ids.shape, jnp.int32),
            pltpu.VMEM((2,) + hidden_in.shape, bf16),
            pltpu.VMEM((groups, 2, rows, part), bf16),
            pltpu.SemaphoreType.DMA((5,)),
        ],
        outs_in=HBM,
    )(cluster_ids, hidden_in, cotangent)
    slabs = call(
        functools.partial(slab_kernel, *sizes),
        "slabs",
        60,
        [HBM] * 4,
        [((2 * half + 16, slab), bf16)] * 4,
        [
            pltpu.SMEM(cluster_ids.shape, jnp.int32),
            pltpu.VMEM((2,) + hidden_in.shape, bf16),
            pltpu.VMEM((2, 2 * half, part), bf16),
            pltpu.VMEM((2, 16, 128), bf16),
            pltpu.VMEM((4, 2 * half + 16, slab), bf16),
            pltpu.SemaphoreType.DMA((7,)),
        ],
        outs_in=HBM,
    )(cluster_ids, hidden_in, cotangent, send)
    recv = lax.all_to_all(send, sections, split_axis=0, concat_axis=0, tiled=True)
    recv = recv.reshape(experts, 2, 2, rows, part)
    slabs = [
        lax.ppermute(block, ("dp", "segment"), slab_route(replicas, turn // 2, turn % 2))
        for turn, block in enumerate(slabs)
    ]
    out, small = call(
        chain_kernel,
        "chain",
        50,
        [HBM] * 7,
        [((experts, 2, rows, part), bf16), ((tokens, 4 * rank + 128), bf16)],
        [
            pltpu.VMEM(recv.shape, bf16),
            pltpu.VMEM((2, width, rank), bf16),
            pltpu.VMEM((2, rank, width), bf16),
            pltpu.VMEM((2, 1, width), bf16),
            pltpu.VMEM((tokens, width), bf16),
            pltpu.VMEM((tokens, width), bf16),
            pltpu.VMEM((tokens, width), f32),
            pltpu.SemaphoreType.DMA((3, 3)),
        ],
        flops=7 * 2 * tokens * width * rank,
        moved=10 * MIB,
    )(recv, *own, *other)
    slices = call(
        functools.partial(repack_kernel, length, capacity),
        "repack",
        16,
        [VMEM] * 4 + [HBM] * 2,
        [((2, replicas - 1 + experts, rows, slab), bf16)]
        + [((2, replicas - 1, rows, slab), bf16)] * (experts - 1),
        [pltpu.SemaphoreType.DMA((experts,))],
    )(*slabs, recv, small)
    small, *slices = lax.optimization_barrier((small, *slices))
    mine = [slices[0]] + [across(slices[step], "expert", step) for step in range(1, experts)]
    mine[:2] = lax.optimization_barrier(tuple(mine[:2]))
    near = [small] + [across(small, "dp", step) for step in range(1, replicas - 1)]
    near[:2] = lax.optimization_barrier(tuple(near[:2]))
    last = across(near[0], "dp", replicas - 1)
    *near, mine[-1] = lax.optimization_barrier((*near, mine[-1]))
    near.append(last)
    theirs = [across(block, "segment", 1) for block in mine]
    smalls = near + [across(piece, "segment", 1) for piece in near]

    back = lax.all_to_all(
        out.reshape(groups, rows, part), sections, split_axis=0, concat_axis=0, tiled=True
    )

    sources = 2 * replicas
    all_tokens = sources * tokens
    out_hidden, grad_dn, grad_upper = call(
        functools.partial(gradient_kernel, experts, sources, sizes),
        "gradients",
        48,
        [HBM] * (2 * experts + sources + 8),
        [(hidden_in.shape, bf16), ((slab, rank), bf16), ((rank, slab), bf16)],
        [
            pltpu.SMEM(cluster_ids.shape, jnp.int32),
            pltpu.VMEM(back.shape, bf16),
            pltpu.VMEM(hidden_in.shape, bf16),
            pltpu.VMEM((slab, rank), bf16),
            pltpu.VMEM((rank, slab), bf16),
            pltpu.VMEM((2, 1, slab), bf16),
            pltpu.VMEM((2, 2, replicas * experts, rows, slab), bf16),
            pltpu.VMEM((all_tokens, 4 * rank + 128), bf16),
            pltpu.VMEM((all_tokens, 6 * 128), f32),
            pltpu.VMEM((2, rank, all_tokens), bf16),
            pltpu.VMEM((slab // 256, all_tokens, 256), bf16),
            pltpu.VMEM((slab // 256, all_tokens, 256), bf16),
            pltpu.VMEM((slab, rank), bf16),
            pltpu.VMEM((slab // 256, rank, 256), bf16),
            pltpu.SemaphoreType.DMA((sources,)),
            pltpu.SemaphoreType.DMA((slab // 256, 2 * experts)),
            pltpu.SemaphoreType.DMA((7 + 2 * (slab // 256),)),
        ],
        outs_in=HBM,
    )(*mine, *theirs, *smalls, *own, *other, cluster_ids, back)
    return (out_hidden, grad_dn[None, None], grad_upper[None, None])


def solution(mesh):
    two = dict(mesh.shape) == {"expert": 4, "dp": 4, "segment": 2}
    on_device = on_device_two_phases if two else on_device_pipelined
    return jax.shard_map(
        on_device,
        mesh=mesh,
        in_specs=(
            P(("expert", "dp"), None, "segment"),
            P(("expert", "dp"), None, "segment"),
            P(("expert", "dp")),
            P("expert", "segment", None, None),
            P("expert", "segment", None, None),
            P("expert", "segment", None),
        ),
        out_specs=(
            P(("expert", "dp"), None, "segment"),
            P("expert", "segment", "dp", None),
            P("expert", "segment", None, "dp"),
        ),
        check_vma=False,
    )
```

```python
import functools

import jax
import jax.numpy as jnp
from jax import lax
from jax.experimental import pallas as pl
from jax.experimental.pallas import tpu as pltpu
from jax.sharding import PartitionSpec as P

MICRO = 4


EPS = 1e-05
C_ZERO = 0.7978845608028654
C_ONE = 0.044715


def shifted(block, axis, distance):
    devices = range(lax.axis_size(axis))
    route = [(i - distance, i) for i in devices if i - distance in devices]
    return lax.ppermute(block, axis, route)


def from_root(block, axis, holder):
    block = jnp.where(lax.axis_index(axis) == holder, block, jnp.zeros_like(block))
    return lax.psum(block, axis)


def gelu_value(z):
    return 0.5 * z * (1.0 + jnp.tanh(C_ZERO * (z + C_ONE * z * z * z)))


def gelu_slope(z):
    tval = jnp.tanh(C_ZERO * (z + C_ONE * z * z * z))
    return 0.5 * (1.0 + tval) + 0.5 * z * (1.0 - tval * tval) * C_ZERO * (1.0 + 3.0 * C_ONE * z * z)


def normalize(hidden):
    wide = hidden.astype(jnp.float32)
    center = wide - jnp.mean(wide, axis=-1, keepdims=True)
    inverse = lax.rsqrt(jnp.mean(center * center, axis=-1, keepdims=True) + EPS)
    return (wide, center * inverse, inverse)


def phase_forward(hidden, w_dn, w_upper, scale):
    wide, normed, inverse = normalize(hidden)
    lowered = (normed * scale).astype(jnp.bfloat16)
    pre = jnp.dot(lowered, w_dn, preferred_element_type=jnp.float32)
    act = gelu_value(pre).astype(jnp.bfloat16)
    leaving = (wide + jnp.dot(act, w_upper, preferred_element_type=jnp.float32)).astype(
        jnp.bfloat16
    )
    return (leaving, pre)


def phase_backward(hidden, grad_in, pre, w_dn, w_upper, scale):
    wide, normed, inverse = normalize(hidden)
    lowered = (normed * scale).astype(jnp.bfloat16)
    act = gelu_value(pre).astype(jnp.bfloat16)
    d_act = jnp.dot(grad_in, w_upper.T, preferred_element_type=jnp.float32)
    d_pre = (d_act * gelu_slope(pre)).astype(jnp.bfloat16)
    d_low = jnp.dot(d_pre, w_dn.T, preferred_element_type=jnp.float32)
    d_norm = d_low * scale
    d_wide = inverse * (
        d_norm
        - jnp.mean(d_norm, axis=-1, keepdims=True)
        - normed * jnp.mean(d_norm * normed, axis=-1, keepdims=True)
    )
    grad_out = (grad_in.astype(jnp.float32) + d_wide).astype(jnp.bfloat16)
    return (grad_out, lowered, act, d_pre)


def put_slot(buffer, value, slot, valid):
    old_value = lax.dynamic_index_in_dim(buffer, slot, 0, keepdims=False)
    return lax.dynamic_update_index_in_dim(buffer, jnp.where(valid, value, old_value), slot, 0)


def on_device_pipelined(hidden_in, cotangent, cluster_ids, w_down, w_up, gain):
    experts = lax.axis_size("expert")
    phases = lax.axis_size("segment")
    phase = lax.axis_index("segment")
    s_local, length, quarter = hidden_in.shape
    capacity = 2 * s_local // experts
    slots = experts * capacity
    same = (cluster_ids[:, None] == cluster_ids[None, :]).astype(jnp.int32)
    earlier = jnp.sum(jnp.tril(same, -1), axis=1)
    target = cluster_ids * capacity + earlier
    place = (jnp.arange(slots, dtype=jnp.int32)[:, None] == target[None, :]).astype(jnp.bfloat16)

    def to_slots(local):
        flat = local.reshape(s_local, -1)
        moved = jnp.dot(place, flat, preferred_element_type=jnp.float32).astype(jnp.bfloat16)
        return moved.reshape((slots,) + local.shape[1:])

    full_in, full_cot = (
        lax.all_gather(hidden_in, "segment", axis=2, tiled=True),
        lax.all_gather(cotangent, "segment", axis=2, tiled=True),
    )
    slot_in, slot_cot = (
        lax.all_to_all(to_slots(full_in), "expert", split_axis=0, concat_axis=0, tiled=True),
        lax.all_to_all(to_slots(full_cot), "expert", split_axis=0, concat_axis=0, tiled=True),
    )
    width = slot_in.shape[2]
    micro_rows = slots * length // MICRO
    inputs = slot_in.reshape(MICRO, micro_rows, width)
    cots = slot_cot.reshape(MICRO, micro_rows, width)
    w_dn = w_down[0, 0]
    w_upper = w_up[0, 0]
    rank = w_dn.shape[1]
    scale = gain[0, 0].astype(jnp.float32)
    ticks = MICRO + phases - 1

    def forward_tick(tick, carry):
        received, saved, pres, results = carry
        which = tick - phase
        valid = (which >= 0) & (which < MICRO)
        slot = jnp.clip(which, 0, MICRO - 1)
        first = lax.dynamic_index_in_dim(inputs, jnp.minimum(tick, MICRO - 1), 0, keepdims=False)
        entering = jnp.where(phase == 0, first, received)
        leaving, pre = phase_forward(entering, w_dn, w_upper, scale)
        saved = put_slot(saved, entering, slot, valid)
        pres = put_slot(pres, pre, slot, valid)
        results = put_slot(results, leaving, slot, valid & (phase == phases - 1))
        received = shifted(leaving, "segment", 1)
        return (received, saved, pres, results)

    start = (
        jnp.zeros((micro_rows, width), jnp.bfloat16),
        jnp.zeros((MICRO, micro_rows, width), jnp.bfloat16),
        jnp.zeros((MICRO, micro_rows, rank), jnp.float32),
        jnp.zeros((MICRO, micro_rows, width), jnp.bfloat16),
    )
    received, saved, pres, results = lax.fori_loop(0, ticks, forward_tick, start)

    def backward_tick(tick, carry):
        received, lows, acts, dpres, grads = carry
        which = tick - (phases - 1 - phase)
        valid = (which >= 0) & (which < MICRO)
        slot = jnp.clip(which, 0, MICRO - 1)
        last = lax.dynamic_index_in_dim(cots, jnp.minimum(tick, MICRO - 1), 0, keepdims=False)
        grad_in = jnp.where(phase == phases - 1, last, received)
        hidden = lax.dynamic_index_in_dim(saved, slot, 0, keepdims=False)
        pre = lax.dynamic_index_in_dim(pres, slot, 0, keepdims=False)
        grad_out, lowered, act, d_pre = phase_backward(hidden, grad_in, pre, w_dn, w_upper, scale)
        lows = put_slot(lows, lowered, slot, valid)
        acts = put_slot(acts, act, slot, valid)
        dpres = put_slot(dpres, d_pre, slot, valid)
        grads = put_slot(grads, grad_in, slot, valid)
        received = shifted(grad_out, "segment", -1)
        return (received, lows, acts, dpres, grads)

    start_back = (
        jnp.zeros((micro_rows, width), jnp.bfloat16),
        jnp.zeros((MICRO, micro_rows, width), jnp.bfloat16),
        jnp.zeros((MICRO, micro_rows, rank), jnp.bfloat16),
        jnp.zeros((MICRO, micro_rows, rank), jnp.bfloat16),
        jnp.zeros((MICRO, micro_rows, width), jnp.bfloat16),
    )
    received, lows, acts, dpres, grads = lax.fori_loop(0, ticks, backward_tick, start_back)
    contract = (((0,), (0,)), ((), ()))
    grad_dn = lax.dot_general(
        lows.reshape(-1, width),
        dpres.reshape(-1, rank),
        contract,
        preferred_element_type=jnp.float32,
    )
    grad_upper = lax.dot_general(
        acts.reshape(-1, rank),
        grads.reshape(-1, width),
        contract,
        preferred_element_type=jnp.float32,
    )
    summed_dn, summed_upper = (
        lax.psum_scatter(
            grad_dn.astype(jnp.bfloat16), "dp", scatter_dimension=0, tiled=True
        ).astype(jnp.float32),
        lax.psum_scatter(
            grad_upper.astype(jnp.bfloat16), "dp", scatter_dimension=1, tiled=True
        ).astype(jnp.float32),
    )
    returned = from_root(results, "segment", phases - 1)
    returned = returned.reshape(slots, length, width)
    own = lax.dynamic_slice_in_dim(returned, phase * quarter, quarter, 2)
    back = lax.all_to_all(own, "expert", split_axis=0, concat_axis=0, tiled=True)
    out_hidden = jnp.dot(place.T, back.reshape(slots, -1), preferred_element_type=jnp.float32)
    out_hidden = out_hidden.astype(jnp.bfloat16).reshape(s_local, length, quarter)
    return (
        out_hidden,
        summed_dn.astype(jnp.bfloat16)[None, None],
        summed_upper.astype(jnp.bfloat16)[None, None],
    )


CHUNK = 512
MIB = 1024 * 1024
TRANS_RHS = (((1,), (1,)), ((), ()))
TRANS_LHS = (((0,), (0,)), ((), ()))


def matmul(left, right, dims=(((1,), (0,)), ((), ()))):
    return lax.dot_general(left, right, dims, preferred_element_type=jnp.float32)


def spread_ids(ids, shape, length):
    lane = lax.broadcasted_iota(jnp.int32, shape, 1)
    spread = jnp.zeros(shape, jnp.int32)
    for n in range(ids.shape[0]):
        spread = jnp.where(lane // length == n, ids[n], spread)
    return spread


def ranked(ids_row, length):
    tokens = ids_row.shape[1]
    kinds = lax.broadcasted_iota(jnp.int32, (8, tokens), 0)
    member = (kinds == ids_row).astype(jnp.float32)
    at_col = lax.broadcasted_iota(jnp.int32, (tokens, tokens), 0)
    at_row = lax.broadcasted_iota(jnp.int32, (tokens, tokens), 1)
    before = (lax.rem(at_col, length) == 0) & (at_col // length < at_row // length)
    counts = matmul(member.astype(jnp.bfloat16), before.astype(jnp.float32).astype(jnp.bfloat16))
    rank = jnp.sum(member * counts, axis=0, keepdims=True)
    total = jnp.sum(member, axis=1, keepdims=True) * (1.0 / length)
    lower = jnp.sum(jnp.where(kinds < ids_row, total, 0.0), axis=0, keepdims=True)
    return rank.astype(jnp.int32), lower.astype(jnp.int32)


def one_hot(target, rows):
    wanted = lax.broadcasted_iota(jnp.int32, (rows, target.shape[1]), 0)
    return (wanted == target).astype(jnp.float32).astype(jnp.bfloat16)


def placements(ids_row, length, capacity, slots):
    rank, lower = ranked(ids_row, length)
    token = lax.rem(lax.broadcasted_iota(jnp.int32, ids_row.shape, 1), length)
    place = rank + lower
    group = lax.rem(place, 2)
    per_core = capacity // 2
    packed = ((ids_row * 2 + group) * per_core + rank // 2) * length + token
    tokens = ids_row.shape[1]
    ordered = group * (tokens // 2) + (place // 2) * length + token
    return one_hot(packed, slots * length), one_hot(ordered, tokens)


def pack_kernel(length, capacity, slots, ids, hidden, cot, send, id_buf, buf, packed, sems):
    groups, _, rows, part = send.shape
    tokens = hidden.shape[0] * length
    arriving = [
        pltpu.make_async_copy(source, target, sems.at[at])
        for at, (source, target) in enumerate(
            ((ids, id_buf), (hidden, buf.at[0]), (cot, buf.at[1]))
        )
    ]
    leaving = [
        pltpu.make_async_copy(packed.at[:, at], send.at[:, at], sems.at[3 + at]) for at in range(2)
    ]
    for copy in arriving:
        copy.start()
    arriving[0].wait()
    ids_row = spread_ids(id_buf, (8, tokens), length)[:1]
    place, _ = placements(ids_row, length, capacity, slots)
    for which in range(2):
        arriving[1 + which].wait()
        moved = matmul(place, buf[which].reshape(tokens, part)).astype(jnp.bfloat16)
        for group in range(groups):
            packed[group, which] = moved[group * rows : (group + 1) * rows]
        leaving[which].start()
    for copy in leaving:
        copy.wait()


def slab_kernel(length, capacity, slots, ids, hidden, cot, _, *refs):
    slabs, refs = refs[:4], refs[4:]
    id_buf, buf, ordered, turned, out_slabs, sems = refs
    s_local, _, part = hidden.shape
    tokens = s_local * length
    slab = part // 2
    half = tokens // 2
    replica = lax.axis_index("dp")
    arriving = [
        pltpu.make_async_copy(source, target, sems.at[at])
        for at, (source, target) in enumerate(
            ((ids, id_buf), (hidden, buf.at[0]), (cot, buf.at[1]))
        )
    ]
    leaving = [
        pltpu.make_async_copy(out_slabs.at[at], slabs[at], sems.at[3 + at]) for at in range(4)
    ]
    for copy in arriving:
        copy.start()
    arriving[0].wait()
    ids_row = spread_ids(id_buf, (16, tokens), length)
    _, by_group = placements(ids_row[:1], length, capacity, slots)
    for group in range(2):
        mine = by_group[group * half : (group + 1) * half]
        clusters = matmul(ids_row.astype(jnp.float32).astype(jnp.bfloat16), mine, TRANS_RHS)
        turned[group] = jnp.concatenate(
            [clusters.astype(jnp.bfloat16), jnp.zeros((16, 128 - half), jnp.bfloat16)], axis=1
        )
    for which in range(2):
        arriving[1 + which].wait()
        flat = buf[which].reshape(tokens, part)
        ordered[which] = matmul(by_group, flat).astype(jnp.bfloat16)
    for turn in range(4):
        pair = (turn // 2) ^ (replica & 1)
        group = (turn % 2) ^ (replica >> 1)
        cols = pl.ds(pl.multiple_of(pair * slab, slab), slab)
        at = pl.ds(pl.multiple_of(group * half, half), half)
        for which in range(2):
            out_slabs[turn, which * half : (which + 1) * half] = ordered[which, at, cols]
        out_slabs[turn, tokens:] = jnp.zeros((16, slab), jnp.bfloat16)
        out_slabs[turn, tokens:, :128] = turned[group]
        leaving[turn].start()
    for copy in leaving:
        copy.wait()


def repack_kernel(length, capacity, *refs):
    slabs, recv, outs, sems = refs[:4], refs[4], refs[6:-1], refs[-1]
    kept, sent = outs[0], outs[1:]
    _, _, rows, slab = kept.shape
    experts = len(outs)
    half = (slabs[0].shape[0] - 16) // 2
    core, replica = lax.axis_index("segment"), lax.axis_index("dp")
    expert = lax.axis_index("expert")
    per_part = recv.shape[4] // slab
    part = replica // per_part
    cols = pl.ds(pl.multiple_of((replica - part * per_part) * slab, slab), slab)
    cuts = [
        pltpu.make_async_copy(
            recv.at[e, part, :, :, cols], kept.at[:, 3 + (e ^ expert)], sems.at[e]
        )
        for e in range(experts)
    ]
    for cut in cuts:
        cut.start()
    far_low = (replica >> 1) ^ core ^ 1

    def place_rows(held, near):
        ids_row = held[2 * half :, :128].astype(jnp.float32)[:1, :half].astype(jnp.int32)
        rank, _ = ranked(ids_row, length)
        token = lax.rem(lax.broadcasted_iota(jnp.int32, ids_row.shape, 1), length)
        step = ids_row ^ expert
        place = one_hot((step * (capacity // 2) + rank) * length + token, experts * rows)
        for which in range(2):
            moved = matmul(place, held[which * half : (which + 1) * half]).astype(jnp.bfloat16)
            kept[which, near - 1] = moved[:rows]
            for step_at, out in enumerate(sent):
                out[which, near - 1] = moved[(step_at + 1) * rows : (step_at + 2) * rows]

    place_rows(jnp.where(far_low == 1, slabs[1][...], slabs[0][...]), 2)
    for low in range(2):
        place_rows(slabs[2 + low][...], 1 + 2 * (low ^ (replica >> 1) ^ core))
    for cut in cuts:
        cut.wait()


def unpack_kernel(length, capacity, slots, ids, back, _, out, id_buf, sem):
    copy = pltpu.make_async_copy(ids, id_buf, sem)
    copy.start()
    groups, rows, width = back.shape
    s_local = out.shape[0]
    copy.wait()
    ids_row = spread_ids(id_buf, (8, s_local * length), length)[:1]
    place, _ = placements(ids_row, length, capacity, slots)
    moved = matmul(place, back[...].reshape(groups * rows, width), TRANS_LHS)
    out[...] = moved.astype(jnp.bfloat16).reshape(s_local, length, width)


def split_three(value):
    top = value.astype(jnp.bfloat16).astype(jnp.float32)
    mid = (value - top).astype(jnp.bfloat16).astype(jnp.float32)
    low = (value - top - mid).astype(jnp.bfloat16).astype(jnp.float32)
    return [top, mid, low]


def side_by_side(columns, tokens):
    lane = lax.broadcasted_iota(jnp.int32, (tokens, 128), 1)
    block = jnp.zeros((tokens, 128), jnp.float32)
    at = 0
    for column in columns:
        for piece in split_three(column):
            block = jnp.where(lane == at, piece, block)
            at += 1
    return block.astype(jnp.bfloat16)


def lanes(value):
    total = value[:, :128]
    for start in range(128, value.shape[1], 128):
        total = total + value[:, start : start + 128]
    return total


def row_sum(parts):
    return jnp.sum(parts, axis=1, keepdims=True)


def chain_kernel(
    recv_in, own_dn, own_up, own_gain, other_dn, other_up, other_gain,
    out, small,
    recv, dn_buf, up_buf, gain_buf, entering, middle, d_norms, sems,
):
    phase = lax.axis_index("segment")
    experts, phases, _, rows, part = recv.shape
    tokens = experts * rows
    width = phases * part
    rank = dn_buf.shape[2]
    own, other = (own_dn, own_up, own_gain), (other_dn, other_up, other_gain)

    def copies(sources, at):
        return [
            pltpu.make_async_copy(source, buffer.at[at], sems.at[at, which])
            for which, (source, buffer) in enumerate(zip(sources, (dn_buf, up_buf, gain_buf)))
        ]

    def fetch(at):
        for this in range(2):

            @pl.when(phase == this)
            def _():
                for copy in copies(own if at == this else other, at):
                    copy.start()

    arriving = [
        pltpu.make_async_copy(recv_in.at[:, :, at], recv.at[:, :, at], sems.at[2, at])
        for at in range(2)
    ]
    arriving[0].start()
    fetch(0)
    waits = [copies(own, at) for at in range(2)]
    cols = range(0, width, CHUNK)

    def block(which, col):
        half, start = col // part, col % part
        return jnp.concatenate(
            [recv[e, half, which, :, start : start + CHUNK] for e in range(experts)], axis=0
        )

    def inverse_of(ref, mean):
        total = jnp.zeros((tokens, 128), jnp.float32)
        for col in cols:
            center = ref[:, col : col + CHUNK].astype(jnp.float32) - mean
            total = total + lanes(center * center)
        return lax.rsqrt(row_sum(total) / width + EPS)

    def down(ref, mean, inverse, at):
        pre = jnp.zeros((tokens, rank), jnp.float32)
        for col in cols:
            here = slice(col, col + CHUNK)
            normed = (ref[:, here].astype(jnp.float32) - mean) * inverse
            lowered = (normed * gain_buf[at, :, here].astype(jnp.float32)).astype(jnp.bfloat16)
            pre = pre + matmul(lowered, dn_buf[at, here, :])
        return pre

    total = jnp.zeros((tokens, 128), jnp.float32)
    arriving[0].wait()
    for col in cols:
        value = block(0, col)
        entering[:, col : col + CHUNK] = value
        total = total + lanes(value.astype(jnp.float32))
    mean_0 = row_sum(total) / width
    inverse_0 = inverse_of(entering, mean_0)
    waits[0][0].wait()
    waits[0][2].wait()
    arriving[1].start()
    fetch(1)
    pre_0 = down(entering, mean_0, inverse_0, 0)
    act_0 = gelu_value(pre_0).astype(jnp.bfloat16)
    slope_0 = gelu_slope(pre_0)

    waits[0][1].wait()
    total = jnp.zeros((tokens, 128), jnp.float32)
    for col in cols:
        here = slice(col, col + CHUNK)
        value = entering[:, here].astype(jnp.float32) + matmul(act_0, up_buf[0, :, here])
        value = value.astype(jnp.bfloat16)
        middle[:, here] = value
        total = total + lanes(value.astype(jnp.float32))
    mean_1 = row_sum(total) / width
    inverse_1 = inverse_of(middle, mean_1)
    for copy in waits[1] + arriving[1:]:
        copy.wait()
    d_act = jnp.zeros((tokens, rank), jnp.float32)
    for col in cols:
        d_act = d_act + matmul(block(1, col), up_buf[1, :, col : col + CHUNK], TRANS_RHS)
    pre_1 = down(middle, mean_1, inverse_1, 1)
    act_1 = gelu_value(pre_1).astype(jnp.bfloat16)
    d_pre_1 = (d_act * gelu_slope(pre_1)).astype(jnp.bfloat16)

    total = jnp.zeros((tokens, 128), jnp.float32)
    cross = jnp.zeros((tokens, 128), jnp.float32)
    for col in cols:
        here = slice(col, col + CHUNK)
        wide = middle[:, here].astype(jnp.float32)
        d_norm = matmul(d_pre_1, dn_buf[1, here, :], TRANS_RHS)
        d_norm = d_norm * gain_buf[1, :, here].astype(jnp.float32)
        d_norms[:, here] = d_norm
        total = total + lanes(d_norm)
        cross = cross + lanes(d_norm * ((wide - mean_1) * inverse_1))
        leaving = (wide + matmul(act_1, up_buf[1, :, here])).astype(jnp.bfloat16)
        half, start = col // part, col % part
        for e in range(experts):
            out[e, half, :, start : start + CHUNK] = leaving[e * rows : (e + 1) * rows]
    shift = row_sum(total) / width
    along = row_sum(cross) / width
    d_act = jnp.zeros((tokens, rank), jnp.float32)
    for col in cols:
        here = slice(col, col + CHUNK)
        normed = (middle[:, here].astype(jnp.float32) - mean_1) * inverse_1
        grad = block(1, col).astype(jnp.float32) + inverse_1 * (
            d_norms[:, here] - shift - normed * along
        )
        d_act = d_act + matmul(grad.astype(jnp.bfloat16), up_buf[0, :, here], TRANS_RHS)
    d_pre_0 = (d_act * slope_0).astype(jnp.bfloat16)
    moments = (mean_0, inverse_0, mean_1, inverse_1, shift, along)
    kept = (act_0, act_1, d_pre_0, d_pre_1, side_by_side(moments, tokens))
    for e in range(experts):
        start = pl.multiple_of((e ^ lax.axis_index("expert")) * rows, rows)
        for at, value in enumerate(kept):
            cols = slice(at * rank, at * rank + value.shape[1])
            small[pl.ds(start, rows), cols] = value[e * rows : (e + 1) * rows]


def gradient_kernel(experts, sources, *refs):
    sides, refs = refs[: 2 * experts], refs[2 * experts :]
    smalls, refs = refs[:sources], refs[sources:]
    own, other, refs = refs[:3], refs[3:6], refs[6:]
    grad_dn, grad_upper = refs[:2]
    (dn_buf, up_buf, gain_buf, wide_buf, small, moments, turned, lows, grads,
     dn_out, up_out, small_sems, wide_sems, sems) = refs[2:]
    core = lax.axis_index("segment")
    place = lax.axis_index("dp")
    rows, slab = smalls[0].shape[0], sides[0].shape[3]
    replicas = sources // 2
    blocks = [side.shape[1] for side in sides[:experts]]
    starts = [sum(blocks[:step]) for step in range(experts)]
    rank = dn_buf.shape[1]
    columns = 256
    chunks = range(0, slab, columns)
    features = pl.ds(pl.multiple_of(place * slab, slab), slab)

    def weight_copies(up, gain_first, dn, gain_second):
        moves = (
            (up.at[:, features], up_buf),
            (gain_first.at[:, features], gain_buf.at[0]),
            (gain_second.at[:, features], gain_buf.at[1]),
            (dn.at[features, :], dn_buf),
        )
        return [
            pltpu.make_async_copy(source, target, sems.at[at])
            for at, (source, target) in enumerate(moves)
        ]

    small_copies = [
        pltpu.make_async_copy(
            source, small.at[at * rows : (at + 1) * rows], small_sems.at[at]
        )
        for at, source in enumerate(smalls)
    ]
    wide_copies = [
        [
            pltpu.make_async_copy(
                side.at[:, :, :, col : col + columns],
                wide_buf.at[
                    at // experts,
                    :,
                    starts[at % experts] : starts[at % experts] + blocks[at % experts],
                    :,
                    col : col + columns,
                ],
                wide_sems.at[col // columns, at],
            )
            for at, side in enumerate(sides)
        ]
        for col in chunks
    ]
    for copy in small_copies:
        copy.start()

    @pl.when(core == 0)
    def _():
        for copy in weight_copies(own[1], own[2], other[0], other[2]):
            copy.start()

    @pl.when(core != 0)
    def _():
        for copy in weight_copies(other[1], other[2], own[0], own[2]):
            copy.start()

    for copies in wide_copies:
        for copy in copies:
            copy.start()
    leaving = []
    for copy in small_copies + weight_copies(own[1], own[2], other[0], other[2]):
        copy.wait()

    def sliced(source, which, here):
        side, near = source // replicas, source % replicas
        at = [
            replicas - 1 + step if near == 0 else starts[step] + near - 1
            for step in range(experts)
        ]
        return jnp.concatenate([wide_buf[side, which, one, :, here] for one in at], axis=0)

    def moment(at, index):
        value = moments[at, index * 128 : (index + 1) * 128]
        return jnp.concatenate([value] * (columns // 128), axis=1)

    def work(first):
        held = lax.broadcasted_iota(jnp.int32, (128, 6 * 128), 0)
        wanted = lax.broadcasted_iota(jnp.int32, (128, 6 * 128), 1) // 128
        adds = (held // 3 == wanted).astype(jnp.float32).astype(jnp.bfloat16)
        moments[...] = matmul(small[:, 4 * rank :], adds)
        act, d_pre = (0, 2) if first else (1, 3)
        turned[0] = small[:, act * rank : (act + 1) * rank].T
        turned[1] = small[:, d_pre * rank : (d_pre + 1) * rank].T
        for index, col in enumerate(chunks):
            here = slice(col, col + columns)
            for copy in wide_copies[index]:
                copy.wait()
            ups = matmul(small[:, :rank], up_buf[:, here])
            scales = [gain_buf[at, :, here].astype(jnp.float32) for at in range(2)]
            if first:
                downs = matmul(small[:, 3 * rank : 4 * rank], dn_buf[here, :], TRANS_RHS)
            for source in range(sources):
                at = slice(source * rows, (source + 1) * rows)
                wide = sliced(source, 0, here).astype(jnp.float32)
                grad_in = sliced(source, 1, here)
                middle = (wide + ups[at]).astype(jnp.bfloat16).astype(jnp.float32)
                inverse = moment(at, 3)
                normed = (middle - moment(at, 2)) * inverse
                if first:
                    entered = (wide - moment(at, 0)) * moment(at, 1)
                    lows[index, at] = (entered * scales[0]).astype(jnp.bfloat16)
                    d_norm = downs[at] * scales[1]
                    grads[index, at] = (
                        grad_in.astype(jnp.float32)
                        + inverse * (d_norm - moment(at, 4) - normed * moment(at, 5))
                    ).astype(jnp.bfloat16)
                else:
                    lows[index, at] = (normed * scales[1]).astype(jnp.bfloat16)
                    grads[index, at] = grad_in
            dn_out[here, :] = matmul(turned[1], lows[index]).astype(jnp.bfloat16).T
            up_out[index] = matmul(turned[0], grads[index]).astype(jnp.bfloat16)
            for copy in out_copies(index, here):
                copy.start()

    def out_copies(index, here):
        return [
            pltpu.make_async_copy(
                dn_out.at[here, :], grad_dn.at[here, :], sems.at[7 + 2 * index]
            ),
            pltpu.make_async_copy(
                up_out.at[index], grad_upper.at[:, here], sems.at[8 + 2 * index]
            ),
        ]

    @pl.when(core == 0)
    def _():
        work(True)

    @pl.when(core != 0)
    def _():
        work(False)

    for index, col in enumerate(chunks):
        leaving += out_copies(index, slice(col, col + columns))
    for copy in leaving:
        copy.wait()


VMEM = pl.BlockSpec(memory_space=pltpu.VMEM)
HBM = pl.BlockSpec(memory_space=pltpu.HBM)


def call(kernel, name, grant, in_specs, outs, scratch=(), outs_in=VMEM, flops=0, moved=MIB):
    return pl.pallas_call(
        kernel,
        out_shape=tuple(jax.ShapeDtypeStruct(*out) for out in outs),
        in_specs=in_specs,
        out_specs=tuple(outs_in for _ in outs),
        scratch_shapes=list(scratch),
        compiler_params=pltpu.CompilerParams(vmem_limit_bytes=grant * MIB),
        cost_estimate=pl.CostEstimate(flops=flops, bytes_accessed=moved, transcendentals=0),
        name=name,
    )


def across(block, axis, distance):
    size = lax.axis_size(axis)
    return lax.ppermute(block, axis, [(i, i ^ distance) for i in range(size)])


def slab_route(replicas, pair, low):
    route = []
    for replica in range(replicas):
        for core in range(2):
            chip = 2 * core + ((replica & 1) ^ pair)
            route.append((2 * replica + core, 2 * chip + ((replica >> 1) ^ low)))
    return route


def on_device_two_phases(hidden_in, cotangent, cluster_ids, w_down, w_up, gain):
    experts = lax.axis_size("expert")
    replicas = lax.axis_size("dp")
    s_local, length, part = hidden_in.shape
    width = 2 * part
    capacity = 2 * s_local // experts
    slots = experts * capacity
    groups = 2 * experts
    rows = slots * length // groups
    tokens = experts * rows
    own = (w_down[0, 0], w_up[0, 0], gain[0])
    rank = own[0].shape[1]
    slab = width // replicas
    bf16, f32 = jnp.bfloat16, jnp.float32
    sizes = (length, capacity, slots)
    sections = ("expert", "segment")

    other = tuple(across(array, "segment", 1) for array in own)
    half = s_local * length // 2
    (send,) = call(
        functools.partial(pack_kernel, *sizes),
        "pack",
        60,
        [HBM] * 3,
        [((groups, 2, rows, part), bf16)],
        [
            pltpu.SMEM(cluster_ids.shape, jnp.int32),
            pltpu.VMEM((2,) + hidden_in.shape, bf16),
            pltpu.VMEM((groups, 2, rows, part), bf16),
            pltpu.SemaphoreType.DMA((5,)),
        ],
        outs_in=HBM,
    )(cluster_ids, hidden_in, cotangent)
    slabs = call(
        functools.partial(slab_kernel, *sizes),
        "slabs",
        60,
        [HBM] * 4,
        [((2 * half + 16, slab), bf16)] * 4,
        [
            pltpu.SMEM(cluster_ids.shape, jnp.int32),
            pltpu.VMEM((2,) + hidden_in.shape, bf16),
            pltpu.VMEM((2, 2 * half, part), bf16),
            pltpu.VMEM((2, 16, 128), bf16),
            pltpu.VMEM((4, 2 * half + 16, slab), bf16),
            pltpu.SemaphoreType.DMA((7,)),
        ],
        outs_in=HBM,
    )(cluster_ids, hidden_in, cotangent, send)
    recv = lax.all_to_all(send, sections, split_axis=0, concat_axis=0, tiled=True)
    recv = recv.reshape(experts, 2, 2, rows, part)
    slabs = [
        lax.ppermute(block, ("dp", "segment"), slab_route(replicas, turn // 2, turn % 2))
        for turn, block in enumerate(slabs)
    ]
    out, small = call(
        chain_kernel,
        "chain",
        50,
        [HBM] * 7,
        [((experts, 2, rows, part), bf16), ((tokens, 4 * rank + 128), bf16)],
        [
            pltpu.VMEM(recv.shape, bf16),
            pltpu.VMEM((2, width, rank), bf16),
            pltpu.VMEM((2, rank, width), bf16),
            pltpu.VMEM((2, 1, width), bf16),
            pltpu.VMEM((tokens, width), bf16),
            pltpu.VMEM((tokens, width), bf16),
            pltpu.VMEM((tokens, width), f32),
            pltpu.SemaphoreType.DMA((3, 3)),
        ],
        flops=7 * 2 * tokens * width * rank,
        moved=10 * MIB,
    )(recv, *own, *other)
    slices = call(
        functools.partial(repack_kernel, length, capacity),
        "repack",
        16,
        [VMEM] * 4 + [HBM] * 2,
        [((2, replicas - 1 + experts, rows, slab), bf16)]
        + [((2, replicas - 1, rows, slab), bf16)] * (experts - 1),
        [pltpu.SemaphoreType.DMA((experts,))],
    )(*slabs, recv, small)
    small, *slices = lax.optimization_barrier((small, *slices))
    mine = [slices[0]] + [across(slices[step], "expert", step) for step in range(1, experts)]
    mine[:2] = lax.optimization_barrier(tuple(mine[:2]))
    near = [small] + [across(small, "dp", step) for step in range(1, replicas - 1)]
    near[:2] = lax.optimization_barrier(tuple(near[:2]))
    last = across(near[0], "dp", replicas - 1)
    near[2], out = lax.optimization_barrier((near[2], out))
    *near, mine[-1] = lax.optimization_barrier((*near, mine[-1]))
    near.append(last)
    theirs = [across(block, "segment", 1) for block in mine]
    smalls = near + [across(piece, "segment", 1) for piece in near]

    back = lax.all_to_all(
        out.reshape(groups, rows, part), sections, split_axis=0, concat_axis=0, tiled=True
    )

    sources = 2 * replicas
    all_tokens = sources * tokens
    grad_dn, grad_upper = call(
        functools.partial(gradient_kernel, experts, sources),
        "gradients",
        60,
        [HBM] * (2 * experts + sources + 6),
        [((slab, rank), bf16), ((rank, slab), bf16)],
        [
            pltpu.VMEM((slab, rank), bf16),
            pltpu.VMEM((rank, slab), bf16),
            pltpu.VMEM((2, 1, slab), bf16),
            pltpu.VMEM((2, 2, replicas * experts, rows, slab), bf16),
            pltpu.VMEM((all_tokens, 4 * rank + 128), bf16),
            pltpu.VMEM((all_tokens, 6 * 128), f32),
            pltpu.VMEM((2, rank, all_tokens), bf16),
            pltpu.VMEM((slab // 256, all_tokens, 256), bf16),
            pltpu.VMEM((slab // 256, all_tokens, 256), bf16),
            pltpu.VMEM((slab, rank), bf16),
            pltpu.VMEM((slab // 256, rank, 256), bf16),
            pltpu.SemaphoreType.DMA((sources,)),
            pltpu.SemaphoreType.DMA((slab // 256, 2 * experts)),
            pltpu.SemaphoreType.DMA((7 + 2 * (slab // 256),)),
        ],
        outs_in=HBM,
    )(*mine, *theirs, *smalls, *own, *other)
    (out_hidden,) = call(
        functools.partial(unpack_kernel, *sizes),
        "unpack",
        60,
        [HBM, VMEM, HBM],
        [(hidden_in.shape, bf16)],
        [pltpu.SMEM(cluster_ids.shape, jnp.int32), pltpu.SemaphoreType.DMA],
    )(cluster_ids, back, grad_dn)
    return (out_hidden, grad_dn[None, None], grad_upper[None, None])


def solution(mesh):
    two = dict(mesh.shape) == {"expert": 4, "dp": 4, "segment": 2}
    on_device = on_device_two_phases if two else on_device_pipelined
    return jax.shard_map(
        on_device,
        mesh=mesh,
        in_specs=(
            P(("expert", "dp"), None, "segment"),
            P(("expert", "dp"), None, "segment"),
            P(("expert", "dp")),
            P("expert", "segment", None, None),
            P("expert", "segment", None, None),
            P("expert", "segment", None),
        ),
        out_specs=(
            P(("expert", "dp"), None, "segment"),
            P("expert", "segment", "dp", None),
            P("expert", "segment", None, "dp"),
        ),
        check_vma=False,
    )
```

```python
import functools

import jax
import jax.numpy as jnp
from jax import lax
from jax.experimental import pallas as pl
from jax.experimental.pallas import tpu as pltpu
from jax.sharding import PartitionSpec as P

MICRO = 4


EPS = 1e-05
C_ZERO = 0.7978845608028654
C_ONE = 0.044715


def shifted(block, axis, distance):
    devices = range(lax.axis_size(axis))
    route = [(i - distance, i) for i in devices if i - distance in devices]
    return lax.ppermute(block, axis, route)


def from_root(block, axis, holder):
    block = jnp.where(lax.axis_index(axis) == holder, block, jnp.zeros_like(block))
    return lax.psum(block, axis)


def gelu_value(z):
    return 0.5 * z * (1.0 + jnp.tanh(C_ZERO * (z + C_ONE * z * z * z)))


def gelu_slope(z):
    tval = jnp.tanh(C_ZERO * (z + C_ONE * z * z * z))
    return 0.5 * (1.0 + tval) + 0.5 * z * (1.0 - tval * tval) * C_ZERO * (1.0 + 3.0 * C_ONE * z * z)


def normalize(hidden):
    wide = hidden.astype(jnp.float32)
    center = wide - jnp.mean(wide, axis=-1, keepdims=True)
    inverse = lax.rsqrt(jnp.mean(center * center, axis=-1, keepdims=True) + EPS)
    return (wide, center * inverse, inverse)


def phase_forward(hidden, w_dn, w_upper, scale):
    wide, normed, inverse = normalize(hidden)
    lowered = (normed * scale).astype(jnp.bfloat16)
    pre = jnp.dot(lowered, w_dn, preferred_element_type=jnp.float32)
    act = gelu_value(pre).astype(jnp.bfloat16)
    leaving = (wide + jnp.dot(act, w_upper, preferred_element_type=jnp.float32)).astype(
        jnp.bfloat16
    )
    return (leaving, pre)


def phase_backward(hidden, grad_in, pre, w_dn, w_upper, scale):
    wide, normed, inverse = normalize(hidden)
    lowered = (normed * scale).astype(jnp.bfloat16)
    act = gelu_value(pre).astype(jnp.bfloat16)
    d_act = jnp.dot(grad_in, w_upper.T, preferred_element_type=jnp.float32)
    d_pre = (d_act * gelu_slope(pre)).astype(jnp.bfloat16)
    d_low = jnp.dot(d_pre, w_dn.T, preferred_element_type=jnp.float32)
    d_norm = d_low * scale
    d_wide = inverse * (
        d_norm
        - jnp.mean(d_norm, axis=-1, keepdims=True)
        - normed * jnp.mean(d_norm * normed, axis=-1, keepdims=True)
    )
    grad_out = (grad_in.astype(jnp.float32) + d_wide).astype(jnp.bfloat16)
    return (grad_out, lowered, act, d_pre)


def put_slot(buffer, value, slot, valid):
    old_value = lax.dynamic_index_in_dim(buffer, slot, 0, keepdims=False)
    return lax.dynamic_update_index_in_dim(buffer, jnp.where(valid, value, old_value), slot, 0)


def on_device_pipelined(hidden_in, cotangent, cluster_ids, w_down, w_up, gain):
    experts = lax.axis_size("expert")
    phases = lax.axis_size("segment")
    phase = lax.axis_index("segment")
    s_local, length, quarter = hidden_in.shape
    capacity = 2 * s_local // experts
    slots = experts * capacity
    same = (cluster_ids[:, None] == cluster_ids[None, :]).astype(jnp.int32)
    earlier = jnp.sum(jnp.tril(same, -1), axis=1)
    target = cluster_ids * capacity + earlier
    place = (jnp.arange(slots, dtype=jnp.int32)[:, None] == target[None, :]).astype(jnp.bfloat16)

    def to_slots(local):
        flat = local.reshape(s_local, -1)
        moved = jnp.dot(place, flat, preferred_element_type=jnp.float32).astype(jnp.bfloat16)
        return moved.reshape((slots,) + local.shape[1:])

    full_in, full_cot = (
        lax.all_gather(hidden_in, "segment", axis=2, tiled=True),
        lax.all_gather(cotangent, "segment", axis=2, tiled=True),
    )
    slot_in, slot_cot = (
        lax.all_to_all(to_slots(full_in), "expert", split_axis=0, concat_axis=0, tiled=True),
        lax.all_to_all(to_slots(full_cot), "expert", split_axis=0, concat_axis=0, tiled=True),
    )
    width = slot_in.shape[2]
    micro_rows = slots * length // MICRO
    inputs = slot_in.reshape(MICRO, micro_rows, width)
    cots = slot_cot.reshape(MICRO, micro_rows, width)
    w_dn = w_down[0, 0]
    w_upper = w_up[0, 0]
    rank = w_dn.shape[1]
    scale = gain[0, 0].astype(jnp.float32)
    ticks = MICRO + phases - 1

    def forward_tick(tick, carry):
        received, saved, pres, results = carry
        which = tick - phase
        valid = (which >= 0) & (which < MICRO)
        slot = jnp.clip(which, 0, MICRO - 1)
        first = lax.dynamic_index_in_dim(inputs, jnp.minimum(tick, MICRO - 1), 0, keepdims=False)
        entering = jnp.where(phase == 0, first, received)
        leaving, pre = phase_forward(entering, w_dn, w_upper, scale)
        saved = put_slot(saved, entering, slot, valid)
        pres = put_slot(pres, pre, slot, valid)
        results = put_slot(results, leaving, slot, valid & (phase == phases - 1))
        received = shifted(leaving, "segment", 1)
        return (received, saved, pres, results)

    start = (
        jnp.zeros((micro_rows, width), jnp.bfloat16),
        jnp.zeros((MICRO, micro_rows, width), jnp.bfloat16),
        jnp.zeros((MICRO, micro_rows, rank), jnp.float32),
        jnp.zeros((MICRO, micro_rows, width), jnp.bfloat16),
    )
    received, saved, pres, results = lax.fori_loop(0, ticks, forward_tick, start)

    def backward_tick(tick, carry):
        received, lows, acts, dpres, grads = carry
        which = tick - (phases - 1 - phase)
        valid = (which >= 0) & (which < MICRO)
        slot = jnp.clip(which, 0, MICRO - 1)
        last = lax.dynamic_index_in_dim(cots, jnp.minimum(tick, MICRO - 1), 0, keepdims=False)
        grad_in = jnp.where(phase == phases - 1, last, received)
        hidden = lax.dynamic_index_in_dim(saved, slot, 0, keepdims=False)
        pre = lax.dynamic_index_in_dim(pres, slot, 0, keepdims=False)
        grad_out, lowered, act, d_pre = phase_backward(hidden, grad_in, pre, w_dn, w_upper, scale)
        lows = put_slot(lows, lowered, slot, valid)
        acts = put_slot(acts, act, slot, valid)
        dpres = put_slot(dpres, d_pre, slot, valid)
        grads = put_slot(grads, grad_in, slot, valid)
        received = shifted(grad_out, "segment", -1)
        return (received, lows, acts, dpres, grads)

    start_back = (
        jnp.zeros((micro_rows, width), jnp.bfloat16),
        jnp.zeros((MICRO, micro_rows, width), jnp.bfloat16),
        jnp.zeros((MICRO, micro_rows, rank), jnp.bfloat16),
        jnp.zeros((MICRO, micro_rows, rank), jnp.bfloat16),
        jnp.zeros((MICRO, micro_rows, width), jnp.bfloat16),
    )
    received, lows, acts, dpres, grads = lax.fori_loop(0, ticks, backward_tick, start_back)
    contract = (((0,), (0,)), ((), ()))
    grad_dn = lax.dot_general(
        lows.reshape(-1, width),
        dpres.reshape(-1, rank),
        contract,
        preferred_element_type=jnp.float32,
    )
    grad_upper = lax.dot_general(
        acts.reshape(-1, rank),
        grads.reshape(-1, width),
        contract,
        preferred_element_type=jnp.float32,
    )
    summed_dn, summed_upper = (
        lax.psum_scatter(
            grad_dn.astype(jnp.bfloat16), "dp", scatter_dimension=0, tiled=True
        ).astype(jnp.float32),
        lax.psum_scatter(
            grad_upper.astype(jnp.bfloat16), "dp", scatter_dimension=1, tiled=True
        ).astype(jnp.float32),
    )
    returned = from_root(results, "segment", phases - 1)
    returned = returned.reshape(slots, length, width)
    own = lax.dynamic_slice_in_dim(returned, phase * quarter, quarter, 2)
    back = lax.all_to_all(own, "expert", split_axis=0, concat_axis=0, tiled=True)
    out_hidden = jnp.dot(place.T, back.reshape(slots, -1), preferred_element_type=jnp.float32)
    out_hidden = out_hidden.astype(jnp.bfloat16).reshape(s_local, length, quarter)
    return (
        out_hidden,
        summed_dn.astype(jnp.bfloat16)[None, None],
        summed_upper.astype(jnp.bfloat16)[None, None],
    )


CHUNK = 512
MIB = 1024 * 1024
TRANS_RHS = (((1,), (1,)), ((), ()))
TRANS_LHS = (((0,), (0,)), ((), ()))


def matmul(left, right, dims=(((1,), (0,)), ((), ()))):
    return lax.dot_general(left, right, dims, preferred_element_type=jnp.float32)


def spread_ids(ids, shape, length):
    lane = lax.broadcasted_iota(jnp.int32, shape, 1)
    spread = jnp.zeros(shape, jnp.int32)
    for n in range(ids.shape[0]):
        spread = jnp.where(lane // length == n, ids[n], spread)
    return spread


def ranked(ids_row, length):
    tokens = ids_row.shape[1]
    kinds = lax.broadcasted_iota(jnp.int32, (8, tokens), 0)
    member = (kinds == ids_row).astype(jnp.float32)
    at_col = lax.broadcasted_iota(jnp.int32, (tokens, tokens), 0)
    at_row = lax.broadcasted_iota(jnp.int32, (tokens, tokens), 1)
    before = (lax.rem(at_col, length) == 0) & (at_col // length < at_row // length)
    counts = matmul(member.astype(jnp.bfloat16), before.astype(jnp.float32).astype(jnp.bfloat16))
    rank = jnp.sum(member * counts, axis=0, keepdims=True)
    total = jnp.sum(member, axis=1, keepdims=True) * (1.0 / length)
    lower = jnp.sum(jnp.where(kinds < ids_row, total, 0.0), axis=0, keepdims=True)
    return rank.astype(jnp.int32), lower.astype(jnp.int32)


def one_hot(target, rows):
    wanted = lax.broadcasted_iota(jnp.int32, (rows, target.shape[1]), 0)
    return (wanted == target).astype(jnp.float32).astype(jnp.bfloat16)


def placements(ids_row, length, capacity, slots):
    rank, lower = ranked(ids_row, length)
    token = lax.rem(lax.broadcasted_iota(jnp.int32, ids_row.shape, 1), length)
    place = rank + lower
    group = lax.rem(place, 2)
    per_core = capacity // 2
    packed = ((ids_row * 2 + group) * per_core + rank // 2) * length + token
    tokens = ids_row.shape[1]
    ordered = group * (tokens // 2) + (place // 2) * length + token
    return one_hot(packed, slots * length), one_hot(ordered, tokens)


def pack_kernel(length, capacity, slots, ids, hidden, cot, send, id_buf, buf, packed, sems):
    groups, _, rows, part = send.shape
    tokens = hidden.shape[0] * length
    strip = part // 4
    arriving = [
        pltpu.make_async_copy(source, target, sems.at[at])
        for at, (source, target) in enumerate(
            ((ids, id_buf), (hidden, buf.at[0]), (cot, buf.at[1]))
        )
    ]
    for copy in arriving:
        copy.start()
    arriving[0].wait()
    ids_row = spread_ids(id_buf, (8, tokens), length)[:1]
    place, _ = placements(ids_row, length, capacity, slots)
    leaving = []
    for which in range(2):
        arriving[1 + which].wait()
        for col in range(0, part, strip):
            here = slice(col, col + strip)
            moved = matmul(place, buf[which, :, :, here].reshape(tokens, strip))
            moved = moved.astype(jnp.bfloat16)
            for group in range(groups):
                packed[group, which, :, here] = moved[group * rows : (group + 1) * rows]
            leaving.append(
                pltpu.make_async_copy(
                    packed.at[:, which, :, here],
                    send.at[:, which, :, here],
                    sems.at[3 + len(leaving)],
                )
            )
            leaving[-1].start()
    for copy in leaving:
        copy.wait()


def slab_kernel(length, capacity, slots, ids, hidden, cot, _, *refs):
    slabs, refs = refs[:4], refs[4:]
    id_buf, buf, ordered, turned, out_slabs, sems = refs
    s_local, _, part = hidden.shape
    tokens = s_local * length
    slab = part // 2
    half = tokens // 2
    replica = lax.axis_index("dp")
    arriving = [
        pltpu.make_async_copy(source, target, sems.at[at])
        for at, (source, target) in enumerate(
            ((ids, id_buf), (hidden, buf.at[0]), (cot, buf.at[1]))
        )
    ]
    leaving = [
        pltpu.make_async_copy(out_slabs.at[at], slabs[at], sems.at[3 + at]) for at in range(4)
    ]
    for copy in arriving:
        copy.start()
    arriving[0].wait()
    ids_row = spread_ids(id_buf, (16, tokens), length)
    _, by_group = placements(ids_row[:1], length, capacity, slots)
    for group in range(2):
        mine = by_group[group * half : (group + 1) * half]
        clusters = matmul(ids_row.astype(jnp.float32).astype(jnp.bfloat16), mine, TRANS_RHS)
        turned[group] = jnp.concatenate(
            [clusters.astype(jnp.bfloat16), jnp.zeros((16, 128 - half), jnp.bfloat16)], axis=1
        )
    for which in range(2):
        arriving[1 + which].wait()
        flat = buf[which].reshape(tokens, part)
        ordered[which] = matmul(by_group, flat).astype(jnp.bfloat16)
    for turn in range(4):
        pair = (turn // 2) ^ (replica & 1)
        group = (turn % 2) ^ (replica >> 1)
        cols = pl.ds(pl.multiple_of(pair * slab, slab), slab)
        at = pl.ds(pl.multiple_of(group * half, half), half)
        for which in range(2):
            out_slabs[turn, which * half : (which + 1) * half] = ordered[which, at, cols]
        out_slabs[turn, tokens:] = jnp.zeros((16, slab), jnp.bfloat16)
        out_slabs[turn, tokens:, :128] = turned[group]
        leaving[turn].start()
    for copy in leaving:
        copy.wait()


def repack_kernel(length, capacity, *refs):
    slabs, recv, outs, sems = refs[:4], refs[4], refs[6:-1], refs[-1]
    kept, sent = outs[0], outs[1:]
    _, _, rows, slab = kept.shape
    experts = len(outs)
    half = (slabs[0].shape[0] - 16) // 2
    core, replica = lax.axis_index("segment"), lax.axis_index("dp")
    expert = lax.axis_index("expert")
    per_part = recv.shape[4] // slab
    part = replica // per_part
    cols = pl.ds(pl.multiple_of((replica - part * per_part) * slab, slab), slab)
    cuts = [
        pltpu.make_async_copy(
            recv.at[e, part, :, :, cols], kept.at[:, 3 + (e ^ expert)], sems.at[e]
        )
        for e in range(experts)
    ]
    for cut in cuts:
        cut.start()
    far_low = (replica >> 1) ^ core ^ 1

    def place_rows(held, near):
        ids_row = held[2 * half :, :128].astype(jnp.float32)[:1, :half].astype(jnp.int32)
        rank, _ = ranked(ids_row, length)
        token = lax.rem(lax.broadcasted_iota(jnp.int32, ids_row.shape, 1), length)
        step = ids_row ^ expert
        place = one_hot((step * (capacity // 2) + rank) * length + token, experts * rows)
        for which in range(2):
            moved = matmul(place, held[which * half : (which + 1) * half]).astype(jnp.bfloat16)
            kept[which, near - 1] = moved[:rows]
            for step_at, out in enumerate(sent):
                out[which, near - 1] = moved[(step_at + 1) * rows : (step_at + 2) * rows]

    place_rows(jnp.where(far_low == 1, slabs[1][...], slabs[0][...]), 2)
    for low in range(2):
        place_rows(slabs[2 + low][...], 1 + 2 * (low ^ (replica >> 1) ^ core))
    for cut in cuts:
        cut.wait()


def unpack(sizes, id_buf, back, out):
    length, capacity, slots = sizes
    groups, rows, width = back.shape
    s_local = out.shape[0]
    ids_row = spread_ids(id_buf, (8, s_local * length), length)[:1]
    place, _ = placements(ids_row, length, capacity, slots)
    moved = matmul(place, back[...].reshape(groups * rows, width), TRANS_LHS)
    out[...] = moved.astype(jnp.bfloat16).reshape(s_local, length, width)


def split_three(value):
    top = value.astype(jnp.bfloat16).astype(jnp.float32)
    mid = (value - top).astype(jnp.bfloat16).astype(jnp.float32)
    low = (value - top - mid).astype(jnp.bfloat16).astype(jnp.float32)
    return [top, mid, low]


def side_by_side(columns, tokens):
    lane = lax.broadcasted_iota(jnp.int32, (tokens, 128), 1)
    block = jnp.zeros((tokens, 128), jnp.float32)
    at = 0
    for column in columns:
        for piece in split_three(column):
            block = jnp.where(lane == at, piece, block)
            at += 1
    return block.astype(jnp.bfloat16)


def lanes(value):
    total = value[:, :128]
    for start in range(128, value.shape[1], 128):
        total = total + value[:, start : start + 128]
    return total


def row_sum(parts):
    return jnp.sum(parts, axis=1, keepdims=True)


def chain_kernel(
    recv_in, own_dn, own_up, own_gain, other_dn, other_up, other_gain,
    out, small,
    recv, dn_buf, up_buf, gain_buf, entering, middle, d_norms, sems,
):
    phase = lax.axis_index("segment")
    experts, phases, _, rows, part = recv.shape
    tokens = experts * rows
    width = phases * part
    rank = dn_buf.shape[2]
    own, other = (own_dn, own_up, own_gain), (other_dn, other_up, other_gain)

    def copies(sources, at):
        return [
            pltpu.make_async_copy(source, buffer.at[at], sems.at[at, which])
            for which, (source, buffer) in enumerate(zip(sources, (dn_buf, up_buf, gain_buf)))
        ]

    def fetch(at):
        for this in range(2):

            @pl.when(phase == this)
            def _():
                for copy in copies(own if at == this else other, at):
                    copy.start()

    arriving = [
        pltpu.make_async_copy(recv_in.at[:, :, at], recv.at[:, :, at], sems.at[2, at])
        for at in range(2)
    ]
    arriving[0].start()
    fetch(0)
    fetch(1)
    arriving[1].start()
    waits = [copies(own, at) for at in range(2)]
    cols = range(0, width, CHUNK)

    def block(which, col):
        half, start = col // part, col % part
        return jnp.concatenate(
            [recv[e, half, which, :, start : start + CHUNK] for e in range(experts)], axis=0
        )

    def inverse_of(ref, mean):
        total = jnp.zeros((tokens, 128), jnp.float32)
        for col in cols:
            center = ref[:, col : col + CHUNK].astype(jnp.float32) - mean
            total = total + lanes(center * center)
        return lax.rsqrt(row_sum(total) / width + EPS)

    def down(ref, mean, inverse, at):
        pre = jnp.zeros((tokens, rank), jnp.float32)
        for col in cols:
            here = slice(col, col + CHUNK)
            normed = (ref[:, here].astype(jnp.float32) - mean) * inverse
            lowered = (normed * gain_buf[at, :, here].astype(jnp.float32)).astype(jnp.bfloat16)
            pre = pre + matmul(lowered, dn_buf[at, here, :])
        return pre

    total = jnp.zeros((tokens, 128), jnp.float32)
    arriving[0].wait()
    for col in cols:
        value = block(0, col)
        entering[:, col : col + CHUNK] = value
        total = total + lanes(value.astype(jnp.float32))
    mean_0 = row_sum(total) / width
    inverse_0 = inverse_of(entering, mean_0)
    waits[0][0].wait()
    waits[0][2].wait()
    pre_0 = down(entering, mean_0, inverse_0, 0)
    act_0 = gelu_value(pre_0).astype(jnp.bfloat16)
    slope_0 = gelu_slope(pre_0)

    waits[0][1].wait()
    total = jnp.zeros((tokens, 128), jnp.float32)
    for col in cols:
        here = slice(col, col + CHUNK)
        value = entering[:, here].astype(jnp.float32) + matmul(act_0, up_buf[0, :, here])
        value = value.astype(jnp.bfloat16)
        middle[:, here] = value
        total = total + lanes(value.astype(jnp.float32))
    mean_1 = row_sum(total) / width
    inverse_1 = inverse_of(middle, mean_1)
    for copy in waits[1] + arriving[1:]:
        copy.wait()
    d_act = jnp.zeros((tokens, rank), jnp.float32)
    for col in cols:
        d_act = d_act + matmul(block(1, col), up_buf[1, :, col : col + CHUNK], TRANS_RHS)
    pre_1 = down(middle, mean_1, inverse_1, 1)
    act_1 = gelu_value(pre_1).astype(jnp.bfloat16)
    d_pre_1 = (d_act * gelu_slope(pre_1)).astype(jnp.bfloat16)

    total = jnp.zeros((tokens, 128), jnp.float32)
    cross = jnp.zeros((tokens, 128), jnp.float32)
    for col in cols:
        here = slice(col, col + CHUNK)
        wide = middle[:, here].astype(jnp.float32)
        d_norm = matmul(d_pre_1, dn_buf[1, here, :], TRANS_RHS)
        d_norm = d_norm * gain_buf[1, :, here].astype(jnp.float32)
        d_norms[:, here] = d_norm
        total = total + lanes(d_norm)
        cross = cross + lanes(d_norm * ((wide - mean_1) * inverse_1))
        leaving = (wide + matmul(act_1, up_buf[1, :, here])).astype(jnp.bfloat16)
        half, start = col // part, col % part
        for e in range(experts):
            out[e, half, :, start : start + CHUNK] = leaving[e * rows : (e + 1) * rows]
    shift = row_sum(total) / width
    along = row_sum(cross) / width
    d_act = jnp.zeros((tokens, rank), jnp.float32)
    for col in cols:
        here = slice(col, col + CHUNK)
        normed = (middle[:, here].astype(jnp.float32) - mean_1) * inverse_1
        grad = block(1, col).astype(jnp.float32) + inverse_1 * (
            d_norms[:, here] - shift - normed * along
        )
        d_act = d_act + matmul(grad.astype(jnp.bfloat16), up_buf[0, :, here], TRANS_RHS)
    d_pre_0 = (d_act * slope_0).astype(jnp.bfloat16)
    moments = (mean_0, inverse_0, mean_1, inverse_1, shift, along)
    kept = (act_0, act_1, d_pre_0, d_pre_1, side_by_side(moments, tokens))
    for e in range(experts):
        start = pl.multiple_of((e ^ lax.axis_index("expert")) * rows, rows)
        for at, value in enumerate(kept):
            cols = slice(at * rank, at * rank + value.shape[1])
            small[pl.ds(start, rows), cols] = value[e * rows : (e + 1) * rows]


def gradient_kernel(experts, sources, sizes, *refs):
    sides, refs = refs[: 2 * experts], refs[2 * experts :]
    smalls, refs = refs[:sources], refs[sources:]
    own, other, refs = refs[:3], refs[3:6], refs[6:]
    ids, back_in, out_hidden, grad_dn, grad_upper = refs[:5]
    (id_buf, back, result, dn_buf, up_buf, gain_buf, wide_buf, small, moments, turned, lows, grads,
     dn_out, up_out, small_sems, wide_sems, sems) = refs[5:]
    core = lax.axis_index("segment")
    place = lax.axis_index("dp")
    rows, slab = smalls[0].shape[0], sides[0].shape[3]
    replicas = sources // 2
    blocks = [side.shape[1] for side in sides[:experts]]
    starts = [sum(blocks[:step]) for step in range(experts)]
    rank = dn_buf.shape[1]
    columns = 256
    chunks = range(0, slab, columns)
    features = pl.ds(pl.multiple_of(place * slab, slab), slab)

    def weight_copies(up, gain_first, dn, gain_second):
        moves = (
            (up.at[:, features], up_buf),
            (gain_first.at[:, features], gain_buf.at[0]),
            (gain_second.at[:, features], gain_buf.at[1]),
            (dn.at[features, :], dn_buf),
        )
        return [
            pltpu.make_async_copy(source, target, sems.at[at])
            for at, (source, target) in enumerate(moves)
        ]

    early = [
        pltpu.make_async_copy(ids, id_buf, sems.at[4]),
        pltpu.make_async_copy(back_in, back, sems.at[5]),
    ]
    small_copies = [
        pltpu.make_async_copy(
            source, small.at[at * rows : (at + 1) * rows], small_sems.at[at]
        )
        for at, source in enumerate(smalls)
    ]
    wide_copies = [
        [
            pltpu.make_async_copy(
                side.at[:, :, :, col : col + columns],
                wide_buf.at[
                    at // experts,
                    :,
                    starts[at % experts] : starts[at % experts] + blocks[at % experts],
                    :,
                    col : col + columns,
                ],
                wide_sems.at[col // columns, at],
            )
            for at, side in enumerate(sides)
        ]
        for col in chunks
    ]
    for copy in early + small_copies:
        copy.start()

    @pl.when(core == 0)
    def _():
        for copy in weight_copies(own[1], own[2], other[0], other[2]):
            copy.start()

    @pl.when(core != 0)
    def _():
        for copy in weight_copies(other[1], other[2], own[0], own[2]):
            copy.start()

    for copies in wide_copies:
        for copy in copies:
            copy.start()
    for copy in early:
        copy.wait()
    unpack(sizes, id_buf, back, result)
    leaving = [pltpu.make_async_copy(result, out_hidden, sems.at[6])]
    leaving[0].start()
    for copy in small_copies + weight_copies(own[1], own[2], other[0], other[2]):
        copy.wait()

    def sliced(source, which, here):
        side, near = source // replicas, source % replicas
        at = [
            replicas - 1 + step if near == 0 else starts[step] + near - 1
            for step in range(experts)
        ]
        return jnp.concatenate([wide_buf[side, which, one, :, here] for one in at], axis=0)

    def moment(at, index):
        value = moments[at, index * 128 : (index + 1) * 128]
        return jnp.concatenate([value] * (columns // 128), axis=1)

    def work(first):
        held = lax.broadcasted_iota(jnp.int32, (128, 6 * 128), 0)
        wanted = lax.broadcasted_iota(jnp.int32, (128, 6 * 128), 1) // 128
        adds = (held // 3 == wanted).astype(jnp.float32).astype(jnp.bfloat16)
        moments[...] = matmul(small[:, 4 * rank :], adds)
        act, d_pre = (0, 2) if first else (1, 3)
        turned[0] = small[:, act * rank : (act + 1) * rank].T
        turned[1] = small[:, d_pre * rank : (d_pre + 1) * rank].T
        for index, col in enumerate(chunks):
            here = slice(col, col + columns)
            for copy in wide_copies[index]:
                copy.wait()
            ups = matmul(small[:, :rank], up_buf[:, here])
            scales = [gain_buf[at, :, here].astype(jnp.float32) for at in range(2)]
            if first:
                downs = matmul(small[:, 3 * rank : 4 * rank], dn_buf[here, :], TRANS_RHS)
            for source in range(sources):
                at = slice(source * rows, (source + 1) * rows)
                wide = sliced(source, 0, here).astype(jnp.float32)
                grad_in = sliced(source, 1, here)
                middle = (wide + ups[at]).astype(jnp.bfloat16).astype(jnp.float32)
                inverse = moment(at, 3)
                normed = (middle - moment(at, 2)) * inverse
                if first:
                    entered = (wide - moment(at, 0)) * moment(at, 1)
                    lows[index, at] = (entered * scales[0]).astype(jnp.bfloat16)
                    d_norm = downs[at] * scales[1]
                    grads[index, at] = (
                        grad_in.astype(jnp.float32)
                        + inverse * (d_norm - moment(at, 4) - normed * moment(at, 5))
                    ).astype(jnp.bfloat16)
                else:
                    lows[index, at] = (normed * scales[1]).astype(jnp.bfloat16)
                    grads[index, at] = grad_in
            dn_out[here, :] = matmul(turned[1], lows[index]).astype(jnp.bfloat16).T
            up_out[index] = matmul(turned[0], grads[index]).astype(jnp.bfloat16)
            for copy in out_copies(index, here):
                copy.start()

    def out_copies(index, here):
        return [
            pltpu.make_async_copy(
                dn_out.at[here, :], grad_dn.at[here, :], sems.at[7 + 2 * index]
            ),
            pltpu.make_async_copy(
                up_out.at[index], grad_upper.at[:, here], sems.at[8 + 2 * index]
            ),
        ]

    @pl.when(core == 0)
    def _():
        work(True)

    @pl.when(core != 0)
    def _():
        work(False)

    for index, col in enumerate(chunks):
        leaving += out_copies(index, slice(col, col + columns))
    for copy in leaving:
        copy.wait()


VMEM = pl.BlockSpec(memory_space=pltpu.VMEM)
HBM = pl.BlockSpec(memory_space=pltpu.HBM)


def call(kernel, name, grant, in_specs, outs, scratch=(), outs_in=VMEM, flops=0, moved=MIB):
    return pl.pallas_call(
        kernel,
        out_shape=tuple(jax.ShapeDtypeStruct(*out) for out in outs),
        in_specs=in_specs,
        out_specs=tuple(outs_in for _ in outs),
        scratch_shapes=list(scratch),
        compiler_params=pltpu.CompilerParams(vmem_limit_bytes=grant * MIB),
        cost_estimate=pl.CostEstimate(flops=flops, bytes_accessed=moved, transcendentals=0),
        name=name,
    )


def across(block, axis, distance):
    size = lax.axis_size(axis)
    return lax.ppermute(block, axis, [(i, i ^ distance) for i in range(size)])


def slab_route(replicas, pair, low):
    route = []
    for replica in range(replicas):
        for core in range(2):
            chip = 2 * core + ((replica & 1) ^ pair)
            route.append((2 * replica + core, 2 * chip + ((replica >> 1) ^ low)))
    return route


def on_device_two_phases(hidden_in, cotangent, cluster_ids, w_down, w_up, gain):
    experts = lax.axis_size("expert")
    replicas = lax.axis_size("dp")
    s_local, length, part = hidden_in.shape
    width = 2 * part
    capacity = 2 * s_local // experts
    slots = experts * capacity
    groups = 2 * experts
    rows = slots * length // groups
    tokens = experts * rows
    own = (w_down[0, 0], w_up[0, 0], gain[0])
    rank = own[0].shape[1]
    slab = width // replicas
    bf16, f32 = jnp.bfloat16, jnp.float32
    sizes = (length, capacity, slots)
    sections = ("expert", "segment")

    other = tuple(across(array, "segment", 1) for array in own)
    half = s_local * length // 2
    (send,) = call(
        functools.partial(pack_kernel, *sizes),
        "pack",
        60,
        [HBM] * 3,
        [((groups, 2, rows, part), bf16)],
        [
            pltpu.SMEM(cluster_ids.shape, jnp.int32),
            pltpu.VMEM((2,) + hidden_in.shape, bf16),
            pltpu.VMEM((groups, 2, rows, part), bf16),
            pltpu.SemaphoreType.DMA((11,)),
        ],
        outs_in=HBM,
    )(cluster_ids, hidden_in, cotangent)
    slabs = call(
        functools.partial(slab_kernel, *sizes),
        "slabs",
        60,
        [HBM] * 4,
        [((2 * half + 16, slab), bf16)] * 4,
        [
            pltpu.SMEM(cluster_ids.shape, jnp.int32),
            pltpu.VMEM((2,) + hidden_in.shape, bf16),
            pltpu.VMEM((2, 2 * half, part), bf16),
            pltpu.VMEM((2, 16, 128), bf16),
            pltpu.VMEM((4, 2 * half + 16, slab), bf16),
            pltpu.SemaphoreType.DMA((7,)),
        ],
        outs_in=HBM,
    )(cluster_ids, hidden_in, cotangent, send)
    recv = lax.all_to_all(send, sections, split_axis=0, concat_axis=0, tiled=True)
    recv = recv.reshape(experts, 2, 2, rows, part)
    slabs = [
        lax.ppermute(block, ("dp", "segment"), slab_route(replicas, turn // 2, turn % 2))
        for turn, block in enumerate(slabs)
    ]
    out, small = call(
        chain_kernel,
        "chain",
        50,
        [HBM] * 7,
        [((experts, 2, rows, part), bf16), ((tokens, 4 * rank + 128), bf16)],
        [
            pltpu.VMEM(recv.shape, bf16),
            pltpu.VMEM((2, width, rank), bf16),
            pltpu.VMEM((2, rank, width), bf16),
            pltpu.VMEM((2, 1, width), bf16),
            pltpu.VMEM((tokens, width), bf16),
            pltpu.VMEM((tokens, width), bf16),
            pltpu.VMEM((tokens, width), f32),
            pltpu.SemaphoreType.DMA((3, 3)),
        ],
        flops=7 * 2 * tokens * width * rank,
        moved=10 * MIB,
    )(recv, *own, *other)
    slices = call(
        functools.partial(repack_kernel, length, capacity),
        "repack",
        16,
        [VMEM] * 4 + [HBM] * 2,
        [((2, replicas - 1 + experts, rows, slab), bf16)]
        + [((2, replicas - 1, rows, slab), bf16)] * (experts - 1),
        [pltpu.SemaphoreType.DMA((experts,))],
    )(*slabs, recv, small)
    small, *slices = lax.optimization_barrier((small, *slices))
    mine = [slices[0]] + [across(slices[step], "expert", step) for step in range(1, experts)]
    mine[:2] = lax.optimization_barrier(tuple(mine[:2]))
    near = [small] + [across(small, "dp", step) for step in range(1, replicas - 1)]
    near[:2] = lax.optimization_barrier(tuple(near[:2]))
    last = across(near[0], "dp", replicas - 1)
    *near, mine[-1] = lax.optimization_barrier((*near, mine[-1]))
    near.append(last)
    theirs = [across(block, "segment", 1) for block in mine]
    smalls = near + [across(piece, "segment", 1) for piece in near]

    back = lax.all_to_all(
        out.reshape(groups, rows, part), sections, split_axis=0, concat_axis=0, tiled=True
    )

    sources = 2 * replicas
    all_tokens = sources * tokens
    out_hidden, grad_dn, grad_upper = call(
        functools.partial(gradient_kernel, experts, sources, sizes),
        "gradients",
        60,
        [HBM] * (2 * experts + sources + 8),
        [(hidden_in.shape, bf16), ((slab, rank), bf16), ((rank, slab), bf16)],
        [
            pltpu.SMEM(cluster_ids.shape, jnp.int32),
            pltpu.VMEM(back.shape, bf16),
            pltpu.VMEM(hidden_in.shape, bf16),
            pltpu.VMEM((slab, rank), bf16),
            pltpu.VMEM((rank, slab), bf16),
            pltpu.VMEM((2, 1, slab), bf16),
            pltpu.VMEM((2, 2, replicas * experts, rows, slab), bf16),
            pltpu.VMEM((all_tokens, 4 * rank + 128), bf16),
            pltpu.VMEM((all_tokens, 6 * 128), f32),
            pltpu.VMEM((2, rank, all_tokens), bf16),
            pltpu.VMEM((slab // 256, all_tokens, 256), bf16),
            pltpu.VMEM((slab // 256, all_tokens, 256), bf16),
            pltpu.VMEM((slab, rank), bf16),
            pltpu.VMEM((slab // 256, rank, 256), bf16),
            pltpu.SemaphoreType.DMA((sources,)),
            pltpu.SemaphoreType.DMA((slab // 256, 2 * experts)),
            pltpu.SemaphoreType.DMA((7 + 2 * (slab // 256),)),
        ],
        outs_in=HBM,
    )(*mine, *theirs, *smalls, *own, *other, cluster_ids, back)
    return (out_hidden, grad_dn[None, None], grad_upper[None, None])


def solution(mesh):
    two = dict(mesh.shape) == {"expert": 4, "dp": 4, "segment": 2}
    on_device = on_device_two_phases if two else on_device_pipelined
    return jax.shard_map(
        on_device,
        mesh=mesh,
        in_specs=(
            P(("expert", "dp"), None, "segment"),
            P(("expert", "dp"), None, "segment"),
            P(("expert", "dp")),
            P("expert", "segment", None, None),
            P("expert", "segment", None, None),
            P("expert", "segment", None),
        ),
        out_specs=(
            P(("expert", "dp"), None, "segment"),
            P("expert", "segment", "dp", None),
            P("expert", "segment", None, "dp"),
        ),
        check_vma=False,
    )
```

```python
import functools

import jax
import jax.numpy as jnp
from jax import lax
from jax.experimental import pallas as pl
from jax.experimental.pallas import tpu as pltpu
from jax.sharding import PartitionSpec as P

MICRO = 4


EPS = 1e-05
C_ZERO = 0.7978845608028654
C_ONE = 0.044715


def shifted(block, axis, distance):
    devices = range(lax.axis_size(axis))
    route = [(i - distance, i) for i in devices if i - distance in devices]
    return lax.ppermute(block, axis, route)


def from_root(block, axis, holder):
    block = jnp.where(lax.axis_index(axis) == holder, block, jnp.zeros_like(block))
    return lax.psum(block, axis)


def gelu_value(z):
    return 0.5 * z * (1.0 + jnp.tanh(C_ZERO * (z + C_ONE * z * z * z)))


def gelu_slope(z):
    tval = jnp.tanh(C_ZERO * (z + C_ONE * z * z * z))
    return 0.5 * (1.0 + tval) + 0.5 * z * (1.0 - tval * tval) * C_ZERO * (1.0 + 3.0 * C_ONE * z * z)


def normalize(hidden):
    wide = hidden.astype(jnp.float32)
    center = wide - jnp.mean(wide, axis=-1, keepdims=True)
    inverse = lax.rsqrt(jnp.mean(center * center, axis=-1, keepdims=True) + EPS)
    return (wide, center * inverse, inverse)


def phase_forward(hidden, w_dn, w_upper, scale):
    wide, normed, inverse = normalize(hidden)
    lowered = (normed * scale).astype(jnp.bfloat16)
    pre = jnp.dot(lowered, w_dn, preferred_element_type=jnp.float32)
    act = gelu_value(pre).astype(jnp.bfloat16)
    leaving = (wide + jnp.dot(act, w_upper, preferred_element_type=jnp.float32)).astype(
        jnp.bfloat16
    )
    return (leaving, pre)


def phase_backward(hidden, grad_in, pre, w_dn, w_upper, scale):
    wide, normed, inverse = normalize(hidden)
    lowered = (normed * scale).astype(jnp.bfloat16)
    act = gelu_value(pre).astype(jnp.bfloat16)
    d_act = jnp.dot(grad_in, w_upper.T, preferred_element_type=jnp.float32)
    d_pre = (d_act * gelu_slope(pre)).astype(jnp.bfloat16)
    d_low = jnp.dot(d_pre, w_dn.T, preferred_element_type=jnp.float32)
    d_norm = d_low * scale
    d_wide = inverse * (
        d_norm
        - jnp.mean(d_norm, axis=-1, keepdims=True)
        - normed * jnp.mean(d_norm * normed, axis=-1, keepdims=True)
    )
    grad_out = (grad_in.astype(jnp.float32) + d_wide).astype(jnp.bfloat16)
    return (grad_out, lowered, act, d_pre)


def put_slot(buffer, value, slot, valid):
    old_value = lax.dynamic_index_in_dim(buffer, slot, 0, keepdims=False)
    return lax.dynamic_update_index_in_dim(buffer, jnp.where(valid, value, old_value), slot, 0)


def on_device_pipelined(hidden_in, cotangent, cluster_ids, w_down, w_up, gain):
    experts = lax.axis_size("expert")
    phases = lax.axis_size("segment")
    phase = lax.axis_index("segment")
    s_local, length, quarter = hidden_in.shape
    capacity = 2 * s_local // experts
    slots = experts * capacity
    same = (cluster_ids[:, None] == cluster_ids[None, :]).astype(jnp.int32)
    earlier = jnp.sum(jnp.tril(same, -1), axis=1)
    target = cluster_ids * capacity + earlier
    place = (jnp.arange(slots, dtype=jnp.int32)[:, None] == target[None, :]).astype(jnp.bfloat16)

    def to_slots(local):
        flat = local.reshape(s_local, -1)
        moved = jnp.dot(place, flat, preferred_element_type=jnp.float32).astype(jnp.bfloat16)
        return moved.reshape((slots,) + local.shape[1:])

    full_in, full_cot = (
        lax.all_gather(hidden_in, "segment", axis=2, tiled=True),
        lax.all_gather(cotangent, "segment", axis=2, tiled=True),
    )
    slot_in, slot_cot = (
        lax.all_to_all(to_slots(full_in), "expert", split_axis=0, concat_axis=0, tiled=True),
        lax.all_to_all(to_slots(full_cot), "expert", split_axis=0, concat_axis=0, tiled=True),
    )
    width = slot_in.shape[2]
    micro_rows = slots * length // MICRO
    inputs = slot_in.reshape(MICRO, micro_rows, width)
    cots = slot_cot.reshape(MICRO, micro_rows, width)
    w_dn = w_down[0, 0]
    w_upper = w_up[0, 0]
    rank = w_dn.shape[1]
    scale = gain[0, 0].astype(jnp.float32)
    ticks = MICRO + phases - 1

    def forward_tick(tick, carry):
        received, saved, pres, results = carry
        which = tick - phase
        valid = (which >= 0) & (which < MICRO)
        slot = jnp.clip(which, 0, MICRO - 1)
        first = lax.dynamic_index_in_dim(inputs, jnp.minimum(tick, MICRO - 1), 0, keepdims=False)
        entering = jnp.where(phase == 0, first, received)
        leaving, pre = phase_forward(entering, w_dn, w_upper, scale)
        saved = put_slot(saved, entering, slot, valid)
        pres = put_slot(pres, pre, slot, valid)
        results = put_slot(results, leaving, slot, valid & (phase == phases - 1))
        received = shifted(leaving, "segment", 1)
        return (received, saved, pres, results)

    start = (
        jnp.zeros((micro_rows, width), jnp.bfloat16),
        jnp.zeros((MICRO, micro_rows, width), jnp.bfloat16),
        jnp.zeros((MICRO, micro_rows, rank), jnp.float32),
        jnp.zeros((MICRO, micro_rows, width), jnp.bfloat16),
    )
    received, saved, pres, results = lax.fori_loop(0, ticks, forward_tick, start)

    def backward_tick(tick, carry):
        received, lows, acts, dpres, grads = carry
        which = tick - (phases - 1 - phase)
        valid = (which >= 0) & (which < MICRO)
        slot = jnp.clip(which, 0, MICRO - 1)
        last = lax.dynamic_index_in_dim(cots, jnp.minimum(tick, MICRO - 1), 0, keepdims=False)
        grad_in = jnp.where(phase == phases - 1, last, received)
        hidden = lax.dynamic_index_in_dim(saved, slot, 0, keepdims=False)
        pre = lax.dynamic_index_in_dim(pres, slot, 0, keepdims=False)
        grad_out, lowered, act, d_pre = phase_backward(hidden, grad_in, pre, w_dn, w_upper, scale)
        lows = put_slot(lows, lowered, slot, valid)
        acts = put_slot(acts, act, slot, valid)
        dpres = put_slot(dpres, d_pre, slot, valid)
        grads = put_slot(grads, grad_in, slot, valid)
        received = shifted(grad_out, "segment", -1)
        return (received, lows, acts, dpres, grads)

    start_back = (
        jnp.zeros((micro_rows, width), jnp.bfloat16),
        jnp.zeros((MICRO, micro_rows, width), jnp.bfloat16),
        jnp.zeros((MICRO, micro_rows, rank), jnp.bfloat16),
        jnp.zeros((MICRO, micro_rows, rank), jnp.bfloat16),
        jnp.zeros((MICRO, micro_rows, width), jnp.bfloat16),
    )
    received, lows, acts, dpres, grads = lax.fori_loop(0, ticks, backward_tick, start_back)
    contract = (((0,), (0,)), ((), ()))
    grad_dn = lax.dot_general(
        lows.reshape(-1, width),
        dpres.reshape(-1, rank),
        contract,
        preferred_element_type=jnp.float32,
    )
    grad_upper = lax.dot_general(
        acts.reshape(-1, rank),
        grads.reshape(-1, width),
        contract,
        preferred_element_type=jnp.float32,
    )
    summed_dn, summed_upper = (
        lax.psum_scatter(
            grad_dn.astype(jnp.bfloat16), "dp", scatter_dimension=0, tiled=True
        ).astype(jnp.float32),
        lax.psum_scatter(
            grad_upper.astype(jnp.bfloat16), "dp", scatter_dimension=1, tiled=True
        ).astype(jnp.float32),
    )
    returned = from_root(results, "segment", phases - 1)
    returned = returned.reshape(slots, length, width)
    own = lax.dynamic_slice_in_dim(returned, phase * quarter, quarter, 2)
    back = lax.all_to_all(own, "expert", split_axis=0, concat_axis=0, tiled=True)
    out_hidden = jnp.dot(place.T, back.reshape(slots, -1), preferred_element_type=jnp.float32)
    out_hidden = out_hidden.astype(jnp.bfloat16).reshape(s_local, length, quarter)
    return (
        out_hidden,
        summed_dn.astype(jnp.bfloat16)[None, None],
        summed_upper.astype(jnp.bfloat16)[None, None],
    )


CHUNK = 512
MIB = 1024 * 1024
TRANS_RHS = (((1,), (1,)), ((), ()))
TRANS_LHS = (((0,), (0,)), ((), ()))


def matmul(left, right, dims=(((1,), (0,)), ((), ()))):
    return lax.dot_general(left, right, dims, preferred_element_type=jnp.float32)


def spread_ids(ids, shape, length):
    lane = lax.broadcasted_iota(jnp.int32, shape, 1)
    spread = jnp.zeros(shape, jnp.int32)
    for n in range(ids.shape[0]):
        spread = jnp.where(lane // length == n, ids[n], spread)
    return spread


def ranked(ids_row, length):
    tokens = ids_row.shape[1]
    kinds = lax.broadcasted_iota(jnp.int32, (8, tokens), 0)
    member = (kinds == ids_row).astype(jnp.float32)
    at_col = lax.broadcasted_iota(jnp.int32, (tokens, tokens), 0)
    at_row = lax.broadcasted_iota(jnp.int32, (tokens, tokens), 1)
    before = (lax.rem(at_col, length) == 0) & (at_col // length < at_row // length)
    counts = matmul(member.astype(jnp.bfloat16), before.astype(jnp.float32).astype(jnp.bfloat16))
    rank = jnp.sum(member * counts, axis=0, keepdims=True)
    total = jnp.sum(member, axis=1, keepdims=True) * (1.0 / length)
    lower = jnp.sum(jnp.where(kinds < ids_row, total, 0.0), axis=0, keepdims=True)
    return rank.astype(jnp.int32), lower.astype(jnp.int32)


def one_hot(target, rows):
    wanted = lax.broadcasted_iota(jnp.int32, (rows, target.shape[1]), 0)
    return (wanted == target).astype(jnp.float32).astype(jnp.bfloat16)


def placements(ids_row, length, capacity, slots):
    rank, lower = ranked(ids_row, length)
    token = lax.rem(lax.broadcasted_iota(jnp.int32, ids_row.shape, 1), length)
    place = rank + lower
    group = lax.rem(place, 2)
    per_core = capacity // 2
    packed = ((ids_row * 2 + group) * per_core + rank // 2) * length + token
    tokens = ids_row.shape[1]
    ordered = group * (tokens // 2) + (place // 2) * length + token
    return one_hot(packed, slots * length), one_hot(ordered, tokens)


def pack_kernel(length, capacity, slots, ids, hidden, cot, send, id_buf, buf, packed, sems):
    groups, _, rows, part = send.shape
    tokens = hidden.shape[0] * length
    arriving = [
        pltpu.make_async_copy(source, target, sems.at[at])
        for at, (source, target) in enumerate(
            ((ids, id_buf), (hidden, buf.at[0]), (cot, buf.at[1]))
        )
    ]
    leaving = [
        pltpu.make_async_copy(packed.at[:, at], send.at[:, at], sems.at[3 + at]) for at in range(2)
    ]
    for copy in arriving:
        copy.start()
    arriving[0].wait()
    ids_row = spread_ids(id_buf, (8, tokens), length)[:1]
    place, _ = placements(ids_row, length, capacity, slots)
    for which in range(2):
        arriving[1 + which].wait()
        moved = matmul(place, buf[which].reshape(tokens, part)).astype(jnp.bfloat16)
        for group in range(groups):
            packed[group, which] = moved[group * rows : (group + 1) * rows]
        leaving[which].start()
    for copy in leaving:
        copy.wait()


def slab_kernel(length, capacity, slots, ids, hidden, cot, _, *refs):
    slabs, refs = refs[:4], refs[4:]
    id_buf, buf, ordered, turned, out_slabs, sems = refs
    s_local, _, part = hidden.shape
    tokens = s_local * length
    slab = part // 2
    half = tokens // 2
    replica = lax.axis_index("dp")
    arriving = [
        pltpu.make_async_copy(source, target, sems.at[at])
        for at, (source, target) in enumerate(
            ((ids, id_buf), (hidden, buf.at[0]), (cot, buf.at[1]))
        )
    ]
    leaving = [
        pltpu.make_async_copy(out_slabs.at[at], slabs[at], sems.at[3 + at]) for at in range(4)
    ]
    for copy in arriving:
        copy.start()
    arriving[0].wait()
    ids_row = spread_ids(id_buf, (16, tokens), length)
    _, by_group = placements(ids_row[:1], length, capacity, slots)
    for group in range(2):
        mine = by_group[group * half : (group + 1) * half]
        clusters = matmul(ids_row.astype(jnp.float32).astype(jnp.bfloat16), mine, TRANS_RHS)
        turned[group] = jnp.concatenate(
            [clusters.astype(jnp.bfloat16), jnp.zeros((16, 128 - half), jnp.bfloat16)], axis=1
        )
    for which in range(2):
        arriving[1 + which].wait()
        flat = buf[which].reshape(tokens, part)
        ordered[which] = matmul(by_group, flat).astype(jnp.bfloat16)
    for turn in range(4):
        pair = (turn // 2) ^ (replica & 1)
        group = (turn % 2) ^ (replica >> 1)
        cols = pl.ds(pl.multiple_of(pair * slab, slab), slab)
        at = pl.ds(pl.multiple_of(group * half, half), half)
        for which in range(2):
            out_slabs[turn, which * half : (which + 1) * half] = ordered[which, at, cols]
        out_slabs[turn, tokens:] = jnp.zeros((16, slab), jnp.bfloat16)
        out_slabs[turn, tokens:, :128] = turned[group]
        leaving[turn].start()
    for copy in leaving:
        copy.wait()


def repack_kernel(length, capacity, *refs):
    slabs, recv, outs, sems = refs[:4], refs[4], refs[6:-1], refs[-1]
    kept, sent = outs[0], outs[1:]
    _, _, rows, slab = kept.shape
    experts = len(outs)
    half = (slabs[0].shape[0] - 16) // 2
    core, replica = lax.axis_index("segment"), lax.axis_index("dp")
    expert = lax.axis_index("expert")
    per_part = recv.shape[4] // slab
    part = replica // per_part
    cols = pl.ds(pl.multiple_of((replica - part * per_part) * slab, slab), slab)
    cuts = [
        pltpu.make_async_copy(
            recv.at[e, part, :, :, cols], kept.at[:, 3 + (e ^ expert)], sems.at[e]
        )
        for e in range(experts)
    ]
    for cut in cuts:
        cut.start()
    far_low = (replica >> 1) ^ core ^ 1

    def place_rows(held, near):
        ids_row = held[2 * half :, :128].astype(jnp.float32)[:1, :half].astype(jnp.int32)
        rank, _ = ranked(ids_row, length)
        token = lax.rem(lax.broadcasted_iota(jnp.int32, ids_row.shape, 1), length)
        step = ids_row ^ expert
        place = one_hot((step * (capacity // 2) + rank) * length + token, experts * rows)
        for which in range(2):
            moved = matmul(place, held[which * half : (which + 1) * half]).astype(jnp.bfloat16)
            kept[which, near - 1] = moved[:rows]
            for step_at, out in enumerate(sent):
                out[which, near - 1] = moved[(step_at + 1) * rows : (step_at + 2) * rows]

    place_rows(jnp.where(far_low == 1, slabs[1][...], slabs[0][...]), 2)
    for low in range(2):
        place_rows(slabs[2 + low][...], 1 + 2 * (low ^ (replica >> 1) ^ core))
    for cut in cuts:
        cut.wait()


def unpack(sizes, id_buf, back, out):
    length, capacity, slots = sizes
    groups, rows, width = back.shape
    s_local = out.shape[0]
    ids_row = spread_ids(id_buf, (8, s_local * length), length)[:1]
    place, _ = placements(ids_row, length, capacity, slots)
    moved = matmul(place, back[...].reshape(groups * rows, width), TRANS_LHS)
    out[...] = moved.astype(jnp.bfloat16).reshape(s_local, length, width)


def split_three(value):
    top = value.astype(jnp.bfloat16).astype(jnp.float32)
    mid = (value - top).astype(jnp.bfloat16).astype(jnp.float32)
    low = (value - top - mid).astype(jnp.bfloat16).astype(jnp.float32)
    return [top, mid, low]


def side_by_side(columns, tokens):
    lane = lax.broadcasted_iota(jnp.int32, (tokens, 128), 1)
    block = jnp.zeros((tokens, 128), jnp.float32)
    at = 0
    for column in columns:
        for piece in split_three(column):
            block = jnp.where(lane == at, piece, block)
            at += 1
    return block.astype(jnp.bfloat16)


def lanes(value):
    total = value[:, :128]
    for start in range(128, value.shape[1], 128):
        total = total + value[:, start : start + 128]
    return total


def row_sum(parts):
    return jnp.sum(parts, axis=1, keepdims=True)


def chain_kernel(
    recv_in, own_dn, own_up, own_gain, other_dn, other_up, other_gain,
    out, small,
    recv, dn_buf, up_buf, gain_buf, entering, middle, d_norms, sems,
):
    phase = lax.axis_index("segment")
    experts, phases, _, rows, part = recv.shape
    tokens = experts * rows
    width = phases * part
    rank = dn_buf.shape[2]
    own, other = (own_dn, own_up, own_gain), (other_dn, other_up, other_gain)

    def copies(sources, at):
        return [
            pltpu.make_async_copy(source, buffer.at[at], sems.at[at, which])
            for which, (source, buffer) in enumerate(zip(sources, (dn_buf, up_buf, gain_buf)))
        ]

    def fetch(at):
        for this in range(2):

            @pl.when(phase == this)
            def _():
                for copy in copies(own if at == this else other, at):
                    copy.start()

    arriving = [
        pltpu.make_async_copy(recv_in.at[:, :, at], recv.at[:, :, at], sems.at[2, at])
        for at in range(2)
    ]
    arriving[0].start()
    fetch(0)
    waits = [copies(own, at) for at in range(2)]
    cols = range(0, width, CHUNK)

    def block(which, col):
        half, start = col // part, col % part
        return jnp.concatenate(
            [recv[e, half, which, :, start : start + CHUNK] for e in range(experts)], axis=0
        )

    def inverse_of(ref, mean):
        total = jnp.zeros((tokens, 128), jnp.float32)
        for col in cols:
            center = ref[:, col : col + CHUNK].astype(jnp.float32) - mean
            total = total + lanes(center * center)
        return lax.rsqrt(row_sum(total) / width + EPS)

    def down(ref, mean, inverse, at):
        pre = jnp.zeros((tokens, rank), jnp.float32)
        for col in cols:
            here = slice(col, col + CHUNK)
            normed = (ref[:, here].astype(jnp.float32) - mean) * inverse
            lowered = (normed * gain_buf[at, :, here].astype(jnp.float32)).astype(jnp.bfloat16)
            pre = pre + matmul(lowered, dn_buf[at, here, :])
        return pre

    total = jnp.zeros((tokens, 128), jnp.float32)
    arriving[0].wait()
    for col in cols:
        value = block(0, col)
        entering[:, col : col + CHUNK] = value
        total = total + lanes(value.astype(jnp.float32))
    mean_0 = row_sum(total) / width
    inverse_0 = inverse_of(entering, mean_0)
    waits[0][0].wait()
    waits[0][2].wait()
    arriving[1].start()
    fetch(1)
    pre_0 = down(entering, mean_0, inverse_0, 0)
    act_0 = gelu_value(pre_0).astype(jnp.bfloat16)
    slope_0 = gelu_slope(pre_0)

    waits[0][1].wait()
    total = jnp.zeros((tokens, 128), jnp.float32)
    for col in cols:
        here = slice(col, col + CHUNK)
        value = entering[:, here].astype(jnp.float32) + matmul(act_0, up_buf[0, :, here])
        value = value.astype(jnp.bfloat16)
        middle[:, here] = value
        total = total + lanes(value.astype(jnp.float32))
    mean_1 = row_sum(total) / width
    inverse_1 = inverse_of(middle, mean_1)
    for copy in waits[1] + arriving[1:]:
        copy.wait()
    d_act = jnp.zeros((tokens, rank), jnp.float32)
    for col in cols:
        d_act = d_act + matmul(block(1, col), up_buf[1, :, col : col + CHUNK], TRANS_RHS)
    pre_1 = down(middle, mean_1, inverse_1, 1)
    act_1 = gelu_value(pre_1).astype(jnp.bfloat16)
    d_pre_1 = (d_act * gelu_slope(pre_1)).astype(jnp.bfloat16)

    total = jnp.zeros((tokens, 128), jnp.float32)
    cross = jnp.zeros((tokens, 128), jnp.float32)
    for col in cols:
        here = slice(col, col + CHUNK)
        wide = middle[:, here].astype(jnp.float32)
        d_norm = matmul(d_pre_1, dn_buf[1, here, :], TRANS_RHS)
        d_norm = d_norm * gain_buf[1, :, here].astype(jnp.float32)
        d_norms[:, here] = d_norm
        total = total + lanes(d_norm)
        cross = cross + lanes(d_norm * ((wide - mean_1) * inverse_1))
        leaving = (wide + matmul(act_1, up_buf[1, :, here])).astype(jnp.bfloat16)
        half, start = col // part, col % part
        for e in range(experts):
            out[e, half, :, start : start + CHUNK] = leaving[e * rows : (e + 1) * rows]
    shift = row_sum(total) / width
    along = row_sum(cross) / width
    d_act = jnp.zeros((tokens, rank), jnp.float32)
    for col in cols:
        here = slice(col, col + CHUNK)
        normed = (middle[:, here].astype(jnp.float32) - mean_1) * inverse_1
        grad = block(1, col).astype(jnp.float32) + inverse_1 * (
            d_norms[:, here] - shift - normed * along
        )
        d_act = d_act + matmul(grad.astype(jnp.bfloat16), up_buf[0, :, here], TRANS_RHS)
    d_pre_0 = (d_act * slope_0).astype(jnp.bfloat16)
    moments = (mean_0, inverse_0, mean_1, inverse_1, shift, along)
    kept = (act_0, act_1, d_pre_0, d_pre_1, side_by_side(moments, tokens))
    for e in range(experts):
        start = pl.multiple_of((e ^ lax.axis_index("expert")) * rows, rows)
        for at, value in enumerate(kept):
            cols = slice(at * rank, at * rank + value.shape[1])
            small[pl.ds(start, rows), cols] = value[e * rows : (e + 1) * rows]


def gradient_kernel(experts, sources, sizes, *refs):
    sides, refs = refs[: 2 * experts], refs[2 * experts :]
    smalls, refs = refs[:sources], refs[sources:]
    own, other, refs = refs[:3], refs[3:6], refs[6:]
    ids, back_in, out_hidden, grad_dn, grad_upper = refs[:5]
    (id_buf, back, result, dn_buf, up_buf, gain_buf, wide_buf, small, moments, turned, lows, grads,
     dn_out, up_out, small_sems, wide_sems, sems) = refs[5:]
    core = lax.axis_index("segment")
    place = lax.axis_index("dp")
    rows, slab = smalls[0].shape[0], sides[0].shape[3]
    replicas = sources // 2
    blocks = [side.shape[1] for side in sides[:experts]]
    starts = [sum(blocks[:step]) for step in range(experts)]
    rank = dn_buf.shape[1]
    columns = 256
    chunks = range(0, slab, columns)
    features = pl.ds(pl.multiple_of(place * slab, slab), slab)

    def weight_copies(up, gain_first, dn, gain_second):
        moves = (
            (up.at[:, features], up_buf),
            (gain_first.at[:, features], gain_buf.at[0]),
            (gain_second.at[:, features], gain_buf.at[1]),
            (dn.at[features, :], dn_buf),
        )
        return [
            pltpu.make_async_copy(source, target, sems.at[at])
            for at, (source, target) in enumerate(moves)
        ]

    early = [
        pltpu.make_async_copy(ids, id_buf, sems.at[4]),
        pltpu.make_async_copy(back_in, back, sems.at[5]),
    ]
    small_copies = [
        pltpu.make_async_copy(
            source, small.at[at * rows : (at + 1) * rows], small_sems.at[at]
        )
        for at, source in enumerate(smalls)
    ]
    wide_copies = [
        [
            pltpu.make_async_copy(
                side.at[:, :, :, col : col + columns],
                wide_buf.at[
                    at // experts,
                    :,
                    starts[at % experts] : starts[at % experts] + blocks[at % experts],
                    :,
                    col : col + columns,
                ],
                wide_sems.at[col // columns, at],
            )
            for at, side in enumerate(sides)
        ]
        for col in chunks
    ]
    for copy in early + small_copies:
        copy.start()

    @pl.when(core == 0)
    def _():
        for copy in weight_copies(own[1], own[2], other[0], other[2]):
            copy.start()

    @pl.when(core != 0)
    def _():
        for copy in weight_copies(other[1], other[2], own[0], own[2]):
            copy.start()

    for copies in wide_copies:
        for copy in copies:
            copy.start()
    for copy in early:
        copy.wait()
    unpack(sizes, id_buf, back, result)
    leaving = [pltpu.make_async_copy(result, out_hidden, sems.at[6])]
    leaving[0].start()
    for copy in small_copies + weight_copies(own[1], own[2], other[0], other[2]):
        copy.wait()

    def sliced(source, which, here):
        side, near = source // replicas, source % replicas
        at = [
            replicas - 1 + step if near == 0 else starts[step] + near - 1
            for step in range(experts)
        ]
        return jnp.concatenate([wide_buf[side, which, one, :, here] for one in at], axis=0)

    def moment(at, index):
        value = moments[at, index * 128 : (index + 1) * 128]
        return jnp.concatenate([value] * (columns // 128), axis=1)

    def work(first):
        held = lax.broadcasted_iota(jnp.int32, (128, 6 * 128), 0)
        wanted = lax.broadcasted_iota(jnp.int32, (128, 6 * 128), 1) // 128
        adds = (held // 3 == wanted).astype(jnp.float32).astype(jnp.bfloat16)
        moments[...] = matmul(small[:, 4 * rank :], adds)
        act, d_pre = (0, 2) if first else (1, 3)
        turned[0] = small[:, act * rank : (act + 1) * rank].T
        turned[1] = small[:, d_pre * rank : (d_pre + 1) * rank].T
        for index, col in enumerate(chunks):
            here = slice(col, col + columns)
            for copy in wide_copies[index]:
                copy.wait()
            ups = matmul(small[:, :rank], up_buf[:, here])
            scales = [gain_buf[at, :, here].astype(jnp.float32) for at in range(2)]
            if first:
                downs = matmul(small[:, 3 * rank : 4 * rank], dn_buf[here, :], TRANS_RHS)
            for source in range(sources):
                at = slice(source * rows, (source + 1) * rows)
                wide = sliced(source, 0, here).astype(jnp.float32)
                grad_in = sliced(source, 1, here)
                middle = (wide + ups[at]).astype(jnp.bfloat16).astype(jnp.float32)
                inverse = moment(at, 3)
                normed = (middle - moment(at, 2)) * inverse
                if first:
                    entered = (wide - moment(at, 0)) * moment(at, 1)
                    lows[index, at] = (entered * scales[0]).astype(jnp.bfloat16)
                    d_norm = downs[at] * scales[1]
                    grads[index, at] = (
                        grad_in.astype(jnp.float32)
                        + inverse * (d_norm - moment(at, 4) - normed * moment(at, 5))
                    ).astype(jnp.bfloat16)
                else:
                    lows[index, at] = (normed * scales[1]).astype(jnp.bfloat16)
                    grads[index, at] = grad_in
            dn_out[here, :] = matmul(turned[1], lows[index]).astype(jnp.bfloat16).T
            up_out[index] = matmul(turned[0], grads[index]).astype(jnp.bfloat16)
            for copy in out_copies(index, here):
                copy.start()

    def out_copies(index, here):
        return [
            pltpu.make_async_copy(
                dn_out.at[here, :], grad_dn.at[here, :], sems.at[7 + 2 * index]
            ),
            pltpu.make_async_copy(
                up_out.at[index], grad_upper.at[:, here], sems.at[8 + 2 * index]
            ),
        ]

    @pl.when(core == 0)
    def _():
        work(True)

    @pl.when(core != 0)
    def _():
        work(False)

    for index, col in enumerate(chunks):
        leaving += out_copies(index, slice(col, col + columns))
    for copy in leaving:
        copy.wait()


VMEM = pl.BlockSpec(memory_space=pltpu.VMEM)
HBM = pl.BlockSpec(memory_space=pltpu.HBM)


def call(kernel, name, grant, in_specs, outs, scratch=(), outs_in=VMEM, flops=0, moved=MIB):
    return pl.pallas_call(
        kernel,
        out_shape=tuple(jax.ShapeDtypeStruct(*out) for out in outs),
        in_specs=in_specs,
        out_specs=tuple(outs_in for _ in outs),
        scratch_shapes=list(scratch),
        compiler_params=pltpu.CompilerParams(vmem_limit_bytes=grant * MIB),
        cost_estimate=pl.CostEstimate(flops=flops, bytes_accessed=moved, transcendentals=0),
        name=name,
    )


def across(block, axis, distance):
    size = lax.axis_size(axis)
    return lax.ppermute(block, axis, [(i, i ^ distance) for i in range(size)])


def slab_route(replicas, pair, low):
    route = []
    for replica in range(replicas):
        for core in range(2):
            chip = 2 * core + ((replica & 1) ^ pair)
            route.append((2 * replica + core, 2 * chip + ((replica >> 1) ^ low)))
    return route


def on_device_two_phases(hidden_in, cotangent, cluster_ids, w_down, w_up, gain):
    experts = lax.axis_size("expert")
    replicas = lax.axis_size("dp")
    s_local, length, part = hidden_in.shape
    width = 2 * part
    capacity = 2 * s_local // experts
    slots = experts * capacity
    groups = 2 * experts
    rows = slots * length // groups
    tokens = experts * rows
    own = (w_down[0, 0], w_up[0, 0], gain[0])
    rank = own[0].shape[1]
    slab = width // replicas
    bf16, f32 = jnp.bfloat16, jnp.float32
    sizes = (length, capacity, slots)
    sections = ("expert", "segment")

    other = tuple(across(array, "segment", 1) for array in own)
    half = s_local * length // 2
    (send,) = call(
        functools.partial(pack_kernel, *sizes),
        "pack",
        60,
        [HBM] * 3,
        [((groups, 2, rows, part), bf16)],
        [
            pltpu.SMEM(cluster_ids.shape, jnp.int32),
            pltpu.VMEM((2,) + hidden_in.shape, bf16),
            pltpu.VMEM((groups, 2, rows, part), bf16),
            pltpu.SemaphoreType.DMA((5,)),
        ],
        outs_in=HBM,
    )(cluster_ids, hidden_in, cotangent)
    slabs = call(
        functools.partial(slab_kernel, *sizes),
        "slabs",
        60,
        [HBM] * 4,
        [((2 * half + 16, slab), bf16)] * 4,
        [
            pltpu.SMEM(cluster_ids.shape, jnp.int32),
            pltpu.VMEM((2,) + hidden_in.shape, bf16),
            pltpu.VMEM((2, 2 * half, part), bf16),
            pltpu.VMEM((2, 16, 128), bf16),
            pltpu.VMEM((4, 2 * half + 16, slab), bf16),
            pltpu.SemaphoreType.DMA((7,)),
        ],
        outs_in=HBM,
    )(cluster_ids, hidden_in, cotangent, send)
    recv = lax.all_to_all(send, sections, split_axis=0, concat_axis=0, tiled=True)
    recv = recv.reshape(experts, 2, 2, rows, part)
    slabs = [
        lax.ppermute(block, ("dp", "segment"), slab_route(replicas, turn // 2, turn % 2))
        for turn, block in enumerate(slabs)
    ]
    out, small = call(
        chain_kernel,
        "chain",
        50,
        [HBM] * 7,
        [((experts, 2, rows, part), bf16), ((tokens, 4 * rank + 128), bf16)],
        [
            pltpu.VMEM(recv.shape, bf16),
            pltpu.VMEM((2, width, rank), bf16),
            pltpu.VMEM((2, rank, width), bf16),
            pltpu.VMEM((2, 1, width), bf16),
            pltpu.VMEM((tokens, width), bf16),
            pltpu.VMEM((tokens, width), bf16),
            pltpu.VMEM((tokens, width), f32),
            pltpu.SemaphoreType.DMA((3, 3)),
        ],
        flops=7 * 2 * tokens * width * rank,
        moved=10 * MIB,
    )(recv, *own, *other)
    slices = call(
        functools.partial(repack_kernel, length, capacity),
        "repack",
        16,
        [VMEM] * 4 + [HBM] * 2,
        [((2, replicas - 1 + experts, rows, slab), bf16)]
        + [((2, replicas - 1, rows, slab), bf16)] * (experts - 1),
        [pltpu.SemaphoreType.DMA((experts,))],
    )(*slabs, recv, small)
    small, *slices = lax.optimization_barrier((small, *slices))
    mine = [slices[0]] + [across(slices[step], "expert", step) for step in range(1, experts)]
    mine[:2] = lax.optimization_barrier(tuple(mine[:2]))
    near = [small] + [across(small, "dp", step) for step in range(1, replicas - 1)]
    near[:2] = lax.optimization_barrier(tuple(near[:2]))
    last = across(near[0], "dp", replicas - 1)
    *near, mine[-1] = lax.optimization_barrier((*near, mine[-1]))
    near.append(last)
    theirs = [across(block, "segment", 1) for block in mine]
    swapped = [across(piece, "segment", 1) for piece in near[:-1]]
    near[-1], *rest = lax.optimization_barrier((near[-1], *theirs[1:], *swapped))
    theirs[1:], swapped = rest[: experts - 1], rest[experts - 1 :]
    smalls = near + swapped + [across(near[-1], "segment", 1)]

    back = lax.all_to_all(
        out.reshape(groups, rows, part), sections, split_axis=0, concat_axis=0, tiled=True
    )

    sources = 2 * replicas
    all_tokens = sources * tokens
    out_hidden, grad_dn, grad_upper = call(
        functools.partial(gradient_kernel, experts, sources, sizes),
        "gradients",
        60,
        [HBM] * (2 * experts + sources + 8),
        [(hidden_in.shape, bf16), ((slab, rank), bf16), ((rank, slab), bf16)],
        [
            pltpu.SMEM(cluster_ids.shape, jnp.int32),
            pltpu.VMEM(back.shape, bf16),
            pltpu.VMEM(hidden_in.shape, bf16),
            pltpu.VMEM((slab, rank), bf16),
            pltpu.VMEM((rank, slab), bf16),
            pltpu.VMEM((2, 1, slab), bf16),
            pltpu.VMEM((2, 2, replicas * experts, rows, slab), bf16),
            pltpu.VMEM((all_tokens, 4 * rank + 128), bf16),
            pltpu.VMEM((all_tokens, 6 * 128), f32),
            pltpu.VMEM((2, rank, all_tokens), bf16),
            pltpu.VMEM((slab // 256, all_tokens, 256), bf16),
            pltpu.VMEM((slab // 256, all_tokens, 256), bf16),
            pltpu.VMEM((slab, rank), bf16),
            pltpu.VMEM((slab // 256, rank, 256), bf16),
            pltpu.SemaphoreType.DMA((sources,)),
            pltpu.SemaphoreType.DMA((slab // 256, 2 * experts)),
            pltpu.SemaphoreType.DMA((7 + 2 * (slab // 256),)),
        ],
        outs_in=HBM,
    )(*mine, *theirs, *smalls, *own, *other, cluster_ids, back)
    return (out_hidden, grad_dn[None, None], grad_upper[None, None])


def solution(mesh):
    two = dict(mesh.shape) == {"expert": 4, "dp": 4, "segment": 2}
    on_device = on_device_two_phases if two else on_device_pipelined
    return jax.shard_map(
        on_device,
        mesh=mesh,
        in_specs=(
            P(("expert", "dp"), None, "segment"),
            P(("expert", "dp"), None, "segment"),
            P(("expert", "dp")),
            P("expert", "segment", None, None),
            P("expert", "segment", None, None),
            P("expert", "segment", None),
        ),
        out_specs=(
            P(("expert", "dp"), None, "segment"),
            P("expert", "segment", "dp", None),
            P("expert", "segment", None, "dp"),
        ),
        check_vma=False,
    )
```

```python
import functools

import jax
import jax.numpy as jnp
from jax import lax
from jax.experimental import pallas as pl
from jax.experimental.pallas import tpu as pltpu
from jax.sharding import PartitionSpec as P

MICRO = 4


EPS = 1e-05
C_ZERO = 0.7978845608028654
C_ONE = 0.044715


def shifted(block, axis, distance):
    devices = range(lax.axis_size(axis))
    route = [(i - distance, i) for i in devices if i - distance in devices]
    return lax.ppermute(block, axis, route)


def from_root(block, axis, holder):
    block = jnp.where(lax.axis_index(axis) == holder, block, jnp.zeros_like(block))
    return lax.psum(block, axis)


def gelu_value(z):
    return 0.5 * z * (1.0 + jnp.tanh(C_ZERO * (z + C_ONE * z * z * z)))


def gelu_slope(z):
    tval = jnp.tanh(C_ZERO * (z + C_ONE * z * z * z))
    return 0.5 * (1.0 + tval) + 0.5 * z * (1.0 - tval * tval) * C_ZERO * (1.0 + 3.0 * C_ONE * z * z)


def normalize(hidden):
    wide = hidden.astype(jnp.float32)
    center = wide - jnp.mean(wide, axis=-1, keepdims=True)
    inverse = lax.rsqrt(jnp.mean(center * center, axis=-1, keepdims=True) + EPS)
    return (wide, center * inverse, inverse)


def phase_forward(hidden, w_dn, w_upper, scale):
    wide, normed, inverse = normalize(hidden)
    lowered = (normed * scale).astype(jnp.bfloat16)
    pre = jnp.dot(lowered, w_dn, preferred_element_type=jnp.float32)
    act = gelu_value(pre).astype(jnp.bfloat16)
    leaving = (wide + jnp.dot(act, w_upper, preferred_element_type=jnp.float32)).astype(
        jnp.bfloat16
    )
    return (leaving, pre)


def phase_backward(hidden, grad_in, pre, w_dn, w_upper, scale):
    wide, normed, inverse = normalize(hidden)
    lowered = (normed * scale).astype(jnp.bfloat16)
    act = gelu_value(pre).astype(jnp.bfloat16)
    d_act = jnp.dot(grad_in, w_upper.T, preferred_element_type=jnp.float32)
    d_pre = (d_act * gelu_slope(pre)).astype(jnp.bfloat16)
    d_low = jnp.dot(d_pre, w_dn.T, preferred_element_type=jnp.float32)
    d_norm = d_low * scale
    d_wide = inverse * (
        d_norm
        - jnp.mean(d_norm, axis=-1, keepdims=True)
        - normed * jnp.mean(d_norm * normed, axis=-1, keepdims=True)
    )
    grad_out = (grad_in.astype(jnp.float32) + d_wide).astype(jnp.bfloat16)
    return (grad_out, lowered, act, d_pre)


def put_slot(buffer, value, slot, valid):
    old_value = lax.dynamic_index_in_dim(buffer, slot, 0, keepdims=False)
    return lax.dynamic_update_index_in_dim(buffer, jnp.where(valid, value, old_value), slot, 0)


def on_device_pipelined(hidden_in, cotangent, cluster_ids, w_down, w_up, gain):
    experts = lax.axis_size("expert")
    phases = lax.axis_size("segment")
    phase = lax.axis_index("segment")
    s_local, length, quarter = hidden_in.shape
    capacity = 2 * s_local // experts
    slots = experts * capacity
    same = (cluster_ids[:, None] == cluster_ids[None, :]).astype(jnp.int32)
    earlier = jnp.sum(jnp.tril(same, -1), axis=1)
    target = cluster_ids * capacity + earlier
    place = (jnp.arange(slots, dtype=jnp.int32)[:, None] == target[None, :]).astype(jnp.bfloat16)

    def to_slots(local):
        flat = local.reshape(s_local, -1)
        moved = jnp.dot(place, flat, preferred_element_type=jnp.float32).astype(jnp.bfloat16)
        return moved.reshape((slots,) + local.shape[1:])

    full_in, full_cot = (
        lax.all_gather(hidden_in, "segment", axis=2, tiled=True),
        lax.all_gather(cotangent, "segment", axis=2, tiled=True),
    )
    slot_in, slot_cot = (
        lax.all_to_all(to_slots(full_in), "expert", split_axis=0, concat_axis=0, tiled=True),
        lax.all_to_all(to_slots(full_cot), "expert", split_axis=0, concat_axis=0, tiled=True),
    )
    width = slot_in.shape[2]
    micro_rows = slots * length // MICRO
    inputs = slot_in.reshape(MICRO, micro_rows, width)
    cots = slot_cot.reshape(MICRO, micro_rows, width)
    w_dn = w_down[0, 0]
    w_upper = w_up[0, 0]
    rank = w_dn.shape[1]
    scale = gain[0, 0].astype(jnp.float32)
    ticks = MICRO + phases - 1

    def forward_tick(tick, carry):
        received, saved, pres, results = carry
        which = tick - phase
        valid = (which >= 0) & (which < MICRO)
        slot = jnp.clip(which, 0, MICRO - 1)
        first = lax.dynamic_index_in_dim(inputs, jnp.minimum(tick, MICRO - 1), 0, keepdims=False)
        entering = jnp.where(phase == 0, first, received)
        leaving, pre = phase_forward(entering, w_dn, w_upper, scale)
        saved = put_slot(saved, entering, slot, valid)
        pres = put_slot(pres, pre, slot, valid)
        results = put_slot(results, leaving, slot, valid & (phase == phases - 1))
        received = shifted(leaving, "segment", 1)
        return (received, saved, pres, results)

    start = (
        jnp.zeros((micro_rows, width), jnp.bfloat16),
        jnp.zeros((MICRO, micro_rows, width), jnp.bfloat16),
        jnp.zeros((MICRO, micro_rows, rank), jnp.float32),
        jnp.zeros((MICRO, micro_rows, width), jnp.bfloat16),
    )
    received, saved, pres, results = lax.fori_loop(0, ticks, forward_tick, start)

    def backward_tick(tick, carry):
        received, lows, acts, dpres, grads = carry
        which = tick - (phases - 1 - phase)
        valid = (which >= 0) & (which < MICRO)
        slot = jnp.clip(which, 0, MICRO - 1)
        last = lax.dynamic_index_in_dim(cots, jnp.minimum(tick, MICRO - 1), 0, keepdims=False)
        grad_in = jnp.where(phase == phases - 1, last, received)
        hidden = lax.dynamic_index_in_dim(saved, slot, 0, keepdims=False)
        pre = lax.dynamic_index_in_dim(pres, slot, 0, keepdims=False)
        grad_out, lowered, act, d_pre = phase_backward(hidden, grad_in, pre, w_dn, w_upper, scale)
        lows = put_slot(lows, lowered, slot, valid)
        acts = put_slot(acts, act, slot, valid)
        dpres = put_slot(dpres, d_pre, slot, valid)
        grads = put_slot(grads, grad_in, slot, valid)
        received = shifted(grad_out, "segment", -1)
        return (received, lows, acts, dpres, grads)

    start_back = (
        jnp.zeros((micro_rows, width), jnp.bfloat16),
        jnp.zeros((MICRO, micro_rows, width), jnp.bfloat16),
        jnp.zeros((MICRO, micro_rows, rank), jnp.bfloat16),
        jnp.zeros((MICRO, micro_rows, rank), jnp.bfloat16),
        jnp.zeros((MICRO, micro_rows, width), jnp.bfloat16),
    )
    received, lows, acts, dpres, grads = lax.fori_loop(0, ticks, backward_tick, start_back)
    contract = (((0,), (0,)), ((), ()))
    grad_dn = lax.dot_general(
        lows.reshape(-1, width),
        dpres.reshape(-1, rank),
        contract,
        preferred_element_type=jnp.float32,
    )
    grad_upper = lax.dot_general(
        acts.reshape(-1, rank),
        grads.reshape(-1, width),
        contract,
        preferred_element_type=jnp.float32,
    )
    summed_dn, summed_upper = (
        lax.psum_scatter(
            grad_dn.astype(jnp.bfloat16), "dp", scatter_dimension=0, tiled=True
        ).astype(jnp.float32),
        lax.psum_scatter(
            grad_upper.astype(jnp.bfloat16), "dp", scatter_dimension=1, tiled=True
        ).astype(jnp.float32),
    )
    returned = from_root(results, "segment", phases - 1)
    returned = returned.reshape(slots, length, width)
    own = lax.dynamic_slice_in_dim(returned, phase * quarter, quarter, 2)
    back = lax.all_to_all(own, "expert", split_axis=0, concat_axis=0, tiled=True)
    out_hidden = jnp.dot(place.T, back.reshape(slots, -1), preferred_element_type=jnp.float32)
    out_hidden = out_hidden.astype(jnp.bfloat16).reshape(s_local, length, quarter)
    return (
        out_hidden,
        summed_dn.astype(jnp.bfloat16)[None, None],
        summed_upper.astype(jnp.bfloat16)[None, None],
    )


CHUNK = 512
MIB = 1024 * 1024
TRANS_RHS = (((1,), (1,)), ((), ()))
TRANS_LHS = (((0,), (0,)), ((), ()))


def matmul(left, right, dims=(((1,), (0,)), ((), ()))):
    return lax.dot_general(left, right, dims, preferred_element_type=jnp.float32)


def spread_ids(ids, shape, length):
    lane = lax.broadcasted_iota(jnp.int32, shape, 1)
    spread = jnp.zeros(shape, jnp.int32)
    for n in range(ids.shape[0]):
        spread = jnp.where(lane // length == n, ids[n], spread)
    return spread


def ranked(ids_row, length):
    tokens = ids_row.shape[1]
    kinds = lax.broadcasted_iota(jnp.int32, (8, tokens), 0)
    member = (kinds == ids_row).astype(jnp.float32)
    at_col = lax.broadcasted_iota(jnp.int32, (tokens, tokens), 0)
    at_row = lax.broadcasted_iota(jnp.int32, (tokens, tokens), 1)
    before = (lax.rem(at_col, length) == 0) & (at_col // length < at_row // length)
    counts = matmul(member.astype(jnp.bfloat16), before.astype(jnp.float32).astype(jnp.bfloat16))
    rank = jnp.sum(member * counts, axis=0, keepdims=True)
    total = jnp.sum(member, axis=1, keepdims=True) * (1.0 / length)
    lower = jnp.sum(jnp.where(kinds < ids_row, total, 0.0), axis=0, keepdims=True)
    return rank.astype(jnp.int32), lower.astype(jnp.int32)


def one_hot(target, rows):
    wanted = lax.broadcasted_iota(jnp.int32, (rows, target.shape[1]), 0)
    return (wanted == target).astype(jnp.float32).astype(jnp.bfloat16)


def placements(ids_row, length, capacity, slots):
    rank, lower = ranked(ids_row, length)
    token = lax.rem(lax.broadcasted_iota(jnp.int32, ids_row.shape, 1), length)
    place = rank + lower
    group = lax.rem(place, 2)
    per_core = capacity // 2
    packed = ((ids_row * 2 + group) * per_core + rank // 2) * length + token
    tokens = ids_row.shape[1]
    ordered = group * (tokens // 2) + (place // 2) * length + token
    return one_hot(packed, slots * length), one_hot(ordered, tokens)


def pack_kernel(length, capacity, slots, ids, hidden, cot, send, id_buf, buf, packed, sems):
    groups, _, rows, part = send.shape
    tokens = hidden.shape[0] * length
    arriving = [
        pltpu.make_async_copy(source, target, sems.at[at])
        for at, (source, target) in enumerate(
            ((ids, id_buf), (hidden, buf.at[0]), (cot, buf.at[1]))
        )
    ]
    leaving = [
        pltpu.make_async_copy(packed.at[:, at], send.at[:, at], sems.at[3 + at]) for at in range(2)
    ]
    for copy in arriving:
        copy.start()
    arriving[0].wait()
    ids_row = spread_ids(id_buf, (8, tokens), length)[:1]
    place, _ = placements(ids_row, length, capacity, slots)
    for which in range(2):
        arriving[1 + which].wait()
        moved = matmul(place, buf[which].reshape(tokens, part)).astype(jnp.bfloat16)
        for group in range(groups):
            packed[group, which] = moved[group * rows : (group + 1) * rows]
        leaving[which].start()
    for copy in leaving:
        copy.wait()


def slab_kernel(length, capacity, slots, ids, hidden, cot, _, *refs):
    slabs, refs = refs[:4], refs[4:]
    id_buf, buf, ordered, turned, out_slabs, sems = refs
    s_local, _, part = hidden.shape
    tokens = s_local * length
    slab = part // 2
    half = tokens // 2
    replica = lax.axis_index("dp")
    arriving = [
        pltpu.make_async_copy(source, target, sems.at[at])
        for at, (source, target) in enumerate(
            ((ids, id_buf), (hidden, buf.at[0]), (cot, buf.at[1]))
        )
    ]
    leaving = [
        pltpu.make_async_copy(out_slabs.at[at], slabs[at], sems.at[3 + at]) for at in range(4)
    ]
    for copy in arriving:
        copy.start()
    arriving[0].wait()
    ids_row = spread_ids(id_buf, (16, tokens), length)
    _, by_group = placements(ids_row[:1], length, capacity, slots)
    for group in range(2):
        mine = by_group[group * half : (group + 1) * half]
        clusters = matmul(ids_row.astype(jnp.float32).astype(jnp.bfloat16), mine, TRANS_RHS)
        turned[group] = jnp.concatenate(
            [clusters.astype(jnp.bfloat16), jnp.zeros((16, 128 - half), jnp.bfloat16)], axis=1
        )
    for which in range(2):
        arriving[1 + which].wait()
        flat = buf[which].reshape(tokens, part)
        ordered[which] = matmul(by_group, flat).astype(jnp.bfloat16)
    for turn in range(4):
        pair = (turn // 2) ^ (replica & 1)
        group = (turn % 2) ^ (replica >> 1)
        cols = pl.ds(pl.multiple_of(pair * slab, slab), slab)
        at = pl.ds(pl.multiple_of(group * half, half), half)
        for which in range(2):
            out_slabs[turn, which * half : (which + 1) * half] = ordered[which, at, cols]
        out_slabs[turn, tokens:] = jnp.zeros((16, slab), jnp.bfloat16)
        out_slabs[turn, tokens:, :128] = turned[group]
        leaving[turn].start()
    for copy in leaving:
        copy.wait()


def repack_kernel(length, capacity, *refs):
    slabs, recv, outs, sems = refs[:4], refs[4], refs[6:-1], refs[-1]
    kept, sent = outs[0], outs[1:]
    _, _, rows, slab = kept.shape
    experts = len(outs)
    half = (slabs[0].shape[0] - 16) // 2
    core, replica = lax.axis_index("segment"), lax.axis_index("dp")
    expert = lax.axis_index("expert")
    per_part = recv.shape[4] // slab
    part = replica // per_part
    cols = pl.ds(pl.multiple_of((replica - part * per_part) * slab, slab), slab)
    cuts = [
        pltpu.make_async_copy(
            recv.at[e, part, :, :, cols], kept.at[:, 3 + (e ^ expert)], sems.at[e]
        )
        for e in range(experts)
    ]
    for cut in cuts:
        cut.start()
    far_low = (replica >> 1) ^ core ^ 1

    def place_rows(held, near):
        ids_row = held[2 * half :, :128].astype(jnp.float32)[:1, :half].astype(jnp.int32)
        rank, _ = ranked(ids_row, length)
        token = lax.rem(lax.broadcasted_iota(jnp.int32, ids_row.shape, 1), length)
        step = ids_row ^ expert
        place = one_hot((step * (capacity // 2) + rank) * length + token, experts * rows)
        for which in range(2):
            moved = matmul(place, held[which * half : (which + 1) * half]).astype(jnp.bfloat16)
            kept[which, near - 1] = moved[:rows]
            for step_at, out in enumerate(sent):
                out[which, near - 1] = moved[(step_at + 1) * rows : (step_at + 2) * rows]

    place_rows(jnp.where(far_low == 1, slabs[1][...], slabs[0][...]), 2)
    for low in range(2):
        place_rows(slabs[2 + low][...], 1 + 2 * (low ^ (replica >> 1) ^ core))
    for cut in cuts:
        cut.wait()


def unpack(sizes, id_buf, back, out):
    length, capacity, slots = sizes
    groups, rows, width = back.shape
    s_local = out.shape[0]
    ids_row = spread_ids(id_buf, (8, s_local * length), length)[:1]
    place, _ = placements(ids_row, length, capacity, slots)
    moved = matmul(place, back[...].reshape(groups * rows, width), TRANS_LHS)
    out[...] = moved.astype(jnp.bfloat16).reshape(s_local, length, width)


def split_three(value):
    top = value.astype(jnp.bfloat16).astype(jnp.float32)
    mid = (value - top).astype(jnp.bfloat16).astype(jnp.float32)
    low = (value - top - mid).astype(jnp.bfloat16).astype(jnp.float32)
    return [top, mid, low]


def side_by_side(columns, tokens):
    lane = lax.broadcasted_iota(jnp.int32, (tokens, 128), 1)
    block = jnp.zeros((tokens, 128), jnp.float32)
    at = 0
    for column in columns:
        for piece in split_three(column):
            block = jnp.where(lane == at, piece, block)
            at += 1
    return block.astype(jnp.bfloat16)


def lanes(value):
    total = value[:, :128]
    for start in range(128, value.shape[1], 128):
        total = total + value[:, start : start + 128]
    return total


def row_sum(parts):
    return jnp.sum(parts, axis=1, keepdims=True)


def chain_kernel(
    recv_in, own_dn, own_up, own_gain, other_dn, other_up, other_gain,
    out, small,
    recv, dn_buf, up_buf, gain_buf, entering, middle, d_norms, sems,
):
    phase = lax.axis_index("segment")
    experts, phases, _, rows, part = recv.shape
    tokens = experts * rows
    width = phases * part
    rank = dn_buf.shape[2]
    own, other = (own_dn, own_up, own_gain), (other_dn, other_up, other_gain)

    def copies(sources, at):
        return [
            pltpu.make_async_copy(source, buffer.at[at], sems.at[at, which])
            for which, (source, buffer) in enumerate(zip(sources, (dn_buf, up_buf, gain_buf)))
        ]

    def fetch(at):
        for this in range(2):

            @pl.when(phase == this)
            def _():
                for copy in copies(own if at == this else other, at):
                    copy.start()

    arriving = [
        pltpu.make_async_copy(recv_in.at[:, :, at], recv.at[:, :, at], sems.at[2, at])
        for at in range(2)
    ]
    arriving[0].start()
    fetch(0)
    waits = [copies(own, at) for at in range(2)]
    cols = range(0, width, CHUNK)

    def block(which, col):
        half, start = col // part, col % part
        return jnp.concatenate(
            [recv[e, half, which, :, start : start + CHUNK] for e in range(experts)], axis=0
        )

    def inverse_of(ref, mean):
        total = jnp.zeros((tokens, 128), jnp.float32)
        for col in cols:
            center = ref[:, col : col + CHUNK].astype(jnp.float32) - mean
            total = total + lanes(center * center)
        return lax.rsqrt(row_sum(total) / width + EPS)

    def down(ref, mean, inverse, at):
        pre = jnp.zeros((tokens, rank), jnp.float32)
        for col in cols:
            here = slice(col, col + CHUNK)
            normed = (ref[:, here].astype(jnp.float32) - mean) * inverse
            lowered = (normed * gain_buf[at, :, here].astype(jnp.float32)).astype(jnp.bfloat16)
            pre = pre + matmul(lowered, dn_buf[at, here, :])
        return pre

    total = jnp.zeros((tokens, 128), jnp.float32)
    arriving[0].wait()
    for col in cols:
        value = block(0, col)
        entering[:, col : col + CHUNK] = value
        total = total + lanes(value.astype(jnp.float32))
    mean_0 = row_sum(total) / width
    inverse_0 = inverse_of(entering, mean_0)
    waits[0][0].wait()
    waits[0][2].wait()
    arriving[1].start()
    fetch(1)
    pre_0 = down(entering, mean_0, inverse_0, 0)
    act_0 = gelu_value(pre_0).astype(jnp.bfloat16)
    slope_0 = gelu_slope(pre_0)

    waits[0][1].wait()
    total = jnp.zeros((tokens, 128), jnp.float32)
    for col in cols:
        here = slice(col, col + CHUNK)
        value = entering[:, here].astype(jnp.float32) + matmul(act_0, up_buf[0, :, here])
        value = value.astype(jnp.bfloat16)
        middle[:, here] = value
        total = total + lanes(value.astype(jnp.float32))
    mean_1 = row_sum(total) / width
    inverse_1 = inverse_of(middle, mean_1)
    for copy in waits[1] + arriving[1:]:
        copy.wait()
    d_act = jnp.zeros((tokens, rank), jnp.float32)
    for col in cols:
        d_act = d_act + matmul(block(1, col), up_buf[1, :, col : col + CHUNK], TRANS_RHS)
    pre_1 = down(middle, mean_1, inverse_1, 1)
    act_1 = gelu_value(pre_1).astype(jnp.bfloat16)
    d_pre_1 = (d_act * gelu_slope(pre_1)).astype(jnp.bfloat16)

    total = jnp.zeros((tokens, 128), jnp.float32)
    cross = jnp.zeros((tokens, 128), jnp.float32)
    for col in cols:
        here = slice(col, col + CHUNK)
        wide = middle[:, here].astype(jnp.float32)
        d_norm = matmul(d_pre_1, dn_buf[1, here, :], TRANS_RHS)
        d_norm = d_norm * gain_buf[1, :, here].astype(jnp.float32)
        d_norms[:, here] = d_norm
        total = total + lanes(d_norm)
        cross = cross + lanes(d_norm * ((wide - mean_1) * inverse_1))
        leaving = (wide + matmul(act_1, up_buf[1, :, here])).astype(jnp.bfloat16)
        half, start = col // part, col % part
        for e in range(experts):
            out[e, half, :, start : start + CHUNK] = leaving[e * rows : (e + 1) * rows]
    shift = row_sum(total) / width
    along = row_sum(cross) / width
    d_act = jnp.zeros((tokens, rank), jnp.float32)
    for col in cols:
        here = slice(col, col + CHUNK)
        normed = (middle[:, here].astype(jnp.float32) - mean_1) * inverse_1
        grad = block(1, col).astype(jnp.float32) + inverse_1 * (
            d_norms[:, here] - shift - normed * along
        )
        d_act = d_act + matmul(grad.astype(jnp.bfloat16), up_buf[0, :, here], TRANS_RHS)
    d_pre_0 = (d_act * slope_0).astype(jnp.bfloat16)
    moments = (mean_0, inverse_0, mean_1, inverse_1, shift, along)
    kept = (act_0, act_1, d_pre_0, d_pre_1, side_by_side(moments, tokens))
    for e in range(experts):
        start = pl.multiple_of((e ^ lax.axis_index("expert")) * rows, rows)
        for at, value in enumerate(kept):
            cols = slice(at * rank, at * rank + value.shape[1])
            small[pl.ds(start, rows), cols] = value[e * rows : (e + 1) * rows]


def stack_kernel(*refs):
    at = 0
    for block in refs[:-1]:
        refs[-1][:, at : at + block.shape[1]] = block[...]
        at += block.shape[1]


def gradient_kernel(experts, sources, sizes, *refs):
    sides, refs = refs[:2], refs[2:]
    smalls, refs = refs[:sources], refs[sources:]
    own, other, refs = refs[:3], refs[3:6], refs[6:]
    ids, back_in, out_hidden, grad_dn, grad_upper = refs[:5]
    (id_buf, back, result, dn_buf, up_buf, gain_buf, wide_buf, small, moments, turned, lows, grads,
     dn_out, up_out, small_sems, wide_sems, sems) = refs[5:]
    core = lax.axis_index("segment")
    place = lax.axis_index("dp")
    rows, slab = smalls[0].shape[0], sides[0].shape[3]
    replicas = sources // 2
    others = replicas - 1
    starts = [0] + [experts + step * others for step in range(1, experts)]
    rank = dn_buf.shape[1]
    columns = 256
    chunks = range(0, slab, columns)
    features = pl.ds(pl.multiple_of(place * slab, slab), slab)

    def weight_copies(up, gain_first, dn, gain_second):
        moves = (
            (up.at[:, features], up_buf),
            (gain_first.at[:, features], gain_buf.at[0]),
            (gain_second.at[:, features], gain_buf.at[1]),
            (dn.at[features, :], dn_buf),
        )
        return [
            pltpu.make_async_copy(source, target, sems.at[at])
            for at, (source, target) in enumerate(moves)
        ]

    early = [
        pltpu.make_async_copy(ids, id_buf, sems.at[4]),
        pltpu.make_async_copy(back_in, back, sems.at[5]),
    ]
    small_copies = [
        pltpu.make_async_copy(
            source, small.at[at * rows : (at + 1) * rows], small_sems.at[at]
        )
        for at, source in enumerate(smalls)
    ]
    wide_copies = [
        [
            pltpu.make_async_copy(
                side.at[:, :, :, col : col + columns],
                wide_buf.at[at, :, :, :, col : col + columns],
                wide_sems.at[col // columns, at],
            )
            for at, side in enumerate(sides)
        ]
        for col in chunks
    ]
    for copy in early + small_copies:
        copy.start()

    @pl.when(core == 0)
    def _():
        for copy in weight_copies(own[1], own[2], other[0], other[2]):
            copy.start()

    @pl.when(core != 0)
    def _():
        for copy in weight_copies(other[1], other[2], own[0], own[2]):
            copy.start()

    for copies in wide_copies:
        for copy in copies:
            copy.start()
    for copy in early:
        copy.wait()
    unpack(sizes, id_buf, back, result)
    leaving = [pltpu.make_async_copy(result, out_hidden, sems.at[6])]
    leaving[0].start()
    for copy in small_copies + weight_copies(own[1], own[2], other[0], other[2]):
        copy.wait()

    def sliced(source, which, here):
        side, near = source // replicas, source % replicas
        at = [
            replicas - 1 + step if near == 0 else starts[step] + near - 1
            for step in range(experts)
        ]
        return jnp.concatenate([wide_buf[side, which, one, :, here] for one in at], axis=0)

    def moment(at, index):
        value = moments[at, index * 128 : (index + 1) * 128]
        return jnp.concatenate([value] * (columns // 128), axis=1)

    def work(first):
        held = lax.broadcasted_iota(jnp.int32, (128, 6 * 128), 0)
        wanted = lax.broadcasted_iota(jnp.int32, (128, 6 * 128), 1) // 128
        adds = (held // 3 == wanted).astype(jnp.float32).astype(jnp.bfloat16)
        moments[...] = matmul(small[:, 4 * rank :], adds)
        act, d_pre = (0, 2) if first else (1, 3)
        turned[0] = small[:, act * rank : (act + 1) * rank].T
        turned[1] = small[:, d_pre * rank : (d_pre + 1) * rank].T
        for index, col in enumerate(chunks):
            here = slice(col, col + columns)
            for copy in wide_copies[index]:
                copy.wait()
            ups = matmul(small[:, :rank], up_buf[:, here])
            scales = [gain_buf[at, :, here].astype(jnp.float32) for at in range(2)]
            if first:
                downs = matmul(small[:, 3 * rank : 4 * rank], dn_buf[here, :], TRANS_RHS)
            for source in range(sources):
                at = slice(source * rows, (source + 1) * rows)
                wide = sliced(source, 0, here).astype(jnp.float32)
                grad_in = sliced(source, 1, here)
                middle = (wide + ups[at]).astype(jnp.bfloat16).astype(jnp.float32)
                inverse = moment(at, 3)
                normed = (middle - moment(at, 2)) * inverse
                if first:
                    entered = (wide - moment(at, 0)) * moment(at, 1)
                    lows[index, at] = (entered * scales[0]).astype(jnp.bfloat16)
                    d_norm = downs[at] * scales[1]
                    grads[index, at] = (
                        grad_in.astype(jnp.float32)
                        + inverse * (d_norm - moment(at, 4) - normed * moment(at, 5))
                    ).astype(jnp.bfloat16)
                else:
                    lows[index, at] = (normed * scales[1]).astype(jnp.bfloat16)
                    grads[index, at] = grad_in
            dn_out[here, :] = matmul(turned[1], lows[index]).astype(jnp.bfloat16).T
            up_out[index] = matmul(turned[0], grads[index]).astype(jnp.bfloat16)
            for copy in out_copies(index, here):
                copy.start()

    def out_copies(index, here):
        return [
            pltpu.make_async_copy(
                dn_out.at[here, :], grad_dn.at[here, :], sems.at[7 + 2 * index]
            ),
            pltpu.make_async_copy(
                up_out.at[index], grad_upper.at[:, here], sems.at[8 + 2 * index]
            ),
        ]

    @pl.when(core == 0)
    def _():
        work(True)

    @pl.when(core != 0)
    def _():
        work(False)

    for index, col in enumerate(chunks):
        leaving += out_copies(index, slice(col, col + columns))
    for copy in leaving:
        copy.wait()


VMEM = pl.BlockSpec(memory_space=pltpu.VMEM)
HBM = pl.BlockSpec(memory_space=pltpu.HBM)


def call(kernel, name, grant, in_specs, outs, scratch=(), outs_in=VMEM, flops=0, moved=MIB):
    return pl.pallas_call(
        kernel,
        out_shape=tuple(jax.ShapeDtypeStruct(*out) for out in outs),
        in_specs=in_specs,
        out_specs=tuple(outs_in for _ in outs),
        scratch_shapes=list(scratch),
        compiler_params=pltpu.CompilerParams(vmem_limit_bytes=grant * MIB),
        cost_estimate=pl.CostEstimate(flops=flops, bytes_accessed=moved, transcendentals=0),
        name=name,
    )


def across(block, axis, distance):
    size = lax.axis_size(axis)
    return lax.ppermute(block, axis, [(i, i ^ distance) for i in range(size)])


def slab_route(replicas, pair, low):
    route = []
    for replica in range(replicas):
        for core in range(2):
            chip = 2 * core + ((replica & 1) ^ pair)
            route.append((2 * replica + core, 2 * chip + ((replica >> 1) ^ low)))
    return route


def on_device_two_phases(hidden_in, cotangent, cluster_ids, w_down, w_up, gain):
    experts = lax.axis_size("expert")
    replicas = lax.axis_size("dp")
    s_local, length, part = hidden_in.shape
    width = 2 * part
    capacity = 2 * s_local // experts
    slots = experts * capacity
    groups = 2 * experts
    rows = slots * length // groups
    tokens = experts * rows
    own = (w_down[0, 0], w_up[0, 0], gain[0])
    rank = own[0].shape[1]
    slab = width // replicas
    bf16, f32 = jnp.bfloat16, jnp.float32
    sizes = (length, capacity, slots)
    sections = ("expert", "segment")

    other = tuple(across(array, "segment", 1) for array in own)
    half = s_local * length // 2
    (send,) = call(
        functools.partial(pack_kernel, *sizes),
        "pack",
        60,
        [HBM] * 3,
        [((groups, 2, rows, part), bf16)],
        [
            pltpu.SMEM(cluster_ids.shape, jnp.int32),
            pltpu.VMEM((2,) + hidden_in.shape, bf16),
            pltpu.VMEM((groups, 2, rows, part), bf16),
            pltpu.SemaphoreType.DMA((5,)),
        ],
        outs_in=HBM,
    )(cluster_ids, hidden_in, cotangent)
    slabs = call(
        functools.partial(slab_kernel, *sizes),
        "slabs",
        60,
        [HBM] * 4,
        [((2 * half + 16, slab), bf16)] * 4,
        [
            pltpu.SMEM(cluster_ids.shape, jnp.int32),
            pltpu.VMEM((2,) + hidden_in.shape, bf16),
            pltpu.VMEM((2, 2 * half, part), bf16),
            pltpu.VMEM((2, 16, 128), bf16),
            pltpu.VMEM((4, 2 * half + 16, slab), bf16),
            pltpu.SemaphoreType.DMA((7,)),
        ],
        outs_in=HBM,
    )(cluster_ids, hidden_in, cotangent, send)
    recv = lax.all_to_all(send, sections, split_axis=0, concat_axis=0, tiled=True)
    recv = recv.reshape(experts, 2, 2, rows, part)
    slabs = [
        lax.ppermute(block, ("dp", "segment"), slab_route(replicas, turn // 2, turn % 2))
        for turn, block in enumerate(slabs)
    ]
    out, small = call(
        chain_kernel,
        "chain",
        50,
        [HBM] * 7,
        [((experts, 2, rows, part), bf16), ((tokens, 4 * rank + 128), bf16)],
        [
            pltpu.VMEM(recv.shape, bf16),
            pltpu.VMEM((2, width, rank), bf16),
            pltpu.VMEM((2, rank, width), bf16),
            pltpu.VMEM((2, 1, width), bf16),
            pltpu.VMEM((tokens, width), bf16),
            pltpu.VMEM((tokens, width), bf16),
            pltpu.VMEM((tokens, width), f32),
            pltpu.SemaphoreType.DMA((3, 3)),
        ],
        flops=7 * 2 * tokens * width * rank,
        moved=10 * MIB,
    )(recv, *own, *other)
    slices = call(
        functools.partial(repack_kernel, length, capacity),
        "repack",
        16,
        [VMEM] * 4 + [HBM] * 2,
        [((2, replicas - 1 + experts, rows, slab), bf16)]
        + [((2, replicas - 1, rows, slab), bf16)] * (experts - 1),
        [pltpu.SemaphoreType.DMA((experts,))],
    )(*slabs, recv, small)
    small, *slices = lax.optimization_barrier((small, *slices))
    mine = [slices[0]] + [across(slices[step], "expert", step) for step in range(1, experts)]
    near = [small] + [across(small, "dp", step) for step in range(1, replicas - 1)]
    near[:2] = lax.optimization_barrier(tuple(near[:2]))
    last = across(near[0], "dp", replicas - 1)
    (stacked,) = call(
        stack_kernel,
        "stack",
        16,
        [VMEM] * experts,
        [((2, replicas * experts, rows, slab), bf16)],
    )(*mine)
    *near, stacked = lax.optimization_barrier((*near, stacked))
    near.append(last)
    theirs = across(stacked, "segment", 1)
    smalls = near + [across(piece, "segment", 1) for piece in near]

    back = lax.all_to_all(
        out.reshape(groups, rows, part), sections, split_axis=0, concat_axis=0, tiled=True
    )

    sources = 2 * replicas
    all_tokens = sources * tokens
    out_hidden, grad_dn, grad_upper = call(
        functools.partial(gradient_kernel, experts, sources, sizes),
        "gradients",
        60,
        [HBM] * (2 + sources + 8),
        [(hidden_in.shape, bf16), ((slab, rank), bf16), ((rank, slab), bf16)],
        [
            pltpu.SMEM(cluster_ids.shape, jnp.int32),
            pltpu.VMEM(back.shape, bf16),
            pltpu.VMEM(hidden_in.shape, bf16),
            pltpu.VMEM((slab, rank), bf16),
            pltpu.VMEM((rank, slab), bf16),
            pltpu.VMEM((2, 1, slab), bf16),
            pltpu.VMEM((2, 2, replicas * experts, rows, slab), bf16),
            pltpu.VMEM((all_tokens, 4 * rank + 128), bf16),
            pltpu.VMEM((all_tokens, 6 * 128), f32),
            pltpu.VMEM((2, rank, all_tokens), bf16),
            pltpu.VMEM((slab // 256, all_tokens, 256), bf16),
            pltpu.VMEM((slab // 256, all_tokens, 256), bf16),
            pltpu.VMEM((slab, rank), bf16),
            pltpu.VMEM((slab // 256, rank, 256), bf16),
            pltpu.SemaphoreType.DMA((sources,)),
            pltpu.SemaphoreType.DMA((slab // 256, 2)),
            pltpu.SemaphoreType.DMA((7 + 2 * (slab // 256),)),
        ],
        outs_in=HBM,
    )(stacked, theirs, *smalls, *own, *other, cluster_ids, back)
    return (out_hidden, grad_dn[None, None], grad_upper[None, None])


def solution(mesh):
    two = dict(mesh.shape) == {"expert": 4, "dp": 4, "segment": 2}
    on_device = on_device_two_phases if two else on_device_pipelined
    return jax.shard_map(
        on_device,
        mesh=mesh,
        in_specs=(
            P(("expert", "dp"), None, "segment"),
            P(("expert", "dp"), None, "segment"),
            P(("expert", "dp")),
            P("expert", "segment", None, None),
            P("expert", "segment", None, None),
            P("expert", "segment", None),
        ),
        out_specs=(
            P(("expert", "dp"), None, "segment"),
            P("expert", "segment", "dp", None),
            P("expert", "segment", None, "dp"),
        ),
        check_vma=False,
    )
```
